32 devices in a mesh: dp: 2 (over x), row: 4 (over y, core), col: 4 (over z).
Axes of the slice: x: 2, y: 2, z: 4, core: 2. Of those that a mesh axis runs over, the one named last changes fastest.
Arguments:
- tokens: bfloat16 [20, 32, 32, 768], P('dp', 'row', 'col')
- cot_tokens: bfloat16 [20, 32, 32, 768], P('dp', 'row', 'col'), may hold values from -6 to 6
- cot_merged: bfloat16 [20, 64, 64, 256], P('dp', 'row', 'col'), may hold values from -6 to 6
- image_counts: int32 [2], P('dp'), may hold values from 5 to 10, as said below
- scale_flags: int32 [20], P('dp'), may hold values from 0 to 3
- shift_flags: int32 [20], P('dp'), may hold values from -1 to 1
- qkv_w: float32 [768, 2304], P('dp'), may hold values from -0.21875 to 0.21875
- attn_out_w: float32 [768, 768], P('dp'), may hold values from -2.5 to 2.5
- fc1_w: float32 [768, 3072], P('dp'), may hold values from -0.21875 to 0.21875
- fc1_b: float32 [3072], P('dp'), may hold values from -3 to 3
- fc2_w: float32 [3072, 768], P('dp'), may hold values from -0.109375 to 0.109375
- fc2_b: float32 [768], P('dp'), may hold values from -2 to 2
- ln1_gain: float32 [768], P('dp'), may hold values from 0.25 to 1.75
- ln1_bias: float32 [768], P('dp'), may hold values from -2 to 2
- ln2_gain: float32 [768], P('dp'), may hold values from 0.25 to 1.75
- ln2_bias: float32 [768], P('dp'), may hold values from -2 to 2
- proj_w: float32 [768, 256], P('dp'), may hold values from -0.21875 to 0.21875
- conv_w: float32 [4, 3, 3, 256, 256], P(None, None, None, 'dp'), may hold values from -0.125 to 0.125
- head_w: float32 [256, 256], P('dp'), may hold values from -0.375 to 0.375
- head_b: float32 [256], P('dp'), may hold values from -3 to 3
- shift_row: float32 [256], P('dp'), may hold values from -4 to 4
Outputs:
- tokens_out: bfloat16 [20, 32, 32, 768], P('dp', 'row', 'col')
- merged_out: bfloat16 [20, 64, 64, 256], P('dp', 'row', 'col')
- grad_tokens: float32 [20, 32, 32, 768], P('dp', 'row', 'col')
- grad_qkv_w: float32 [768, 2304], P('dp')
- grad_attn_out_w: float32 [768, 768], P('dp')
- grad_fc1_w: float32 [768, 3072], P('dp')
- grad_fc1_b: float32 [3072], P('dp')
- grad_fc2_w: float32 [3072, 768], P('dp')
- grad_fc2_b: float32 [768], P('dp')
- grad_ln1_gain: float32 [768], P('dp')
- grad_ln1_bias: float32 [768], P('dp')
- grad_ln2_gain: float32 [768], P('dp')
- grad_ln2_bias: float32 [768], P('dp')
- grad_proj_w: float32 [768, 256], P('dp')
- grad_conv_w: float32 [4, 3, 3, 256, 256], P(None, None, None, 'dp')
- grad_head_w: float32 [256, 256], P('dp')
- grad_head_b: float32 [256], P('dp')
- grad_shift_row: float32 [256], P('dp')
The draws below stay inside these ranges and needn't reach their ends.
Inputs may be any that keep to these rules, and one draw needn't show every extreme that they name: `image_counts`: slots of a group below its count hold images, the rest are empty; some group is full and another holds the least count.
All inputs are finite; a program needn't handle non-finite values.
Results may differ from the reference program's by a relative error of at most 0.024.
Values may be sent and summed in bfloat16 or wider, within the bound.
A program may use at most 384 MiB of HBM per device.

```python
import math
import jax
import jax.numpy as jnp
from jax import lax

D = 768
HEADS = 12
HEAD_DIM = 64
FF = 3072
FEAT = 256
GRID = 32
CAP = 10
SLOTS = 20
N_DP = 2


def draw_tokens(key, part):
    key = jax.random.fold_in(key, 11)
    entry_key, scale_key = jax.random.split(key)
    extent = (SLOTS, GRID, GRID, D)
    entries = jax.random.normal(entry_key, extent, jnp.float32)
    smallest = 0.3
    largest = 3.0
    row_scale = jnp.exp(jax.random.uniform(scale_key, (SLOTS, GRID, GRID, 1), jnp.float32, math.log(smallest), math.log(largest)))
    return (entries * row_scale).astype(jnp.bfloat16)


def draw_image_counts(key, part):
    key = jax.random.fold_in(key, 23)
    count_key, full_key, least_key = jax.random.split(key, 3)
    counts = jax.random.randint(count_key, (N_DP,), (CAP + 1) // 2, CAP + 1)
    chosen = jax.random.randint(full_key, (), 0, N_DP)
    other = (chosen + 1 + jax.random.randint(least_key, (), 0, N_DP - 1)) % N_DP
    group_index = jnp.arange(N_DP)
    counts = jnp.where(group_index == chosen, CAP, counts)
    counts = jnp.where(group_index == other, (CAP + 1) // 2, counts)
    return counts.astype(jnp.int32)


def draw_scale_flags(key, part):
    key = jax.random.fold_in(key, 31)
    flag_key, low_key, high_key = jax.random.split(key, 3)
    flags = jax.random.randint(flag_key, (SLOTS,), 0, 4)
    lowest_at = jax.random.randint(low_key, (), 0, SLOTS)
    highest_at = (lowest_at + 1 + jax.random.randint(high_key, (), 0, SLOTS - 1)) % SLOTS
    slot_index = jnp.arange(SLOTS)
    flags = jnp.where(slot_index == lowest_at, 0, flags)
    flags = jnp.where(slot_index == highest_at, 3, flags)
    return flags.astype(jnp.int32)


def with_ends(values, stream_key, least, high):
    shape = values.shape
    index_at = [jax.random.randint(jax.random.fold_in(stream_key, axis), (), 0, shape[axis]) for axis in range(len(shape))]
    values = values.at[tuple(index_at)].set(least)
    longest = shape.index(max(shape))
    index_at[longest] = (index_at[longest] + 1) % shape[longest]
    return values.at[tuple(index_at)].set(high)


def levels(own_key, shape, cuts, low, high):
    def one(axis_at, shards_of):
        steps = jax.random.uniform(jax.random.fold_in(jax.random.fold_in(own_key, 6), axis_at), (shards_of,), jnp.float32, low / len(cuts), high / len(cuts))
        return jnp.repeat(jnp.exp(steps), shape[axis_at] // shards_of).reshape((-1,) + (1,) * (len(shape) - axis_at - 1))

    level = one(*cuts[0])
    for cut in cuts[1:]:
        level = level * one(*cut)
    return level


def centred(stream_key, shape, scale, limit, shards=(), held_as=jnp.bfloat16):
    values = scale * jax.random.normal(stream_key, shape, jnp.float32)
    if shards:
        values = values * levels(stream_key, shape, shards, -0.22, 0.18)
    return jnp.clip(values, -limit, limit).astype(held_as)


def setup_inputs(seed: int = 0) -> dict:
    keys = jax.random.split(jax.random.key(seed), 22)
    return {
        "tokens": draw_tokens(jax.random.fold_in(keys[21], 71), 0),
        "cot_tokens": centred(keys[1], (SLOTS, GRID, GRID, D), 1.0, 6.0, ((0, 2), (1, 4), (2, 4))),
        "cot_merged": centred(keys[2], (SLOTS, 2 * GRID, 2 * GRID, FEAT), 1.0, 6.0, ((0, 2), (1, 4), (2, 4))),
        "image_counts": draw_image_counts(jax.random.fold_in(keys[21], 71), 0),
        "scale_flags": draw_scale_flags(jax.random.fold_in(keys[21], 71), 0),
        "shift_flags": with_ends(jax.random.randint(keys[5], (SLOTS,), -1, 2), jax.random.fold_in(keys[5], 1), -1, 1).astype(jnp.int32),
        "qkv_w": centred(keys[6], (D, 3 * D), D ** -0.5, 0.21875, ((0, 2),), jnp.float32),
        "attn_out_w": centred(keys[7], (D, D), (max(D // 128, 1)) ** -0.5, 2.5, ((0, 2),), jnp.float32),
        "fc1_w": centred(keys[8], (D, FF), D ** -0.5, 0.21875, ((0, 2),), jnp.float32),
        "fc1_b": centred(keys[9], (FF,), 0.5, 3.0, ((0, 2),), jnp.float32),
        "fc2_w": centred(keys[10], (FF, D), FF ** -0.5, 0.109375, ((0, 2),), jnp.float32),
        "fc2_b": centred(keys[11], (D,), 0.3, 2.0, ((0, 2),), jnp.float32),
        "ln1_gain": jnp.clip(1.0 + 0.15 * jax.random.normal(keys[12], (D,), jnp.float32), 0.25, 1.75),
        "ln1_bias": centred(keys[13], (D,), 0.3, 2.0, ((0, 2),), jnp.float32),
        "ln2_gain": jnp.clip(1.0 + 0.15 * jax.random.normal(keys[14], (D,), jnp.float32), 0.25, 1.75),
        "ln2_bias": centred(keys[15], (D,), 0.3, 2.0, ((0, 2),), jnp.float32),
        "proj_w": centred(keys[16], (D, FEAT), D ** -0.5, 0.21875, ((0, 2),), jnp.float32),
        "conv_w": centred(keys[17], (4, 3, 3, FEAT, FEAT), (9 * FEAT) ** -0.5, 0.125, ((3, 2),), jnp.float32),
        "head_w": centred(keys[18], (FEAT, FEAT), FEAT ** -0.5, 0.375, ((0, 2),), jnp.float32),
        "head_b": centred(keys[19], (FEAT,), 0.5, 3.0, ((0, 2),), jnp.float32),
        "shift_row": centred(keys[20], (FEAT,), 1.0, 4.0, ((0, 2),), jnp.float32),
    }


epsilon = 1e-06
highest = lax.Precision.HIGHEST

@jax.custom_vjp
def low(v):
    return lax.optimization_barrier(v.astype(jnp.bfloat16)).astype(jnp.float32)

@jax.custom_vjp
def low_back(v):
    return v

def low_keep(v):
    return (low(v), None)

def low_pass(kept, grad):
    return (grad,)

def back_keep(v):
    return (v, None)

def back_low(kept, grad):
    return (low(grad),)
low.defvjp(low_keep, low_pass)
low_back.defvjp(back_keep, back_low)

def product(first_op, second_op):
    return jnp.dot(first_op, second_op, precision=highest, preferred_element_type=jnp.float32)

def norm_rows(stream, gain_row, bias_row):
    centre = stream - lax.optimization_barrier(jnp.mean(stream, -1, keepdims=True))
    spread = lax.optimization_barrier(jnp.mean(centre * centre, -1, keepdims=True))
    return centre * lax.rsqrt(spread + epsilon) * gain_row + bias_row

def double_axis(padded, axis_index):
    leading = jnp.moveaxis(padded, axis_index, 0)
    middle_part = leading[1:-1]
    even_part = 0.75 * middle_part + 0.25 * leading[:-2]
    odd_part = 0.75 * middle_part + 0.25 * leading[2:]
    joined = jnp.stack([even_part, odd_part], 1).reshape((2 * middle_part.shape[0],) + middle_part.shape[1:])
    return jnp.moveaxis(joined, 0, axis_index)

def upsample(coarse_map):
    padded = jnp.pad(coarse_map, ((1, 1), (1, 1), (0, 0)), mode='edge')
    return double_axis(double_axis(padded, 0), 1)

def convolve(feature, kernel):
    return lax.conv_general_dilated(feature[None], kernel, (1, 1), 'SAME', dimension_numbers=('NHWC', 'HWIO', 'NHWC'), precision=highest)[0]

def image_forward(params, image, present, factor, shift_sign):
    w_qkv, w_out, w_up, b_up, w_down, b_down, gain_one, bias_one, gain_two, bias_two, w_proj, w_conv, w_head, b_head, w_shift = [low(master) for master in params]
    grid_side = image.shape[0]
    stream = image.reshape(grid_side * grid_side, -1)
    model_width = stream.shape[1]
    normed = low(norm_rows(stream, gain_one, bias_one))
    projected = low(low_back(product(normed, w_qkv)))
    queries = projected[:, :model_width].reshape(-1, HEADS, HEAD_DIM)
    keys_part = projected[:, model_width:2 * model_width].reshape(-1, HEADS, HEAD_DIM)
    values_part = projected[:, 2 * model_width:].reshape(-1, HEADS, HEAD_DIM)
    scores = low_back(jnp.einsum('qhd,khd->hqk', queries, keys_part, precision=highest) * HEAD_DIM ** (-0.5))
    attention = low(jax.nn.softmax(scores, -1))
    attended = jnp.einsum('hqk,khd->qhd', attention, values_part, precision=highest).reshape(-1, model_width)
    attended = low(low_back(attended))
    after_attn = stream + low_back(product(attended, w_out))
    normed_two = low(norm_rows(after_attn, gain_two, bias_two))
    hidden = low_back(product(normed_two, w_up) + b_up)
    activated = low(jax.nn.gelu(hidden))
    after_mlp = after_attn + low_back(product(activated, w_down) + b_down)
    tokens_low = low(after_mlp)
    feature = low_back(product(tokens_low, w_proj)).reshape(grid_side, grid_side, -1)
    for unit_index in range(2):
        first_out = low_back(convolve(low(jax.nn.gelu(feature)), w_conv[2 * unit_index]))
        second_out = low_back(convolve(low(jax.nn.gelu(first_out)), w_conv[2 * unit_index + 1]))
        feature = feature + second_out
    upsampled = low(low_back(upsample(low(feature))))
    channels = upsampled.shape[2]
    head_out = low_back(product(upsampled.reshape(-1, channels), w_head) + b_head)
    merged = (head_out * factor + shift_sign * w_shift) * present
    return ((tokens_low * present).reshape(image.shape), merged.reshape(2 * grid_side, 2 * grid_side, channels))

def reference(tokens, cot_tokens, cot_merged, image_counts, scale_flags, shift_flags, qkv_w, attn_out_w, fc1_w, fc1_b, fc2_w, fc2_b, ln1_gain, ln1_bias, ln2_gain, ln2_bias, proj_w, conv_w, head_w, head_b, shift_row):
    params = (qkv_w, attn_out_w, fc1_w, fc1_b, fc2_w, fc2_b, ln1_gain, ln1_bias, ln2_gain, ln2_bias, proj_w, conv_w, head_w, head_b, shift_row)
    slot_index = jnp.arange(SLOTS, dtype=jnp.int32)
    present = (slot_index % CAP < image_counts[slot_index // CAP]).astype(jnp.float32)
    factor = 0.5 + 0.5 * scale_flags.astype(jnp.float32)
    shift_sign = shift_flags.astype(jnp.float32)
    starting = jax.tree.map(jnp.zeros_like, params)

    def accumulate(totals, sample_in):
        image, image_cot, merged_cot, alive, scale_one, sign_one = sample_in

        def forward(weights, pixels):
            return image_forward(weights, pixels, alive, scale_one, sign_one)
        outputs, pullback = jax.vjp(forward, params, image.astype(jnp.float32))
        weight_grads, image_grad = pullback((image_cot.astype(jnp.float32), merged_cot.astype(jnp.float32)))
        totals = jax.tree.map(lambda running, addition: running + addition, totals, weight_grads)
        return (totals, (outputs[0].astype(jnp.bfloat16), outputs[1].astype(jnp.bfloat16), image_grad))
    totals, stacked = lax.scan(accumulate, starting, (tokens, cot_tokens, cot_merged, present, factor, shift_sign))
    return (stacked[0], stacked[1], stacked[2], totals[0], totals[1], totals[2], totals[3], totals[4], totals[5], totals[6], totals[7], totals[8], totals[9], totals[10], totals[11], totals[12], totals[13], totals[14])
```

```python
import functools

import jax
import jax.numpy as jnp
from jax import lax
from jax.experimental import pallas as pl
from jax.experimental.pallas import tpu as pltpu
from jax.sharding import PartitionSpec as P

HEADS = 12
HEAD_DIM = 64


epsilon = 1e-06


def extended(value, sides, width):
    for axis, dim in sides:
        peers, length = (lax.axis_size(axis), value.shape[dim])
        up = [(i, (i + 1) % peers) for i in range(peers - 1)]
        down = [(j, i) for i, j in up]
        last = lax.slice_in_dim(value, length - width, length, axis=dim)
        leading = lax.slice_in_dim(value, 0, width, axis=dim)
        before = lax.ppermute(last, axis, up)
        after = lax.ppermute(leading, axis, down)
        value = jnp.concatenate([before, value, after], axis=dim)
    return value


def norm_rows(stream, gain_row, bias_row):
    centre = stream - jnp.mean(stream, -1, keepdims=True)
    spread = jnp.mean(centre * centre, -1, keepdims=True)
    factor = lax.rsqrt(spread + epsilon)
    scaled = centre * factor
    return (scaled * gain_row + bias_row, scaled, factor)


def norm_back(cotangent, scaled, factor, gain_row):
    gained = cotangent * gain_row
    inner = (
        gained
        - jnp.mean(gained, -1, keepdims=True)
        - scaled * jnp.mean(gained * scaled, -1, keepdims=True)
    )
    return (factor * inner, jnp.sum(cotangent * scaled, 0), jnp.sum(cotangent, 0))


def gelu_grad(inputs, cotangent):
    return jax.vjp(jax.nn.gelu, inputs)[1](cotangent)[0]


def outer_product(first_op, second_op):
    return lax.dot_general(
        first_op, second_op, (((0,), (0,)), ((), ())), preferred_element_type=jnp.float32
    )


def back_product(first_op, weight):
    return lax.dot_general(
        first_op, weight, (((1,), (1,)), ((), ())), preferred_element_type=jnp.float32
    )


def add_rims(tile_map):
    return extended(tile_map, (("row", 1), ("col", 2)), 1)


def clamp_edges(padded):
    first_row = lax.axis_index("row") == 0
    last_row = lax.axis_index("row") == lax.axis_size("row") - 1
    upper = jnp.where(first_row, padded[:, 1:2], padded[:, 0:1])
    lower = jnp.where(last_row, padded[:, -2:-1], padded[:, -1:])
    padded = jnp.concatenate([upper, padded[:, 1:-1], lower], 1)
    first_col = lax.axis_index("col") == 0
    last_col = lax.axis_index("col") == lax.axis_size("col") - 1
    left_side = jnp.where(first_col, padded[:, :, 1:2], padded[:, :, 0:1])
    right_side = jnp.where(last_col, padded[:, :, -2:-1], padded[:, :, -1:])
    return jnp.concatenate([left_side, padded[:, :, 1:-1], right_side], 2)


def patches(padded):
    tall = padded.shape[1] - 2
    broad = padded.shape[2] - 2
    pieces = [
        padded[:, row_shift : row_shift + tall, col_shift : col_shift + broad]
        for row_shift in range(3)
        for col_shift in range(3)
    ]
    return jnp.concatenate(pieces, -1).reshape(-1, 9 * padded.shape[3])


def conv_apply(padded, kernel):
    result = jnp.dot(
        patches(padded), kernel.reshape(-1, kernel.shape[3]), preferred_element_type=jnp.float32
    )
    return result.reshape(padded.shape[0], padded.shape[1] - 2, padded.shape[2] - 2, -1)


def flip_kernel(kernel):
    return jnp.transpose(kernel[::-1, ::-1], (0, 1, 3, 2))


def double_axis(padded, axis_index):
    leading = jnp.moveaxis(padded, axis_index, 0)
    middle_part = leading[1:-1]
    even_part = 0.75 * middle_part + 0.25 * leading[:-2]
    odd_part = 0.75 * middle_part + 0.25 * leading[2:]
    joined = jnp.stack([even_part, odd_part], 1).reshape(
        (2 * middle_part.shape[0],) + middle_part.shape[1:]
    )
    return jnp.moveaxis(joined, 0, axis_index)


def halve_axis(padded, axis_index):
    leading = jnp.moveaxis(padded, axis_index, 0)
    even_part = leading[1:-1:2]
    odd_part = leading[2:-1:2]
    before_part = leading[0:-2:2]
    after_part = leading[3::2]
    joined = 0.75 * (even_part + odd_part) + 0.25 * (before_part + after_part)
    return jnp.moveaxis(joined, 0, axis_index)


def on_device(
    tokens,
    cot_tokens,
    cot_merged,
    image_counts,
    scale_flags,
    shift_flags,
    qkv_w,
    attn_out_w,
    fc1_w,
    fc1_b,
    fc2_w,
    fc2_b,
    ln1_gain,
    ln1_bias,
    ln2_gain,
    ln2_bias,
    proj_w,
    conv_w,
    head_w,
    head_b,
    shift_row,
):
    lowered = [
        master.astype(jnp.bfloat16)
        for master in (
            qkv_w,
            attn_out_w,
            fc1_w,
            fc1_b,
            fc2_w,
            fc2_b,
            ln1_gain,
            ln1_bias,
            ln2_gain,
            ln2_bias,
            proj_w,
            conv_w,
            head_w,
            head_b,
            shift_row,
        )
    ]
    gathered = (
        lax.all_gather(lowered[0], "dp", axis=0, tiled=True),
        lax.all_gather(lowered[1], "dp", axis=0, tiled=True),
        lax.all_gather(lowered[2], "dp", axis=0, tiled=True),
        lax.all_gather(lowered[3], "dp", axis=0, tiled=True),
        lax.all_gather(lowered[4], "dp", axis=0, tiled=True),
        lax.all_gather(lowered[5], "dp", axis=0, tiled=True),
        lax.all_gather(lowered[6], "dp", axis=0, tiled=True),
        lax.all_gather(lowered[7], "dp", axis=0, tiled=True),
        lax.all_gather(lowered[8], "dp", axis=0, tiled=True),
        lax.all_gather(lowered[9], "dp", axis=0, tiled=True),
        lax.all_gather(lowered[10], "dp", axis=0, tiled=True),
        lax.all_gather(lowered[11], "dp", axis=3, tiled=True),
        lax.all_gather(lowered[12], "dp", axis=0, tiled=True),
        lax.all_gather(lowered[13], "dp", axis=0, tiled=True),
        lax.all_gather(lowered[14], "dp", axis=0, tiled=True),
    )
    (
        w_qkv,
        w_out,
        w_up,
        b_up,
        w_down,
        b_down,
        gain_one,
        bias_one,
        gain_two,
        bias_two,
        w_proj,
        w_conv,
        w_head,
        b_head,
        w_shift,
    ) = gathered
    images = tokens.shape[0]
    tile_rows = tokens.shape[1]
    tile_cols = tokens.shape[2]
    tile_size = tile_rows * tile_cols
    model_width = tokens.shape[3]
    temper = HEAD_DIM ** (-0.5)
    present = (jnp.arange(images) < image_counts[0]).astype(jnp.float32)
    factor = 0.5 + 0.5 * scale_flags.astype(jnp.float32)
    shift_sign = shift_flags.astype(jnp.float32)
    present_rows = jnp.repeat(present, tile_size)[:, None]
    stream = tokens.astype(jnp.float32).reshape(-1, model_width)
    normed, scaled_one, factor_one = norm_rows(
        stream, gain_one.astype(jnp.float32), bias_one.astype(jnp.float32)
    )
    normed_low = normed.astype(jnp.bfloat16)
    projected = jnp.dot(normed_low, w_qkv, preferred_element_type=jnp.float32).astype(jnp.bfloat16)
    queries = projected[:, :model_width].reshape(images, tile_size, HEADS, HEAD_DIM)
    keys_own = projected[:, model_width : 2 * model_width].reshape(images, tile_size, model_width)
    values_own = projected[:, 2 * model_width :].reshape(images, tile_size, model_width)
    keys_all, values_all = (
        lax.all_gather(keys_own, ("row", "col"), axis=1, tiled=True),
        lax.all_gather(values_own, ("row", "col"), axis=1, tiled=True),
    )
    keys_heads = keys_all.reshape(images, -1, HEADS, HEAD_DIM)
    values_heads = values_all.reshape(images, -1, HEADS, HEAD_DIM)
    scores = (
        jnp.einsum("nqhd,nkhd->nhqk", queries, keys_heads, preferred_element_type=jnp.float32)
        * temper
    )
    highest_score = jnp.max(scores, -1, keepdims=True)
    exponent = jnp.exp(scores - highest_score)
    denominator = jnp.sum(exponent, -1, keepdims=True)
    log_total = highest_score + jnp.log(denominator)
    attention_low = (exponent / denominator).astype(jnp.bfloat16)
    attended = jnp.einsum(
        "nhqk,nkhd->nqhd", attention_low, values_heads, preferred_element_type=jnp.float32
    )
    attended = attended.reshape(-1, model_width).astype(jnp.bfloat16)
    after_attn = stream + jnp.dot(attended, w_out, preferred_element_type=jnp.float32)
    normed_two, scaled_two, factor_two = norm_rows(
        after_attn, gain_two.astype(jnp.float32), bias_two.astype(jnp.float32)
    )
    normed_two_low = normed_two.astype(jnp.bfloat16)
    hidden = jnp.dot(normed_two_low, w_up, preferred_element_type=jnp.float32) + b_up.astype(
        jnp.float32
    )
    hidden_low = jax.nn.gelu(hidden).astype(jnp.bfloat16)
    after_mlp = after_attn + (
        jnp.dot(hidden_low, w_down, preferred_element_type=jnp.float32) + b_down.astype(jnp.float32)
    )
    tokens_low = after_mlp.astype(jnp.bfloat16)
    tokens_out = (
        (tokens_low.astype(jnp.float32) * present_rows).astype(jnp.bfloat16).reshape(tokens.shape)
    )
    feature = jnp.dot(tokens_low, w_proj, preferred_element_type=jnp.float32).reshape(
        images, tile_rows, tile_cols, -1
    )
    channels = feature.shape[3]
    stored = []
    for unit_index in range(2):
        first_in = add_rims(jax.nn.gelu(feature).astype(jnp.bfloat16))
        first_out = conv_apply(first_in, w_conv[2 * unit_index])
        second_in = add_rims(jax.nn.gelu(first_out).astype(jnp.bfloat16))
        second_out = conv_apply(second_in, w_conv[2 * unit_index + 1])
        stored.append((feature, first_in, first_out, second_in))
        feature = feature + second_out
    coarse_map = clamp_edges(add_rims(feature.astype(jnp.bfloat16))).astype(jnp.float32)
    upsampled = double_axis(double_axis(coarse_map, 1), 2).astype(jnp.bfloat16)
    fine_rows = upsampled.reshape(-1, channels)
    head_out = jnp.dot(fine_rows, w_head, preferred_element_type=jnp.float32) + b_head.astype(
        jnp.float32
    )
    head_out = head_out.reshape(images, -1, channels)
    merged = (
        head_out * factor[:, None, None] + shift_sign[:, None, None] * w_shift.astype(jnp.float32)
    ) * present[:, None, None]
    merged_out = merged.astype(jnp.bfloat16).reshape(cot_merged.shape)
    gathered = (
        lax.all_gather(lowered[0], "dp", axis=0, tiled=True),
        lax.all_gather(lowered[1], "dp", axis=0, tiled=True),
        lax.all_gather(lowered[2], "dp", axis=0, tiled=True),
        lax.all_gather(lowered[3], "dp", axis=0, tiled=True),
        lax.all_gather(lowered[4], "dp", axis=0, tiled=True),
        lax.all_gather(lowered[5], "dp", axis=0, tiled=True),
        lax.all_gather(lowered[6], "dp", axis=0, tiled=True),
        lax.all_gather(lowered[7], "dp", axis=0, tiled=True),
        lax.all_gather(lowered[8], "dp", axis=0, tiled=True),
        lax.all_gather(lowered[9], "dp", axis=0, tiled=True),
        lax.all_gather(lowered[10], "dp", axis=0, tiled=True),
        lax.all_gather(lowered[11], "dp", axis=3, tiled=True),
        lax.all_gather(lowered[12], "dp", axis=0, tiled=True),
        lax.all_gather(lowered[13], "dp", axis=0, tiled=True),
        lax.all_gather(lowered[14], "dp", axis=0, tiled=True),
    )
    (
        w_qkv,
        w_out,
        w_up,
        b_up,
        w_down,
        b_down,
        gain_one,
        bias_one,
        gain_two,
        bias_two,
        w_proj,
        w_conv,
        w_head,
        b_head,
        w_shift,
    ) = gathered
    merged_grad = (
        cot_merged.astype(jnp.float32).reshape(images, -1, channels) * present[:, None, None]
    )
    grad_shift = jnp.sum(merged_grad * shift_sign[:, None, None], (0, 1))
    head_grad = (merged_grad * factor[:, None, None]).astype(jnp.bfloat16).reshape(-1, channels)
    grad_head_b = jnp.sum(head_grad.astype(jnp.float32), 0)
    grad_head_w = outer_product(fine_rows, head_grad)
    fine_grad = back_product(head_grad, w_head).astype(jnp.bfloat16).reshape(upsampled.shape)
    spread_grad = clamp_edges(extended(fine_grad, (("row", 1), ("col", 2)), 1)).astype(jnp.float32)
    feature_grad = halve_axis(halve_axis(spread_grad, 1), 2)
    conv_grads = [None, None, None, None]
    for unit_index in (1, 0):
        unit_input, first_in, first_out, second_in = stored[unit_index]
        second_grad = feature_grad.astype(jnp.bfloat16)
        conv_grads[2 * unit_index + 1] = outer_product(
            patches(second_in), second_grad.reshape(-1, channels)
        )
        middle_grad = conv_apply(add_rims(second_grad), flip_kernel(w_conv[2 * unit_index + 1]))
        first_grad = gelu_grad(first_out, middle_grad).astype(jnp.bfloat16)
        conv_grads[2 * unit_index] = outer_product(
            patches(first_in), first_grad.reshape(-1, channels)
        )
        inner_grad = conv_apply(add_rims(first_grad), flip_kernel(w_conv[2 * unit_index]))
        feature_grad = feature_grad + gelu_grad(unit_input, inner_grad)
    grad_conv = jnp.stack(conv_grads).reshape(4, 3, 3, channels, channels)
    proj_grad = feature_grad.astype(jnp.bfloat16).reshape(-1, channels)
    grad_proj = outer_product(tokens_low, proj_grad)
    stream_grad = cot_tokens.astype(jnp.float32).reshape(
        -1, model_width
    ) * present_rows + back_product(proj_grad, w_proj)
    down_grad = stream_grad.astype(jnp.bfloat16)
    grad_down_b = jnp.sum(down_grad.astype(jnp.float32), 0)
    grad_down_w = outer_product(hidden_low, down_grad)
    up_grad = gelu_grad(hidden, back_product(down_grad, w_down)).astype(jnp.bfloat16)
    grad_up_b = jnp.sum(up_grad.astype(jnp.float32), 0)
    grad_up_w = outer_product(normed_two_low, up_grad)
    norm_grad, grad_gain_two, grad_bias_two = norm_back(
        back_product(up_grad, w_up), scaled_two, factor_two, gain_two.astype(jnp.float32)
    )
    stream_grad = stream_grad + norm_grad
    branch_grad = stream_grad.astype(jnp.bfloat16)
    grad_out_w = outer_product(attended, branch_grad)
    attended_grad = (
        back_product(branch_grad, w_out)
        .astype(jnp.bfloat16)
        .reshape(images, tile_size, HEADS, HEAD_DIM)
    )
    keys_heads = keys_all.reshape(images, -1, HEADS, HEAD_DIM)
    values_heads = values_all.reshape(images, -1, HEADS, HEAD_DIM)
    scores = (
        jnp.einsum("nqhd,nkhd->nhqk", queries, keys_heads, preferred_element_type=jnp.float32)
        * temper
    )
    attention_full = jnp.exp(scores - log_total)
    attention_low = attention_full.astype(jnp.bfloat16)
    prob_grad = jnp.einsum(
        "nqhd,nkhd->nhqk", attended_grad, values_heads, preferred_element_type=jnp.float32
    )
    centre = jnp.sum(attention_full * prob_grad, -1, keepdims=True)
    score_grad = (attention_full * (prob_grad - centre)).astype(jnp.bfloat16)
    query_grad = (
        jnp.einsum("nhqk,nkhd->nqhd", score_grad, keys_heads, preferred_element_type=jnp.float32)
        * temper
    )
    key_part = (
        jnp.einsum("nhqk,nqhd->knhd", score_grad, queries, preferred_element_type=jnp.float32)
        * temper
    )
    value_part = jnp.einsum(
        "nhqk,nqhd->knhd", attention_low, attended_grad, preferred_element_type=jnp.float32
    )
    pair_grad = lax.psum_scatter(
        jnp.concatenate(
            [
                key_part.reshape(lax.axis_size(("row", "col")) * tile_size, images, model_width),
                value_part.reshape(lax.axis_size(("row", "col")) * tile_size, images, model_width),
            ],
            2,
        ).astype(jnp.bfloat16),
        ("row", "col"),
        scatter_dimension=0,
        tiled=True,
    ).astype(jnp.float32)
    pair_grad = jnp.transpose(pair_grad, (1, 0, 2))
    mixed_grad = jnp.concatenate([query_grad.reshape(images, tile_size, model_width), pair_grad], 2)
    mixed_grad = mixed_grad.astype(jnp.bfloat16).reshape(-1, 3 * model_width)
    grad_qkv = outer_product(normed_low, mixed_grad)
    norm_grad, grad_gain_one, grad_bias_one = norm_back(
        back_product(mixed_grad, w_qkv), scaled_one, factor_one, gain_one.astype(jnp.float32)
    )
    input_grad = (stream_grad + norm_grad).reshape(tokens.shape)
    shards = (
        lax.psum_scatter(
            grad_qkv.astype(jnp.bfloat16), "dp", scatter_dimension=0, tiled=True
        ).astype(jnp.float32),
        lax.psum_scatter(
            grad_out_w.astype(jnp.bfloat16), "dp", scatter_dimension=0, tiled=True
        ).astype(jnp.float32),
        lax.psum_scatter(
            grad_up_w.astype(jnp.bfloat16), "dp", scatter_dimension=0, tiled=True
        ).astype(jnp.float32),
        lax.psum_scatter(
            grad_up_b.astype(jnp.bfloat16), "dp", scatter_dimension=0, tiled=True
        ).astype(jnp.float32),
        lax.psum_scatter(
            grad_down_w.astype(jnp.bfloat16), "dp", scatter_dimension=0, tiled=True
        ).astype(jnp.float32),
        lax.psum_scatter(
            grad_down_b.astype(jnp.bfloat16), "dp", scatter_dimension=0, tiled=True
        ).astype(jnp.float32),
        lax.psum_scatter(
            grad_gain_one.astype(jnp.bfloat16), "dp", scatter_dimension=0, tiled=True
        ).astype(jnp.float32),
        lax.psum_scatter(
            grad_bias_one.astype(jnp.bfloat16), "dp", scatter_dimension=0, tiled=True
        ).astype(jnp.float32),
        lax.psum_scatter(
            grad_gain_two.astype(jnp.bfloat16), "dp", scatter_dimension=0, tiled=True
        ).astype(jnp.float32),
        lax.psum_scatter(
            grad_bias_two.astype(jnp.bfloat16), "dp", scatter_dimension=0, tiled=True
        ).astype(jnp.float32),
        lax.psum_scatter(
            grad_proj.astype(jnp.bfloat16), "dp", scatter_dimension=0, tiled=True
        ).astype(jnp.float32),
        lax.psum_scatter(
            grad_conv.astype(jnp.bfloat16), "dp", scatter_dimension=3, tiled=True
        ).astype(jnp.float32),
        lax.psum_scatter(
            grad_head_w.astype(jnp.bfloat16), "dp", scatter_dimension=0, tiled=True
        ).astype(jnp.float32),
        lax.psum_scatter(
            grad_head_b.astype(jnp.bfloat16), "dp", scatter_dimension=0, tiled=True
        ).astype(jnp.float32),
        lax.psum_scatter(
            grad_shift.astype(jnp.bfloat16), "dp", scatter_dimension=0, tiled=True
        ).astype(jnp.float32),
    )
    totals = (
        lax.psum(shards[0].astype(jnp.bfloat16), ("row", "col")).astype(jnp.float32),
        lax.psum(shards[1].astype(jnp.bfloat16), ("row", "col")).astype(jnp.float32),
        lax.psum(shards[2].astype(jnp.bfloat16), ("row", "col")).astype(jnp.float32),
        lax.psum(shards[3].astype(jnp.bfloat16), ("row", "col")).astype(jnp.float32),
        lax.psum(shards[4].astype(jnp.bfloat16), ("row", "col")).astype(jnp.float32),
        lax.psum(shards[5].astype(jnp.bfloat16), ("row", "col")).astype(jnp.float32),
        lax.psum(shards[6].astype(jnp.bfloat16), ("row", "col")).astype(jnp.float32),
        lax.psum(shards[7].astype(jnp.bfloat16), ("row", "col")).astype(jnp.float32),
        lax.psum(shards[8].astype(jnp.bfloat16), ("row", "col")).astype(jnp.float32),
        lax.psum(shards[9].astype(jnp.bfloat16), ("row", "col")).astype(jnp.float32),
        lax.psum(shards[10].astype(jnp.bfloat16), ("row", "col")).astype(jnp.float32),
        lax.psum(shards[11].astype(jnp.bfloat16), ("row", "col")).astype(jnp.float32),
        lax.psum(shards[12].astype(jnp.bfloat16), ("row", "col")).astype(jnp.float32),
        lax.psum(shards[13].astype(jnp.bfloat16), ("row", "col")).astype(jnp.float32),
        lax.psum(shards[14].astype(jnp.bfloat16), ("row", "col")).astype(jnp.float32),
    )
    return (
        tokens_out,
        merged_out,
        input_grad,
        totals[0],
        totals[1],
        totals[2],
        totals[3],
        totals[4],
        totals[5],
        totals[6],
        totals[7],
        totals[8],
        totals[9],
        totals[10],
        totals[11],
        totals[12],
        totals[13],
        totals[14],
    )


LOG2E = 1.4426950408889634
MESH = pl.DeviceIdType.MESH
HALO = 6
PATCH = 112
VMEM_LIMIT = 58 << 20


def place():
    dp, row, col = (lax.axis_index(axis) for axis in ("dp", "row", "col"))
    return dp, lax.div(row, 2), lax.rem(row, 2), col


def flip(bit):
    return 1 - bit


def send(src, dst, send_sem, recv_sem, dp, y, core, z):
    return pltpu.make_async_remote_copy(
        src_ref=src,
        dst_ref=dst,
        send_sem=send_sem,
        recv_sem=recv_sem,
        device_id={"dp": dp, "row": y * 2 + core, "col": z},
        device_id_type=MESH,
    )


def landed(ref, sem):
    return pltpu.make_async_copy(ref, ref, sem)


def to_images_start(src, dst, send_sem, recv_sem, sizes):
    chips, slots, cols = sizes
    dp, y, core, z = place()
    own = core * cols + z
    for step in range(chips):
        far_y = lax.rem(y + step // cols, 2)
        far_z = lax.rem(z + step % cols, cols)
        slot = far_y * cols + far_z
        copy = send(
            src.at[slot], dst.at[0, own], send_sem.at[step], recv_sem.at[own], dp, far_y, y, far_z
        )
        if step == 0:
            local = pltpu.make_async_copy(src.at[slot], dst.at[0, own], recv_sem.at[own])
            pl.when(core == y)(local.start)
            pl.when(core != y)(copy.start)
        else:
            copy.start()
    for extra in range(slots - chips):
        chip = 2 * chips - slots + extra
        send(
            src.at[chips + extra],
            dst.at[1, own],
            send_sem.at[chips + extra],
            recv_sem.at[chips + own],
            1 - dp,
            chip // cols,
            y,
            chip % cols,
        ).start()


def to_images_wait(src, dst, send_sem, recv_sem, sizes):
    chips, slots, cols = sizes
    dp, y, core, z = place()
    for step in range(slots):
        left = landed(src.at[0], send_sem.at[step])
        if step == 0:
            pl.when(core != y)(left.wait)
        else:
            left.wait()
    for tile in range(chips):
        landed(dst.at[0, tile], recv_sem.at[tile]).wait()

    @pl.when(y * cols + z >= 2 * chips - slots)
    def _():
        for tile in range(chips):
            landed(dst.at[1, tile], recv_sem.at[chips + tile]).wait()


def to_tiles_start(src, dst, send_sem, recv_sem, sizes):
    chips, slots, cols = sizes
    dp, y, core, z = place()
    slot = y * cols + z
    for step in range(chips):
        far_core = lax.rem(core + step // cols, 2)
        far_z = lax.rem(z + step % cols, cols)
        tile = far_core * cols + far_z
        copy = send(
            src.at[tile], dst.at[slot], send_sem.at[step], recv_sem.at[slot], dp, core, far_core, far_z
        )
        if step == 0:
            local = pltpu.make_async_copy(src.at[tile], dst.at[slot], recv_sem.at[slot])
            pl.when(core == y)(local.start)
            pl.when(core != y)(copy.start)
        else:
            copy.start()

    @pl.when(slot >= 2 * chips - slots)
    def _():
        for step in range(chips):
            far_core = step // cols
            far_z = step % cols
            other = slot + slots - chips
            send(
                src.at[step],
                dst.at[other],
                send_sem.at[chips + step],
                recv_sem.at[other],
                1 - dp,
                core,
                far_core,
                far_z,
            ).start()


def to_tiles_wait(src, dst, send_sem, recv_sem, sizes):
    chips, slots, cols = sizes
    dp, y, core, z = place()
    for step in range(chips):
        left = landed(src.at[0], send_sem.at[step])
        if step == 0:
            pl.when(core != y)(left.wait)
        else:
            left.wait()

    @pl.when(y * cols + z >= 2 * chips - slots)
    def _():
        for step in range(chips):
            landed(src.at[0], send_sem.at[chips + step]).wait()

    for slot in range(slots):
        landed(dst.at[slot], recv_sem.at[slot]).wait()


BITS = ("dp", "y", "z1", "z2")


def mate(bit):
    dp, y, core, z = place()
    low, high = lax.rem(z, 2), lax.div(z, 2)
    if bit == "core":
        return dp, y, 1 - core, z
    if bit == "dp":
        return 1 - dp, y, core, z
    if bit == "y":
        return dp, 1 - y, core, z
    if bit == "z1":
        return dp, y, core, high * 2 + 1 - low
    return dp, y, core, (1 - high) * 2 + low


def bit_of(bit):
    dp, y, core, z = place()
    return {
        "dp": dp,
        "y": y,
        "core": core,
        "z1": lax.rem(z, 2),
        "z2": lax.div(z, 2),
    }[bit]


PIECE_BITS = ("y", "z1", "core")
GATHER_ORDERS = (("dp", "z1", "y", "core"), ("dp", "y", "z1", "core"))


def gather_steps(half, whole, local_sem, send_sem, recv_sem, order):
    held = {bit: bit_of(bit) for bit in PIECE_BITS}
    dp = bit_of("dp")
    copies = []

    def start(step):
        bit = order[step]
        at = tuple(held[b] if held[b] is not None else slice(None) for b in PIECE_BITS)
        if bit == "dp":
            src = half.at[(slice(None),) + at]
            far = whole.at[(slice(None), dp) + at]
            for piece in range(8):
                of = (slice(None), piece // 4, piece // 2 % 2, piece % 2)
                local = pltpu.make_async_copy(
                    half.at[of], whole.at[of[:1] + (dp,) + of[1:]], local_sem.at[piece]
                )
                local.start()
                copies.append(local)
        else:
            src = whole.at[(slice(None), 1 - dp) + at]
            far = src
        copy = send(src, far, send_sem.at[step], recv_sem.at[step], *mate(bit))
        copy.start()
        copies.append(copy)

    def wait(step):
        while copies:
            copies.pop().wait()
        if order[step] != "dp":
            held[order[step]] = None

    return len(order), start, wait


def pipeline(jobs):
    for slot in range(max(delay + steps for delay, steps, _, _ in jobs) + 1):
        for delay, steps, start, wait in jobs:
            step = slot - delay
            if 0 < step <= steps:
                wait(step - 1)
            if 0 <= step < steps:
                start(step)


def in_kernel(sizes, names, *refs):
    n = len(names)
    tiles, refs = refs[:3], refs[3:]
    halves, refs = refs[:n], refs[n:]
    images, refs = refs[:3], refs[3:]
    wholes, refs = refs[:n], refs[n:]
    tile_send, tile_recv, local_sem, send_sem, recv_sem = refs
    for i in range(3):
        to_images_start(tiles[i], images[i], tile_send.at[i], tile_recv.at[i], sizes)
    jobs = []
    for i in range(n):
        steps, start, wait = gather_steps(
            halves[i],
            wholes[i],
            local_sem.at[i],
            send_sem.at[i],
            recv_sem.at[i],
            GATHER_ORDERS[i % 2],
        )
        jobs.append((i // 2, steps, start, wait))
    pipeline(jobs)
    for i in range(3):
        to_images_wait(tiles[i], images[i], tile_send.at[i], tile_recv.at[i], sizes)


def bring_in(tiles, halves, sizes):
    chips, slots, cols = sizes
    names = list(halves)
    cut = {}
    for name, half in halves.items():
        lead, rows, width = half.shape
        cut[name] = half.reshape(lead, 2, 2, 2, rows // 8, width)
    out_shape = [
        jax.ShapeDtypeStruct((2, chips) + tile.shape[1:], tile.dtype) for tile in tiles
    ] + [
        jax.ShapeDtypeStruct((cut[name].shape[0], 2) + cut[name].shape[1:], jnp.bfloat16)
        for name in names
    ]
    n = len(names)
    outs = pl.pallas_call(
        functools.partial(in_kernel, sizes, names),
        out_shape=out_shape,
        in_specs=[pl.BlockSpec(memory_space=pltpu.HBM)] * (3 + n),
        out_specs=[pl.BlockSpec(memory_space=pltpu.HBM)] * (3 + n),
        scratch_shapes=[
            pltpu.SemaphoreType.DMA((3, slots)),
            pltpu.SemaphoreType.DMA((3, 2 * chips)),
            pltpu.SemaphoreType.DMA((n, 8)),
            pltpu.SemaphoreType.DMA((n, 4)),
            pltpu.SemaphoreType.DMA((n, 4)),
        ],
        compiler_params=pltpu.CompilerParams(
            has_side_effects=True, vmem_limit_bytes=VMEM_LIMIT
        ),
    )(*tiles, *(cut[name] for name in names))
    wholes = {}
    for name, whole in zip(names, outs[3:]):
        lead, rows, width = halves[name].shape
        wholes[name] = whole.reshape(lead, 2 * rows, width)
    return outs[:3], wholes


def patch_kernel(sizes, src, dst, send_sem, recv_sem):
    to_tiles_start(src, dst, send_sem, recv_sem, sizes)
    to_tiles_wait(src, dst, send_sem, recv_sem, sizes)


def patches_out(patch, sizes):
    chips, slots, cols = sizes
    return pl.pallas_call(
        functools.partial(patch_kernel, sizes),
        out_shape=jax.ShapeDtypeStruct((slots,) + patch.shape[1:], patch.dtype),
        in_specs=[pl.BlockSpec(memory_space=pltpu.HBM)],
        out_specs=pl.BlockSpec(memory_space=pltpu.HBM),
        scratch_shapes=[
            pltpu.SemaphoreType.DMA((2 * chips,)),
            pltpu.SemaphoreType.DMA((slots,)),
        ],
        compiler_params=pltpu.CompilerParams(
            has_side_effects=True, vmem_limit_bytes=VMEM_LIMIT
        ),
    )(patch)


SUM_ORDERS = (
    ("dp", "y", "z1", "z2"),
    ("y", "dp", "z1", "z2"),
    ("z1", "dp", "y", "z2"),
)
BACK_ORDERS = (
    ("z2", "z1", "y", "core"),
    ("z2", "y", "z1", "core"),
    ("z2", "y", "z1", "core"),
)


def reduce_steps(grad, out, acc, recvs, sems, orders):
    local_sem, send_sem, recv_sem = sems
    sum_order, back_order = orders
    half = grad.shape[-1] // 2
    core = bit_of("core")
    mine = pl.ds(pl.multiple_of(core * half, 128), half)
    theirs = pl.ds(pl.multiple_of((1 - core) * half, 128), half)
    kept = {bit: None for bit in BITS}
    whole = slice(None)
    copies = []
    forward = 1 + len(sum_order)

    def index():
        return tuple(whole if kept[b] is None else kept[b] for b in BITS)

    def add(recv):
        free = [b for b in BITS if kept[b] is None]

        def body(i, _):
            bits, left = {}, i
            for b in reversed(free):
                bits[b] = lax.rem(left, 2)
                left = lax.div(left, 2)
            at = tuple(bits[b] if b in bits else kept[b] for b in BITS)
            here = (whole,) + at
            there = (whole,) + tuple(bits[b] for b in free)
            total = acc[here].astype(jnp.float32) + recv[there].astype(jnp.float32)
            acc[here] = total.astype(acc.dtype)
            return 0

        lax.fori_loop(0, 2 ** len(free), body, 0)

    def start(step):
        if step == 0:
            local = pltpu.make_async_copy(grad.at[..., mine], acc, local_sem.at[0])
            local.start()
            copies.append(local)
            copy = send(
                grad.at[..., theirs], recvs[0], send_sem.at[0], recv_sem.at[0], *mate("core")
            )
        elif step < forward:
            bit = sum_order[step - 1]
            kept[bit] = 1 - bit_of(bit)
            src = acc.at[(whole,) + index()]
            kept[bit] = bit_of(bit)
            copy = send(src, recvs[step], send_sem.at[step], recv_sem.at[step], *mate(bit))
        elif step == forward:
            at = (whole,) + index()[1:] + (whole, mine)
            copy = pltpu.make_async_copy(acc.at[(whole,) + index()], out.at[at], local_sem.at[1])
            kept.pop("dp")
            kept["core"] = mine
        else:
            bit = back_order[step - forward - 1]
            at = (whole,) + tuple(whole if kept[b] is None else kept[b] for b in BITS[1:])
            at = at + (whole, mine)
            copy = send(
                out.at[at], out.at[at], send_sem.at[step - 1], recv_sem.at[step - 1], *mate(bit)
            )
        copy.start()
        copies.append(copy)

    def wait(step):
        while copies:
            copies.pop().wait()
        if step < forward:
            add(recvs[step])
        elif step > forward:
            kept[back_order[step - forward - 1]] = None

    return forward + 1 + len(back_order), start, wait


def recv_shapes(shape, order):
    lead, rows, width = shape[0], shape[5], shape[6]
    free, out = 4, []
    for step in range(1 + len(order)):
        out.append((lead,) + (2,) * (4 - step) + (rows, width // 2))
    return out


def out_kernel(sizes, n, delays, *refs):
    tiles, refs = refs[:2], refs[2:]
    grads, refs = refs[:n], refs[n:]
    slots, refs = refs[:2], refs[2:]
    outs, refs = refs[:n], refs[n:]
    accs, refs = refs[:n], refs[n:]
    recvs, refs = refs[: 5 * n], refs[5 * n :]
    tile_send, tile_recv, local_sem, send_sem, recv_sem = refs
    for i in range(2):
        to_tiles_start(tiles[i], slots[i], tile_send.at[i], tile_recv.at[i], sizes)
    jobs = []
    for i in range(n):
        steps, start, wait = reduce_steps(
            grads[i],
            outs[i],
            accs[i],
            recvs[5 * i : 5 * i + 5],
            (local_sem.at[i], send_sem.at[i], recv_sem.at[i]),
            (SUM_ORDERS[i % 3], BACK_ORDERS[i % 3]),
        )
        jobs.append((delays[i], steps, start, wait))
    pipeline(jobs)
    for i in range(2):
        to_tiles_wait(tiles[i], slots[i], tile_send.at[i], tile_recv.at[i], sizes)


def bring_out(tiles, grads, sizes):
    chips, slots, cols = sizes
    names = list(grads)
    n = len(names)
    cut = []
    for name in names:
        lead, rows, width = grads[name].shape
        cut.append(grads[name].reshape(lead, 2, 2, 2, 2, rows // 16, width))
    accs = [pltpu.VMEM(g.shape[:-1] + (g.shape[-1] // 2,), jnp.bfloat16) for g in cut]
    recvs = [
        pltpu.VMEM(shape, jnp.bfloat16)
        for i, g in enumerate(cut)
        for shape in recv_shapes(g.shape, SUM_ORDERS[i % 3])
    ]
    outs = pl.pallas_call(
        functools.partial(out_kernel, sizes, n, [i // 2 for i in range(n)]),
        out_shape=[
            jax.ShapeDtypeStruct((slots,) + tile.shape[1:], tile.dtype) for tile in tiles
        ]
        + [jax.ShapeDtypeStruct(g.shape[:1] + g.shape[2:], jnp.bfloat16) for g in cut],
        in_specs=[pl.BlockSpec(memory_space=pltpu.HBM)] * (2 + n),
        out_specs=[pl.BlockSpec(memory_space=pltpu.HBM)] * (2 + n),
        scratch_shapes=accs
        + recvs
        + [
            pltpu.SemaphoreType.DMA((2, 2 * chips)),
            pltpu.SemaphoreType.DMA((2, slots)),
            pltpu.SemaphoreType.DMA((n, 2)),
            pltpu.SemaphoreType.DMA((n, 9)),
            pltpu.SemaphoreType.DMA((n, 9)),
        ],
        compiler_params=pltpu.CompilerParams(
            has_side_effects=True, vmem_limit_bytes=VMEM_LIMIT
        ),
    )(*tiles, *cut)
    sums = {}
    for name, out in zip(names, outs[2:]):
        lead, rows, width = grads[name].shape
        sums[name] = out.reshape(lead, rows // 2, width)
    return outs[:2], sums


SCALE = HEAD_DIM**-0.5


def attend_kernel(q_ref, k_ref, v_ref, o_ref, log_ref):
    lane = lax.broadcasted_iota(jnp.int32, (1, 128), 1)
    sub = lax.broadcasted_iota(jnp.int32, (128, 1), 0)
    k, v, q = k_ref[...], v_ref[...], q_ref[...]
    out = jnp.zeros((128, q.shape[0]), jnp.float32)
    for h in range(2):
        mine = (lane >= 64) == (h == 1)
        scores = lax.dot_general(
            k, jnp.where(mine, q, 0), (((1,), (1,)), ((), ())), preferred_element_type=jnp.float32
        )
        top = jnp.max(scores, 0, keepdims=True) * (SCALE * LOG2E)
        e = jnp.exp2(scores * (SCALE * LOG2E) - top)
        total = jnp.sum(e, 0, keepdims=True)
        part = lax.dot_general(
            v, e.astype(jnp.bfloat16), (((0,), (0,)), ((), ())), preferred_element_type=jnp.float32
        )
        out = jnp.where((sub >= 64) == (h == 1), part / total, out)
        log_ref[0, h : h + 1, :] = top + jnp.log2(total)
    o_ref[...] = out.T


def attend_back_kernel(q_ref, k_ref, v_ref, o_ref, log_ref, g_ref, dq_ref, dk_ref, dv_ref):
    lane = lax.broadcasted_iota(jnp.int32, (1, 128), 1)
    sub = lax.broadcasted_iota(jnp.int32, (128, 1), 0)
    k, v, q, g = k_ref[...], v_ref[...], q_ref[...], g_ref[...]
    product = (g.astype(jnp.float32) * o_ref[...]).T
    dq = jnp.zeros((128, q.shape[0]), jnp.float32)
    for h in range(2):
        mine = (lane >= 64) == (h == 1)
        q_own, g_own = jnp.where(mine, q, 0), jnp.where(mine, g, 0)
        centre = jnp.sum(product[h * 64 : (h + 1) * 64], 0, keepdims=True)
        scores = lax.dot_general(
            k, q_own, (((1,), (1,)), ((), ())), preferred_element_type=jnp.float32
        )
        p = jnp.exp2(scores * (SCALE * LOG2E) - log_ref[0, h : h + 1, :])
        dp = lax.dot_general(
            v, g_own, (((1,), (1,)), ((), ())), preferred_element_type=jnp.float32
        )
        ds = (p * (dp - centre)).astype(jnp.bfloat16)
        dq_own = lax.dot_general(
            k, ds, (((0,), (0,)), ((), ())), preferred_element_type=jnp.float32
        )
        dq = jnp.where((sub >= 64) == (h == 1), dq_own * SCALE, dq)
        dk = jnp.dot(ds, q_own, preferred_element_type=jnp.float32) * SCALE
        dv = jnp.dot(p.astype(jnp.bfloat16), g_own, preferred_element_type=jnp.float32)
        if h == 0:
            dk_ref[...], dv_ref[...] = dk, dv
        else:
            dk_ref[...] += dk
            dv_ref[...] += dv
    dq_ref[...] = dq.T


def pair_block(rows):
    return pl.BlockSpec((rows, 128), lambda i: (0, i))


def attend(q, k, v):
    rows, width = q.shape
    logs = pl.BlockSpec((1, 2, rows), lambda i: (i, 0, 0))
    return pl.pallas_call(
        attend_kernel,
        grid=(width // 128,),
        in_specs=[pair_block(rows), pair_block(k.shape[0]), pair_block(k.shape[0])],
        out_specs=[pair_block(rows), logs],
        out_shape=[
            jax.ShapeDtypeStruct((rows, width), jnp.float32),
            jax.ShapeDtypeStruct((width // 128, 2, rows), jnp.float32),
        ],
        compiler_params=pltpu.CompilerParams(vmem_limit_bytes=VMEM_LIMIT),
    )(q, k, v)


def attend_back(q, k, v, o, logs, g):
    rows, width = q.shape
    keys = k.shape[0]
    own, both = pair_block(rows), pair_block(keys)
    return pl.pallas_call(
        attend_back_kernel,
        grid=(width // 128,),
        in_specs=[own, both, both, own, pl.BlockSpec((1, 2, rows), lambda i: (i, 0, 0)), own],
        out_specs=[own, both, both],
        out_shape=[jax.ShapeDtypeStruct((n, width), jnp.float32) for n in (rows, keys, keys)],
        compiler_params=pltpu.CompilerParams(vmem_limit_bytes=VMEM_LIMIT),
    )(q, k, v, o, logs, g)


GELU_K, GELU_C = 0.7978845608028654, 0.044715


def gelu_slope(v):
    t = jnp.tanh(GELU_K * (v + GELU_C * v * v * v))
    return 0.5 * (1.0 + t) + 0.5 * v * (1.0 - t * t) * (GELU_K * (1.0 + 3.0 * GELU_C * v * v))


def block(row, size):
    return pl.ds(pl.multiple_of(row * size, size), size)


def turned(core, row, last):
    return core * (last - 2 * row) + row


def triple(dst, value, cols):
    rows, feat = value.shape
    col = lax.rem(lax.broadcasted_iota(jnp.int32, (rows, 1), 0), cols)
    left = jnp.where(col == 0, 0.0, pltpu.roll(value, 1, 0))
    right = jnp.where(col == cols - 1, 0.0, pltpu.roll(value, rows - 1, 0))
    body = pl.ds(cols, rows)
    dst[body, 0:feat] = left.astype(dst.dtype)
    dst[body, feat : 2 * feat] = value.astype(dst.dtype)
    dst[body, 2 * feat :] = right.astype(dst.dtype)


def clear_ends(dst, cols):
    zero = jnp.zeros((cols, dst.shape[1]), dst.dtype)
    dst[0:cols, :] = zero
    dst[dst.shape[0] - cols :, :] = zero


def project_kernel(tiles, cols, token_ref, w_ref, out_ref, scratch):
    tile_rows, tile_cols = tiles
    core = place()[2]
    scratch[...] = jnp.dot(token_ref[...], w_ref[...], preferred_element_type=jnp.float32)
    for r in range(2 * tile_rows):
        row = turned(core, r, 2 * tile_rows - 1)
        for z in range(cols):
            at = ((r // tile_rows) * cols + z) * tile_rows + r % tile_rows
            out_ref[block(row * cols + z, tile_cols), :] = scratch[
                at * tile_cols : (at + 1) * tile_cols, :
            ]


def conv_rows(src, w_ref, first, core, cols):
    rows = src.shape[0] - 2 * cols
    total = 0.0
    for a in range(3):
        total = total + jnp.dot(
            src[a * cols : a * cols + rows, :],
            w_ref[first + turned(core, a, 2)],
            preferred_element_type=jnp.float32,
        )
    return total


def maps_kernel(
    cols, f_ref, beyond_ref, w_ref, f0_ref, first0_ref, f1_ref, first1_ref, out_ref, wide
):
    core = place()[2]
    own = f_ref.shape[0]
    f0_ref[0:own, :] = f_ref[...]
    for i in range(HALO):
        f0_ref[own + i * cols : own + (i + 1) * cols, :] = beyond_ref[
            (HALO - 1 - i) * cols : (HALO - i) * cols, :
        ]
    clear_ends(wide, cols)
    for unit, (f, first, after) in enumerate(
        ((f0_ref, first0_ref, f1_ref), (f1_ref, first1_ref, None))
    ):
        triple(wide, jax.nn.gelu(f[...]), cols)
        first[...] = conv_rows(wide, w_ref, 6 * unit, core, cols)
        triple(wide, jax.nn.gelu(first[...]), cols)
        result = f[...] + conv_rows(wide, w_ref, 6 * unit + 3, core, cols)
        if after is not None:
            after[...] = result
    result = result.astype(out_ref.dtype)
    rows = own // cols + 2
    for j in range(rows):
        i = max(j - 1, 0)
        out_ref[block(turned(core, j, rows - 1), cols), :] = result[i * cols : (i + 1) * cols]


def kernel_grads(wide, grad, out_ref, first, core, cols):
    own = grad.shape[0]
    for a in range(3):
        out_ref[first + turned(core, a, 2)] = outer_product(
            wide[a * cols : a * cols + own, :], grad
        ).astype(out_ref.dtype)


def conv_back_rows(src, w_ref, first, core, cols):
    rows, feat = src.shape[0] - 2 * cols, w_ref.shape[2]
    total = 0.0
    for a in range(3):
        tap = w_ref[first + turned(core, 2 - a, 2)]
        for b in range(3):
            total = total + back_product(
                src[a * cols : a * cols + rows, b * feat : (b + 1) * feat],
                tap[(2 - b) * feat : (3 - b) * feat],
            )
    return total


def maps_back_kernel(
    tiles,
    cols,
    tall_ref,
    far_ref,
    f0_ref,
    first0_ref,
    f1_ref,
    first1_ref,
    w_ref,
    g_ref,
    out_ref,
    wide,
    wide_g,
    total,
    parted,
):
    tile_rows, tile_cols = tiles
    core = place()[2]
    own_rows = 2 * tile_rows
    own = own_rows * cols * tile_cols
    line = cols * tile_cols
    edge = own_rows + 1

    def near(i):
        return tall_ref[block(turned(core, i, edge), line), :]

    def far(i):
        return far_ref[block(turned(1 - core, i, edge), line), :]

    for i in range(own_rows + 4):
        at = i * line
        if i < own_rows:
            value = near(i + 1)
            if i == 0:
                value = value + near(0)
            if i == own_rows - 1:
                value = value + far(edge)
        else:
            value = far(2 * own_rows - i)
            if i == own_rows:
                value = value + near(edge)
        total[at : at + line, :] = value
    rest = (own_rows + 4) * line
    total[rest:, :] = jnp.zeros((total.shape[0] - rest, total.shape[1]), jnp.float32)
    clear_ends(wide, line)
    clear_ends(wide_g, line)
    for unit, (f, first) in ((1, (f1_ref, first1_ref)), (0, (f0_ref, first0_ref))):
        triple(wide, jax.nn.gelu(first[...]), line)
        triple(wide_g, total[...], line)
        kernel_grads(
            wide, total[0:own, :].astype(wide.dtype), g_ref, 6 * unit + 3, core, line
        )
        middle = conv_back_rows(wide_g, w_ref, 6 * unit + 3, core, line)
        middle = gelu_slope(first[...]) * middle
        triple(wide, jax.nn.gelu(f[...]), line)
        triple(wide_g, middle, line)
        kernel_grads(wide, middle[0:own].astype(wide.dtype), g_ref, 6 * unit, core, line)
        inner = conv_back_rows(wide_g, w_ref, 6 * unit, core, line)
        total[...] += gelu_slope(f[...]) * inner
    for r in range(own_rows):
        row = turned(core, r, own_rows - 1)
        for z in range(cols):
            at = ((r // tile_rows) * cols + z) * tile_rows + r % tile_rows
            parted[at * tile_cols : (at + 1) * tile_cols, :] = total[
                block(row * cols + z, tile_cols), :
            ]
    out_ref[...] = parted[...].astype(out_ref.dtype)


def in_vmem(count):
    return [pl.BlockSpec(memory_space=pltpu.VMEM)] * count


def plain_call(kernel, inputs, out_shape, scratch):
    return pl.pallas_call(
        kernel,
        out_shape=out_shape,
        in_specs=in_vmem(len(inputs)),
        out_specs=in_vmem(len(out_shape)),
        scratch_shapes=scratch,
        compiler_params=pltpu.CompilerParams(vmem_limit_bytes=VMEM_LIMIT),
    )(*inputs)


def project(tokens_low, w_proj, tiles, cols):
    shape = (tokens_low.shape[0], w_proj.shape[1])
    return plain_call(
        functools.partial(project_kernel, tiles, cols),
        (tokens_low, w_proj),
        [jax.ShapeDtypeStruct(shape, jnp.float32)],
        [pltpu.VMEM(shape, jnp.float32)],
    )[0]


def maps_forward(feature, beyond, w_conv, line):
    rows, feat = feature.shape
    ext = jax.ShapeDtypeStruct((rows + HALO * line, feat), jnp.float32)
    return plain_call(
        functools.partial(maps_kernel, line),
        (feature, beyond, w_conv),
        [ext] * 4 + [jax.ShapeDtypeStruct((rows + 2 * line, feat), jnp.bfloat16)],
        [pltpu.VMEM((rows + (HALO + 2) * line, 3 * feat), jnp.bfloat16)],
    )


def maps_backward(tall, far, saved, w_conv, tiles, cols):
    rows, feat = saved[0].shape
    line = cols * tiles[1]
    own = 2 * tiles[0] * line
    return plain_call(
        functools.partial(maps_back_kernel, tiles, cols),
        (tall, far, *saved, w_conv),
        [
            jax.ShapeDtypeStruct(w_conv.shape, jnp.bfloat16),
            jax.ShapeDtypeStruct((own, feat), jnp.bfloat16),
        ],
        [pltpu.VMEM((rows + 2 * line, 3 * feat), jnp.bfloat16)] * 2
        + [pltpu.VMEM((rows, feat), jnp.float32), pltpu.VMEM((own, feat), jnp.float32)],
    )


def swap_cores(value):
    return lax.ppermute(value, "row", [(0, 1), (1, 0), (2, 3), (3, 2)])


def halve_patch(grad, axis):
    grad = jnp.moveaxis(grad, axis, 0)
    even, odd = grad[0::2], grad[1::2]
    zero = jnp.zeros_like(even[:1])
    middle = jnp.concatenate([zero, 0.75 * (even + odd), zero])
    before = jnp.concatenate([0.25 * even, zero, zero])
    after = jnp.concatenate([zero, zero, 0.25 * odd])
    return jnp.moveaxis(middle + before + after, 0, axis)


def on_chip(
    chips,
    tokens,
    cot_tokens,
    cot_merged,
    image_counts,
    scale_flags,
    shift_flags,
    qkv_w,
    attn_out_w,
    fc1_w,
    fc1_b,
    fc2_w,
    fc2_b,
    ln1_gain,
    ln1_bias,
    ln2_gain,
    ln2_bias,
    proj_w,
    conv_w,
    head_w,
    head_b,
    shift_row,
):
    slots, tile_rows, tile_cols, width = tokens.shape
    cols = lax.axis_size("col")
    sizes = (chips, slots, cols)
    tile = tile_rows * tile_cols
    feat = proj_w.shape[1]
    half_rows, all_cols = 2 * tile_rows, cols * tile_cols
    dp, y, core, z = place()
    low = jnp.bfloat16
    count = image_counts[0]
    present = (jnp.arange(slots) < count).astype(jnp.float32)
    factor = 0.5 + 0.5 * scale_flags.astype(jnp.float32)
    shift_sign = shift_flags.astype(jnp.float32)
    full_group = count == slots
    chip = y * cols + z
    borrowed = jnp.logical_and(jnp.logical_not(full_group), chip >= 2 * chips - slots)
    image_present = jnp.where(
        jnp.logical_or(jnp.logical_or(full_group, borrowed), chip < count), 1.0, 0.0
    )

    vectors = (fc1_b, fc2_b, ln1_gain, ln1_bias, ln2_gain, ln2_bias, head_b, shift_row)
    lengths = [v.shape[0] for v in vectors]
    own_small = jnp.concatenate([v.astype(low) for v in vectors] + [head_w.astype(low).reshape(-1)])
    far_small = lax.ppermute(own_small, "dp", [(0, 1), (1, 0)])
    lower = jnp.where(dp == 0, own_small, far_small).astype(jnp.float32)
    upper = jnp.where(dp == 0, far_small, own_small).astype(jnp.float32)
    small, at = [], 0
    for length in lengths:
        small.append(jnp.concatenate([lower[at : at + length], upper[at : at + length]]))
        at += length
    b_up, b_down, gain_one, bias_one, gain_two, bias_two, b_head, w_shift = small
    w_head = jnp.concatenate([lower[at:], upper[at:]]).reshape(feat, feat).astype(low)

    merged_grad = cot_merged.astype(jnp.float32).reshape(slots, -1, feat) * present[:, None, None]
    grad_shift = jnp.sum(merged_grad * shift_sign[:, None, None], (0, 1))
    head_grad = (merged_grad * factor[:, None, None]).astype(low).reshape(-1, feat)
    grad_head_b = jnp.sum(head_grad.astype(jnp.float32), 0)
    fine_grad = back_product(head_grad, w_head).astype(low).reshape(cot_merged.shape)
    patch_grad = halve_patch(halve_patch(fine_grad.astype(jnp.float32), 1), 2).astype(low)
    cells = (tile_rows + 2) * (tile_cols + 2)
    patch_grad = jnp.pad(
        patch_grad.reshape(slots, cells, feat), ((0, 0), (0, PATCH - cells), (0, 0))
    )

    halves = {
        "qkv": qkv_w[None],
        "out": attn_out_w[None],
        "fc1": fc1_w[None],
        "fc2": fc2_w[None],
        "conv": conv_w.reshape((36,) + conv_w.shape[3:]),
        "proj": proj_w[None],
    }
    halves = {name: half.astype(low) for name, half in halves.items()}
    (images, image_cots, image_patches), weights = bring_in(
        (tokens.reshape(slots, tile, width), cot_tokens.reshape(slots, tile, width), patch_grad),
        halves,
        sizes,
    )
    w_qkv, w_out, w_up, w_down, w_proj = (
        weights[name][0] for name in ("qkv", "out", "fc1", "fc2", "proj")
    )
    w_conv = weights["conv"].reshape(12, 3 * feat, feat)

    def chosen(pair):
        return jnp.where(borrowed, pair[1], pair[0])

    stream = chosen(images).reshape(-1, width).astype(jnp.float32)
    rows = stream.shape[0]

    normed, scaled_one, factor_one = norm_rows(stream, gain_one, bias_one)
    normed_low = normed.astype(low)
    projected = jnp.dot(normed_low, w_qkv, preferred_element_type=jnp.float32).astype(low)
    queries, pair_own = projected[:, :width], projected[:, width:]
    pair_far = swap_cores(pair_own)
    keys = jnp.concatenate([pair_own[:, :width], pair_far[:, :width]])
    values = jnp.concatenate([pair_own[:, width:], pair_far[:, width:]])
    attended_wide, logs = attend(queries, keys, values)
    attended = attended_wide.astype(low)
    after_attn = stream + jnp.dot(attended, w_out, preferred_element_type=jnp.float32)
    normed_two, scaled_two, factor_two = norm_rows(after_attn, gain_two, bias_two)
    normed_two_low = normed_two.astype(low)
    hidden = jnp.dot(normed_two_low, w_up, preferred_element_type=jnp.float32) + b_up
    hidden_low = jax.nn.gelu(hidden).astype(low)
    after_mlp = after_attn + (
        jnp.dot(hidden_low, w_down, preferred_element_type=jnp.float32) + b_down
    )
    tokens_low = after_mlp.astype(low)
    tiles = (tile_rows, tile_cols)
    feature = project(tokens_low, w_proj, tiles, cols)
    beyond = swap_cores(feature[(half_rows - HALO) * all_cols :])
    *saved, coarse = maps_forward(feature, beyond, w_conv, all_cols)

    coarse = coarse.reshape(half_rows + 2, all_cols, feat)
    coarse = jnp.concatenate([coarse[:, :1], coarse, coarse[:, -1:]], 1)
    cuts = [
        coarse[
            r * tile_rows : (r + 1) * tile_rows + 2, c * tile_cols : (c + 1) * tile_cols + 2
        ].reshape(cells, feat)
        for r in range(2)
        for c in range(cols)
    ]
    patch = jnp.pad(jnp.stack(cuts), ((0, 0), (0, PATCH - cells), (0, 0)))
    patch = patches_out(patch, sizes)[:, :cells]
    patch = patch.reshape(slots, tile_rows + 2, tile_cols + 2, feat).astype(jnp.float32)
    patch = jnp.where(present[:, None, None, None] > 0, patch, 0.0)
    upsampled = double_axis(double_axis(patch, 1), 2).astype(low)
    fine_rows = upsampled.reshape(-1, feat)
    head_out = jnp.dot(fine_rows, w_head, preferred_element_type=jnp.float32) + b_head
    head_out = head_out.reshape(slots, -1, feat)
    merged = (head_out * factor[:, None, None] + shift_sign[:, None, None] * w_shift) * present[
        :, None, None
    ]
    merged_out = merged.astype(low).reshape(cot_merged.shape)
    grad_head_w = outer_product(fine_rows, head_grad)

    parts = chosen(image_patches)[:, :cells].astype(jnp.float32)
    parts = parts.reshape(2, cols, tile_rows + 2, tile_cols + 2, feat)
    wide = sum(
        jnp.pad(parts[:, c], ((0, 0), (0, 0), (c * tile_cols, (cols - 1 - c) * tile_cols), (0, 0)))
        for c in range(cols)
    )
    wide = jnp.concatenate(
        [wide[:, :, 1:2] + wide[:, :, :1], wide[:, :, 2:-2], wide[:, :, -2:-1] + wide[:, :, -1:]], 2
    )
    tall = jnp.pad(wide[0], ((0, tile_rows), (0, 0), (0, 0))) + jnp.pad(
        wide[1], ((tile_rows, 0), (0, 0), (0, 0))
    )
    tall = tall.reshape(-1, feat)
    grad_conv, proj_grad = maps_backward(tall, swap_cores(tall), saved, w_conv, tiles, cols)
    grad_conv = grad_conv.reshape(36, feat, feat)

    grad_proj = outer_product(tokens_low, proj_grad)
    stream_grad = chosen(image_cots).reshape(rows, width).astype(jnp.float32)
    stream_grad = jnp.where(image_present > 0, stream_grad, 0.0) + back_product(proj_grad, w_proj)
    down_grad = stream_grad.astype(low)
    grad_down_b = jnp.sum(down_grad.astype(jnp.float32), 0)
    grad_down_w = outer_product(hidden_low, down_grad)
    up_grad = gelu_grad(hidden, back_product(down_grad, w_down)).astype(low)
    grad_up_b = jnp.sum(up_grad.astype(jnp.float32), 0)
    grad_up_w = outer_product(normed_two_low, up_grad)
    norm_grad, grad_gain_two, grad_bias_two = norm_back(
        back_product(up_grad, w_up), scaled_two, factor_two, gain_two
    )
    stream_grad = stream_grad + norm_grad
    branch_grad = stream_grad.astype(low)
    grad_out_w = outer_product(attended, branch_grad)
    attended_grad = back_product(branch_grad, w_out).astype(low)
    query_grad, key_grad, value_grad = attend_back(
        queries, keys, values, attended_wide, logs, attended_grad
    )
    pair_grad = jnp.concatenate([key_grad, value_grad], 1)
    pair_grad = pair_grad[:rows] + swap_cores(pair_grad[rows:].astype(low)).astype(jnp.float32)
    mixed_grad = jnp.concatenate([query_grad, pair_grad], 1).astype(low)
    grad_qkv = outer_product(normed_low, mixed_grad)
    norm_grad, grad_gain_one, grad_bias_one = norm_back(
        back_product(mixed_grad, w_qkv), scaled_one, factor_one, gain_one
    )
    input_grad = (stream_grad + norm_grad).astype(low)

    vector_grads = (
        grad_up_b,
        grad_down_b,
        grad_gain_one,
        grad_bias_one,
        grad_gain_two,
        grad_bias_two,
        grad_head_b,
        grad_shift,
    )
    packed = jnp.concatenate([v.reshape(2, -1) for v in vector_grads], 1).astype(low)
    room = 128 * feat
    packed = jnp.pad(packed, ((0, 0), (0, room - packed.shape[1]))).reshape(256, feat)
    grads = {
        "conv": grad_conv,
        "fc2": grad_down_w.astype(low)[None],
        "fc1": grad_up_w.astype(low)[None],
        "qkv": grad_qkv.astype(low)[None],
        "out": grad_out_w.astype(low)[None],
        "proj": grad_proj.astype(low)[None],
        "head": grad_head_w.astype(low)[None],
        "small": packed[None],
    }
    (slot_tokens, slot_grads), sums = bring_out(
        (tokens_low.reshape(chips, tile, width), input_grad.reshape(chips, tile, width)),
        grads,
        sizes,
    )
    here = present[:, None, None] > 0
    tokens_out = jnp.where(here, slot_tokens, 0).reshape(tokens.shape)
    grad_tokens = jnp.where(here, slot_grads.astype(jnp.float32), 0.0).reshape(tokens.shape)
    sums = {name: value.astype(jnp.float32) for name, value in sums.items()}
    packed = sums["small"].reshape(-1)
    pieces, at = [], 0
    for length in lengths:
        pieces.append(packed[at : at + length])
        at += length
    return (
        tokens_out,
        merged_out,
        grad_tokens,
        sums["qkv"][0],
        sums["out"][0],
        sums["fc1"][0],
        pieces[0],
        sums["fc2"][0],
        pieces[1],
        pieces[2],
        pieces[3],
        pieces[4],
        pieces[5],
        sums["proj"][0],
        sums["conv"].reshape(conv_w.shape),
        sums["head"][0],
        pieces[6],
        pieces[7],
    )


def solution(mesh):
    groups, tile_rows, tile_cols = (mesh.shape[axis] for axis in ("dp", "row", "col"))
    chips = tile_rows // 2 * tile_cols
    fits = groups == 2 and tile_rows == 4 and tile_cols == 4
    placed = (
        P("dp", "row", "col", None),
        P("dp", "row", "col", None),
        P("dp", "row", "col", None),
        P("dp"),
        P("dp"),
        P("dp"),
        P("dp", None),
        P("dp", None),
        P("dp", None),
        P("dp"),
        P("dp", None),
        P("dp"),
        P("dp"),
        P("dp"),
        P("dp"),
        P("dp"),
        P("dp", None),
        P(None, None, None, "dp", None),
        P("dp", None),
        P("dp"),
        P("dp"),
    )
    return jax.shard_map(
        functools.partial(on_chip, chips) if fits else on_device,
        mesh=mesh,
        in_specs=placed,
        out_specs=(
            P("dp", "row", "col", None),
            P("dp", "row", "col", None),
            P("dp", "row", "col", None),
            P("dp", None),
            P("dp", None),
            P("dp", None),
            P("dp"),
            P("dp", None),
            P("dp"),
            P("dp"),
            P("dp"),
            P("dp"),
            P("dp"),
            P("dp", None),
            P(None, None, None, "dp", None),
            P("dp", None),
            P("dp"),
            P("dp"),
        ),
        check_vma=False,
    )
```

```python
import functools

import jax
import jax.numpy as jnp
from jax import lax
from jax.experimental import pallas as pl
from jax.experimental.pallas import tpu as pltpu
from jax.sharding import PartitionSpec as P

HEADS = 12
HEAD_DIM = 64


epsilon = 1e-06


def extended(value, sides, width):
    for axis, dim in sides:
        peers, length = (lax.axis_size(axis), value.shape[dim])
        up = [(i, (i + 1) % peers) for i in range(peers - 1)]
        down = [(j, i) for i, j in up]
        last = lax.slice_in_dim(value, length - width, length, axis=dim)
        leading = lax.slice_in_dim(value, 0, width, axis=dim)
        before = lax.ppermute(last, axis, up)
        after = lax.ppermute(leading, axis, down)
        value = jnp.concatenate([before, value, after], axis=dim)
    return value


def norm_rows(stream, gain_row, bias_row):
    centre = stream - jnp.mean(stream, -1, keepdims=True)
    spread = jnp.mean(centre * centre, -1, keepdims=True)
    factor = lax.rsqrt(spread + epsilon)
    scaled = centre * factor
    return (scaled * gain_row + bias_row, scaled, factor)


def norm_back(cotangent, scaled, factor, gain_row):
    gained = cotangent * gain_row
    inner = (
        gained
        - jnp.mean(gained, -1, keepdims=True)
        - scaled * jnp.mean(gained * scaled, -1, keepdims=True)
    )
    return (factor * inner, jnp.sum(cotangent * scaled, 0), jnp.sum(cotangent, 0))


def gelu_grad(inputs, cotangent):
    return jax.vjp(jax.nn.gelu, inputs)[1](cotangent)[0]


def outer_product(first_op, second_op):
    return lax.dot_general(
        first_op, second_op, (((0,), (0,)), ((), ())), preferred_element_type=jnp.float32
    )


def back_product(first_op, weight):
    return lax.dot_general(
        first_op, weight, (((1,), (1,)), ((), ())), preferred_element_type=jnp.float32
    )


def add_rims(tile_map):
    return extended(tile_map, (("row", 1), ("col", 2)), 1)


def clamp_edges(padded):
    first_row = lax.axis_index("row") == 0
    last_row = lax.axis_index("row") == lax.axis_size("row") - 1
    upper = jnp.where(first_row, padded[:, 1:2], padded[:, 0:1])
    lower = jnp.where(last_row, padded[:, -2:-1], padded[:, -1:])
    padded = jnp.concatenate([upper, padded[:, 1:-1], lower], 1)
    first_col = lax.axis_index("col") == 0
    last_col = lax.axis_index("col") == lax.axis_size("col") - 1
    left_side = jnp.where(first_col, padded[:, :, 1:2], padded[:, :, 0:1])
    right_side = jnp.where(last_col, padded[:, :, -2:-1], padded[:, :, -1:])
    return jnp.concatenate([left_side, padded[:, :, 1:-1], right_side], 2)


def patches(padded):
    tall = padded.shape[1] - 2
    broad = padded.shape[2] - 2
    pieces = [
        padded[:, row_shift : row_shift + tall, col_shift : col_shift + broad]
        for row_shift in range(3)
        for col_shift in range(3)
    ]
    return jnp.concatenate(pieces, -1).reshape(-1, 9 * padded.shape[3])


def conv_apply(padded, kernel):
    result = jnp.dot(
        patches(padded), kernel.reshape(-1, kernel.shape[3]), preferred_element_type=jnp.float32
    )
    return result.reshape(padded.shape[0], padded.shape[1] - 2, padded.shape[2] - 2, -1)


def flip_kernel(kernel):
    return jnp.transpose(kernel[::-1, ::-1], (0, 1, 3, 2))


def double_axis(padded, axis_index):
    leading = jnp.moveaxis(padded, axis_index, 0)
    middle_part = leading[1:-1]
    even_part = 0.75 * middle_part + 0.25 * leading[:-2]
    odd_part = 0.75 * middle_part + 0.25 * leading[2:]
    joined = jnp.stack([even_part, odd_part], 1).reshape(
        (2 * middle_part.shape[0],) + middle_part.shape[1:]
    )
    return jnp.moveaxis(joined, 0, axis_index)


def halve_axis(padded, axis_index):
    leading = jnp.moveaxis(padded, axis_index, 0)
    even_part = leading[1:-1:2]
    odd_part = leading[2:-1:2]
    before_part = leading[0:-2:2]
    after_part = leading[3::2]
    joined = 0.75 * (even_part + odd_part) + 0.25 * (before_part + after_part)
    return jnp.moveaxis(joined, 0, axis_index)


def on_device(
    tokens,
    cot_tokens,
    cot_merged,
    image_counts,
    scale_flags,
    shift_flags,
    qkv_w,
    attn_out_w,
    fc1_w,
    fc1_b,
    fc2_w,
    fc2_b,
    ln1_gain,
    ln1_bias,
    ln2_gain,
    ln2_bias,
    proj_w,
    conv_w,
    head_w,
    head_b,
    shift_row,
):
    lowered = [
        master.astype(jnp.bfloat16)
        for master in (
            qkv_w,
            attn_out_w,
            fc1_w,
            fc1_b,
            fc2_w,
            fc2_b,
            ln1_gain,
            ln1_bias,
            ln2_gain,
            ln2_bias,
            proj_w,
            conv_w,
            head_w,
            head_b,
            shift_row,
        )
    ]
    gathered = (
        lax.all_gather(lowered[0], "dp", axis=0, tiled=True),
        lax.all_gather(lowered[1], "dp", axis=0, tiled=True),
        lax.all_gather(lowered[2], "dp", axis=0, tiled=True),
        lax.all_gather(lowered[3], "dp", axis=0, tiled=True),
        lax.all_gather(lowered[4], "dp", axis=0, tiled=True),
        lax.all_gather(lowered[5], "dp", axis=0, tiled=True),
        lax.all_gather(lowered[6], "dp", axis=0, tiled=True),
        lax.all_gather(lowered[7], "dp", axis=0, tiled=True),
        lax.all_gather(lowered[8], "dp", axis=0, tiled=True),
        lax.all_gather(lowered[9], "dp", axis=0, tiled=True),
        lax.all_gather(lowered[10], "dp", axis=0, tiled=True),
        lax.all_gather(lowered[11], "dp", axis=3, tiled=True),
        lax.all_gather(lowered[12], "dp", axis=0, tiled=True),
        lax.all_gather(lowered[13], "dp", axis=0, tiled=True),
        lax.all_gather(lowered[14], "dp", axis=0, tiled=True),
    )
    (
        w_qkv,
        w_out,
        w_up,
        b_up,
        w_down,
        b_down,
        gain_one,
        bias_one,
        gain_two,
        bias_two,
        w_proj,
        w_conv,
        w_head,
        b_head,
        w_shift,
    ) = gathered
    images = tokens.shape[0]
    tile_rows = tokens.shape[1]
    tile_cols = tokens.shape[2]
    tile_size = tile_rows * tile_cols
    model_width = tokens.shape[3]
    temper = HEAD_DIM ** (-0.5)
    present = (jnp.arange(images) < image_counts[0]).astype(jnp.float32)
    factor = 0.5 + 0.5 * scale_flags.astype(jnp.float32)
    shift_sign = shift_flags.astype(jnp.float32)
    present_rows = jnp.repeat(present, tile_size)[:, None]
    stream = tokens.astype(jnp.float32).reshape(-1, model_width)
    normed, scaled_one, factor_one = norm_rows(
        stream, gain_one.astype(jnp.float32), bias_one.astype(jnp.float32)
    )
    normed_low = normed.astype(jnp.bfloat16)
    projected = jnp.dot(normed_low, w_qkv, preferred_element_type=jnp.float32).astype(jnp.bfloat16)
    queries = projected[:, :model_width].reshape(images, tile_size, HEADS, HEAD_DIM)
    keys_own = projected[:, model_width : 2 * model_width].reshape(images, tile_size, model_width)
    values_own = projected[:, 2 * model_width :].reshape(images, tile_size, model_width)
    keys_all, values_all = (
        lax.all_gather(keys_own, ("row", "col"), axis=1, tiled=True),
        lax.all_gather(values_own, ("row", "col"), axis=1, tiled=True),
    )
    keys_heads = keys_all.reshape(images, -1, HEADS, HEAD_DIM)
    values_heads = values_all.reshape(images, -1, HEADS, HEAD_DIM)
    scores = (
        jnp.einsum("nqhd,nkhd->nhqk", queries, keys_heads, preferred_element_type=jnp.float32)
        * temper
    )
    highest_score = jnp.max(scores, -1, keepdims=True)
    exponent = jnp.exp(scores - highest_score)
    denominator = jnp.sum(exponent, -1, keepdims=True)
    log_total = highest_score + jnp.log(denominator)
    attention_low = (exponent / denominator).astype(jnp.bfloat16)
    attended = jnp.einsum(
        "nhqk,nkhd->nqhd", attention_low, values_heads, preferred_element_type=jnp.float32
    )
    attended = attended.reshape(-1, model_width).astype(jnp.bfloat16)
    after_attn = stream + jnp.dot(attended, w_out, preferred_element_type=jnp.float32)
    normed_two, scaled_two, factor_two = norm_rows(
        after_attn, gain_two.astype(jnp.float32), bias_two.astype(jnp.float32)
    )
    normed_two_low = normed_two.astype(jnp.bfloat16)
    hidden = jnp.dot(normed_two_low, w_up, preferred_element_type=jnp.float32) + b_up.astype(
        jnp.float32
    )
    hidden_low = jax.nn.gelu(hidden).astype(jnp.bfloat16)
    after_mlp = after_attn + (
        jnp.dot(hidden_low, w_down, preferred_element_type=jnp.float32) + b_down.astype(jnp.float32)
    )
    tokens_low = after_mlp.astype(jnp.bfloat16)
    tokens_out = (
        (tokens_low.astype(jnp.float32) * present_rows).astype(jnp.bfloat16).reshape(tokens.shape)
    )
    feature = jnp.dot(tokens_low, w_proj, preferred_element_type=jnp.float32).reshape(
        images, tile_rows, tile_cols, -1
    )
    channels = feature.shape[3]
    stored = []
    for unit_index in range(2):
        first_in = add_rims(jax.nn.gelu(feature).astype(jnp.bfloat16))
        first_out = conv_apply(first_in, w_conv[2 * unit_index])
        second_in = add_rims(jax.nn.gelu(first_out).astype(jnp.bfloat16))
        second_out = conv_apply(second_in, w_conv[2 * unit_index + 1])
        stored.append((feature, first_in, first_out, second_in))
        feature = feature + second_out
    coarse_map = clamp_edges(add_rims(feature.astype(jnp.bfloat16))).astype(jnp.float32)
    upsampled = double_axis(double_axis(coarse_map, 1), 2).astype(jnp.bfloat16)
    fine_rows = upsampled.reshape(-1, channels)
    head_out = jnp.dot(fine_rows, w_head, preferred_element_type=jnp.float32) + b_head.astype(
        jnp.float32
    )
    head_out = head_out.reshape(images, -1, channels)
    merged = (
        head_out * factor[:, None, None] + shift_sign[:, None, None] * w_shift.astype(jnp.float32)
    ) * present[:, None, None]
    merged_out = merged.astype(jnp.bfloat16).reshape(cot_merged.shape)
    gathered = (
        lax.all_gather(lowered[0], "dp", axis=0, tiled=True),
        lax.all_gather(lowered[1], "dp", axis=0, tiled=True),
        lax.all_gather(lowered[2], "dp", axis=0, tiled=True),
        lax.all_gather(lowered[3], "dp", axis=0, tiled=True),
        lax.all_gather(lowered[4], "dp", axis=0, tiled=True),
        lax.all_gather(lowered[5], "dp", axis=0, tiled=True),
        lax.all_gather(lowered[6], "dp", axis=0, tiled=True),
        lax.all_gather(lowered[7], "dp", axis=0, tiled=True),
        lax.all_gather(lowered[8], "dp", axis=0, tiled=True),
        lax.all_gather(lowered[9], "dp", axis=0, tiled=True),
        lax.all_gather(lowered[10], "dp", axis=0, tiled=True),
        lax.all_gather(lowered[11], "dp", axis=3, tiled=True),
        lax.all_gather(lowered[12], "dp", axis=0, tiled=True),
        lax.all_gather(lowered[13], "dp", axis=0, tiled=True),
        lax.all_gather(lowered[14], "dp", axis=0, tiled=True),
    )
    (
        w_qkv,
        w_out,
        w_up,
        b_up,
        w_down,
        b_down,
        gain_one,
        bias_one,
        gain_two,
        bias_two,
        w_proj,
        w_conv,
        w_head,
        b_head,
        w_shift,
    ) = gathered
    merged_grad = (
        cot_merged.astype(jnp.float32).reshape(images, -1, channels) * present[:, None, None]
    )
    grad_shift = jnp.sum(merged_grad * shift_sign[:, None, None], (0, 1))
    head_grad = (merged_grad * factor[:, None, None]).astype(jnp.bfloat16).reshape(-1, channels)
    grad_head_b = jnp.sum(head_grad.astype(jnp.float32), 0)
    grad_head_w = outer_product(fine_rows, head_grad)
    fine_grad = back_product(head_grad, w_head).astype(jnp.bfloat16).reshape(upsampled.shape)
    spread_grad = clamp_edges(extended(fine_grad, (("row", 1), ("col", 2)), 1)).astype(jnp.float32)
    feature_grad = halve_axis(halve_axis(spread_grad, 1), 2)
    conv_grads = [None, None, None, None]
    for unit_index in (1, 0):
        unit_input, first_in, first_out, second_in = stored[unit_index]
        second_grad = feature_grad.astype(jnp.bfloat16)
        conv_grads[2 * unit_index + 1] = outer_product(
            patches(second_in), second_grad.reshape(-1, channels)
        )
        middle_grad = conv_apply(add_rims(second_grad), flip_kernel(w_conv[2 * unit_index + 1]))
        first_grad = gelu_grad(first_out, middle_grad).astype(jnp.bfloat16)
        conv_grads[2 * unit_index] = outer_product(
            patches(first_in), first_grad.reshape(-1, channels)
        )
        inner_grad = conv_apply(add_rims(first_grad), flip_kernel(w_conv[2 * unit_index]))
        feature_grad = feature_grad + gelu_grad(unit_input, inner_grad)
    grad_conv = jnp.stack(conv_grads).reshape(4, 3, 3, channels, channels)
    proj_grad = feature_grad.astype(jnp.bfloat16).reshape(-1, channels)
    grad_proj = outer_product(tokens_low, proj_grad)
    stream_grad = cot_tokens.astype(jnp.float32).reshape(
        -1, model_width
    ) * present_rows + back_product(proj_grad, w_proj)
    down_grad = stream_grad.astype(jnp.bfloat16)
    grad_down_b = jnp.sum(down_grad.astype(jnp.float32), 0)
    grad_down_w = outer_product(hidden_low, down_grad)
    up_grad = gelu_grad(hidden, back_product(down_grad, w_down)).astype(jnp.bfloat16)
    grad_up_b = jnp.sum(up_grad.astype(jnp.float32), 0)
    grad_up_w = outer_product(normed_two_low, up_grad)
    norm_grad, grad_gain_two, grad_bias_two = norm_back(
        back_product(up_grad, w_up), scaled_two, factor_two, gain_two.astype(jnp.float32)
    )
    stream_grad = stream_grad + norm_grad
    branch_grad = stream_grad.astype(jnp.bfloat16)
    grad_out_w = outer_product(attended, branch_grad)
    attended_grad = (
        back_product(branch_grad, w_out)
        .astype(jnp.bfloat16)
        .reshape(images, tile_size, HEADS, HEAD_DIM)
    )
    keys_heads = keys_all.reshape(images, -1, HEADS, HEAD_DIM)
    values_heads = values_all.reshape(images, -1, HEADS, HEAD_DIM)
    scores = (
        jnp.einsum("nqhd,nkhd->nhqk", queries, keys_heads, preferred_element_type=jnp.float32)
        * temper
    )
    attention_full = jnp.exp(scores - log_total)
    attention_low = attention_full.astype(jnp.bfloat16)
    prob_grad = jnp.einsum(
        "nqhd,nkhd->nhqk", attended_grad, values_heads, preferred_element_type=jnp.float32
    )
    centre = jnp.sum(attention_full * prob_grad, -1, keepdims=True)
    score_grad = (attention_full * (prob_grad - centre)).astype(jnp.bfloat16)
    query_grad = (
        jnp.einsum("nhqk,nkhd->nqhd", score_grad, keys_heads, preferred_element_type=jnp.float32)
        * temper
    )
    key_part = (
        jnp.einsum("nhqk,nqhd->knhd", score_grad, queries, preferred_element_type=jnp.float32)
        * temper
    )
    value_part = jnp.einsum(
        "nhqk,nqhd->knhd", attention_low, attended_grad, preferred_element_type=jnp.float32
    )
    pair_grad = lax.psum_scatter(
        jnp.concatenate(
            [
                key_part.reshape(lax.axis_size(("row", "col")) * tile_size, images, model_width),
                value_part.reshape(lax.axis_size(("row", "col")) * tile_size, images, model_width),
            ],
            2,
        ).astype(jnp.bfloat16),
        ("row", "col"),
        scatter_dimension=0,
        tiled=True,
    ).astype(jnp.float32)
    pair_grad = jnp.transpose(pair_grad, (1, 0, 2))
    mixed_grad = jnp.concatenate([query_grad.reshape(images, tile_size, model_width), pair_grad], 2)
    mixed_grad = mixed_grad.astype(jnp.bfloat16).reshape(-1, 3 * model_width)
    grad_qkv = outer_product(normed_low, mixed_grad)
    norm_grad, grad_gain_one, grad_bias_one = norm_back(
        back_product(mixed_grad, w_qkv), scaled_one, factor_one, gain_one.astype(jnp.float32)
    )
    input_grad = (stream_grad + norm_grad).reshape(tokens.shape)
    shards = (
        lax.psum_scatter(
            grad_qkv.astype(jnp.bfloat16), "dp", scatter_dimension=0, tiled=True
        ).astype(jnp.float32),
        lax.psum_scatter(
            grad_out_w.astype(jnp.bfloat16), "dp", scatter_dimension=0, tiled=True
        ).astype(jnp.float32),
        lax.psum_scatter(
            grad_up_w.astype(jnp.bfloat16), "dp", scatter_dimension=0, tiled=True
        ).astype(jnp.float32),
        lax.psum_scatter(
            grad_up_b.astype(jnp.bfloat16), "dp", scatter_dimension=0, tiled=True
        ).astype(jnp.float32),
        lax.psum_scatter(
            grad_down_w.astype(jnp.bfloat16), "dp", scatter_dimension=0, tiled=True
        ).astype(jnp.float32),
        lax.psum_scatter(
            grad_down_b.astype(jnp.bfloat16), "dp", scatter_dimension=0, tiled=True
        ).astype(jnp.float32),
        lax.psum_scatter(
            grad_gain_one.astype(jnp.bfloat16), "dp", scatter_dimension=0, tiled=True
        ).astype(jnp.float32),
        lax.psum_scatter(
            grad_bias_one.astype(jnp.bfloat16), "dp", scatter_dimension=0, tiled=True
        ).astype(jnp.float32),
        lax.psum_scatter(
            grad_gain_two.astype(jnp.bfloat16), "dp", scatter_dimension=0, tiled=True
        ).astype(jnp.float32),
        lax.psum_scatter(
            grad_bias_two.astype(jnp.bfloat16), "dp", scatter_dimension=0, tiled=True
        ).astype(jnp.float32),
        lax.psum_scatter(
            grad_proj.astype(jnp.bfloat16), "dp", scatter_dimension=0, tiled=True
        ).astype(jnp.float32),
        lax.psum_scatter(
            grad_conv.astype(jnp.bfloat16), "dp", scatter_dimension=3, tiled=True
        ).astype(jnp.float32),
        lax.psum_scatter(
            grad_head_w.astype(jnp.bfloat16), "dp", scatter_dimension=0, tiled=True
        ).astype(jnp.float32),
        lax.psum_scatter(
            grad_head_b.astype(jnp.bfloat16), "dp", scatter_dimension=0, tiled=True
        ).astype(jnp.float32),
        lax.psum_scatter(
            grad_shift.astype(jnp.bfloat16), "dp", scatter_dimension=0, tiled=True
        ).astype(jnp.float32),
    )
    totals = (
        lax.psum(shards[0].astype(jnp.bfloat16), ("row", "col")).astype(jnp.float32),
        lax.psum(shards[1].astype(jnp.bfloat16), ("row", "col")).astype(jnp.float32),
        lax.psum(shards[2].astype(jnp.bfloat16), ("row", "col")).astype(jnp.float32),
        lax.psum(shards[3].astype(jnp.bfloat16), ("row", "col")).astype(jnp.float32),
        lax.psum(shards[4].astype(jnp.bfloat16), ("row", "col")).astype(jnp.float32),
        lax.psum(shards[5].astype(jnp.bfloat16), ("row", "col")).astype(jnp.float32),
        lax.psum(shards[6].astype(jnp.bfloat16), ("row", "col")).astype(jnp.float32),
        lax.psum(shards[7].astype(jnp.bfloat16), ("row", "col")).astype(jnp.float32),
        lax.psum(shards[8].astype(jnp.bfloat16), ("row", "col")).astype(jnp.float32),
        lax.psum(shards[9].astype(jnp.bfloat16), ("row", "col")).astype(jnp.float32),
        lax.psum(shards[10].astype(jnp.bfloat16), ("row", "col")).astype(jnp.float32),
        lax.psum(shards[11].astype(jnp.bfloat16), ("row", "col")).astype(jnp.float32),
        lax.psum(shards[12].astype(jnp.bfloat16), ("row", "col")).astype(jnp.float32),
        lax.psum(shards[13].astype(jnp.bfloat16), ("row", "col")).astype(jnp.float32),
        lax.psum(shards[14].astype(jnp.bfloat16), ("row", "col")).astype(jnp.float32),
    )
    return (
        tokens_out,
        merged_out,
        input_grad,
        totals[0],
        totals[1],
        totals[2],
        totals[3],
        totals[4],
        totals[5],
        totals[6],
        totals[7],
        totals[8],
        totals[9],
        totals[10],
        totals[11],
        totals[12],
        totals[13],
        totals[14],
    )


LOG2E = 1.4426950408889634
MESH = pl.DeviceIdType.MESH
HALO = 6
PATCH = 112
VMEM_LIMIT = 58 << 20


def place():
    dp, row, col = (lax.axis_index(axis) for axis in ("dp", "row", "col"))
    return dp, lax.div(row, 2), lax.rem(row, 2), col


def flip(bit):
    return 1 - bit


def send(src, dst, send_sem, recv_sem, dp, y, core, z):
    return pltpu.make_async_remote_copy(
        src_ref=src,
        dst_ref=dst,
        send_sem=send_sem,
        recv_sem=recv_sem,
        device_id={"dp": dp, "row": y * 2 + core, "col": z},
        device_id_type=MESH,
    )


def landed(ref, sem):
    return pltpu.make_async_copy(ref, ref, sem)


def to_images_start(src, dst, send_sem, recv_sem, sizes):
    chips, slots, cols = sizes
    dp, y, core, z = place()
    own = core * cols + z
    for step in range(chips):
        far_y = lax.rem(y + step // cols, 2)
        far_z = lax.rem(z + step % cols, cols)
        slot = far_y * cols + far_z
        copy = send(
            src.at[slot], dst.at[0, own], send_sem.at[step], recv_sem.at[own], dp, far_y, y, far_z
        )
        if step == 0:
            local = pltpu.make_async_copy(src.at[slot], dst.at[0, own], recv_sem.at[own])
            pl.when(core == y)(local.start)
            pl.when(core != y)(copy.start)
        else:
            copy.start()
    for extra in range(slots - chips):
        chip = 2 * chips - slots + extra
        send(
            src.at[chips + extra],
            dst.at[1, own],
            send_sem.at[chips + extra],
            recv_sem.at[chips + own],
            1 - dp,
            chip // cols,
            y,
            chip % cols,
        ).start()


def to_images_wait(src, dst, send_sem, recv_sem, sizes):
    chips, slots, cols = sizes
    dp, y, core, z = place()
    for step in range(slots):
        left = landed(src.at[0], send_sem.at[step])
        if step == 0:
            pl.when(core != y)(left.wait)
        else:
            left.wait()
    for tile in range(chips):
        landed(dst.at[0, tile], recv_sem.at[tile]).wait()

    @pl.when(y * cols + z >= 2 * chips - slots)
    def _():
        for tile in range(chips):
            landed(dst.at[1, tile], recv_sem.at[chips + tile]).wait()


def to_tiles_start(src, dst, send_sem, recv_sem, sizes):
    chips, slots, cols = sizes
    dp, y, core, z = place()
    slot = y * cols + z
    for step in range(chips):
        far_core = lax.rem(core + step // cols, 2)
        far_z = lax.rem(z + step % cols, cols)
        tile = far_core * cols + far_z
        copy = send(
            src.at[tile], dst.at[slot], send_sem.at[step], recv_sem.at[slot], dp, core, far_core, far_z
        )
        if step == 0:
            local = pltpu.make_async_copy(src.at[tile], dst.at[slot], recv_sem.at[slot])
            pl.when(core == y)(local.start)
            pl.when(core != y)(copy.start)
        else:
            copy.start()

    @pl.when(slot >= 2 * chips - slots)
    def _():
        for step in range(chips):
            far_core = step // cols
            far_z = step % cols
            other = slot + slots - chips
            send(
                src.at[step],
                dst.at[other],
                send_sem.at[chips + step],
                recv_sem.at[other],
                1 - dp,
                core,
                far_core,
                far_z,
            ).start()


def to_tiles_wait(src, dst, send_sem, recv_sem, sizes):
    chips, slots, cols = sizes
    dp, y, core, z = place()
    for step in range(chips):
        left = landed(src.at[0], send_sem.at[step])
        if step == 0:
            pl.when(core != y)(left.wait)
        else:
            left.wait()

    @pl.when(y * cols + z >= 2 * chips - slots)
    def _():
        for step in range(chips):
            landed(src.at[0], send_sem.at[chips + step]).wait()

    for slot in range(slots):
        landed(dst.at[slot], recv_sem.at[slot]).wait()


BITS = ("dp", "y", "z1", "z2")


def mate(bit):
    dp, y, core, z = place()
    low, high = lax.rem(z, 2), lax.div(z, 2)
    if bit == "core":
        return dp, y, 1 - core, z
    if bit == "dp":
        return 1 - dp, y, core, z
    if bit == "y":
        return dp, 1 - y, core, z
    if bit == "z1":
        return dp, y, core, high * 2 + 1 - low
    return dp, y, core, (1 - high) * 2 + low


def bit_of(bit):
    dp, y, core, z = place()
    return {
        "dp": dp,
        "y": y,
        "core": core,
        "z1": lax.rem(z, 2),
        "z2": lax.div(z, 2),
    }[bit]


class Gather:
    def __init__(self, whole, send_sem, recv_sem, order):
        self.whole, self.sems, self.order = whole, (send_sem, recv_sem), order + ("core",)
        self.rows = whole.shape[-2] // 16
        self.next, self.copy = 0, None

    def at(self, step):
        dp, core = bit_of("dp"), bit_of("core")
        first, second = (bit_of(bit) for bit in self.order[:2])
        start = (core * 4, core * 4 + second * 2, core * 4 + second * 2 + first)
        if step == 0:
            piece, size = dp * 8 + start[2], 1
        else:
            piece, size = (1 - dp) * 8 + start[3 - step], 2 ** (step - 1)
        rows = pl.ds(pl.multiple_of(piece * self.rows, 16), size * self.rows)
        return self.whole.at[(slice(None),) * (len(self.whole.shape) - 2) + (rows,)]

    def tick(self):
        if self.copy is not None:
            self.copy.wait()
            self.copy = None
        if self.next < 4:
            bit = (("dp",) + self.order)[self.next]
            part = self.at(self.next)
            self.copy = send(
                part, part, self.sems[0].at[self.next], self.sems[1].at[self.next], *mate(bit)
            )
            self.copy.start()
            self.next += 1

    def finish(self):
        while self.copy is not None:
            self.tick()


def pipeline(jobs):
    for slot in range(max(delay + steps for delay, steps, _, _ in jobs) + 1):
        for delay, steps, start, wait in jobs:
            step = slot - delay
            if 0 < step <= steps:
                wait(step - 1)
            if 0 <= step < steps:
                start(step)


def patch_kernel(sizes, src, dst, send_sem, recv_sem):
    to_tiles_start(src, dst, send_sem, recv_sem, sizes)
    to_tiles_wait(src, dst, send_sem, recv_sem, sizes)


def patches_out(patch, sizes):
    chips, slots, cols = sizes
    return pl.pallas_call(
        functools.partial(patch_kernel, sizes),
        out_shape=jax.ShapeDtypeStruct((slots,) + patch.shape[1:], patch.dtype),
        in_specs=[pl.BlockSpec(memory_space=pltpu.HBM)],
        out_specs=pl.BlockSpec(memory_space=pltpu.HBM),
        scratch_shapes=[
            pltpu.SemaphoreType.DMA((2 * chips,)),
            pltpu.SemaphoreType.DMA((slots,)),
        ],
        compiler_params=pltpu.CompilerParams(
            has_side_effects=True, vmem_limit_bytes=VMEM_LIMIT
        ),
    )(patch)


SUM_ORDERS = (
    ("dp", "y", "z1", "z2"),
    ("y", "z1", "dp", "z2"),
    ("z1", "dp", "y", "z2"),
)
BACK_ORDERS = (
    ("z2", "z1", "y", "core"),
    ("z2", "y", "z1", "core"),
    ("z2", "z1", "y", "core"),
)
TURNS = {
    "conv": (0, 0),
    "fc2": (1, 0),
    "fc1": (2, 0),
    "qkv": (2, 1),
    "out": (1, 1),
    "proj": (0, 1),
    "head": (0, 1),
    "small": (0, 1),
}


def reduce_steps(grad, out, acc, recvs, sems, orders):
    local_sem, send_sem, recv_sem = sems
    sum_order, back_order = orders
    half = grad.shape[-1] // 2
    core = bit_of("core")
    mine = pl.ds(pl.multiple_of(core * half, 128), half)
    theirs = pl.ds(pl.multiple_of((1 - core) * half, 128), half)
    kept = {bit: None for bit in BITS}
    whole = slice(None)
    copies = []
    forward = 1 + len(sum_order)

    def index():
        return tuple(whole if kept[b] is None else kept[b] for b in BITS)

    def add(recv):
        free = [b for b in BITS if kept[b] is None]

        def body(i, _):
            bits, left = {}, i
            for b in reversed(free):
                bits[b] = lax.rem(left, 2)
                left = lax.div(left, 2)
            at = tuple(bits[b] if b in bits else kept[b] for b in BITS)
            here = (whole,) + at
            there = (whole,) + tuple(bits[b] for b in free)
            total = acc[here].astype(jnp.float32) + recv[there].astype(jnp.float32)
            acc[here] = total.astype(acc.dtype)
            return 0

        lax.fori_loop(0, 2 ** len(free), body, 0)

    def start(step):
        if step == 0:
            local = pltpu.make_async_copy(grad.at[..., mine], acc, local_sem.at[0])
            local.start()
            copies.append(local)
            copy = send(
                grad.at[..., theirs], recvs[0], send_sem.at[0], recv_sem.at[0], *mate("core")
            )
        elif step < forward:
            bit = sum_order[step - 1]
            kept[bit] = 1 - bit_of(bit)
            src = acc.at[(whole,) + index()]
            kept[bit] = bit_of(bit)
            copy = send(src, recvs[step], send_sem.at[step], recv_sem.at[step], *mate(bit))
        elif step == forward:
            at = (whole,) + index()[1:] + (whole, mine)
            copy = pltpu.make_async_copy(acc.at[(whole,) + index()], out.at[at], local_sem.at[1])
            kept.pop("dp")
            kept["core"] = mine
        else:
            bit = back_order[step - forward - 1]
            at = (whole,) + tuple(whole if kept[b] is None else kept[b] for b in BITS[1:])
            at = at + (whole, mine)
            copy = send(
                out.at[at], out.at[at], send_sem.at[step - 1], recv_sem.at[step - 1], *mate(bit)
            )
        copy.start()
        copies.append(copy)

    def wait(step):
        while copies:
            copies.pop().wait()
        if step < forward:
            add(recvs[step])
        elif step > forward:
            kept[back_order[step - forward - 1]] = None

    return forward + 1 + len(back_order), start, wait


def recv_shapes(shape):
    lead, rows, width = shape[0], shape[5], shape[6]
    return [(lead,) + (2,) * free + (rows, width // 2) for free in (4, 3, 2, 1, 0)]


def out_kernel(sizes, turns, *refs):
    n = len(turns)
    tiles, refs = refs[:2], refs[2:]
    grads, refs = refs[:n], refs[n:]
    slots, refs = refs[:2], refs[2:]
    outs, refs = refs[:n], refs[n:]
    accs, refs = refs[:n], refs[n:]
    recvs, refs = refs[: 5 * n], refs[5 * n :]
    tile_send, tile_recv, local_sem, send_sem, recv_sem = refs
    for i in range(2):
        to_tiles_start(tiles[i], slots[i], tile_send.at[i], tile_recv.at[i], sizes)
    jobs = []
    for i in range(n):
        steps, start, wait = reduce_steps(
            grads[i],
            outs[i],
            accs[i],
            recvs[5 * i : 5 * i + 5],
            (local_sem.at[i], send_sem.at[i], recv_sem.at[i]),
            (SUM_ORDERS[turns[i][0]], BACK_ORDERS[turns[i][0]]),
        )
        jobs.append((turns[i][1], steps, start, wait))
    pipeline(jobs)
    for i in range(2):
        to_tiles_wait(tiles[i], slots[i], tile_send.at[i], tile_recv.at[i], sizes)


def bring_out(tiles, grads, sizes):
    chips, slots, cols = sizes
    names = list(grads)
    n = len(names)
    cut = []
    for name in names:
        lead, rows, width = grads[name].shape
        cut.append(grads[name].reshape(lead, 2, 2, 2, 2, rows // 16, width))
    accs = [pltpu.VMEM(g.shape[:-1] + (g.shape[-1] // 2,), jnp.bfloat16) for g in cut]
    recvs = [
        pltpu.VMEM(shape, jnp.bfloat16)
        for g in cut
        for shape in recv_shapes(g.shape)
    ]
    outs = pl.pallas_call(
        functools.partial(out_kernel, sizes, [TURNS[name] for name in names]),
        out_shape=[
            jax.ShapeDtypeStruct((slots,) + tile.shape[1:], tile.dtype) for tile in tiles
        ]
        + [jax.ShapeDtypeStruct(g.shape[:1] + g.shape[2:], jnp.bfloat16) for g in cut],
        in_specs=[pl.BlockSpec(memory_space=pltpu.HBM)] * (2 + n),
        out_specs=[pl.BlockSpec(memory_space=pltpu.HBM)] * (2 + n),
        scratch_shapes=accs
        + recvs
        + [
            pltpu.SemaphoreType.DMA((2, 2 * chips)),
            pltpu.SemaphoreType.DMA((2, slots)),
            pltpu.SemaphoreType.DMA((n, 2)),
            pltpu.SemaphoreType.DMA((n, 9)),
            pltpu.SemaphoreType.DMA((n, 9)),
        ],
        compiler_params=pltpu.CompilerParams(
            has_side_effects=True, vmem_limit_bytes=VMEM_LIMIT
        ),
    )(*tiles, *cut)
    sums = {}
    for name, out in zip(names, outs[2:]):
        lead, rows, width = grads[name].shape
        sums[name] = out.reshape(lead, rows // 2, width)
    return outs[:2], sums


SCALE = HEAD_DIM**-0.5


def attend_pair(q, k, v):
    lane = lax.broadcasted_iota(jnp.int32, (1, 128), 1)
    sub = lax.broadcasted_iota(jnp.int32, (128, 1), 0)
    out = jnp.zeros((128, q.shape[0]), jnp.float32)
    logs = []
    for h in range(2):
        mine = (lane >= 64) == (h == 1)
        scores = lax.dot_general(
            k, jnp.where(mine, q, 0), (((1,), (1,)), ((), ())), preferred_element_type=jnp.float32
        )
        top = jnp.max(scores, 0, keepdims=True) * (SCALE * LOG2E)
        e = jnp.exp2(scores * (SCALE * LOG2E) - top)
        total = jnp.sum(e, 0, keepdims=True)
        part = lax.dot_general(
            v, e.astype(jnp.bfloat16), (((0,), (0,)), ((), ())), preferred_element_type=jnp.float32
        )
        out = jnp.where((sub >= 64) == (h == 1), part / total, out)
        logs.append(top + jnp.log2(total))
    return out.T, logs


def attend_back_kernel(q_ref, k_ref, v_ref, o_ref, log_ref, g_ref, dq_ref, dk_ref, dv_ref):
    lane = lax.broadcasted_iota(jnp.int32, (1, 128), 1)
    sub = lax.broadcasted_iota(jnp.int32, (128, 1), 0)
    k, v, q, g = k_ref[...], v_ref[...], q_ref[...], g_ref[...]
    product = (g.astype(jnp.float32) * o_ref[...]).T
    dq = jnp.zeros((128, q.shape[0]), jnp.float32)
    for h in range(2):
        mine = (lane >= 64) == (h == 1)
        q_own, g_own = jnp.where(mine, q, 0), jnp.where(mine, g, 0)
        centre = jnp.sum(product[h * 64 : (h + 1) * 64], 0, keepdims=True)
        scores = lax.dot_general(
            k, q_own, (((1,), (1,)), ((), ())), preferred_element_type=jnp.float32
        )
        p = jnp.exp2(scores * (SCALE * LOG2E) - log_ref[0, h : h + 1, :])
        dp = lax.dot_general(
            v, g_own, (((1,), (1,)), ((), ())), preferred_element_type=jnp.float32
        )
        ds = (p * (dp - centre)).astype(jnp.bfloat16)
        dq_own = lax.dot_general(
            k, ds, (((0,), (0,)), ((), ())), preferred_element_type=jnp.float32
        )
        dq = jnp.where((sub >= 64) == (h == 1), dq_own * SCALE, dq)
        dk = jnp.dot(ds, q_own, preferred_element_type=jnp.float32) * SCALE
        dv = jnp.dot(p.astype(jnp.bfloat16), g_own, preferred_element_type=jnp.float32)
        if h == 0:
            dk_ref[...], dv_ref[...] = dk, dv
        else:
            dk_ref[...] += dk
            dv_ref[...] += dv
    dq_ref[...] = dq.T


def pair_block(rows):
    return pl.BlockSpec((rows, 128), lambda i: (0, i))


def attend_back(q, k, v, o, logs, g):
    rows, width = q.shape
    keys = k.shape[0]
    own, both = pair_block(rows), pair_block(keys)
    return pl.pallas_call(
        attend_back_kernel,
        grid=(width // 128,),
        in_specs=[own, both, both, own, pl.BlockSpec((1, 2, rows), lambda i: (i, 0, 0)), own],
        out_specs=[own, both, both],
        out_shape=[jax.ShapeDtypeStruct((n, width), jnp.float32) for n in (rows, keys, keys)],
        compiler_params=pltpu.CompilerParams(vmem_limit_bytes=VMEM_LIMIT),
    )(q, k, v, o, logs, g)


GELU_K, GELU_C = 0.7978845608028654, 0.044715


def gelu_slope(v):
    t = jnp.tanh(GELU_K * (v + GELU_C * v * v * v))
    return 0.5 * (1.0 + t) + 0.5 * v * (1.0 - t * t) * (GELU_K * (1.0 + 3.0 * GELU_C * v * v))


def block(row, size):
    return pl.ds(pl.multiple_of(row * size, size), size)


def turned(core, row, last):
    return core * (last - 2 * row) + row


def triple(dst, value, cols):
    rows, feat = value.shape
    col = lax.rem(lax.broadcasted_iota(jnp.int32, (rows, 1), 0), cols)
    left = jnp.where(col == 0, 0.0, pltpu.roll(value, 1, 0))
    right = jnp.where(col == cols - 1, 0.0, pltpu.roll(value, rows - 1, 0))
    body = pl.ds(cols, rows)
    dst[body, 0:feat] = left.astype(dst.dtype)
    dst[body, feat : 2 * feat] = value.astype(dst.dtype)
    dst[body, 2 * feat :] = right.astype(dst.dtype)


def clear_ends(dst, cols):
    zero = jnp.zeros((cols, dst.shape[1]), dst.dtype)
    dst[0:cols, :] = zero
    dst[dst.shape[0] - cols :, :] = zero


def taps(w_ref, line):
    value = w_ref[pl.ds(line * 3, 3)]
    return value.reshape(3 * value.shape[1], value.shape[2])


def conv_rows(src, w_ref, first, core, cols):
    rows = src.shape[0] - 2 * cols
    total = 0.0
    for a in range(3):
        total = total + jnp.dot(
            src[a * cols : a * cols + rows, :],
            taps(w_ref, first + turned(core, a, 2)),
            preferred_element_type=jnp.float32,
        )
    return total


def maps_forward(cols, own, f0_ref, first0_ref, f1_ref, first1_ref, w_ref, out_ref, wide):
    core = place()[2]
    clear_ends(wide, cols)
    for unit, (f, first, after) in enumerate(
        ((f0_ref, first0_ref, f1_ref), (f1_ref, first1_ref, None))
    ):
        triple(wide, jax.nn.gelu(f[...]), cols)
        first[...] = conv_rows(wide, w_ref, 6 * unit, core, cols)
        triple(wide, jax.nn.gelu(first[...]), cols)
        result = f[...] + conv_rows(wide, w_ref, 6 * unit + 3, core, cols)
        if after is not None:
            after[...] = result
    result = result.astype(out_ref.dtype)
    rows = own // cols + 2
    for j in range(rows):
        i = max(j - 1, 0)
        out_ref[block(turned(core, j, rows - 1), cols), :] = result[i * cols : (i + 1) * cols]


def kernel_grads(wide, grad, out_ref, first, core, cols):
    own = grad.shape[0]
    for a in range(3):
        out_ref[first + turned(core, a, 2)] = outer_product(
            wide[a * cols : a * cols + own, :], grad
        ).astype(out_ref.dtype)


def conv_back_rows(src, w_ref, first, core, cols):
    rows, feat = src.shape[0] - 2 * cols, w_ref.shape[2]
    total = 0.0
    for a in range(3):
        tap = taps(w_ref, first + turned(core, 2 - a, 2))
        for b in range(3):
            total = total + back_product(
                src[a * cols : a * cols + rows, b * feat : (b + 1) * feat],
                tap[(2 - b) * feat : (3 - b) * feat],
            )
    return total


def maps_back_kernel(
    tiles,
    cols,
    tall_ref,
    far_ref,
    f0_ref,
    first0_ref,
    f1_ref,
    first1_ref,
    w_ref,
    g_ref,
    out_ref,
    wide,
    wide_g,
    total,
    parted,
):
    tile_rows, tile_cols = tiles
    core = place()[2]
    own_rows = 2 * tile_rows
    own = own_rows * cols * tile_cols
    line = cols * tile_cols
    edge = own_rows + 1

    def near(i):
        return tall_ref[block(turned(core, i, edge), line), :]

    def far(i):
        return far_ref[block(turned(1 - core, i, edge), line), :]

    for i in range(own_rows + 4):
        at = i * line
        if i < own_rows:
            value = near(i + 1)
            if i == 0:
                value = value + near(0)
            if i == own_rows - 1:
                value = value + far(edge)
        else:
            value = far(2 * own_rows - i)
            if i == own_rows:
                value = value + near(edge)
        total[at : at + line, :] = value
    rest = (own_rows + 4) * line
    total[rest:, :] = jnp.zeros((total.shape[0] - rest, total.shape[1]), jnp.float32)
    clear_ends(wide, line)
    clear_ends(wide_g, line)
    for unit, (f, first) in ((1, (f1_ref, first1_ref)), (0, (f0_ref, first0_ref))):
        triple(wide, jax.nn.gelu(first[...]), line)
        triple(wide_g, total[...], line)
        kernel_grads(
            wide, total[0:own, :].astype(wide.dtype), g_ref, 6 * unit + 3, core, line
        )
        middle = conv_back_rows(wide_g, w_ref, 6 * unit + 3, core, line)
        middle = gelu_slope(first[...]) * middle
        triple(wide, jax.nn.gelu(f[...]), line)
        triple(wide_g, middle, line)
        kernel_grads(wide, middle[0:own].astype(wide.dtype), g_ref, 6 * unit, core, line)
        inner = conv_back_rows(wide_g, w_ref, 6 * unit, core, line)
        total[...] += gelu_slope(f[...]) * inner
    for r in range(own_rows):
        row = turned(core, r, own_rows - 1)
        for z in range(cols):
            at = ((r // tile_rows) * cols + z) * tile_rows + r % tile_rows
            parted[at * tile_cols : (at + 1) * tile_cols, :] = total[
                block(row * cols + z, tile_cols), :
            ]
    out_ref[...] = parted[...].astype(out_ref.dtype)


def in_vmem(count):
    return [pl.BlockSpec(memory_space=pltpu.VMEM)] * count


def plain_call(kernel, inputs, out_shape, scratch):
    return pl.pallas_call(
        kernel,
        out_shape=out_shape,
        in_specs=in_vmem(len(inputs)),
        out_specs=in_vmem(len(out_shape)),
        scratch_shapes=scratch,
        compiler_params=pltpu.CompilerParams(vmem_limit_bytes=VMEM_LIMIT),
    )(*inputs)


def maps_backward(tall, far, saved, w_conv, tiles, cols):
    rows, feat = saved[0].shape
    line = cols * tiles[1]
    own = 2 * tiles[0] * line
    return plain_call(
        functools.partial(maps_back_kernel, tiles, cols),
        (tall, far, *saved, w_conv),
        [
            jax.ShapeDtypeStruct((12, 3 * feat, feat), jnp.bfloat16),
            jax.ShapeDtypeStruct((own, feat), jnp.bfloat16),
        ],
        [pltpu.VMEM((rows + 2 * line, 3 * feat), jnp.bfloat16)] * 2
        + [pltpu.VMEM((rows, feat), jnp.float32), pltpu.VMEM((own, feat), jnp.float32)],
    )


WEIGHTS = ("qkv", "out", "fc1", "fc2", "proj", "conv")
GATHER_ORDERS = (("z1", "y"), ("y", "z1"), ("z1", "y"), ("y", "z1"), ("z1", "y"), ("y", "z1"))
VECTORS = ("fc1_b", "fc2_b", "ln1_gain", "ln1_bias", "ln2_gain", "ln2_bias")
SAVED = ("x", "q", "k", "v", "o", "logs", "after_attn", "hidden", "tokens_low")
MAPS = ("f0", "first0", "f1", "first1", "coarse")
STAGES = 4


def chunks_of(name, master, whole, dp):
    if name == "conv":
        half = master.shape[1]
        rows = pl.ds(pl.multiple_of(dp * half, 16), half)
        return [(master.at[t], whole.at[t, rows]) for t in range(master.shape[0])]
    half, width = master.shape
    step = half if width > 1024 or half <= 512 else 384
    wide = min(width, 768)
    out = []
    for r in range(0, half, step):
        for c in range(0, width, wide):
            rows = pl.ds(pl.multiple_of(dp * half + r, 16), step)
            out.append((master.at[pl.ds(r, step), pl.ds(c, wide)], whole.at[rows, pl.ds(c, wide)]))
    return out


def forward_kernel(sizes, tiles, *refs):
    chips, slots, cols = sizes
    tile_rows, tile_cols = tiles
    refs = list(refs)

    def take(names):
        taken = {name: refs.pop(0) for name in names}
        return taken

    tile_in = take(("tokens", "cots", "patches"))
    masters = take(WEIGHTS)
    vectors = take(VECTORS)
    flag = refs.pop(0)
    image_out = take(("cots", "patches"))
    whole_out = take(WEIGHTS)
    vector_out = take(VECTORS)
    saved = take(SAVED)
    maps = take(MAPS)
    image = refs.pop(0)
    whole = take(WEIGHTS)
    far_vectors = take(VECTORS)
    keys, values, f0, hidden_low, flat, wide, stage = (refs.pop(0) for _ in range(7))
    tile_send, tile_recv, gather_send, gather_recv, vec_send, vec_recv, stage_sem, core_sem, out_sem = refs
    dp, y, core, z = place()
    low, f32 = jnp.bfloat16, jnp.float32

    to_images_start(tile_in["tokens"], image, tile_send.at[0], tile_recv.at[0], sizes)
    vector_copies = []
    for i, name in enumerate(VECTORS):
        copy = send(
            vectors[name], far_vectors[name], vec_send.at[i], vec_recv.at[i], *mate("dp")
        )
        copy.start()
        vector_copies.append(copy)

    work = [(name, c) for name in WEIGHTS for c in chunks_of(name, masters[name], whole[name], dp)]
    incoming = {}

    def fetch(i):
        if i < len(work):
            source = work[i][1][0]
            slot = stage.at[i % STAGES, pl.ds(0, source.shape[0]), pl.ds(0, source.shape[1])]
            incoming[i] = pltpu.make_async_copy(source, slot, stage_sem.at[i % STAGES])
            incoming[i].start()

    gathers = {
        name: Gather(whole[name], gather_send.at[i], gather_recv.at[i], GATHER_ORDERS[i])
        for i, name in enumerate(WEIGHTS)
    }
    begun = []
    done = [0]
    for i in range(STAGES - 1):
        fetch(i)

    def round_next(name):
        while done[0] < len(work) and work[done[0]][0] == name:
            i = done[0]
            fetch(i + STAGES - 1)
            incoming.pop(i).wait()
            target = work[i][1][1]
            target[...] = stage[i % STAGES, : target.shape[0], : target.shape[1]].astype(low)
            done[0] += 1
        gathers[name].tick()
        begun.append(gathers[name])

    def tick():
        for gather in begun:
            gather.tick()

    out_copies = []

    def keep(src, dst):
        copy = pltpu.make_async_copy(src, dst, out_sem.at[len(out_copies)])
        copy.start()
        out_copies.append(copy)

    round_next("qkv")
    round_next("out")
    round_next("fc1")
    tick()
    round_next("fc2")
    tick()
    round_next("proj")
    gathers["qkv"].tick()
    gathers["out"].tick()
    round_next("conv")
    gathers["qkv"].finish()
    for copy in vector_copies:
        copy.wait()
    vec = {}
    for name in VECTORS:
        own, far = vectors[name][...], far_vectors[name][...]
        row = jnp.concatenate(
            [jnp.where(dp == 0, own, far), jnp.where(dp == 0, far, own)], axis=1
        )
        vec[name] = row.astype(low).astype(f32)
        vector_out[name][...] = vec[name]
    to_images_wait(tile_in["tokens"], image, tile_send.at[0], tile_recv.at[0], sizes)
    to_images_start(tile_in["patches"], image_out["patches"], tile_send.at[1], tile_recv.at[1], sizes)
    to_images_start(tile_in["cots"], image_out["cots"], tile_send.at[2], tile_recv.at[2], sizes)

    width = image.shape[3]
    x = jnp.where(flag[0:1, 0:1] > 0, image[1].astype(f32), image[0].astype(f32))
    x = x.reshape(-1, width)
    rows = x.shape[0]
    saved["x"][...] = x.astype(low)
    normed = norm_rows(x, vec["ln1_gain"], vec["ln1_bias"])[0].astype(low)
    mine = pl.ds(0, rows)
    theirs = pl.ds(rows, rows)
    core_copies = []
    for i, ref in ((1, keys), (2, values), (0, None)):
        part = jnp.dot(
            normed, whole["qkv"][:, i * width : (i + 1) * width], preferred_element_type=f32
        ).astype(low)
        if ref is None:
            saved["q"][...] = part
        else:
            ref[mine, :] = part
            copy = send(
                ref.at[mine], ref.at[theirs], core_sem.at[0, i], core_sem.at[1, i], *mate("core")
            )
            copy.start()
            core_copies.append(copy)
    tick()
    for copy in core_copies:
        copy.wait()
    keep(keys, saved["k"])
    keep(values, saved["v"])
    for name in ("qkv",):
        keep(whole[name], whole_out[name])

    for pair in range(width // 128):
        lanes = pl.ds(pair * 128, 128)
        out, logs = attend_pair(saved["q"][:, lanes], keys[:, lanes], values[:, lanes])
        saved["o"][:, lanes] = out
        for h in range(2):
            saved["logs"][pair, h : h + 1, :] = logs[h]
        if pair % 2 == 1:
            tick()
    gathers["out"].finish()
    after_attn = saved["x"][...].astype(f32) + jnp.dot(
        saved["o"][...].astype(low), whole["out"][...], preferred_element_type=f32
    )
    saved["after_attn"][...] = after_attn
    normed_two = norm_rows(after_attn, vec["ln2_gain"], vec["ln2_bias"])[0].astype(low)
    gathers["fc1"].finish()
    for c in range(0, hidden_low.shape[1], width):
        part = pl.ds(c, width)
        hidden = jnp.dot(normed_two, whole["fc1"][:, part], preferred_element_type=f32)
        hidden = hidden + vec["fc1_b"][:, c : c + width]
        saved["hidden"][:, part] = hidden
        hidden_low[:, part] = jax.nn.gelu(hidden).astype(low)
    gathers["fc2"].finish()
    after_mlp = saved["after_attn"][...] + (
        jnp.dot(hidden_low[...], whole["fc2"][...], preferred_element_type=f32) + vec["fc2_b"]
    )
    tokens_low = after_mlp.astype(low)
    saved["tokens_low"][...] = tokens_low
    gathers["proj"].finish()

    flat[...] = jnp.dot(tokens_low, whole["proj"][...], preferred_element_type=f32)
    half_rows, line = 2 * tile_rows, cols * tile_cols
    for r in range(half_rows):
        row = turned(core, r, half_rows - 1)
        for zz in range(cols):
            at = ((r // tile_rows) * cols + zz) * tile_rows + r % tile_rows
            f0[block(row * cols + zz, tile_cols), :] = flat[at * tile_cols : (at + 1) * tile_cols, :]
    core_copies = []
    for i in range(HALO):
        copy = send(
            f0.at[pl.ds((half_rows - 1 - i) * line, line)],
            f0.at[pl.ds((half_rows + i) * line, line)],
            core_sem.at[0, 3 + i],
            core_sem.at[1, 3 + i],
            *mate("core"),
        )
        copy.start()
        core_copies.append(copy)
    gathers["conv"].finish()
    for copy in core_copies:
        copy.wait()
    for name in WEIGHTS[1:]:
        keep(whole[name], whole_out[name])
    keep(f0, maps["f0"])
    maps_forward(
        line, rows, f0, maps["first0"], maps["f1"], maps["first1"], whole["conv"], maps["coarse"], wide
    )
    for copy in out_copies:
        copy.wait()
    to_images_wait(
        tile_in["patches"], image_out["patches"], tile_send.at[1], tile_recv.at[1], sizes
    )
    to_images_wait(tile_in["cots"], image_out["cots"], tile_send.at[2], tile_recv.at[2], sizes)


def run_forward(tile_in, masters, vectors, flag, sizes, tiles):
    chips, slots, cols = sizes
    low, f32 = jnp.bfloat16, jnp.float32
    shape = jax.ShapeDtypeStruct
    tile, width = tile_in[0].shape[1:]
    feat = masters["proj"].shape[1]
    hidden = masters["fc1"].shape[1]
    rows, line = chips * tile, cols * tiles[1]
    ext = rows + HALO * line
    wholes = {
        name: shape(m.shape[:-2] + (2 * m.shape[-2], m.shape[-1]), low) for name, m in masters.items()
    }
    saved = {
        "x": shape((rows, width), low),
        "q": shape((rows, width), low),
        "k": shape((2 * rows, width), low),
        "v": shape((2 * rows, width), low),
        "o": shape((rows, width), f32),
        "logs": shape((width // 128, 2, rows), f32),
        "after_attn": shape((rows, width), f32),
        "hidden": shape((rows, hidden), f32),
        "tokens_low": shape((rows, width), low),
    }
    maps = {name: shape((ext, feat), f32) for name in MAPS[:-1]}
    maps["coarse"] = shape((rows + 2 * line, feat), low)
    far = [shape((2, chips) + t.shape[1:], t.dtype) for t in tile_in]
    hbm, vmem = pl.BlockSpec(memory_space=pltpu.HBM), pl.BlockSpec(memory_space=pltpu.VMEM)
    out_shape = (
        far[1:]
        + [wholes[name] for name in WEIGHTS]
        + [shape((1, 2 * vectors[name].shape[1]), f32) for name in VECTORS]
        + [saved[name] for name in SAVED]
        + [maps[name] for name in MAPS]
    )
    out_specs = (
        [hbm] * (2 + len(WEIGHTS))
        + [vmem] * len(VECTORS)
        + [hbm if name in ("k", "v") else vmem for name in SAVED]
        + [hbm if name == "f0" else vmem for name in MAPS]
    )
    n = len(WEIGHTS)
    outs = pl.pallas_call(
        functools.partial(forward_kernel, sizes, tiles),
        out_shape=out_shape,
        in_specs=[hbm] * (3 + n) + [vmem] * (len(VECTORS) + 1),
        out_specs=out_specs,
        scratch_shapes=[pltpu.VMEM(far[0].shape, low)]
        + [pltpu.VMEM(wholes[name].shape, low) for name in WEIGHTS]
        + [pltpu.VMEM(vectors[name].shape, f32) for name in VECTORS]
        + [
            pltpu.VMEM((2 * rows, width), low),
            pltpu.VMEM((2 * rows, width), low),
            pltpu.VMEM((ext, feat), f32),
            pltpu.VMEM((rows, hidden), low),
            pltpu.VMEM((rows, feat), f32),
            pltpu.VMEM((ext + 2 * line, 3 * feat), low),
            pltpu.VMEM((STAGES, 384, 768), f32),
            pltpu.SemaphoreType.DMA((3, slots)),
            pltpu.SemaphoreType.DMA((3, 2 * chips)),
            pltpu.SemaphoreType.DMA((n, 4)),
            pltpu.SemaphoreType.DMA((n, 4)),
            pltpu.SemaphoreType.DMA((len(VECTORS),)),
            pltpu.SemaphoreType.DMA((len(VECTORS),)),
            pltpu.SemaphoreType.DMA((STAGES,)),
            pltpu.SemaphoreType.DMA((2, 3 + HALO)),
            pltpu.SemaphoreType.DMA((n + 3,)),
        ],
        compiler_params=pltpu.CompilerParams(
            has_side_effects=True, vmem_limit_bytes=VMEM_LIMIT
        ),
    )(
        *tile_in,
        *(masters[name] for name in WEIGHTS),
        *(vectors[name] for name in VECTORS),
        flag,
    )
    outs = list(outs)
    images = [outs.pop(0) for _ in range(2)]
    return (images,) + tuple(
        {name: outs.pop(0) for name in names} for names in (WEIGHTS, VECTORS, SAVED, MAPS)
    )


def swap_cores(value):
    return lax.ppermute(value, "row", [(0, 1), (1, 0), (2, 3), (3, 2)])


def halve_patch(grad, axis):
    grad = jnp.moveaxis(grad, axis, 0)
    even, odd = grad[0::2], grad[1::2]
    zero = jnp.zeros_like(even[:1])
    middle = jnp.concatenate([zero, 0.75 * (even + odd), zero])
    before = jnp.concatenate([0.25 * even, zero, zero])
    after = jnp.concatenate([zero, zero, 0.25 * odd])
    return jnp.moveaxis(middle + before + after, 0, axis)


def on_chip(
    chips,
    tokens,
    cot_tokens,
    cot_merged,
    image_counts,
    scale_flags,
    shift_flags,
    qkv_w,
    attn_out_w,
    fc1_w,
    fc1_b,
    fc2_w,
    fc2_b,
    ln1_gain,
    ln1_bias,
    ln2_gain,
    ln2_bias,
    proj_w,
    conv_w,
    head_w,
    head_b,
    shift_row,
):
    slots, tile_rows, tile_cols, width = tokens.shape
    cols = lax.axis_size("col")
    sizes = (chips, slots, cols)
    tile = tile_rows * tile_cols
    feat = proj_w.shape[1]
    half_rows, all_cols = 2 * tile_rows, cols * tile_cols
    dp, y, core, z = place()
    low = jnp.bfloat16
    count = image_counts[0]
    present = (jnp.arange(slots) < count).astype(jnp.float32)
    factor = 0.5 + 0.5 * scale_flags.astype(jnp.float32)
    shift_sign = shift_flags.astype(jnp.float32)
    full_group = count == slots
    chip = y * cols + z
    borrowed = jnp.logical_and(jnp.logical_not(full_group), chip >= 2 * chips - slots)
    image_present = jnp.where(
        jnp.logical_or(jnp.logical_or(full_group, borrowed), chip < count), 1.0, 0.0
    )

    def both_halves(value):
        far = lax.ppermute(value, "dp", [(0, 1), (1, 0)])
        return jnp.where(dp == 0, jnp.stack([value, far]), jnp.stack([far, value]))

    w_head = both_halves(head_w.astype(low)).reshape(feat, feat)
    rows_small = both_halves(jnp.stack([head_b, shift_row]))
    b_head, w_shift = (
        rows_small[:, i].reshape(-1).astype(low).astype(jnp.float32) for i in range(2)
    )

    merged_grad = cot_merged.astype(jnp.float32).reshape(slots, -1, feat) * present[:, None, None]
    grad_shift = jnp.sum(merged_grad * shift_sign[:, None, None], (0, 1))
    head_grad = (merged_grad * factor[:, None, None]).astype(low).reshape(-1, feat)
    grad_head_b = jnp.sum(head_grad.astype(jnp.float32), 0)
    fine_grad = back_product(head_grad, w_head).astype(low).reshape(cot_merged.shape)
    patch_grad = halve_patch(halve_patch(fine_grad.astype(jnp.float32), 1), 2).astype(low)
    cells = (tile_rows + 2) * (tile_cols + 2)
    patch_grad = jnp.pad(
        patch_grad.reshape(slots, cells, feat), ((0, 0), (0, PATCH - cells), (0, 0))
    )

    vectors = (fc1_b, fc2_b, ln1_gain, ln1_bias, ln2_gain, ln2_bias)
    (image_cots, image_patches), weights, vec, saved, maps = run_forward(
        (tokens.reshape(slots, tile, width), cot_tokens.reshape(slots, tile, width), patch_grad),
        {
            "qkv": qkv_w,
            "out": attn_out_w,
            "fc1": fc1_w,
            "fc2": fc2_w,
            "proj": proj_w,
            "conv": conv_w.reshape((36,) + conv_w.shape[3:]),
        },
        {name: v[None] for name, v in zip(VECTORS, vectors)},
        jnp.full((8, 128), borrowed.astype(jnp.float32)),
        sizes,
        (tile_rows, tile_cols),
    )
    w_qkv, w_out, w_up, w_down, w_proj, w_conv = (weights[name] for name in WEIGHTS)
    gain_one, bias_one, gain_two, bias_two = (vec[name] for name in VECTORS[2:])

    def chosen(pair):
        return jnp.where(borrowed, pair[1], pair[0])

    rows = chips * tile
    tiles = (tile_rows, tile_cols)
    tokens_low = saved["tokens_low"]

    coarse = maps["coarse"].reshape(half_rows + 2, all_cols, feat)
    coarse = jnp.concatenate([coarse[:, :1], coarse, coarse[:, -1:]], 1)
    cuts = [
        coarse[
            r * tile_rows : (r + 1) * tile_rows + 2, c * tile_cols : (c + 1) * tile_cols + 2
        ].reshape(cells, feat)
        for r in range(2)
        for c in range(cols)
    ]
    patch = jnp.pad(jnp.stack(cuts), ((0, 0), (0, PATCH - cells), (0, 0)))
    patch = patches_out(patch, sizes)[:, :cells]
    patch = patch.reshape(slots, tile_rows + 2, tile_cols + 2, feat).astype(jnp.float32)
    patch = jnp.where(present[:, None, None, None] > 0, patch, 0.0)
    upsampled = double_axis(double_axis(patch, 1), 2).astype(low)
    fine_rows = upsampled.reshape(-1, feat)
    head_out = jnp.dot(fine_rows, w_head, preferred_element_type=jnp.float32) + b_head
    head_out = head_out.reshape(slots, -1, feat)
    merged = (head_out * factor[:, None, None] + shift_sign[:, None, None] * w_shift) * present[
        :, None, None
    ]
    merged_out = merged.astype(low).reshape(cot_merged.shape)
    grad_head_w = outer_product(fine_rows, head_grad)

    parts = chosen(image_patches)[:, :cells].astype(jnp.float32)
    parts = parts.reshape(2, cols, tile_rows + 2, tile_cols + 2, feat)
    wide = sum(
        jnp.pad(parts[:, c], ((0, 0), (0, 0), (c * tile_cols, (cols - 1 - c) * tile_cols), (0, 0)))
        for c in range(cols)
    )
    wide = jnp.concatenate(
        [wide[:, :, 1:2] + wide[:, :, :1], wide[:, :, 2:-2], wide[:, :, -2:-1] + wide[:, :, -1:]], 2
    )
    tall = jnp.pad(wide[0], ((0, tile_rows), (0, 0), (0, 0))) + jnp.pad(
        wide[1], ((tile_rows, 0), (0, 0), (0, 0))
    )
    tall = tall.reshape(-1, feat)
    grad_conv, proj_grad = maps_backward(
        tall, swap_cores(tall), [maps[name] for name in MAPS[:-1]], w_conv, tiles, cols
    )
    grad_conv = grad_conv.reshape(36, feat, feat)

    normed, scaled_one, factor_one = norm_rows(saved["x"].astype(jnp.float32), gain_one, bias_one)
    normed_low = normed.astype(low)
    normed_two, scaled_two, factor_two = norm_rows(saved["after_attn"], gain_two, bias_two)
    normed_two_low = normed_two.astype(low)
    hidden = saved["hidden"]
    hidden_low = jax.nn.gelu(hidden).astype(low)
    attended = saved["o"].astype(low)
    grad_proj = outer_product(tokens_low, proj_grad)
    stream_grad = chosen(image_cots).reshape(rows, width).astype(jnp.float32)
    stream_grad = jnp.where(image_present > 0, stream_grad, 0.0) + back_product(proj_grad, w_proj)
    down_grad = stream_grad.astype(low)
    grad_down_b = jnp.sum(down_grad.astype(jnp.float32), 0)
    grad_down_w = outer_product(hidden_low, down_grad)
    up_grad = gelu_grad(hidden, back_product(down_grad, w_down)).astype(low)
    grad_up_b = jnp.sum(up_grad.astype(jnp.float32), 0)
    grad_up_w = outer_product(normed_two_low, up_grad)
    norm_grad, grad_gain_two, grad_bias_two = norm_back(
        back_product(up_grad, w_up), scaled_two, factor_two, gain_two
    )
    stream_grad = stream_grad + norm_grad
    branch_grad = stream_grad.astype(low)
    grad_out_w = outer_product(attended, branch_grad)
    attended_grad = back_product(branch_grad, w_out).astype(low)
    query_grad, key_grad, value_grad = attend_back(
        *(saved[name] for name in ("q", "k", "v", "o", "logs")), attended_grad
    )
    pair_grad = jnp.concatenate([key_grad, value_grad], 1)
    pair_grad = pair_grad[:rows] + swap_cores(pair_grad[rows:].astype(low)).astype(jnp.float32)
    mixed_grad = jnp.concatenate([query_grad, pair_grad], 1).astype(low)
    grad_qkv = outer_product(normed_low, mixed_grad)
    norm_grad, grad_gain_one, grad_bias_one = norm_back(
        back_product(mixed_grad, w_qkv), scaled_one, factor_one, gain_one
    )
    input_grad = (stream_grad + norm_grad).astype(low)

    vector_grads = (
        grad_up_b,
        grad_down_b,
        grad_gain_one,
        grad_bias_one,
        grad_gain_two,
        grad_bias_two,
        grad_head_b,
        grad_shift,
    )
    packed = jnp.concatenate([v.reshape(2, -1) for v in vector_grads], 1).astype(low)
    room = 128 * feat
    packed = jnp.pad(packed, ((0, 0), (0, room - packed.shape[1]))).reshape(256, feat)
    grads = {
        "conv": grad_conv,
        "fc2": grad_down_w.astype(low)[None],
        "fc1": grad_up_w.astype(low)[None],
        "qkv": grad_qkv.astype(low)[None],
        "out": grad_out_w.astype(low)[None],
        "proj": grad_proj.astype(low)[None],
        "head": grad_head_w.astype(low)[None],
        "small": packed[None],
    }
    (slot_tokens, slot_grads), sums = bring_out(
        (tokens_low.reshape(chips, tile, width), input_grad.reshape(chips, tile, width)),
        grads,
        sizes,
    )
    here = present[:, None, None] > 0
    tokens_out = jnp.where(here, slot_tokens, 0).reshape(tokens.shape)
    grad_tokens = jnp.where(here, slot_grads.astype(jnp.float32), 0.0).reshape(tokens.shape)
    sums = {name: value.astype(jnp.float32) for name, value in sums.items()}
    packed = sums["small"].reshape(-1)
    pieces, at = [], 0
    for length in (v.shape[0] for v in vectors + (head_b, shift_row)):
        pieces.append(packed[at : at + length])
        at += length
    return (
        tokens_out,
        merged_out,
        grad_tokens,
        sums["qkv"][0],
        sums["out"][0],
        sums["fc1"][0],
        pieces[0],
        sums["fc2"][0],
        pieces[1],
        pieces[2],
        pieces[3],
        pieces[4],
        pieces[5],
        sums["proj"][0],
        sums["conv"].reshape(conv_w.shape),
        sums["head"][0],
        pieces[6],
        pieces[7],
    )


def solution(mesh):
    groups, tile_rows, tile_cols = (mesh.shape[axis] for axis in ("dp", "row", "col"))
    chips = tile_rows // 2 * tile_cols
    fits = groups == 2 and tile_rows == 4 and tile_cols == 4
    placed = (
        P("dp", "row", "col", None),
        P("dp", "row", "col", None),
        P("dp", "row", "col", None),
        P("dp"),
        P("dp"),
        P("dp"),
        P("dp", None),
        P("dp", None),
        P("dp", None),
        P("dp"),
        P("dp", None),
        P("dp"),
        P("dp"),
        P("dp"),
        P("dp"),
        P("dp"),
        P("dp", None),
        P(None, None, None, "dp", None),
        P("dp", None),
        P("dp"),
        P("dp"),
    )
    return jax.shard_map(
        functools.partial(on_chip, chips) if fits else on_device,
        mesh=mesh,
        in_specs=placed,
        out_specs=(
            P("dp", "row", "col", None),
            P("dp", "row", "col", None),
            P("dp", "row", "col", None),
            P("dp", None),
            P("dp", None),
            P("dp", None),
            P("dp"),
            P("dp", None),
            P("dp"),
            P("dp"),
            P("dp"),
            P("dp"),
            P("dp"),
            P("dp", None),
            P(None, None, None, "dp", None),
            P("dp", None),
            P("dp"),
            P("dp"),
        ),
        check_vma=False,
    )
```

```python
import functools

import jax
import jax.numpy as jnp
from jax import lax
from jax.experimental import pallas as pl
from jax.experimental.pallas import tpu as pltpu
from jax.sharding import PartitionSpec as P

HEADS = 12
HEAD_DIM = 64


epsilon = 1e-06


def extended(value, sides, width):
    for axis, dim in sides:
        peers, length = (lax.axis_size(axis), value.shape[dim])
        up = [(i, (i + 1) % peers) for i in range(peers - 1)]
        down = [(j, i) for i, j in up]
        last = lax.slice_in_dim(value, length - width, length, axis=dim)
        leading = lax.slice_in_dim(value, 0, width, axis=dim)
        before = lax.ppermute(last, axis, up)
        after = lax.ppermute(leading, axis, down)
        value = jnp.concatenate([before, value, after], axis=dim)
    return value


def norm_rows(stream, gain_row, bias_row):
    centre = stream - jnp.mean(stream, -1, keepdims=True)
    spread = jnp.mean(centre * centre, -1, keepdims=True)
    factor = lax.rsqrt(spread + epsilon)
    scaled = centre * factor
    return (scaled * gain_row + bias_row, scaled, factor)


def norm_back(cotangent, scaled, factor, gain_row):
    gained = cotangent * gain_row
    inner = (
        gained
        - jnp.mean(gained, -1, keepdims=True)
        - scaled * jnp.mean(gained * scaled, -1, keepdims=True)
    )
    return (factor * inner, jnp.sum(cotangent * scaled, 0), jnp.sum(cotangent, 0))


def gelu_grad(inputs, cotangent):
    return jax.vjp(jax.nn.gelu, inputs)[1](cotangent)[0]


def outer_product(first_op, second_op):
    return lax.dot_general(
        first_op, second_op, (((0,), (0,)), ((), ())), preferred_element_type=jnp.float32
    )


def back_product(first_op, weight):
    return lax.dot_general(
        first_op, weight, (((1,), (1,)), ((), ())), preferred_element_type=jnp.float32
    )


def add_rims(tile_map):
    return extended(tile_map, (("row", 1), ("col", 2)), 1)


def clamp_edges(padded):
    first_row = lax.axis_index("row") == 0
    last_row = lax.axis_index("row") == lax.axis_size("row") - 1
    upper = jnp.where(first_row, padded[:, 1:2], padded[:, 0:1])
    lower = jnp.where(last_row, padded[:, -2:-1], padded[:, -1:])
    padded = jnp.concatenate([upper, padded[:, 1:-1], lower], 1)
    first_col = lax.axis_index("col") == 0
    last_col = lax.axis_index("col") == lax.axis_size("col") - 1
    left_side = jnp.where(first_col, padded[:, :, 1:2], padded[:, :, 0:1])
    right_side = jnp.where(last_col, padded[:, :, -2:-1], padded[:, :, -1:])
    return jnp.concatenate([left_side, padded[:, :, 1:-1], right_side], 2)


def patches(padded):
    tall = padded.shape[1] - 2
    broad = padded.shape[2] - 2
    pieces = [
        padded[:, row_shift : row_shift + tall, col_shift : col_shift + broad]
        for row_shift in range(3)
        for col_shift in range(3)
    ]
    return jnp.concatenate(pieces, -1).reshape(-1, 9 * padded.shape[3])


def conv_apply(padded, kernel):
    result = jnp.dot(
        patches(padded), kernel.reshape(-1, kernel.shape[3]), preferred_element_type=jnp.float32
    )
    return result.reshape(padded.shape[0], padded.shape[1] - 2, padded.shape[2] - 2, -1)


def flip_kernel(kernel):
    return jnp.transpose(kernel[::-1, ::-1], (0, 1, 3, 2))


def double_axis(padded, axis_index):
    leading = jnp.moveaxis(padded, axis_index, 0)
    middle_part = leading[1:-1]
    even_part = 0.75 * middle_part + 0.25 * leading[:-2]
    odd_part = 0.75 * middle_part + 0.25 * leading[2:]
    joined = jnp.stack([even_part, odd_part], 1).reshape(
        (2 * middle_part.shape[0],) + middle_part.shape[1:]
    )
    return jnp.moveaxis(joined, 0, axis_index)


def halve_axis(padded, axis_index):
    leading = jnp.moveaxis(padded, axis_index, 0)
    even_part = leading[1:-1:2]
    odd_part = leading[2:-1:2]
    before_part = leading[0:-2:2]
    after_part = leading[3::2]
    joined = 0.75 * (even_part + odd_part) + 0.25 * (before_part + after_part)
    return jnp.moveaxis(joined, 0, axis_index)


def on_device(
    tokens,
    cot_tokens,
    cot_merged,
    image_counts,
    scale_flags,
    shift_flags,
    qkv_w,
    attn_out_w,
    fc1_w,
    fc1_b,
    fc2_w,
    fc2_b,
    ln1_gain,
    ln1_bias,
    ln2_gain,
    ln2_bias,
    proj_w,
    conv_w,
    head_w,
    head_b,
    shift_row,
):
    lowered = [
        master.astype(jnp.bfloat16)
        for master in (
            qkv_w,
            attn_out_w,
            fc1_w,
            fc1_b,
            fc2_w,
            fc2_b,
            ln1_gain,
            ln1_bias,
            ln2_gain,
            ln2_bias,
            proj_w,
            conv_w,
            head_w,
            head_b,
            shift_row,
        )
    ]
    gathered = (
        lax.all_gather(lowered[0], "dp", axis=0, tiled=True),
        lax.all_gather(lowered[1], "dp", axis=0, tiled=True),
        lax.all_gather(lowered[2], "dp", axis=0, tiled=True),
        lax.all_gather(lowered[3], "dp", axis=0, tiled=True),
        lax.all_gather(lowered[4], "dp", axis=0, tiled=True),
        lax.all_gather(lowered[5], "dp", axis=0, tiled=True),
        lax.all_gather(lowered[6], "dp", axis=0, tiled=True),
        lax.all_gather(lowered[7], "dp", axis=0, tiled=True),
        lax.all_gather(lowered[8], "dp", axis=0, tiled=True),
        lax.all_gather(lowered[9], "dp", axis=0, tiled=True),
        lax.all_gather(lowered[10], "dp", axis=0, tiled=True),
        lax.all_gather(lowered[11], "dp", axis=3, tiled=True),
        lax.all_gather(lowered[12], "dp", axis=0, tiled=True),
        lax.all_gather(lowered[13], "dp", axis=0, tiled=True),
        lax.all_gather(lowered[14], "dp", axis=0, tiled=True),
    )
    (
        w_qkv,
        w_out,
        w_up,
        b_up,
        w_down,
        b_down,
        gain_one,
        bias_one,
        gain_two,
        bias_two,
        w_proj,
        w_conv,
        w_head,
        b_head,
        w_shift,
    ) = gathered
    images = tokens.shape[0]
    tile_rows = tokens.shape[1]
    tile_cols = tokens.shape[2]
    tile_size = tile_rows * tile_cols
    model_width = tokens.shape[3]
    temper = HEAD_DIM ** (-0.5)
    present = (jnp.arange(images) < image_counts[0]).astype(jnp.float32)
    factor = 0.5 + 0.5 * scale_flags.astype(jnp.float32)
    shift_sign = shift_flags.astype(jnp.float32)
    present_rows = jnp.repeat(present, tile_size)[:, None]
    stream = tokens.astype(jnp.float32).reshape(-1, model_width)
    normed, scaled_one, factor_one = norm_rows(
        stream, gain_one.astype(jnp.float32), bias_one.astype(jnp.float32)
    )
    normed_low = normed.astype(jnp.bfloat16)
    projected = jnp.dot(normed_low, w_qkv, preferred_element_type=jnp.float32).astype(jnp.bfloat16)
    queries = projected[:, :model_width].reshape(images, tile_size, HEADS, HEAD_DIM)
    keys_own = projected[:, model_width : 2 * model_width].reshape(images, tile_size, model_width)
    values_own = projected[:, 2 * model_width :].reshape(images, tile_size, model_width)
    keys_all, values_all = (
        lax.all_gather(keys_own, ("row", "col"), axis=1, tiled=True),
        lax.all_gather(values_own, ("row", "col"), axis=1, tiled=True),
    )
    keys_heads = keys_all.reshape(images, -1, HEADS, HEAD_DIM)
    values_heads = values_all.reshape(images, -1, HEADS, HEAD_DIM)
    scores = (
        jnp.einsum("nqhd,nkhd->nhqk", queries, keys_heads, preferred_element_type=jnp.float32)
        * temper
    )
    highest_score = jnp.max(scores, -1, keepdims=True)
    exponent = jnp.exp(scores - highest_score)
    denominator = jnp.sum(exponent, -1, keepdims=True)
    log_total = highest_score + jnp.log(denominator)
    attention_low = (exponent / denominator).astype(jnp.bfloat16)
    attended = jnp.einsum(
        "nhqk,nkhd->nqhd", attention_low, values_heads, preferred_element_type=jnp.float32
    )
    attended = attended.reshape(-1, model_width).astype(jnp.bfloat16)
    after_attn = stream + jnp.dot(attended, w_out, preferred_element_type=jnp.float32)
    normed_two, scaled_two, factor_two = norm_rows(
        after_attn, gain_two.astype(jnp.float32), bias_two.astype(jnp.float32)
    )
    normed_two_low = normed_two.astype(jnp.bfloat16)
    hidden = jnp.dot(normed_two_low, w_up, preferred_element_type=jnp.float32) + b_up.astype(
        jnp.float32
    )
    hidden_low = jax.nn.gelu(hidden).astype(jnp.bfloat16)
    after_mlp = after_attn + (
        jnp.dot(hidden_low, w_down, preferred_element_type=jnp.float32) + b_down.astype(jnp.float32)
    )
    tokens_low = after_mlp.astype(jnp.bfloat16)
    tokens_out = (
        (tokens_low.astype(jnp.float32) * present_rows).astype(jnp.bfloat16).reshape(tokens.shape)
    )
    feature = jnp.dot(tokens_low, w_proj, preferred_element_type=jnp.float32).reshape(
        images, tile_rows, tile_cols, -1
    )
    channels = feature.shape[3]
    stored = []
    for unit_index in range(2):
        first_in = add_rims(jax.nn.gelu(feature).astype(jnp.bfloat16))
        first_out = conv_apply(first_in, w_conv[2 * unit_index])
        second_in = add_rims(jax.nn.gelu(first_out).astype(jnp.bfloat16))
        second_out = conv_apply(second_in, w_conv[2 * unit_index + 1])
        stored.append((feature, first_in, first_out, second_in))
        feature = feature + second_out
    coarse_map = clamp_edges(add_rims(feature.astype(jnp.bfloat16))).astype(jnp.float32)
    upsampled = double_axis(double_axis(coarse_map, 1), 2).astype(jnp.bfloat16)
    fine_rows = upsampled.reshape(-1, channels)
    head_out = jnp.dot(fine_rows, w_head, preferred_element_type=jnp.float32) + b_head.astype(
        jnp.float32
    )
    head_out = head_out.reshape(images, -1, channels)
    merged = (
        head_out * factor[:, None, None] + shift_sign[:, None, None] * w_shift.astype(jnp.float32)
    ) * present[:, None, None]
    merged_out = merged.astype(jnp.bfloat16).reshape(cot_merged.shape)
    gathered = (
        lax.all_gather(lowered[0], "dp", axis=0, tiled=True),
        lax.all_gather(lowered[1], "dp", axis=0, tiled=True),
        lax.all_gather(lowered[2], "dp", axis=0, tiled=True),
        lax.all_gather(lowered[3], "dp", axis=0, tiled=True),
        lax.all_gather(lowered[4], "dp", axis=0, tiled=True),
        lax.all_gather(lowered[5], "dp", axis=0, tiled=True),
        lax.all_gather(lowered[6], "dp", axis=0, tiled=True),
        lax.all_gather(lowered[7], "dp", axis=0, tiled=True),
        lax.all_gather(lowered[8], "dp", axis=0, tiled=True),
        lax.all_gather(lowered[9], "dp", axis=0, tiled=True),
        lax.all_gather(lowered[10], "dp", axis=0, tiled=True),
        lax.all_gather(lowered[11], "dp", axis=3, tiled=True),
        lax.all_gather(lowered[12], "dp", axis=0, tiled=True),
        lax.all_gather(lowered[13], "dp", axis=0, tiled=True),
        lax.all_gather(lowered[14], "dp", axis=0, tiled=True),
    )
    (
        w_qkv,
        w_out,
        w_up,
        b_up,
        w_down,
        b_down,
        gain_one,
        bias_one,
        gain_two,
        bias_two,
        w_proj,
        w_conv,
        w_head,
        b_head,
        w_shift,
    ) = gathered
    merged_grad = (
        cot_merged.astype(jnp.float32).reshape(images, -1, channels) * present[:, None, None]
    )
    grad_shift = jnp.sum(merged_grad * shift_sign[:, None, None], (0, 1))
    head_grad = (merged_grad * factor[:, None, None]).astype(jnp.bfloat16).reshape(-1, channels)
    grad_head_b = jnp.sum(head_grad.astype(jnp.float32), 0)
    grad_head_w = outer_product(fine_rows, head_grad)
    fine_grad = back_product(head_grad, w_head).astype(jnp.bfloat16).reshape(upsampled.shape)
    spread_grad = clamp_edges(extended(fine_grad, (("row", 1), ("col", 2)), 1)).astype(jnp.float32)
    feature_grad = halve_axis(halve_axis(spread_grad, 1), 2)
    conv_grads = [None, None, None, None]
    for unit_index in (1, 0):
        unit_input, first_in, first_out, second_in = stored[unit_index]
        second_grad = feature_grad.astype(jnp.bfloat16)
        conv_grads[2 * unit_index + 1] = outer_product(
            patches(second_in), second_grad.reshape(-1, channels)
        )
        middle_grad = conv_apply(add_rims(second_grad), flip_kernel(w_conv[2 * unit_index + 1]))
        first_grad = gelu_grad(first_out, middle_grad).astype(jnp.bfloat16)
        conv_grads[2 * unit_index] = outer_product(
            patches(first_in), first_grad.reshape(-1, channels)
        )
        inner_grad = conv_apply(add_rims(first_grad), flip_kernel(w_conv[2 * unit_index]))
        feature_grad = feature_grad + gelu_grad(unit_input, inner_grad)
    grad_conv = jnp.stack(conv_grads).reshape(4, 3, 3, channels, channels)
    proj_grad = feature_grad.astype(jnp.bfloat16).reshape(-1, channels)
    grad_proj = outer_product(tokens_low, proj_grad)
    stream_grad = cot_tokens.astype(jnp.float32).reshape(
        -1, model_width
    ) * present_rows + back_product(proj_grad, w_proj)
    down_grad = stream_grad.astype(jnp.bfloat16)
    grad_down_b = jnp.sum(down_grad.astype(jnp.float32), 0)
    grad_down_w = outer_product(hidden_low, down_grad)
    up_grad = gelu_grad(hidden, back_product(down_grad, w_down)).astype(jnp.bfloat16)
    grad_up_b = jnp.sum(up_grad.astype(jnp.float32), 0)
    grad_up_w = outer_product(normed_two_low, up_grad)
    norm_grad, grad_gain_two, grad_bias_two = norm_back(
        back_product(up_grad, w_up), scaled_two, factor_two, gain_two.astype(jnp.float32)
    )
    stream_grad = stream_grad + norm_grad
    branch_grad = stream_grad.astype(jnp.bfloat16)
    grad_out_w = outer_product(attended, branch_grad)
    attended_grad = (
        back_product(branch_grad, w_out)
        .astype(jnp.bfloat16)
        .reshape(images, tile_size, HEADS, HEAD_DIM)
    )
    keys_heads = keys_all.reshape(images, -1, HEADS, HEAD_DIM)
    values_heads = values_all.reshape(images, -1, HEADS, HEAD_DIM)
    scores = (
        jnp.einsum("nqhd,nkhd->nhqk", queries, keys_heads, preferred_element_type=jnp.float32)
        * temper
    )
    attention_full = jnp.exp(scores - log_total)
    attention_low = attention_full.astype(jnp.bfloat16)
    prob_grad = jnp.einsum(
        "nqhd,nkhd->nhqk", attended_grad, values_heads, preferred_element_type=jnp.float32
    )
    centre = jnp.sum(attention_full * prob_grad, -1, keepdims=True)
    score_grad = (attention_full * (prob_grad - centre)).astype(jnp.bfloat16)
    query_grad = (
        jnp.einsum("nhqk,nkhd->nqhd", score_grad, keys_heads, preferred_element_type=jnp.float32)
        * temper
    )
    key_part = (
        jnp.einsum("nhqk,nqhd->knhd", score_grad, queries, preferred_element_type=jnp.float32)
        * temper
    )
    value_part = jnp.einsum(
        "nhqk,nqhd->knhd", attention_low, attended_grad, preferred_element_type=jnp.float32
    )
    pair_grad = lax.psum_scatter(
        jnp.concatenate(
            [
                key_part.reshape(lax.axis_size(("row", "col")) * tile_size, images, model_width),
                value_part.reshape(lax.axis_size(("row", "col")) * tile_size, images, model_width),
            ],
            2,
        ).astype(jnp.bfloat16),
        ("row", "col"),
        scatter_dimension=0,
        tiled=True,
    ).astype(jnp.float32)
    pair_grad = jnp.transpose(pair_grad, (1, 0, 2))
    mixed_grad = jnp.concatenate([query_grad.reshape(images, tile_size, model_width), pair_grad], 2)
    mixed_grad = mixed_grad.astype(jnp.bfloat16).reshape(-1, 3 * model_width)
    grad_qkv = outer_product(normed_low, mixed_grad)
    norm_grad, grad_gain_one, grad_bias_one = norm_back(
        back_product(mixed_grad, w_qkv), scaled_one, factor_one, gain_one.astype(jnp.float32)
    )
    input_grad = (stream_grad + norm_grad).reshape(tokens.shape)
    shards = (
        lax.psum_scatter(
            grad_qkv.astype(jnp.bfloat16), "dp", scatter_dimension=0, tiled=True
        ).astype(jnp.float32),
        lax.psum_scatter(
            grad_out_w.astype(jnp.bfloat16), "dp", scatter_dimension=0, tiled=True
        ).astype(jnp.float32),
        lax.psum_scatter(
            grad_up_w.astype(jnp.bfloat16), "dp", scatter_dimension=0, tiled=True
        ).astype(jnp.float32),
        lax.psum_scatter(
            grad_up_b.astype(jnp.bfloat16), "dp", scatter_dimension=0, tiled=True
        ).astype(jnp.float32),
        lax.psum_scatter(
            grad_down_w.astype(jnp.bfloat16), "dp", scatter_dimension=0, tiled=True
        ).astype(jnp.float32),
        lax.psum_scatter(
            grad_down_b.astype(jnp.bfloat16), "dp", scatter_dimension=0, tiled=True
        ).astype(jnp.float32),
        lax.psum_scatter(
            grad_gain_one.astype(jnp.bfloat16), "dp", scatter_dimension=0, tiled=True
        ).astype(jnp.float32),
        lax.psum_scatter(
            grad_bias_one.astype(jnp.bfloat16), "dp", scatter_dimension=0, tiled=True
        ).astype(jnp.float32),
        lax.psum_scatter(
            grad_gain_two.astype(jnp.bfloat16), "dp", scatter_dimension=0, tiled=True
        ).astype(jnp.float32),
        lax.psum_scatter(
            grad_bias_two.astype(jnp.bfloat16), "dp", scatter_dimension=0, tiled=True
        ).astype(jnp.float32),
        lax.psum_scatter(
            grad_proj.astype(jnp.bfloat16), "dp", scatter_dimension=0, tiled=True
        ).astype(jnp.float32),
        lax.psum_scatter(
            grad_conv.astype(jnp.bfloat16), "dp", scatter_dimension=3, tiled=True
        ).astype(jnp.float32),
        lax.psum_scatter(
            grad_head_w.astype(jnp.bfloat16), "dp", scatter_dimension=0, tiled=True
        ).astype(jnp.float32),
        lax.psum_scatter(
            grad_head_b.astype(jnp.bfloat16), "dp", scatter_dimension=0, tiled=True
        ).astype(jnp.float32),
        lax.psum_scatter(
            grad_shift.astype(jnp.bfloat16), "dp", scatter_dimension=0, tiled=True
        ).astype(jnp.float32),
    )
    totals = (
        lax.psum(shards[0].astype(jnp.bfloat16), ("row", "col")).astype(jnp.float32),
        lax.psum(shards[1].astype(jnp.bfloat16), ("row", "col")).astype(jnp.float32),
        lax.psum(shards[2].astype(jnp.bfloat16), ("row", "col")).astype(jnp.float32),
        lax.psum(shards[3].astype(jnp.bfloat16), ("row", "col")).astype(jnp.float32),
        lax.psum(shards[4].astype(jnp.bfloat16), ("row", "col")).astype(jnp.float32),
        lax.psum(shards[5].astype(jnp.bfloat16), ("row", "col")).astype(jnp.float32),
        lax.psum(shards[6].astype(jnp.bfloat16), ("row", "col")).astype(jnp.float32),
        lax.psum(shards[7].astype(jnp.bfloat16), ("row", "col")).astype(jnp.float32),
        lax.psum(shards[8].astype(jnp.bfloat16), ("row", "col")).astype(jnp.float32),
        lax.psum(shards[9].astype(jnp.bfloat16), ("row", "col")).astype(jnp.float32),
        lax.psum(shards[10].astype(jnp.bfloat16), ("row", "col")).astype(jnp.float32),
        lax.psum(shards[11].astype(jnp.bfloat16), ("row", "col")).astype(jnp.float32),
        lax.psum(shards[12].astype(jnp.bfloat16), ("row", "col")).astype(jnp.float32),
        lax.psum(shards[13].astype(jnp.bfloat16), ("row", "col")).astype(jnp.float32),
        lax.psum(shards[14].astype(jnp.bfloat16), ("row", "col")).astype(jnp.float32),
    )
    return (
        tokens_out,
        merged_out,
        input_grad,
        totals[0],
        totals[1],
        totals[2],
        totals[3],
        totals[4],
        totals[5],
        totals[6],
        totals[7],
        totals[8],
        totals[9],
        totals[10],
        totals[11],
        totals[12],
        totals[13],
        totals[14],
    )


LOG2E = 1.4426950408889634
MESH = pl.DeviceIdType.MESH
HALO = 6
PATCH = 112
VMEM_LIMIT = 58 << 20


def place():
    dp, row, col = (lax.axis_index(axis) for axis in ("dp", "row", "col"))
    return dp, lax.div(row, 2), lax.rem(row, 2), col


def flip(bit):
    return 1 - bit


def send(src, dst, send_sem, recv_sem, dp, y, core, z):
    return pltpu.make_async_remote_copy(
        src_ref=src,
        dst_ref=dst,
        send_sem=send_sem,
        recv_sem=recv_sem,
        device_id={"dp": dp, "row": y * 2 + core, "col": z},
        device_id_type=MESH,
    )


def landed(ref, sem):
    return pltpu.make_async_copy(ref, ref, sem)


def to_images_start(src, dst, send_sem, recv_sem, sizes):
    chips, slots, cols = sizes
    dp, y, core, z = place()
    own = core * cols + z
    for step in range(chips):
        far_y = lax.rem(y + step // cols, 2)
        far_z = lax.rem(z + step % cols, cols)
        slot = far_y * cols + far_z
        copy = send(
            src.at[slot], dst.at[0, own], send_sem.at[step], recv_sem.at[own], dp, far_y, y, far_z
        )
        if step == 0:
            local = pltpu.make_async_copy(src.at[slot], dst.at[0, own], recv_sem.at[own])
            pl.when(core == y)(local.start)
            pl.when(core != y)(copy.start)
        else:
            copy.start()
    for extra in range(slots - chips):
        chip = 2 * chips - slots + extra
        send(
            src.at[chips + extra],
            dst.at[1, own],
            send_sem.at[chips + extra],
            recv_sem.at[chips + own],
            1 - dp,
            chip // cols,
            y,
            chip % cols,
        ).start()


def to_images_wait(src, dst, send_sem, recv_sem, sizes):
    chips, slots, cols = sizes
    dp, y, core, z = place()
    for step in range(slots):
        left = landed(src.at[0], send_sem.at[step])
        if step == 0:
            pl.when(core != y)(left.wait)
        else:
            left.wait()
    for tile in range(chips):
        landed(dst.at[0, tile], recv_sem.at[tile]).wait()

    @pl.when(y * cols + z >= 2 * chips - slots)
    def _():
        for tile in range(chips):
            landed(dst.at[1, tile], recv_sem.at[chips + tile]).wait()


def to_tiles_start(src, dst, send_sem, recv_sem, sizes):
    chips, slots, cols = sizes
    dp, y, core, z = place()
    slot = y * cols + z
    for step in range(chips):
        far_core = lax.rem(core + step // cols, 2)
        far_z = lax.rem(z + step % cols, cols)
        tile = far_core * cols + far_z
        copy = send(
            src.at[tile], dst.at[slot], send_sem.at[step], recv_sem.at[slot], dp, core, far_core, far_z
        )
        if step == 0:
            local = pltpu.make_async_copy(src.at[tile], dst.at[slot], recv_sem.at[slot])
            pl.when(core == y)(local.start)
            pl.when(core != y)(copy.start)
        else:
            copy.start()

    @pl.when(slot >= 2 * chips - slots)
    def _():
        for step in range(chips):
            far_core = step // cols
            far_z = step % cols
            other = slot + slots - chips
            send(
                src.at[step],
                dst.at[other],
                send_sem.at[chips + step],
                recv_sem.at[other],
                1 - dp,
                core,
                far_core,
                far_z,
            ).start()


def to_tiles_wait(src, dst, send_sem, recv_sem, sizes):
    chips, slots, cols = sizes
    dp, y, core, z = place()
    for step in range(chips):
        left = landed(src.at[0], send_sem.at[step])
        if step == 0:
            pl.when(core != y)(left.wait)
        else:
            left.wait()

    @pl.when(y * cols + z >= 2 * chips - slots)
    def _():
        for step in range(chips):
            landed(src.at[0], send_sem.at[chips + step]).wait()

    for slot in range(slots):
        landed(dst.at[slot], recv_sem.at[slot]).wait()


BITS = ("dp", "y", "z1", "z2")


def mate(bit):
    dp, y, core, z = place()
    low, high = lax.rem(z, 2), lax.div(z, 2)
    if bit == "core":
        return dp, y, 1 - core, z
    if bit == "dp":
        return 1 - dp, y, core, z
    if bit == "y":
        return dp, 1 - y, core, z
    if bit == "z1":
        return dp, y, core, high * 2 + 1 - low
    return dp, y, core, (1 - high) * 2 + low


def bit_of(bit):
    dp, y, core, z = place()
    return {
        "dp": dp,
        "y": y,
        "core": core,
        "z1": lax.rem(z, 2),
        "z2": lax.div(z, 2),
    }[bit]


class Gather:
    def __init__(self, whole, send_sem, recv_sem, split):
        self.whole, self.send_sem, self.recv_sem = whole, send_sem, recv_sem
        if split:
            self.orders = (("core", "y", "z1"), ("core", "z1", "y"))
        else:
            self.orders = (("core", "y"),)
        self.next, self.copies = 0, []

    def at(self, step, side):
        order = self.orders[side]
        count = 2 ** len(order)
        rows = self.whole.shape[-2] // (2 * count)
        piece = 0
        for i, bit in enumerate(order):
            if i <= len(order) - max(step, 1):
                piece = piece + bit_of(bit) * 2 ** (len(order) - 1 - i)
        half = bit_of("dp") if step == 0 else 1 - bit_of("dp")
        size = 1 if step == 0 else 2 ** (step - 1)
        part = pl.ds(pl.multiple_of((half * count + piece) * rows, 16), size * rows)
        width = self.whole.shape[-1] // len(self.orders)
        return self.whole.at[
            (slice(None),) * (len(self.whole.shape) - 2) + (part, pl.ds(side * width, width))
        ]

    def tick(self):
        while self.copies:
            self.copies.pop().wait()
        if self.next <= len(self.orders[0]):
            for side, order in enumerate(self.orders):
                bit = (("dp",) + order[::-1])[self.next]
                part = self.at(self.next, side)
                sems = (self.send_sem.at[side, self.next], self.recv_sem.at[side, self.next])
                copy = send(part, part, *sems, *mate(bit))
                copy.start()
                self.copies.append(copy)
            self.next += 1

    def finish(self):
        while self.copies:
            self.tick()


TURNS = {
    "conv": ("dp", ("y", "z1", "z2"), ("z2", "z1", "y", "core")),
    "fc2": ("y", ("z1", "dp", "z2"), ("z2", "y", "z1", "core")),
    "fc1": ("z1", ("dp", "y", "z2"), ("z2", "y", "z1", "core")),
    "out": (None, ("y", "z1", "dp", "z2"), ("z2", "y", "z1", "core")),
    "proj": (None, ("y", "dp", "z1", "z2"), ("z2", "z1", "y", "core")),
    "head": (None, ("y", "dp", "z1", "z2"), ("z2", "z1", "y", "core")),
    "qkv": (None, ("dp", "y", "z1", "z2"), ("z2", "z1", "y", "core")),
    "small": (None, ("z1", "dp", "y", "z2"), ("z2", "y", "z1", "core")),
}
EARLY = ("conv", "fc2", "fc1")
WHOLE = ("out", "proj", "head")


class Reduce:
    def __init__(self, turn, near, away, acc, recvs, out, sems):
        self.gone, self.sum_order, self.back_order = turn
        self.near, self.away, self.acc, self.recvs, self.out, self.sems = (
            near,
            away,
            acc,
            recvs,
            out,
            sems,
        )
        self.dims = [bit for bit in BITS if bit != self.gone]
        self.kept = {bit: None for bit in BITS}
        if self.gone is not None:
            self.kept[self.gone] = bit_of(self.gone)
        half = out.shape[-1] // 2
        self.mine = pl.ds(pl.multiple_of(bit_of("core") * half, 128), half)
        self.step, self.copies = 0, []
        self.forward = 1 + len(self.sum_order)
        self.last = self.forward + len(self.back_order)

    def index(self):
        free = slice(None)
        return (free,) + tuple(free if self.kept[b] is None else self.kept[b] for b in self.dims)

    def add(self, recv):
        acc, kept, whole = self.acc, self.kept, slice(None)
        free = [b for b in self.dims if kept[b] is None]

        def body(i, _):
            bits, left = {}, i
            for b in reversed(free):
                bits[b] = lax.rem(left, 2)
                left = lax.div(left, 2)
            here = (whole,) + tuple(bits[b] if b in bits else kept[b] for b in self.dims)
            there = (whole,) + tuple(bits[b] for b in free)
            total = acc[here].astype(jnp.float32) + recv[there].astype(jnp.float32)
            acc[here] = total.astype(acc.dtype)
            return 0

        lax.fori_loop(0, 2 ** len(free), body, 0)

    def begin(self, copy):
        copy.start()
        self.copies.append(copy)

    def travel(self, src, dst, step, bit):
        _, send_sem, recv_sem = self.sems
        self.begin(send(src, dst, send_sem.at[step], recv_sem.at[step], *mate(bit)))

    def tick(self):
        step, whole, kept = self.step, slice(None), self.kept
        local_sem = self.sems[0]
        while self.copies:
            self.copies.pop().wait()
        if 0 < step <= self.forward:
            self.add(self.recvs[step - 1])
        if step == self.forward:
            kept["core"] = bit_of("core")
            at = (whole,) + tuple(kept[b] for b in BITS[1:]) + (whole, self.mine)
            self.begin(
                pltpu.make_async_copy(self.acc.at[self.index()], self.out.at[at], local_sem.at[1])
            )
        elif step == 0:
            if self.near is not None:
                self.begin(pltpu.make_async_copy(self.near, self.acc, local_sem.at[0]))
            self.travel(self.away, self.recvs[0], 0, self.gone or "core")
        elif step < self.forward:
            bit = self.sum_order[step - 1]
            kept[bit] = 1 - bit_of(bit)
            src = self.acc.at[self.index()]
            kept[bit] = bit_of(bit)
            self.travel(src, self.recvs[step], step, bit)
        elif step <= self.last:
            if step > self.forward + 1:
                kept[self.back_order[step - self.forward - 2]] = None
            bit = self.back_order[step - self.forward - 1]
            at = (whole,) + tuple(whole if kept[b] is None else kept[b] for b in BITS[1:])
            at = self.out.at[at + (whole, whole if kept["core"] is None else self.mine)]
            self.travel(at, at, step - 1, bit)
        self.step += 1

    def busy(self):
        return self.step <= self.last + 1


def recv_shapes(shape):
    free = len(shape) - 3
    return [shape[:1] + (2,) * left + shape[-2:] for left in range(free, -1, -1)]


def early_sum(near, other, bit):
    lead, rows, width = near.shape
    total = near.astype(jnp.float32) + swap_cores(other).astype(jnp.float32)
    total = total.astype(jnp.bfloat16).reshape(lead, 2, 2, 2, 2, rows // 16, width)
    axis, own = 1 + BITS.index(bit), bit_of(bit)
    keep = lax.dynamic_index_in_dim(total, own, axis, keepdims=False)
    away = lax.dynamic_index_in_dim(total, 1 - own, axis, keepdims=False)
    return keep, away


SCALE = HEAD_DIM**-0.5


def attend_pair(q, k, v):
    lane = lax.broadcasted_iota(jnp.int32, (1, 128), 1)
    sub = lax.broadcasted_iota(jnp.int32, (128, 1), 0)
    out = jnp.zeros((128, q.shape[0]), jnp.float32)
    logs = []
    for h in range(2):
        mine = (lane >= 64) == (h == 1)
        scores = lax.dot_general(
            k, jnp.where(mine, q, 0), (((1,), (1,)), ((), ())), preferred_element_type=jnp.float32
        )
        top = jnp.max(scores, 0, keepdims=True) * (SCALE * LOG2E)
        e = jnp.exp2(scores * (SCALE * LOG2E) - top)
        total = jnp.sum(e, 0, keepdims=True)
        part = lax.dot_general(
            v, e.astype(jnp.bfloat16), (((0,), (0,)), ((), ())), preferred_element_type=jnp.float32
        )
        out = jnp.where((sub >= 64) == (h == 1), part / total, out)
        logs.append(top + jnp.log2(total))
    return out.T, logs


def attend_pair_back(q, k, v, o, logs, g):
    lane = lax.broadcasted_iota(jnp.int32, (1, 128), 1)
    sub = lax.broadcasted_iota(jnp.int32, (128, 1), 0)
    product = (g.astype(jnp.float32) * o).T
    dq = jnp.zeros((128, q.shape[0]), jnp.float32)
    dk = dv = 0.0
    for h in range(2):
        mine = (lane >= 64) == (h == 1)
        q_own, g_own = jnp.where(mine, q, 0), jnp.where(mine, g, 0)
        centre = jnp.sum(product[h * 64 : (h + 1) * 64], 0, keepdims=True)
        scores = lax.dot_general(
            k, q_own, (((1,), (1,)), ((), ())), preferred_element_type=jnp.float32
        )
        p = jnp.exp2(scores * (SCALE * LOG2E) - logs[h])
        dp = lax.dot_general(
            v, g_own, (((1,), (1,)), ((), ())), preferred_element_type=jnp.float32
        )
        ds = (p * (dp - centre)).astype(jnp.bfloat16)
        dq_own = lax.dot_general(
            k, ds, (((0,), (0,)), ((), ())), preferred_element_type=jnp.float32
        )
        dq = jnp.where((sub >= 64) == (h == 1), dq_own * SCALE, dq)
        dk = dk + jnp.dot(ds, q_own, preferred_element_type=jnp.float32) * SCALE
        dv = dv + jnp.dot(p.astype(jnp.bfloat16), g_own, preferred_element_type=jnp.float32)
    return dq.T, dk, dv


BACK_INPUTS = ("q", "k", "v", "o", "logs", "g", "x", "stream", "w_qkv", "gain", "bias", "small")
LN_ROWS = 8


def backward_kernel(sizes, *refs):
    refs = list(refs)

    def take(names):
        return {name: refs.pop(0) for name in names}

    ref = take(BACK_INPUTS)
    tiles = refs.pop(0)
    near, away, grads = take(EARLY), take(EARLY), take(WHOLE)
    slot_tokens, slot_grads = refs.pop(0), refs.pop(0)
    outs = take(TURNS)
    accs = take(TURNS)
    recvs = {name: [refs.pop(0) for _ in range(4 if TURNS[name][0] else 5)] for name in TURNS}
    mixed, far_out, far_in, own_pair, grad_tile, small_wide = (refs.pop(0) for _ in range(6))
    outbox = take(("qkv", "small"))
    tile_send, tile_recv, core_sem, local_sem, send_sem, recv_sem = refs
    low, f32 = jnp.bfloat16, jnp.float32
    core = bit_of("core")

    jobs = {}
    for i, name in enumerate(TURNS):
        sems = (local_sem.at[i], send_sem.at[i], recv_sem.at[i])
        if name in EARLY:
            source = (near[name], away[name])
        elif name in WHOLE:
            half = grads[name].shape[-1] // 2
            source = tuple(
                grads[name].at[..., pl.ds(pl.multiple_of(side * half, 128), half)]
                for side in (core, 1 - core)
            )
        else:
            source = (None, outbox[name])
        jobs[name] = Reduce(TURNS[name], *source, accs[name], recvs[name], outs[name], sems)

    def tick(*names):
        for name in names:
            jobs[name].tick()

    tick(*EARLY)
    tick(*WHOLE)
    to_tiles_start(tiles, slot_tokens, tile_send.at[0], tile_recv.at[0], sizes)
    rows, width = ref["q"].shape
    for pair in range(width // 128):
        lanes = pl.ds(pair * 128, 128)
        dq, dk, dv = attend_pair_back(
            ref["q"][:, lanes],
            ref["k"][:, lanes],
            ref["v"][:, lanes],
            ref["o"][:, lanes],
            [ref["logs"][pair, h : h + 1, :] for h in range(2)],
            ref["g"][:, lanes],
        )
        mixed[:, lanes] = dq.astype(low)
        for i, value in enumerate((dk, dv)):
            to = pl.ds(i * width + pair * 128, 128)
            own_pair[:, to] = value[:rows]
            far_out[:, to] = value[rows:].astype(low)
        if pair == 2:
            tick(*WHOLE)
    pair_copy = send(far_out, far_in, core_sem.at[0], core_sem.at[1], *mate("core"))
    pair_copy.start()
    stream = ref["x"][...].astype(f32)
    normed, scaled, factor = norm_rows(stream, ref["gain"][...], ref["bias"][...])
    normed = normed.astype(low)
    pair_copy.wait()
    mixed[:, width:] = (own_pair[...] + far_in[...].astype(f32)).astype(low)

    half = mixed.shape[1] // 2
    for side, target in ((1 - core, outbox["qkv"]), (core, accs["qkv"])):
        for c in range(0, half, 384):
            part = mixed[:, pl.ds(pl.multiple_of(side * half + c, 128), 384)]
            value = outer_product(normed, part).astype(low)
            target[..., c : c + 384] = value.reshape(target.shape[:-1] + (384,))
        if target is outbox["qkv"]:
            tick(*EARLY)
    tick("qkv")
    tick(*WHOLE)
    grad = back_product(mixed[...], ref["w_qkv"][...])
    gained, grad_gain, grad_bias = norm_back(grad, scaled, factor, ref["gain"][...])
    grad_tile[...] = (ref["stream"][...] + gained).astype(low).reshape(grad_tile.shape)

    small_wide[...] = ref["small"][...]
    for v, value in enumerate((grad_gain, grad_bias)):
        value = value.reshape(1, width)
        for j in range(width // 128):
            side, at = divmod(j, width // 256)
            row = side * (small_wide.shape[0] // 2) + LN_ROWS + 2 * v + at // 2
            small_wide[row : row + 1, at % 2 * 128 : at % 2 * 128 + 128] = value[
                :, j * 128 : (j + 1) * 128
            ]
    for side, target in ((core, accs["small"]), (1 - core, outbox["small"])):
        part = small_wide[:, pl.ds(pl.multiple_of(side * 128, 128), 128)].astype(low)
        target[...] = part.reshape(target.shape)
    tick("small")
    to_tiles_start(grad_tile, slot_grads, tile_send.at[1], tile_recv.at[1], sizes)
    while any(job.busy() for job in jobs.values()):
        for job in jobs.values():
            if job.busy():
                job.tick()
    to_tiles_wait(tiles, slot_tokens, tile_send.at[0], tile_recv.at[0], sizes)
    to_tiles_wait(grad_tile, slot_grads, tile_send.at[1], tile_recv.at[1], sizes)


def run_backward(inputs, tiles, early, grads, sizes):
    chips, slots, _ = sizes
    low, f32 = jnp.bfloat16, jnp.float32
    rows, width = inputs["q"].shape
    cut, accs = {}, {}
    for name in TURNS:
        if name in EARLY:
            accs[name] = early[name][0].shape
            continue
        if name in WHOLE:
            lead, height, across = grads[name].shape
            cut[name] = grads[name].reshape(lead, 2, 2, 2, 2, height // 16, across)
        else:
            lead = 1
            height, across = (width, 3 * width) if name == "qkv" else inputs["small"].shape
        accs[name] = (lead, 2, 2, 2, 2, height // 16, across // 2)
    shape = jax.ShapeDtypeStruct
    out_shape = [shape((slots,) + tiles.shape[1:], low)] * 2 + [
        shape(acc[:1] + (2, 2, 2, acc[-2], 2 * acc[-1]), low) for acc in accs.values()
    ]
    recvs = [value for acc in accs.values() for value in recv_shapes(acc)]
    hbm, vmem = pl.BlockSpec(memory_space=pltpu.HBM), pl.BlockSpec(memory_space=pltpu.VMEM)
    n = len(TURNS)
    slot_tokens, slot_grads, *sums = pl.pallas_call(
        functools.partial(backward_kernel, sizes),
        out_shape=out_shape,
        in_specs=[vmem] * len(BACK_INPUTS) + [hbm] * (1 + 2 * len(EARLY) + len(WHOLE)),
        out_specs=[hbm] * (2 + n),
        scratch_shapes=[pltpu.VMEM(value, low) for value in list(accs.values()) + recvs]
        + [
            pltpu.VMEM((rows, 3 * width), low),
            pltpu.VMEM((rows, 2 * width), low),
            pltpu.VMEM((rows, 2 * width), low),
            pltpu.VMEM((rows, 2 * width), f32),
            pltpu.VMEM(tiles.shape, low),
            pltpu.VMEM(inputs["small"].shape, f32),
            pltpu.VMEM(accs["qkv"], low),
            pltpu.VMEM(accs["small"], low),
            pltpu.SemaphoreType.DMA((2, 2 * chips)),
            pltpu.SemaphoreType.DMA((2, slots)),
            pltpu.SemaphoreType.DMA((2,)),
            pltpu.SemaphoreType.DMA((n, 2)),
            pltpu.SemaphoreType.DMA((n, 9)),
            pltpu.SemaphoreType.DMA((n, 9)),
        ],
        compiler_params=pltpu.CompilerParams(
            has_side_effects=True, vmem_limit_bytes=VMEM_LIMIT
        ),
    )(
        *(inputs[name] for name in BACK_INPUTS),
        tiles,
        *(early[name][0] for name in EARLY),
        *(early[name][1] for name in EARLY),
        *(cut[name] for name in WHOLE),
    )
    return (
        slot_tokens,
        slot_grads,
        {
            name: out.reshape(out.shape[0], 8 * out.shape[4], out.shape[5])
            for name, out in zip(TURNS, sums)
        },
    )


GELU_K, GELU_C = 0.7978845608028654, 0.044715


def gelu_slope(v):
    t = jnp.tanh(GELU_K * (v + GELU_C * v * v * v))
    return 0.5 * (1.0 + t) + 0.5 * v * (1.0 - t * t) * (GELU_K * (1.0 + 3.0 * GELU_C * v * v))


def block(row, size):
    return pl.ds(pl.multiple_of(row * size, size), size)


def turned(core, row, last):
    return core * (last - 2 * row) + row


def triple(dst, value, cols):
    rows, feat = value.shape
    col = lax.rem(lax.broadcasted_iota(jnp.int32, (rows, 1), 0), cols)
    left = jnp.where(col == 0, 0.0, pltpu.roll(value, 1, 0))
    right = jnp.where(col == cols - 1, 0.0, pltpu.roll(value, rows - 1, 0))
    body = pl.ds(cols, rows)
    dst[body, 0:feat] = left.astype(dst.dtype)
    dst[body, feat : 2 * feat] = value.astype(dst.dtype)
    dst[body, 2 * feat :] = right.astype(dst.dtype)


def clear_ends(dst, cols):
    zero = jnp.zeros((cols, dst.shape[1]), dst.dtype)
    dst[0:cols, :] = zero
    dst[dst.shape[0] - cols :, :] = zero


def taps(w_ref, line):
    value = w_ref[pl.ds(line * 3, 3)]
    return value.reshape(3 * value.shape[1], value.shape[2])


def conv_rows(src, w_ref, first, core, cols):
    rows = src.shape[0] - 2 * cols
    total = 0.0
    for a in range(3):
        total = total + jnp.dot(
            src[a * cols : a * cols + rows, :],
            taps(w_ref, first + turned(core, a, 2)),
            preferred_element_type=jnp.float32,
        )
    return total


def maps_forward(cols, own, f0_ref, first0_ref, f1_ref, first1_ref, w_ref, out_ref, wide):
    core = place()[2]
    clear_ends(wide, cols)
    for unit, (f, first, after) in enumerate(
        ((f0_ref, first0_ref, f1_ref), (f1_ref, first1_ref, None))
    ):
        triple(wide, jax.nn.gelu(f[...]), cols)
        first[...] = conv_rows(wide, w_ref, 6 * unit, core, cols)
        triple(wide, jax.nn.gelu(first[...]), cols)
        result = f[...] + conv_rows(wide, w_ref, 6 * unit + 3, core, cols)
        if after is not None:
            after[...] = result
    result = result.astype(out_ref.dtype)
    rows = own // cols + 2
    for j in range(rows):
        i = max(j - 1, 0)
        out_ref[block(turned(core, j, rows - 1), cols), :] = result[i * cols : (i + 1) * cols]


def kernel_grads(wide, grad, out_ref, first, core, cols):
    own = grad.shape[0]
    for a in range(3):
        value = outer_product(wide[a * cols : a * cols + own, :], grad)
        half = value.shape[1] // 2
        left, right = value[:, :half], value[:, half:]
        at = first + turned(core, a, 2)
        near, other = out_ref
        near[at] = jnp.where(core == 0, left, right).astype(near.dtype)
        other[at] = jnp.where(core == 0, right, left).astype(other.dtype)


def conv_back_rows(src, w_ref, first, core, cols):
    rows, feat = src.shape[0] - 2 * cols, w_ref.shape[2]
    total = 0.0
    for a in range(3):
        tap = taps(w_ref, first + turned(core, 2 - a, 2))
        for b in range(3):
            total = total + back_product(
                src[a * cols : a * cols + rows, b * feat : (b + 1) * feat],
                tap[(2 - b) * feat : (3 - b) * feat],
            )
    return total


def maps_back_kernel(
    tiles,
    cols,
    tall_ref,
    far_ref,
    f0_ref,
    first0_ref,
    f1_ref,
    first1_ref,
    w_ref,
    patch_ref,
    near_ref,
    other_ref,
    out_ref,
    slot_ref,
    wide,
    wide_g,
    total,
    parted,
    tile_send,
    tile_recv,
):
    chips = patch_ref.shape[0]
    sizes = (chips, slot_ref.shape[0], cols)
    to_tiles_start(patch_ref, slot_ref, tile_send, tile_recv, sizes)
    g_ref = (near_ref, other_ref)
    tile_rows, tile_cols = tiles
    core = place()[2]
    own_rows = 2 * tile_rows
    own = own_rows * cols * tile_cols
    line = cols * tile_cols
    edge = own_rows + 1

    def near(i):
        return tall_ref[block(turned(core, i, edge), line), :]

    def far(i):
        return far_ref[block(turned(1 - core, i, edge), line), :]

    for i in range(own_rows + 4):
        at = i * line
        if i < own_rows:
            value = near(i + 1)
            if i == 0:
                value = value + near(0)
            if i == own_rows - 1:
                value = value + far(edge)
        else:
            value = far(2 * own_rows - i)
            if i == own_rows:
                value = value + near(edge)
        total[at : at + line, :] = value
    rest = (own_rows + 4) * line
    total[rest:, :] = jnp.zeros((total.shape[0] - rest, total.shape[1]), jnp.float32)
    clear_ends(wide, line)
    clear_ends(wide_g, line)
    for unit, (f, first) in ((1, (f1_ref, first1_ref)), (0, (f0_ref, first0_ref))):
        triple(wide, jax.nn.gelu(first[...]), line)
        triple(wide_g, total[...], line)
        kernel_grads(
            wide, total[0:own, :].astype(wide.dtype), g_ref, 6 * unit + 3, core, line
        )
        middle = conv_back_rows(wide_g, w_ref, 6 * unit + 3, core, line)
        middle = gelu_slope(first[...]) * middle
        triple(wide, jax.nn.gelu(f[...]), line)
        triple(wide_g, middle, line)
        kernel_grads(wide, middle[0:own].astype(wide.dtype), g_ref, 6 * unit, core, line)
        inner = conv_back_rows(wide_g, w_ref, 6 * unit, core, line)
        total[...] += gelu_slope(f[...]) * inner
    for r in range(own_rows):
        row = turned(core, r, own_rows - 1)
        for z in range(cols):
            at = ((r // tile_rows) * cols + z) * tile_rows + r % tile_rows
            parted[at * tile_cols : (at + 1) * tile_cols, :] = total[
                block(row * cols + z, tile_cols), :
            ]
    out_ref[...] = parted[...].astype(out_ref.dtype)
    to_tiles_wait(patch_ref, slot_ref, tile_send, tile_recv, sizes)


def in_vmem(count):
    return [pl.BlockSpec(memory_space=pltpu.VMEM)] * count


def maps_backward(tall, far, saved, w_conv, patch, slots, tiles, cols):
    rows, feat = saved[0].shape
    line = cols * tiles[1]
    own = 2 * tiles[0] * line
    low, f32 = jnp.bfloat16, jnp.float32
    hbm = pl.BlockSpec(memory_space=pltpu.HBM)
    half = jax.ShapeDtypeStruct((12, 3 * feat, feat // 2), low)
    return pl.pallas_call(
        functools.partial(maps_back_kernel, tiles, cols),
        out_shape=[
            half,
            half,
            jax.ShapeDtypeStruct((own, feat), low),
            jax.ShapeDtypeStruct((slots,) + patch.shape[1:], low),
        ],
        in_specs=in_vmem(3 + len(saved)) + [hbm],
        out_specs=in_vmem(3) + [hbm],
        scratch_shapes=[pltpu.VMEM((rows + 2 * line, 3 * feat), low)] * 2
        + [
            pltpu.VMEM((rows, feat), f32),
            pltpu.VMEM((own, feat), f32),
            pltpu.SemaphoreType.DMA((2 * patch.shape[0],)),
            pltpu.SemaphoreType.DMA((slots,)),
        ],
        compiler_params=pltpu.CompilerParams(
            has_side_effects=True, vmem_limit_bytes=VMEM_LIMIT
        ),
    )(tall, far, *saved, w_conv, patch)


WEIGHTS = ("qkv", "out", "fc1", "fc2", "proj", "conv")
VECTORS = ("fc1_b", "fc2_b", "ln1_gain", "ln1_bias", "ln2_gain", "ln2_bias")
SAVED = ("x", "q", "k", "v", "o", "logs", "after_attn", "hidden", "tokens_low")
MAPS = ("f0", "first0", "f1", "first1", "coarse")
STAGES = 4


def chunks_of(name, master, whole, dp):
    if name == "conv":
        half = master.shape[1]
        rows = pl.ds(pl.multiple_of(dp * half, 16), half)
        return [(master.at[t], whole.at[t, rows]) for t in range(master.shape[0])]
    half, width = master.shape
    step = half if width > 1024 or half <= 512 else 384
    wide = min(width, 768)
    out = []
    for r in range(0, half, step):
        for c in range(0, width, wide):
            rows = pl.ds(pl.multiple_of(dp * half + r, 16), step)
            out.append((master.at[pl.ds(r, step), pl.ds(c, wide)], whole.at[rows, pl.ds(c, wide)]))
    return out


def forward_kernel(sizes, tiles, *refs):
    chips, slots, cols = sizes
    tile_rows, tile_cols = tiles
    refs = list(refs)

    def take(names):
        taken = {name: refs.pop(0) for name in names}
        return taken

    tile_in = take(("tokens", "cots", "patches"))
    masters = take(WEIGHTS)
    vectors = take(VECTORS)
    flag = refs.pop(0)
    image_out = take(("cots", "patches"))
    whole_out = take(WEIGHTS)
    vector_out = take(VECTORS)
    saved = take(SAVED)
    maps = take(MAPS)
    image = refs.pop(0)
    whole = take(WEIGHTS)
    far_vectors = take(VECTORS)
    keys, values, f0, hidden_low, flat, wide, stage = (refs.pop(0) for _ in range(7))
    kept = take(("o", "after_attn", "hidden", "first0", "f1", "first1"))
    tile_send, tile_recv, gather_send, gather_recv, vec_send, vec_recv, stage_sem, core_sem, out_sem = refs
    dp, y, core, z = place()
    low, f32 = jnp.bfloat16, jnp.float32

    to_images_start(tile_in["tokens"], image, tile_send.at[0], tile_recv.at[0], sizes)
    vector_copies = []
    for i, name in enumerate(VECTORS):
        copy = send(
            vectors[name], far_vectors[name], vec_send.at[i], vec_recv.at[i], *mate("dp")
        )
        copy.start()
        vector_copies.append(copy)

    work = [(name, c) for name in WEIGHTS for c in chunks_of(name, masters[name], whole[name], dp)]
    incoming = {}

    def fetch(i):
        if i < len(work):
            source = work[i][1][0]
            slot = stage.at[i % STAGES, pl.ds(0, source.shape[0]), pl.ds(0, source.shape[1])]
            incoming[i] = pltpu.make_async_copy(source, slot, stage_sem.at[i % STAGES])
            incoming[i].start()

    gathers = {
        name: Gather(whole[name], gather_send.at[i], gather_recv.at[i], name in ("qkv", "out"))
        for i, name in enumerate(WEIGHTS)
    }
    done = [0]
    for i in range(STAGES - 1):
        fetch(i)

    def round_next(name):
        while done[0] < len(work) and work[done[0]][0] == name:
            i = done[0]
            fetch(i + STAGES - 1)
            incoming.pop(i).wait()
            target = work[i][1][1]
            target[...] = stage[i % STAGES, : target.shape[0], : target.shape[1]].astype(low)
            done[0] += 1

    def tick(*names):
        for name in names:
            gathers[name].tick()

    out_copies = []

    def keep(src, dst):
        copy = pltpu.make_async_copy(src, dst, out_sem.at[len(out_copies)])
        copy.start()
        out_copies.append(copy)

    round_next("qkv")
    tick("qkv")
    round_next("out")
    tick("out")
    round_next("fc1")
    tick("qkv", "fc1")
    round_next("fc2")
    round_next("proj")
    tick("qkv")
    round_next("conv")
    tick("out", "qkv", "fc1", "fc2")
    gathers["qkv"].finish()
    for copy in vector_copies:
        copy.wait()
    vec = {}
    for name in VECTORS:
        own, far = vectors[name][...], far_vectors[name][...]
        row = jnp.concatenate(
            [jnp.where(dp == 0, own, far), jnp.where(dp == 0, far, own)], axis=1
        )
        vec[name] = row.astype(low).astype(f32)
        vector_out[name][...] = vec[name]
    to_images_wait(tile_in["tokens"], image, tile_send.at[0], tile_recv.at[0], sizes)

    width = image.shape[3]
    x = jnp.where(flag[0:1, 0:1] > 0, image[1].astype(f32), image[0].astype(f32))
    x = x.reshape(-1, width)
    rows = x.shape[0]
    saved["x"][...] = x.astype(low)
    normed = norm_rows(x, vec["ln1_gain"], vec["ln1_bias"])[0].astype(low)
    mine = pl.ds(0, rows)
    theirs = pl.ds(rows, rows)
    core_copies = []
    for i, ref in ((1, keys), (2, values), (0, None)):
        part = jnp.dot(
            normed, whole["qkv"][:, i * width : (i + 1) * width], preferred_element_type=f32
        ).astype(low)
        if ref is None:
            saved["q"][...] = part
        else:
            ref[mine, :] = part
            copy = send(
                ref.at[mine], ref.at[theirs], core_sem.at[0, i], core_sem.at[1, i], *mate("core")
            )
            copy.start()
            core_copies.append(copy)
    tick("out")
    for copy in core_copies:
        copy.wait()
    tick("fc1", "fc2", "conv", "proj")
    to_images_start(tile_in["patches"], image_out["patches"], tile_send.at[1], tile_recv.at[1], sizes)
    keep(keys, saved["k"])
    keep(values, saved["v"])
    for name in ("qkv",):
        keep(whole[name], whole_out[name])

    for pair in range(width // 128):
        lanes = pl.ds(pair * 128, 128)
        out, logs = attend_pair(saved["q"][:, lanes], keys[:, lanes], values[:, lanes])
        kept["o"][:, lanes] = out
        for h in range(2):
            saved["logs"][pair, h : h + 1, :] = logs[h]
        if pair == 1:
            tick("out")
    gathers["out"].finish()
    tick("fc2", "conv", "proj")
    to_images_start(tile_in["cots"], image_out["cots"], tile_send.at[2], tile_recv.at[2], sizes)
    after_attn = saved["x"][...].astype(f32) + jnp.dot(
        kept["o"][...].astype(low), whole["out"][...], preferred_element_type=f32
    )
    kept["after_attn"][...] = after_attn
    keep(kept["o"], saved["o"])
    keep(kept["after_attn"], saved["after_attn"])
    normed_two = norm_rows(after_attn, vec["ln2_gain"], vec["ln2_bias"])[0].astype(low)
    gathers["fc1"].finish()
    for c in range(0, hidden_low.shape[1], width):
        part = pl.ds(c, width)
        hidden = jnp.dot(normed_two, whole["fc1"][:, part], preferred_element_type=f32)
        hidden = hidden + vec["fc1_b"][:, c : c + width]
        kept["hidden"][:, part] = hidden
        hidden_low[:, part] = jax.nn.gelu(hidden).astype(low)
    keep(kept["hidden"], saved["hidden"])
    gathers["fc2"].finish()
    after_mlp = kept["after_attn"][...] + (
        jnp.dot(hidden_low[...], whole["fc2"][...], preferred_element_type=f32) + vec["fc2_b"]
    )
    tokens_low = after_mlp.astype(low)
    saved["tokens_low"][...] = tokens_low
    tick("conv")
    gathers["proj"].finish()

    flat[...] = jnp.dot(tokens_low, whole["proj"][...], preferred_element_type=f32)
    half_rows, line = 2 * tile_rows, cols * tile_cols
    for r in range(half_rows):
        row = turned(core, r, half_rows - 1)
        for zz in range(cols):
            at = ((r // tile_rows) * cols + zz) * tile_rows + r % tile_rows
            f0[block(row * cols + zz, tile_cols), :] = flat[at * tile_cols : (at + 1) * tile_cols, :]
    core_copies = []
    for i in range(HALO):
        copy = send(
            f0.at[pl.ds((half_rows - 1 - i) * line, line)],
            f0.at[pl.ds((half_rows + i) * line, line)],
            core_sem.at[0, 3 + i],
            core_sem.at[1, 3 + i],
            *mate("core"),
        )
        copy.start()
        core_copies.append(copy)
    gathers["conv"].finish()
    for copy in core_copies:
        copy.wait()
    for name in WEIGHTS[1:]:
        keep(whole[name], whole_out[name])
    keep(f0, maps["f0"])
    maps_forward(
        line, rows, f0, kept["first0"], kept["f1"], kept["first1"], whole["conv"], maps["coarse"], wide
    )
    for name in ("first0", "f1", "first1"):
        keep(kept[name], maps[name])
    for copy in out_copies:
        copy.wait()
    to_images_wait(
        tile_in["patches"], image_out["patches"], tile_send.at[1], tile_recv.at[1], sizes
    )
    to_images_wait(tile_in["cots"], image_out["cots"], tile_send.at[2], tile_recv.at[2], sizes)


def run_forward(tile_in, masters, vectors, flag, sizes, tiles):
    chips, slots, cols = sizes
    low, f32 = jnp.bfloat16, jnp.float32
    shape = jax.ShapeDtypeStruct
    tile, width = tile_in[0].shape[1:]
    feat = masters["proj"].shape[1]
    hidden = masters["fc1"].shape[1]
    rows, line = chips * tile, cols * tiles[1]
    ext = rows + HALO * line
    wholes = {
        name: shape(m.shape[:-2] + (2 * m.shape[-2], m.shape[-1]), low) for name, m in masters.items()
    }
    saved = {
        "x": shape((rows, width), low),
        "q": shape((rows, width), low),
        "k": shape((2 * rows, width), low),
        "v": shape((2 * rows, width), low),
        "o": shape((rows, width), f32),
        "logs": shape((width // 128, 2, rows), f32),
        "after_attn": shape((rows, width), f32),
        "hidden": shape((rows, hidden), f32),
        "tokens_low": shape((rows, width), low),
    }
    maps = {name: shape((ext, feat), f32) for name in MAPS[:-1]}
    maps["coarse"] = shape((rows + 2 * line, feat), low)
    far = [shape((2, chips) + t.shape[1:], t.dtype) for t in tile_in]
    hbm, vmem = pl.BlockSpec(memory_space=pltpu.HBM), pl.BlockSpec(memory_space=pltpu.VMEM)
    out_shape = (
        far[1:]
        + [wholes[name] for name in WEIGHTS]
        + [shape((1, 2 * vectors[name].shape[1]), f32) for name in VECTORS]
        + [saved[name] for name in SAVED]
        + [maps[name] for name in MAPS]
    )
    out_specs = (
        [hbm] * (2 + len(WEIGHTS))
        + [vmem] * len(VECTORS)
        + [hbm if name in ("k", "v", "o", "after_attn", "hidden") else vmem for name in SAVED]
        + [vmem if name == "coarse" else hbm for name in MAPS]
    )
    n = len(WEIGHTS)
    outs = pl.pallas_call(
        functools.partial(forward_kernel, sizes, tiles),
        out_shape=out_shape,
        in_specs=[hbm] * (3 + n) + [vmem] * (len(VECTORS) + 1),
        out_specs=out_specs,
        scratch_shapes=[pltpu.VMEM(far[0].shape, low)]
        + [pltpu.VMEM(wholes[name].shape, low) for name in WEIGHTS]
        + [pltpu.VMEM(vectors[name].shape, f32) for name in VECTORS]
        + [
            pltpu.VMEM((2 * rows, width), low),
            pltpu.VMEM((2 * rows, width), low),
            pltpu.VMEM((ext, feat), f32),
            pltpu.VMEM((rows, hidden), low),
            pltpu.VMEM((rows, feat), f32),
            pltpu.VMEM((ext + 2 * line, 3 * feat), low),
            pltpu.VMEM((STAGES, 384, 768), f32),
            pltpu.VMEM((rows, width), f32),
            pltpu.VMEM((rows, width), f32),
            pltpu.VMEM((rows, hidden), f32),
            pltpu.VMEM((ext, feat), f32),
            pltpu.VMEM((ext, feat), f32),
            pltpu.VMEM((ext, feat), f32),
            pltpu.SemaphoreType.DMA((3, slots)),
            pltpu.SemaphoreType.DMA((3, 2 * chips)),
            pltpu.SemaphoreType.DMA((n, 2, 4)),
            pltpu.SemaphoreType.DMA((n, 2, 4)),
            pltpu.SemaphoreType.DMA((len(VECTORS),)),
            pltpu.SemaphoreType.DMA((len(VECTORS),)),
            pltpu.SemaphoreType.DMA((STAGES,)),
            pltpu.SemaphoreType.DMA((2, 3 + HALO)),
            pltpu.SemaphoreType.DMA((n + 9,)),
        ],
        compiler_params=pltpu.CompilerParams(
            has_side_effects=True, vmem_limit_bytes=VMEM_LIMIT
        ),
    )(
        *tile_in,
        *(masters[name] for name in WEIGHTS),
        *(vectors[name] for name in VECTORS),
        flag,
    )
    outs = list(outs)
    images = [outs.pop(0) for _ in range(2)]
    return (images,) + tuple(
        {name: outs.pop(0) for name in names} for names in (WEIGHTS, VECTORS, SAVED, MAPS)
    )


def swap_cores(value):
    return lax.ppermute(value, "row", [(0, 1), (1, 0), (2, 3), (3, 2)])


def halve_patch(grad, axis):
    grad = jnp.moveaxis(grad, axis, 0)
    even, odd = grad[0::2], grad[1::2]
    zero = jnp.zeros_like(even[:1])
    middle = jnp.concatenate([zero, 0.75 * (even + odd), zero])
    before = jnp.concatenate([0.25 * even, zero, zero])
    after = jnp.concatenate([zero, zero, 0.25 * odd])
    return jnp.moveaxis(middle + before + after, 0, axis)


def on_chip(
    chips,
    tokens,
    cot_tokens,
    cot_merged,
    image_counts,
    scale_flags,
    shift_flags,
    qkv_w,
    attn_out_w,
    fc1_w,
    fc1_b,
    fc2_w,
    fc2_b,
    ln1_gain,
    ln1_bias,
    ln2_gain,
    ln2_bias,
    proj_w,
    conv_w,
    head_w,
    head_b,
    shift_row,
):
    slots, tile_rows, tile_cols, width = tokens.shape
    cols = lax.axis_size("col")
    sizes = (chips, slots, cols)
    tile = tile_rows * tile_cols
    feat = proj_w.shape[1]
    half_rows, all_cols = 2 * tile_rows, cols * tile_cols
    dp, y, core, z = place()
    low = jnp.bfloat16
    count = image_counts[0]
    present = (jnp.arange(slots) < count).astype(jnp.float32)
    factor = 0.5 + 0.5 * scale_flags.astype(jnp.float32)
    shift_sign = shift_flags.astype(jnp.float32)
    full_group = count == slots
    chip = y * cols + z
    borrowed = jnp.logical_and(jnp.logical_not(full_group), chip >= 2 * chips - slots)
    image_present = jnp.where(
        jnp.logical_or(jnp.logical_or(full_group, borrowed), chip < count), 1.0, 0.0
    )

    def both_halves(value):
        far = lax.ppermute(value, "dp", [(0, 1), (1, 0)])
        return jnp.where(dp == 0, jnp.stack([value, far]), jnp.stack([far, value]))

    w_head = both_halves(head_w.astype(low)).reshape(feat, feat)
    rows_small = both_halves(jnp.stack([head_b, shift_row]))
    b_head, w_shift = (
        rows_small[:, i].reshape(-1).astype(low).astype(jnp.float32) for i in range(2)
    )

    merged_grad = cot_merged.astype(jnp.float32).reshape(slots, -1, feat) * present[:, None, None]
    grad_shift = jnp.sum(merged_grad * shift_sign[:, None, None], (0, 1))
    head_grad = (merged_grad * factor[:, None, None]).astype(low).reshape(-1, feat)
    grad_head_b = jnp.sum(head_grad.astype(jnp.float32), 0)
    fine_grad = back_product(head_grad, w_head).astype(low).reshape(cot_merged.shape)
    patch_grad = halve_patch(halve_patch(fine_grad.astype(jnp.float32), 1), 2).astype(low)
    cells = (tile_rows + 2) * (tile_cols + 2)
    patch_grad = jnp.pad(
        patch_grad.reshape(slots, cells, feat), ((0, 0), (0, PATCH - cells), (0, 0))
    )

    vectors = (fc1_b, fc2_b, ln1_gain, ln1_bias, ln2_gain, ln2_bias)
    (image_cots, image_patches), weights, vec, saved, maps = run_forward(
        (tokens.reshape(slots, tile, width), cot_tokens.reshape(slots, tile, width), patch_grad),
        {
            "qkv": qkv_w,
            "out": attn_out_w,
            "fc1": fc1_w,
            "fc2": fc2_w,
            "proj": proj_w,
            "conv": conv_w.reshape((36,) + conv_w.shape[3:]),
        },
        {name: v[None] for name, v in zip(VECTORS, vectors)},
        jnp.full((8, 128), borrowed.astype(jnp.float32)),
        sizes,
        (tile_rows, tile_cols),
    )
    w_qkv, w_out, w_up, w_down, w_proj, w_conv = (weights[name] for name in WEIGHTS)
    gain_one, bias_one, gain_two, bias_two = (vec[name] for name in VECTORS[2:])

    def chosen(pair):
        return jnp.where(borrowed, pair[1], pair[0])

    rows = chips * tile
    tiles = (tile_rows, tile_cols)
    tokens_low = saved["tokens_low"]

    coarse = maps["coarse"].reshape(half_rows + 2, all_cols, feat)
    coarse = jnp.concatenate([coarse[:, :1], coarse, coarse[:, -1:]], 1)
    cuts = [
        coarse[
            r * tile_rows : (r + 1) * tile_rows + 2, c * tile_cols : (c + 1) * tile_cols + 2
        ].reshape(cells, feat)
        for r in range(2)
        for c in range(cols)
    ]
    patch = jnp.pad(jnp.stack(cuts), ((0, 0), (0, PATCH - cells), (0, 0)))
    parts = chosen(image_patches)[:, :cells].astype(jnp.float32)
    parts = parts.reshape(2, cols, tile_rows + 2, tile_cols + 2, feat)
    wide = sum(
        jnp.pad(parts[:, c], ((0, 0), (0, 0), (c * tile_cols, (cols - 1 - c) * tile_cols), (0, 0)))
        for c in range(cols)
    )
    wide = jnp.concatenate(
        [wide[:, :, 1:2] + wide[:, :, :1], wide[:, :, 2:-2], wide[:, :, -2:-1] + wide[:, :, -1:]], 2
    )
    tall = jnp.pad(wide[0], ((0, tile_rows), (0, 0), (0, 0))) + jnp.pad(
        wide[1], ((tile_rows, 0), (0, 0), (0, 0))
    )
    tall = tall.reshape(-1, feat)
    *grad_conv, proj_grad, slot_patch = maps_backward(
        tall, swap_cores(tall), [maps[name] for name in MAPS[:-1]], w_conv, patch, slots, tiles, cols
    )
    grad_conv = early_sum(*(g.reshape(36, feat, feat // 2) for g in grad_conv), TURNS["conv"][0])

    patch = slot_patch[:, :cells]
    patch = patch.reshape(slots, tile_rows + 2, tile_cols + 2, feat).astype(jnp.float32)
    patch = jnp.where(present[:, None, None, None] > 0, patch, 0.0)
    upsampled = double_axis(double_axis(patch, 1), 2).astype(low)
    fine_rows = upsampled.reshape(-1, feat)
    head_out = jnp.dot(fine_rows, w_head, preferred_element_type=jnp.float32) + b_head
    head_out = head_out.reshape(slots, -1, feat)
    merged = (head_out * factor[:, None, None] + shift_sign[:, None, None] * w_shift) * present[
        :, None, None
    ]
    merged_out = merged.astype(low).reshape(cot_merged.shape)
    grad_head_w = outer_product(fine_rows, head_grad)

    normed_two, scaled_two, factor_two = norm_rows(saved["after_attn"], gain_two, bias_two)
    normed_two_low = normed_two.astype(low)
    hidden = saved["hidden"]
    hidden_low = jax.nn.gelu(hidden).astype(low)
    attended = saved["o"].astype(low)
    grad_proj = outer_product(tokens_low, proj_grad)
    stream_grad = chosen(image_cots).reshape(rows, width).astype(jnp.float32)
    stream_grad = jnp.where(image_present > 0, stream_grad, 0.0) + back_product(proj_grad, w_proj)
    down_grad = stream_grad.astype(low)
    grad_down_b = jnp.sum(down_grad.astype(jnp.float32), 0)

    def halves_of(first_op, second_op):
        half = second_op.shape[1] // 2
        return [
            outer_product(
                first_op, lax.dynamic_slice_in_dim(second_op, side * half, half, 1)
            ).astype(low)[None]
            for side in (core, 1 - core)
        ]

    grad_down_w = early_sum(*halves_of(hidden_low, down_grad), TURNS["fc2"][0])
    up_grad = gelu_grad(hidden, back_product(down_grad, w_down)).astype(low)
    grad_up_b = jnp.sum(up_grad.astype(jnp.float32), 0)
    grad_up_w = early_sum(*halves_of(normed_two_low, up_grad), TURNS["fc1"][0])
    norm_grad, grad_gain_two, grad_bias_two = norm_back(
        back_product(up_grad, w_up), scaled_two, factor_two, gain_two
    )
    stream_grad = stream_grad + norm_grad
    branch_grad = stream_grad.astype(low)
    grad_out_w = outer_product(attended, branch_grad)
    attended_grad = back_product(branch_grad, w_out).astype(low)
    blank = jnp.zeros((2, (width // 2 + feat - 1) // feat * feat), jnp.float32)
    packed = []
    for v in (grad_up_b, grad_down_b, None, None, grad_gain_two, grad_bias_two, grad_head_b, grad_shift):
        if v is None:
            packed.append(blank)
            continue
        v = v.reshape(2, -1)
        packed.append(jnp.pad(v, ((0, 0), (0, -v.shape[1] % feat))))
    starts, at = [], 0
    for v in packed:
        starts.append(at)
        at += v.shape[1]
    packed = jnp.pad(jnp.concatenate(packed, 1), ((0, 0), (0, 128 * feat - at)))
    slot_tokens, slot_grads, sums = run_backward(
        {
            **{name: saved[name] for name in ("q", "k", "v", "o", "logs", "x")},
            "g": attended_grad,
            "stream": stream_grad,
            "w_qkv": w_qkv,
            "gain": gain_one,
            "bias": bias_one,
            "small": packed.reshape(256, feat),
        },
        tokens_low.reshape(chips, tile, width),
        {"conv": grad_conv, "fc2": grad_down_w, "fc1": grad_up_w},
        {
            "out": grad_out_w.astype(low)[None],
            "proj": grad_proj.astype(low)[None],
            "head": grad_head_w.astype(low)[None],
        },
        sizes,
    )
    here = present[:, None, None] > 0
    tokens_out = jnp.where(here, slot_tokens, 0).reshape(tokens.shape)
    grad_tokens = jnp.where(here, slot_grads.astype(jnp.float32), 0.0).reshape(tokens.shape)
    sums = {name: value.astype(jnp.float32) for name, value in sums.items()}
    packed = sums["small"].reshape(-1)
    pieces = [
        packed[at : at + v.shape[0]] for at, v in zip(starts, vectors + (head_b, shift_row))
    ]
    return (
        tokens_out,
        merged_out,
        grad_tokens,
        sums["qkv"][0],
        sums["out"][0],
        sums["fc1"][0],
        pieces[0],
        sums["fc2"][0],
        pieces[1],
        pieces[2],
        pieces[3],
        pieces[4],
        pieces[5],
        sums["proj"][0],
        sums["conv"].reshape(conv_w.shape),
        sums["head"][0],
        pieces[6],
        pieces[7],
    )


def solution(mesh):
    groups, tile_rows, tile_cols = (mesh.shape[axis] for axis in ("dp", "row", "col"))
    chips = tile_rows // 2 * tile_cols
    fits = groups == 2 and tile_rows == 4 and tile_cols == 4
    placed = (
        P("dp", "row", "col", None),
        P("dp", "row", "col", None),
        P("dp", "row", "col", None),
        P("dp"),
        P("dp"),
        P("dp"),
        P("dp", None),
        P("dp", None),
        P("dp", None),
        P("dp"),
        P("dp", None),
        P("dp"),
        P("dp"),
        P("dp"),
        P("dp"),
        P("dp"),
        P("dp", None),
        P(None, None, None, "dp", None),
        P("dp", None),
        P("dp"),
        P("dp"),
    )
    return jax.shard_map(
        functools.partial(on_chip, chips) if fits else on_device,
        mesh=mesh,
        in_specs=placed,
        out_specs=(
            P("dp", "row", "col", None),
            P("dp", "row", "col", None),
            P("dp", "row", "col", None),
            P("dp", None),
            P("dp", None),
            P("dp", None),
            P("dp"),
            P("dp", None),
            P("dp"),
            P("dp"),
            P("dp"),
            P("dp"),
            P("dp"),
            P("dp", None),
            P(None, None, None, "dp", None),
            P("dp", None),
            P("dp"),
            P("dp"),
        ),
        check_vma=False,
    )
```

```python
import functools

import jax
import jax.numpy as jnp
from jax import lax
from jax.experimental import pallas as pl
from jax.experimental.pallas import tpu as pltpu
from jax.sharding import PartitionSpec as P

HEADS = 12
HEAD_DIM = 64


epsilon = 1e-06


def extended(value, sides, width):
    for axis, dim in sides:
        peers, length = (lax.axis_size(axis), value.shape[dim])
        up = [(i, (i + 1) % peers) for i in range(peers - 1)]
        down = [(j, i) for i, j in up]
        last = lax.slice_in_dim(value, length - width, length, axis=dim)
        leading = lax.slice_in_dim(value, 0, width, axis=dim)
        before = lax.ppermute(last, axis, up)
        after = lax.ppermute(leading, axis, down)
        value = jnp.concatenate([before, value, after], axis=dim)
    return value


def norm_rows(stream, gain_row, bias_row):
    centre = stream - jnp.mean(stream, -1, keepdims=True)
    spread = jnp.mean(centre * centre, -1, keepdims=True)
    factor = lax.rsqrt(spread + epsilon)
    scaled = centre * factor
    return (scaled * gain_row + bias_row, scaled, factor)


def norm_back(cotangent, scaled, factor, gain_row):
    gained = cotangent * gain_row
    inner = (
        gained
        - jnp.mean(gained, -1, keepdims=True)
        - scaled * jnp.mean(gained * scaled, -1, keepdims=True)
    )
    return (factor * inner, jnp.sum(cotangent * scaled, 0), jnp.sum(cotangent, 0))


def gelu_grad(inputs, cotangent):
    return jax.vjp(jax.nn.gelu, inputs)[1](cotangent)[0]


def outer_product(first_op, second_op):
    return lax.dot_general(
        first_op, second_op, (((0,), (0,)), ((), ())), preferred_element_type=jnp.float32
    )


def back_product(first_op, weight):
    return lax.dot_general(
        first_op, weight, (((1,), (1,)), ((), ())), preferred_element_type=jnp.float32
    )


def add_rims(tile_map):
    return extended(tile_map, (("row", 1), ("col", 2)), 1)


def clamp_edges(padded):
    first_row = lax.axis_index("row") == 0
    last_row = lax.axis_index("row") == lax.axis_size("row") - 1
    upper = jnp.where(first_row, padded[:, 1:2], padded[:, 0:1])
    lower = jnp.where(last_row, padded[:, -2:-1], padded[:, -1:])
    padded = jnp.concatenate([upper, padded[:, 1:-1], lower], 1)
    first_col = lax.axis_index("col") == 0
    last_col = lax.axis_index("col") == lax.axis_size("col") - 1
    left_side = jnp.where(first_col, padded[:, :, 1:2], padded[:, :, 0:1])
    right_side = jnp.where(last_col, padded[:, :, -2:-1], padded[:, :, -1:])
    return jnp.concatenate([left_side, padded[:, :, 1:-1], right_side], 2)


def patches(padded):
    tall = padded.shape[1] - 2
    broad = padded.shape[2] - 2
    pieces = [
        padded[:, row_shift : row_shift + tall, col_shift : col_shift + broad]
        for row_shift in range(3)
        for col_shift in range(3)
    ]
    return jnp.concatenate(pieces, -1).reshape(-1, 9 * padded.shape[3])


def conv_apply(padded, kernel):
    result = jnp.dot(
        patches(padded), kernel.reshape(-1, kernel.shape[3]), preferred_element_type=jnp.float32
    )
    return result.reshape(padded.shape[0], padded.shape[1] - 2, padded.shape[2] - 2, -1)


def flip_kernel(kernel):
    return jnp.transpose(kernel[::-1, ::-1], (0, 1, 3, 2))


def double_axis(padded, axis_index):
    leading = jnp.moveaxis(padded, axis_index, 0)
    middle_part = leading[1:-1]
    even_part = 0.75 * middle_part + 0.25 * leading[:-2]
    odd_part = 0.75 * middle_part + 0.25 * leading[2:]
    joined = jnp.stack([even_part, odd_part], 1).reshape(
        (2 * middle_part.shape[0],) + middle_part.shape[1:]
    )
    return jnp.moveaxis(joined, 0, axis_index)


def halve_axis(padded, axis_index):
    leading = jnp.moveaxis(padded, axis_index, 0)
    even_part = leading[1:-1:2]
    odd_part = leading[2:-1:2]
    before_part = leading[0:-2:2]
    after_part = leading[3::2]
    joined = 0.75 * (even_part + odd_part) + 0.25 * (before_part + after_part)
    return jnp.moveaxis(joined, 0, axis_index)


def on_device(
    tokens,
    cot_tokens,
    cot_merged,
    image_counts,
    scale_flags,
    shift_flags,
    qkv_w,
    attn_out_w,
    fc1_w,
    fc1_b,
    fc2_w,
    fc2_b,
    ln1_gain,
    ln1_bias,
    ln2_gain,
    ln2_bias,
    proj_w,
    conv_w,
    head_w,
    head_b,
    shift_row,
):
    lowered = [
        master.astype(jnp.bfloat16)
        for master in (
            qkv_w,
            attn_out_w,
            fc1_w,
            fc1_b,
            fc2_w,
            fc2_b,
            ln1_gain,
            ln1_bias,
            ln2_gain,
            ln2_bias,
            proj_w,
            conv_w,
            head_w,
            head_b,
            shift_row,
        )
    ]
    gathered = (
        lax.all_gather(lowered[0], "dp", axis=0, tiled=True),
        lax.all_gather(lowered[1], "dp", axis=0, tiled=True),
        lax.all_gather(lowered[2], "dp", axis=0, tiled=True),
        lax.all_gather(lowered[3], "dp", axis=0, tiled=True),
        lax.all_gather(lowered[4], "dp", axis=0, tiled=True),
        lax.all_gather(lowered[5], "dp", axis=0, tiled=True),
        lax.all_gather(lowered[6], "dp", axis=0, tiled=True),
        lax.all_gather(lowered[7], "dp", axis=0, tiled=True),
        lax.all_gather(lowered[8], "dp", axis=0, tiled=True),
        lax.all_gather(lowered[9], "dp", axis=0, tiled=True),
        lax.all_gather(lowered[10], "dp", axis=0, tiled=True),
        lax.all_gather(lowered[11], "dp", axis=3, tiled=True),
        lax.all_gather(lowered[12], "dp", axis=0, tiled=True),
        lax.all_gather(lowered[13], "dp", axis=0, tiled=True),
        lax.all_gather(lowered[14], "dp", axis=0, tiled=True),
    )
    (
        w_qkv,
        w_out,
        w_up,
        b_up,
        w_down,
        b_down,
        gain_one,
        bias_one,
        gain_two,
        bias_two,
        w_proj,
        w_conv,
        w_head,
        b_head,
        w_shift,
    ) = gathered
    images = tokens.shape[0]
    tile_rows = tokens.shape[1]
    tile_cols = tokens.shape[2]
    tile_size = tile_rows * tile_cols
    model_width = tokens.shape[3]
    temper = HEAD_DIM ** (-0.5)
    present = (jnp.arange(images) < image_counts[0]).astype(jnp.float32)
    factor = 0.5 + 0.5 * scale_flags.astype(jnp.float32)
    shift_sign = shift_flags.astype(jnp.float32)
    present_rows = jnp.repeat(present, tile_size)[:, None]
    stream = tokens.astype(jnp.float32).reshape(-1, model_width)
    normed, scaled_one, factor_one = norm_rows(
        stream, gain_one.astype(jnp.float32), bias_one.astype(jnp.float32)
    )
    normed_low = normed.astype(jnp.bfloat16)
    projected = jnp.dot(normed_low, w_qkv, preferred_element_type=jnp.float32).astype(jnp.bfloat16)
    queries = projected[:, :model_width].reshape(images, tile_size, HEADS, HEAD_DIM)
    keys_own = projected[:, model_width : 2 * model_width].reshape(images, tile_size, model_width)
    values_own = projected[:, 2 * model_width :].reshape(images, tile_size, model_width)
    keys_all, values_all = (
        lax.all_gather(keys_own, ("row", "col"), axis=1, tiled=True),
        lax.all_gather(values_own, ("row", "col"), axis=1, tiled=True),
    )
    keys_heads = keys_all.reshape(images, -1, HEADS, HEAD_DIM)
    values_heads = values_all.reshape(images, -1, HEADS, HEAD_DIM)
    scores = (
        jnp.einsum("nqhd,nkhd->nhqk", queries, keys_heads, preferred_element_type=jnp.float32)
        * temper
    )
    highest_score = jnp.max(scores, -1, keepdims=True)
    exponent = jnp.exp(scores - highest_score)
    denominator = jnp.sum(exponent, -1, keepdims=True)
    log_total = highest_score + jnp.log(denominator)
    attention_low = (exponent / denominator).astype(jnp.bfloat16)
    attended = jnp.einsum(
        "nhqk,nkhd->nqhd", attention_low, values_heads, preferred_element_type=jnp.float32
    )
    attended = attended.reshape(-1, model_width).astype(jnp.bfloat16)
    after_attn = stream + jnp.dot(attended, w_out, preferred_element_type=jnp.float32)
    normed_two, scaled_two, factor_two = norm_rows(
        after_attn, gain_two.astype(jnp.float32), bias_two.astype(jnp.float32)
    )
    normed_two_low = normed_two.astype(jnp.bfloat16)
    hidden = jnp.dot(normed_two_low, w_up, preferred_element_type=jnp.float32) + b_up.astype(
        jnp.float32
    )
    hidden_low = jax.nn.gelu(hidden).astype(jnp.bfloat16)
    after_mlp = after_attn + (
        jnp.dot(hidden_low, w_down, preferred_element_type=jnp.float32) + b_down.astype(jnp.float32)
    )
    tokens_low = after_mlp.astype(jnp.bfloat16)
    tokens_out = (
        (tokens_low.astype(jnp.float32) * present_rows).astype(jnp.bfloat16).reshape(tokens.shape)
    )
    feature = jnp.dot(tokens_low, w_proj, preferred_element_type=jnp.float32).reshape(
        images, tile_rows, tile_cols, -1
    )
    channels = feature.shape[3]
    stored = []
    for unit_index in range(2):
        first_in = add_rims(jax.nn.gelu(feature).astype(jnp.bfloat16))
        first_out = conv_apply(first_in, w_conv[2 * unit_index])
        second_in = add_rims(jax.nn.gelu(first_out).astype(jnp.bfloat16))
        second_out = conv_apply(second_in, w_conv[2 * unit_index + 1])
        stored.append((feature, first_in, first_out, second_in))
        feature = feature + second_out
    coarse_map = clamp_edges(add_rims(feature.astype(jnp.bfloat16))).astype(jnp.float32)
    upsampled = double_axis(double_axis(coarse_map, 1), 2).astype(jnp.bfloat16)
    fine_rows = upsampled.reshape(-1, channels)
    head_out = jnp.dot(fine_rows, w_head, preferred_element_type=jnp.float32) + b_head.astype(
        jnp.float32
    )
    head_out = head_out.reshape(images, -1, channels)
    merged = (
        head_out * factor[:, None, None] + shift_sign[:, None, None] * w_shift.astype(jnp.float32)
    ) * present[:, None, None]
    merged_out = merged.astype(jnp.bfloat16).reshape(cot_merged.shape)
    gathered = (
        lax.all_gather(lowered[0], "dp", axis=0, tiled=True),
        lax.all_gather(lowered[1], "dp", axis=0, tiled=True),
        lax.all_gather(lowered[2], "dp", axis=0, tiled=True),
        lax.all_gather(lowered[3], "dp", axis=0, tiled=True),
        lax.all_gather(lowered[4], "dp", axis=0, tiled=True),
        lax.all_gather(lowered[5], "dp", axis=0, tiled=True),
        lax.all_gather(lowered[6], "dp", axis=0, tiled=True),
        lax.all_gather(lowered[7], "dp", axis=0, tiled=True),
        lax.all_gather(lowered[8], "dp", axis=0, tiled=True),
        lax.all_gather(lowered[9], "dp", axis=0, tiled=True),
        lax.all_gather(lowered[10], "dp", axis=0, tiled=True),
        lax.all_gather(lowered[11], "dp", axis=3, tiled=True),
        lax.all_gather(lowered[12], "dp", axis=0, tiled=True),
        lax.all_gather(lowered[13], "dp", axis=0, tiled=True),
        lax.all_gather(lowered[14], "dp", axis=0, tiled=True),
    )
    (
        w_qkv,
        w_out,
        w_up,
        b_up,
        w_down,
        b_down,
        gain_one,
        bias_one,
        gain_two,
        bias_two,
        w_proj,
        w_conv,
        w_head,
        b_head,
        w_shift,
    ) = gathered
    merged_grad = (
        cot_merged.astype(jnp.float32).reshape(images, -1, channels) * present[:, None, None]
    )
    grad_shift = jnp.sum(merged_grad * shift_sign[:, None, None], (0, 1))
    head_grad = (merged_grad * factor[:, None, None]).astype(jnp.bfloat16).reshape(-1, channels)
    grad_head_b = jnp.sum(head_grad.astype(jnp.float32), 0)
    grad_head_w = outer_product(fine_rows, head_grad)
    fine_grad = back_product(head_grad, w_head).astype(jnp.bfloat16).reshape(upsampled.shape)
    spread_grad = clamp_edges(extended(fine_grad, (("row", 1), ("col", 2)), 1)).astype(jnp.float32)
    feature_grad = halve_axis(halve_axis(spread_grad, 1), 2)
    conv_grads = [None, None, None, None]
    for unit_index in (1, 0):
        unit_input, first_in, first_out, second_in = stored[unit_index]
        second_grad = feature_grad.astype(jnp.bfloat16)
        conv_grads[2 * unit_index + 1] = outer_product(
            patches(second_in), second_grad.reshape(-1, channels)
        )
        middle_grad = conv_apply(add_rims(second_grad), flip_kernel(w_conv[2 * unit_index + 1]))
        first_grad = gelu_grad(first_out, middle_grad).astype(jnp.bfloat16)
        conv_grads[2 * unit_index] = outer_product(
            patches(first_in), first_grad.reshape(-1, channels)
        )
        inner_grad = conv_apply(add_rims(first_grad), flip_kernel(w_conv[2 * unit_index]))
        feature_grad = feature_grad + gelu_grad(unit_input, inner_grad)
    grad_conv = jnp.stack(conv_grads).reshape(4, 3, 3, channels, channels)
    proj_grad = feature_grad.astype(jnp.bfloat16).reshape(-1, channels)
    grad_proj = outer_product(tokens_low, proj_grad)
    stream_grad = cot_tokens.astype(jnp.float32).reshape(
        -1, model_width
    ) * present_rows + back_product(proj_grad, w_proj)
    down_grad = stream_grad.astype(jnp.bfloat16)
    grad_down_b = jnp.sum(down_grad.astype(jnp.float32), 0)
    grad_down_w = outer_product(hidden_low, down_grad)
    up_grad = gelu_grad(hidden, back_product(down_grad, w_down)).astype(jnp.bfloat16)
    grad_up_b = jnp.sum(up_grad.astype(jnp.float32), 0)
    grad_up_w = outer_product(normed_two_low, up_grad)
    norm_grad, grad_gain_two, grad_bias_two = norm_back(
        back_product(up_grad, w_up), scaled_two, factor_two, gain_two.astype(jnp.float32)
    )
    stream_grad = stream_grad + norm_grad
    branch_grad = stream_grad.astype(jnp.bfloat16)
    grad_out_w = outer_product(attended, branch_grad)
    attended_grad = (
        back_product(branch_grad, w_out)
        .astype(jnp.bfloat16)
        .reshape(images, tile_size, HEADS, HEAD_DIM)
    )
    keys_heads = keys_all.reshape(images, -1, HEADS, HEAD_DIM)
    values_heads = values_all.reshape(images, -1, HEADS, HEAD_DIM)
    scores = (
        jnp.einsum("nqhd,nkhd->nhqk", queries, keys_heads, preferred_element_type=jnp.float32)
        * temper
    )
    attention_full = jnp.exp(scores - log_total)
    attention_low = attention_full.astype(jnp.bfloat16)
    prob_grad = jnp.einsum(
        "nqhd,nkhd->nhqk", attended_grad, values_heads, preferred_element_type=jnp.float32
    )
    centre = jnp.sum(attention_full * prob_grad, -1, keepdims=True)
    score_grad = (attention_full * (prob_grad - centre)).astype(jnp.bfloat16)
    query_grad = (
        jnp.einsum("nhqk,nkhd->nqhd", score_grad, keys_heads, preferred_element_type=jnp.float32)
        * temper
    )
    key_part = (
        jnp.einsum("nhqk,nqhd->knhd", score_grad, queries, preferred_element_type=jnp.float32)
        * temper
    )
    value_part = jnp.einsum(
        "nhqk,nqhd->knhd", attention_low, attended_grad, preferred_element_type=jnp.float32
    )
    pair_grad = lax.psum_scatter(
        jnp.concatenate(
            [
                key_part.reshape(lax.axis_size(("row", "col")) * tile_size, images, model_width),
                value_part.reshape(lax.axis_size(("row", "col")) * tile_size, images, model_width),
            ],
            2,
        ).astype(jnp.bfloat16),
        ("row", "col"),
        scatter_dimension=0,
        tiled=True,
    ).astype(jnp.float32)
    pair_grad = jnp.transpose(pair_grad, (1, 0, 2))
    mixed_grad = jnp.concatenate([query_grad.reshape(images, tile_size, model_width), pair_grad], 2)
    mixed_grad = mixed_grad.astype(jnp.bfloat16).reshape(-1, 3 * model_width)
    grad_qkv = outer_product(normed_low, mixed_grad)
    norm_grad, grad_gain_one, grad_bias_one = norm_back(
        back_product(mixed_grad, w_qkv), scaled_one, factor_one, gain_one.astype(jnp.float32)
    )
    input_grad = (stream_grad + norm_grad).reshape(tokens.shape)
    shards = (
        lax.psum_scatter(
            grad_qkv.astype(jnp.bfloat16), "dp", scatter_dimension=0, tiled=True
        ).astype(jnp.float32),
        lax.psum_scatter(
            grad_out_w.astype(jnp.bfloat16), "dp", scatter_dimension=0, tiled=True
        ).astype(jnp.float32),
        lax.psum_scatter(
            grad_up_w.astype(jnp.bfloat16), "dp", scatter_dimension=0, tiled=True
        ).astype(jnp.float32),
        lax.psum_scatter(
            grad_up_b.astype(jnp.bfloat16), "dp", scatter_dimension=0, tiled=True
        ).astype(jnp.float32),
        lax.psum_scatter(
            grad_down_w.astype(jnp.bfloat16), "dp", scatter_dimension=0, tiled=True
        ).astype(jnp.float32),
        lax.psum_scatter(
            grad_down_b.astype(jnp.bfloat16), "dp", scatter_dimension=0, tiled=True
        ).astype(jnp.float32),
        lax.psum_scatter(
            grad_gain_one.astype(jnp.bfloat16), "dp", scatter_dimension=0, tiled=True
        ).astype(jnp.float32),
        lax.psum_scatter(
            grad_bias_one.astype(jnp.bfloat16), "dp", scatter_dimension=0, tiled=True
        ).astype(jnp.float32),
        lax.psum_scatter(
            grad_gain_two.astype(jnp.bfloat16), "dp", scatter_dimension=0, tiled=True
        ).astype(jnp.float32),
        lax.psum_scatter(
            grad_bias_two.astype(jnp.bfloat16), "dp", scatter_dimension=0, tiled=True
        ).astype(jnp.float32),
        lax.psum_scatter(
            grad_proj.astype(jnp.bfloat16), "dp", scatter_dimension=0, tiled=True
        ).astype(jnp.float32),
        lax.psum_scatter(
            grad_conv.astype(jnp.bfloat16), "dp", scatter_dimension=3, tiled=True
        ).astype(jnp.float32),
        lax.psum_scatter(
            grad_head_w.astype(jnp.bfloat16), "dp", scatter_dimension=0, tiled=True
        ).astype(jnp.float32),
        lax.psum_scatter(
            grad_head_b.astype(jnp.bfloat16), "dp", scatter_dimension=0, tiled=True
        ).astype(jnp.float32),
        lax.psum_scatter(
            grad_shift.astype(jnp.bfloat16), "dp", scatter_dimension=0, tiled=True
        ).astype(jnp.float32),
    )
    totals = (
        lax.psum(shards[0].astype(jnp.bfloat16), ("row", "col")).astype(jnp.float32),
        lax.psum(shards[1].astype(jnp.bfloat16), ("row", "col")).astype(jnp.float32),
        lax.psum(shards[2].astype(jnp.bfloat16), ("row", "col")).astype(jnp.float32),
        lax.psum(shards[3].astype(jnp.bfloat16), ("row", "col")).astype(jnp.float32),
        lax.psum(shards[4].astype(jnp.bfloat16), ("row", "col")).astype(jnp.float32),
        lax.psum(shards[5].astype(jnp.bfloat16), ("row", "col")).astype(jnp.float32),
        lax.psum(shards[6].astype(jnp.bfloat16), ("row", "col")).astype(jnp.float32),
        lax.psum(shards[7].astype(jnp.bfloat16), ("row", "col")).astype(jnp.float32),
        lax.psum(shards[8].astype(jnp.bfloat16), ("row", "col")).astype(jnp.float32),
        lax.psum(shards[9].astype(jnp.bfloat16), ("row", "col")).astype(jnp.float32),
        lax.psum(shards[10].astype(jnp.bfloat16), ("row", "col")).astype(jnp.float32),
        lax.psum(shards[11].astype(jnp.bfloat16), ("row", "col")).astype(jnp.float32),
        lax.psum(shards[12].astype(jnp.bfloat16), ("row", "col")).astype(jnp.float32),
        lax.psum(shards[13].astype(jnp.bfloat16), ("row", "col")).astype(jnp.float32),
        lax.psum(shards[14].astype(jnp.bfloat16), ("row", "col")).astype(jnp.float32),
    )
    return (
        tokens_out,
        merged_out,
        input_grad,
        totals[0],
        totals[1],
        totals[2],
        totals[3],
        totals[4],
        totals[5],
        totals[6],
        totals[7],
        totals[8],
        totals[9],
        totals[10],
        totals[11],
        totals[12],
        totals[13],
        totals[14],
    )


LOG2E = 1.4426950408889634
MESH = pl.DeviceIdType.MESH
HALO = 6
PATCH = 112
VMEM_LIMIT = 58 << 20


def place():
    dp, row, col = (lax.axis_index(axis) for axis in ("dp", "row", "col"))
    return dp, lax.div(row, 2), lax.rem(row, 2), col


def slot_of(y, z, cols):
    return 2 * lax.rem(z + cols + cols // 2 - y, cols) + y


def chip_of(slot, cols):
    y = slot % 2
    return y, (slot // 2 + cols // 2 + y) % cols


def send(src, dst, send_sem, recv_sem, dp, y, core, z):
    return pltpu.make_async_remote_copy(
        src_ref=src,
        dst_ref=dst,
        send_sem=send_sem,
        recv_sem=recv_sem,
        device_id={"dp": dp, "row": y * 2 + core, "col": z},
        device_id_type=MESH,
    )


def landed(ref, sem):
    return pltpu.make_async_copy(ref, ref, sem)


def to_images_start(src, dst, send_sem, recv_sem, sizes):
    chips, slots, cols = sizes
    dp, y, core, z = place()
    own = core * cols + z
    for step in range(chips):
        far_y = lax.rem(y + step // cols, 2)
        far_z = lax.rem(z + step % cols, cols)
        slot = slot_of(far_y, far_z, cols)
        copy = send(
            src.at[slot], dst.at[0, own], send_sem.at[step], recv_sem.at[own], dp, far_y, y, far_z
        )
        if step == 0:
            local = pltpu.make_async_copy(src.at[slot], dst.at[0, own], recv_sem.at[own])
            pl.when(core == y)(local.start)
            pl.when(core != y)(copy.start)
        else:
            copy.start()
    for extra in range(slots - chips):
        to_y, to_z = chip_of(2 * chips - slots + extra, cols)
        send(
            src.at[chips + extra],
            dst.at[1, own],
            send_sem.at[chips + extra],
            recv_sem.at[chips + own],
            1 - dp,
            to_y,
            y,
            to_z,
        ).start()


def to_images_wait(src, dst, send_sem, recv_sem, sizes):
    chips, slots, cols = sizes
    dp, y, core, z = place()
    for step in range(slots):
        left = landed(src.at[0], send_sem.at[step])
        if step == 0:
            pl.when(core != y)(left.wait)
        else:
            left.wait()
    for tile in range(chips):
        landed(dst.at[0, tile], recv_sem.at[tile]).wait()

    @pl.when(slot_of(y, z, cols) >= 2 * chips - slots)
    def _():
        for tile in range(chips):
            landed(dst.at[1, tile], recv_sem.at[chips + tile]).wait()


def to_tiles_start(src, dst, send_sem, recv_sem, sizes):
    chips, slots, cols = sizes
    dp, y, core, z = place()
    slot = slot_of(y, z, cols)
    for step in range(chips):
        far_core = lax.rem(core + step // cols, 2)
        far_z = lax.rem(z + step % cols, cols)
        tile = far_core * cols + far_z
        copy = send(
            src.at[tile], dst.at[slot], send_sem.at[step], recv_sem.at[slot], dp, core, far_core, far_z
        )
        if step == 0:
            local = pltpu.make_async_copy(src.at[tile], dst.at[slot], recv_sem.at[slot])
            pl.when(core == y)(local.start)
            pl.when(core != y)(copy.start)
        else:
            copy.start()

    @pl.when(slot >= 2 * chips - slots)
    def _():
        for step in range(chips):
            far_core = step // cols
            far_z = step % cols
            other = slot + slots - chips
            send(
                src.at[step],
                dst.at[other],
                send_sem.at[chips + step],
                recv_sem.at[other],
                1 - dp,
                core,
                far_core,
                far_z,
            ).start()


def to_tiles_wait(src, dst, send_sem, recv_sem, sizes):
    chips, slots, cols = sizes
    dp, y, core, z = place()
    for step in range(chips):
        left = landed(src.at[0], send_sem.at[step])
        if step == 0:
            pl.when(core != y)(left.wait)
        else:
            left.wait()

    @pl.when(slot_of(y, z, cols) >= 2 * chips - slots)
    def _():
        for step in range(chips):
            landed(src.at[0], send_sem.at[chips + step]).wait()

    for slot in range(slots):
        landed(dst.at[slot], recv_sem.at[slot]).wait()


BITS = ("dp", "y", "z1", "z2")


def mate(bit):
    dp, y, core, z = place()
    low, high = lax.rem(z, 2), lax.div(z, 2)
    if bit == "core":
        return dp, y, 1 - core, z
    if bit == "dp":
        return 1 - dp, y, core, z
    if bit == "y":
        return dp, 1 - y, core, z
    if bit == "z1":
        return dp, y, core, high * 2 + 1 - low
    return dp, y, core, (1 - high) * 2 + low


def bit_of(bit):
    dp, y, core, z = place()
    return {
        "dp": dp,
        "y": y,
        "core": core,
        "z1": lax.rem(z, 2),
        "z2": lax.div(z, 2),
    }[bit]


class Gather:
    def __init__(self, whole, send_sem, recv_sem, split):
        self.whole, self.send_sem, self.recv_sem = whole, send_sem, recv_sem
        if split:
            self.orders = (("core", "y", "z1"), ("core", "z1", "y"))
        else:
            self.orders = (("core", "y"),)
        self.next, self.copies = 0, []

    def at(self, step, side):
        order = self.orders[side]
        count = 2 ** len(order)
        rows = self.whole.shape[-2] // (2 * count)
        piece = 0
        for i, bit in enumerate(order):
            if i <= len(order) - max(step, 1):
                piece = piece + bit_of(bit) * 2 ** (len(order) - 1 - i)
        half = bit_of("dp") if step == 0 else 1 - bit_of("dp")
        size = 1 if step == 0 else 2 ** (step - 1)
        part = pl.ds(pl.multiple_of((half * count + piece) * rows, 16), size * rows)
        width = self.whole.shape[-1] // len(self.orders)
        return self.whole.at[
            (slice(None),) * (len(self.whole.shape) - 2) + (part, pl.ds(side * width, width))
        ]

    def tick(self):
        while self.copies:
            self.copies.pop().wait()
        if self.next <= len(self.orders[0]):
            for side, order in enumerate(self.orders):
                bit = (("dp",) + order[::-1])[self.next]
                part = self.at(self.next, side)
                sems = (self.send_sem.at[side, self.next], self.recv_sem.at[side, self.next])
                copy = send(part, part, *sems, *mate(bit))
                copy.start()
                self.copies.append(copy)
            self.next += 1

    def finish(self):
        while self.copies:
            self.tick()


TURNS = {
    "conv": ("z1", ("dp", "z2", "y"), ("z2", "z1", "y", "core")),
    "small": (None, ("dp", "y", "z1", "z2"), ("y", "z1", "z2", "core")),
    "fc1": ("z1", ("y", "dp", "z2"), ("z2", "y", "z1", "core")),
    "proj": (None, ("dp", "z2", "z1", "y"), ("z1", "y", "z2", "core")),
    "head": (None, ("dp", "y", "z2", "z1"), ("y", "z2", "z1", "core")),
    "fc2": ("y", ("dp", "z1", "z2"), ("z2", "z1", "y", "core")),
    "qkv": (None, ("dp", "y", "z1", "z2"), ("z2", "y", "z1", "core")),
    "out": (None, ("dp", "y", "z1", "z2"), ("y", "z2", "z1", "core")),
}
EARLY = ("conv", "fc2", "fc1")
ARRIVED = ("conv",)
WHOLE = ("out", "proj", "head")


class Reduce:
    def __init__(self, turn, near, away, acc, recvs, out, sems, arrived=False):
        self.arrived = arrived
        self.gone, self.sum_order, self.back_order = turn
        self.near, self.away, self.acc, self.recvs, self.out, self.sems = (
            near,
            away,
            acc,
            recvs,
            out,
            sems,
        )
        self.dims = [bit for bit in BITS if bit != self.gone]
        self.kept = {bit: None for bit in BITS}
        if self.gone is not None:
            self.kept[self.gone] = bit_of(self.gone)
        half = out.shape[-1] // 2
        self.mine = pl.ds(pl.multiple_of(bit_of("core") * half, 128), half)
        self.step, self.copies = 0, []
        self.forward = 1 + len(self.sum_order)
        self.last = self.forward + len(self.back_order)

    def index(self):
        free = slice(None)
        return (free,) + tuple(free if self.kept[b] is None else self.kept[b] for b in self.dims)

    def add(self, recv):
        acc, kept, whole = self.acc, self.kept, slice(None)
        free = [b for b in self.dims if kept[b] is None]

        def body(i, _):
            bits, left = {}, i
            for b in reversed(free):
                bits[b] = lax.rem(left, 2)
                left = lax.div(left, 2)
            here = (whole,) + tuple(bits[b] if b in bits else kept[b] for b in self.dims)
            there = (whole,) + tuple(bits[b] for b in free)
            total = acc[here].astype(jnp.float32) + recv[there].astype(jnp.float32)
            acc[here] = total.astype(acc.dtype)
            return 0

        lax.fori_loop(0, 2 ** len(free), body, 0)

    def begin(self, copy):
        copy.start()
        self.copies.append(copy)

    def travel(self, src, dst, step, bit):
        _, send_sem, recv_sem = self.sems
        self.begin(send(src, dst, send_sem.at[step], recv_sem.at[step], *mate(bit)))

    def tick(self):
        step, whole, kept = self.step, slice(None), self.kept
        local_sem = self.sems[0]
        while self.copies:
            self.copies.pop().wait()
        if 0 < step <= self.forward:
            self.add(self.recvs[step - 1])
        if step == self.forward:
            kept["core"] = bit_of("core")
            at = (whole,) + tuple(kept[b] for b in BITS[1:]) + (whole, self.mine)
            self.begin(
                pltpu.make_async_copy(self.acc.at[self.index()], self.out.at[at], local_sem.at[1])
            )
        elif step == 0:
            if self.near is not None:
                self.begin(pltpu.make_async_copy(self.near, self.acc, local_sem.at[0]))
            if self.arrived:
                self.begin(pltpu.make_async_copy(self.away, self.recvs[0], local_sem.at[1]))
            else:
                self.travel(self.away, self.recvs[0], 0, self.gone or "core")
        elif step < self.forward:
            bit = self.sum_order[step - 1]
            kept[bit] = 1 - bit_of(bit)
            src = self.acc.at[self.index()]
            kept[bit] = bit_of(bit)
            self.travel(src, self.recvs[step], step, bit)
        elif step <= self.last:
            if step > self.forward + 1:
                kept[self.back_order[step - self.forward - 2]] = None
            bit = self.back_order[step - self.forward - 1]
            at = (whole,) + tuple(whole if kept[b] is None else kept[b] for b in BITS[1:])
            at = self.out.at[at + (whole, whole if kept["core"] is None else self.mine)]
            self.travel(at, at, step - 1, bit)
        self.step += 1

    def busy(self):
        return self.step <= self.last + 1


def across(value, bit):
    if bit == "dp":
        return lax.ppermute(value, "dp", [(0, 1), (1, 0)])
    if bit == "y":
        return lax.ppermute(value, "row", [(0, 2), (1, 3), (2, 0), (3, 1)])
    return lax.ppermute(value, "col", [(i, i + 1 - 2 * (i % 2)) for i in range(4)])


def recv_shapes(shape):
    free = len(shape) - 3
    return [shape[:1] + (2,) * left + shape[-2:] for left in range(free, -1, -1)]


def early_sum(near, other, bit):
    lead, rows, width = near.shape
    total = near.astype(jnp.float32) + swap_cores(other).astype(jnp.float32)
    total = total.astype(jnp.bfloat16).reshape(lead, 2, 2, 2, 2, rows // 16, width)
    axis, own = 1 + BITS.index(bit), bit_of(bit)
    keep = lax.dynamic_index_in_dim(total, own, axis, keepdims=False)
    away = lax.dynamic_index_in_dim(total, 1 - own, axis, keepdims=False)
    return keep, away


SCALE = HEAD_DIM**-0.5


def attend_pair(q, k, v):
    lane = lax.broadcasted_iota(jnp.int32, (1, 128), 1)
    sub = lax.broadcasted_iota(jnp.int32, (128, 1), 0)
    out = jnp.zeros((128, q.shape[0]), jnp.float32)
    logs = []
    for h in range(2):
        mine = (lane >= 64) == (h == 1)
        scores = lax.dot_general(
            k, jnp.where(mine, q, 0), (((1,), (1,)), ((), ())), preferred_element_type=jnp.float32
        )
        top = jnp.max(scores, 0, keepdims=True) * (SCALE * LOG2E)
        e = jnp.exp2(scores * (SCALE * LOG2E) - top)
        total = jnp.sum(e, 0, keepdims=True)
        part = lax.dot_general(
            v, e.astype(jnp.bfloat16), (((0,), (0,)), ((), ())), preferred_element_type=jnp.float32
        )
        out = jnp.where((sub >= 64) == (h == 1), part / total, out)
        logs.append(top + jnp.log2(total))
    return out.T, logs


def attend_pair_back(q, k, v, o, logs, g):
    lane = lax.broadcasted_iota(jnp.int32, (1, 128), 1)
    sub = lax.broadcasted_iota(jnp.int32, (128, 1), 0)
    product = (g.astype(jnp.float32) * o).T
    dq = jnp.zeros((128, q.shape[0]), jnp.float32)
    dk = dv = 0.0
    for h in range(2):
        mine = (lane >= 64) == (h == 1)
        q_own, g_own = jnp.where(mine, q, 0), jnp.where(mine, g, 0)
        centre = jnp.sum(product[h * 64 : (h + 1) * 64], 0, keepdims=True)
        scores = lax.dot_general(
            k, q_own, (((1,), (1,)), ((), ())), preferred_element_type=jnp.float32
        )
        p = jnp.exp2(scores * (SCALE * LOG2E) - logs[h])
        dp = lax.dot_general(
            v, g_own, (((1,), (1,)), ((), ())), preferred_element_type=jnp.float32
        )
        ds = (p * (dp - centre)).astype(jnp.bfloat16)
        dq_own = lax.dot_general(
            k, ds, (((0,), (0,)), ((), ())), preferred_element_type=jnp.float32
        )
        dq = jnp.where((sub >= 64) == (h == 1), dq_own * SCALE, dq)
        dk = dk + jnp.dot(ds, q_own, preferred_element_type=jnp.float32) * SCALE
        dv = dv + jnp.dot(p.astype(jnp.bfloat16), g_own, preferred_element_type=jnp.float32)
    return dq.T, dk, dv


BACK_INPUTS = ("q", "k", "v", "o", "logs", "g", "x", "stream", "w_qkv", "gain", "bias", "small")
LN_ROWS = 8
PLAN = (
    ("fc1", "head", "proj"),
    ("fc2", "out", "conv"),
    ("proj", "out", "conv"),
    (),
    ("head", "conv", "out"),
    (),
    ("out", "proj"),
    (),
    ("fc2", "out", "conv"),
)


def backward_kernel(sizes, *refs):
    refs = list(refs)

    def take(names):
        return {name: refs.pop(0) for name in names}

    ref = take(BACK_INPUTS)
    tiles = refs.pop(0)
    near, away, grads = take(EARLY), take(EARLY), take(WHOLE)
    slot_tokens, slot_grads = refs.pop(0), refs.pop(0)
    outs = take(TURNS)
    accs = take(TURNS)
    recvs = {name: [refs.pop(0) for _ in range(4 if TURNS[name][0] else 5)] for name in TURNS}
    mixed, far_out, far_in, own_pair, grad_tile, small_wide = (refs.pop(0) for _ in range(6))
    outbox = take(("qkv", "small"))
    tile_send, tile_recv, core_sem, local_sem, send_sem, recv_sem = refs
    low, f32 = jnp.bfloat16, jnp.float32
    core = bit_of("core")

    jobs = {}
    for i, name in enumerate(TURNS):
        sems = (local_sem.at[i], send_sem.at[i], recv_sem.at[i])
        if name in EARLY:
            source = (near[name], away[name])
        elif name in WHOLE:
            half = grads[name].shape[-1] // 2
            source = tuple(
                grads[name].at[..., pl.ds(pl.multiple_of(side * half, 128), half)]
                for side in (core, 1 - core)
            )
        else:
            source = (None, outbox[name])
        jobs[name] = Reduce(
            TURNS[name], *source, accs[name], recvs[name], outs[name], sems, name in ARRIVED
        )

    def tick(*names):
        for name in names:
            jobs[name].tick()

    tick(*PLAN[0])
    to_tiles_start(tiles, slot_tokens, tile_send.at[0], tile_recv.at[0], sizes)
    rows, width = ref["q"].shape
    for pair in range(width // 128):
        lanes = pl.ds(pair * 128, 128)
        dq, dk, dv = attend_pair_back(
            ref["q"][:, lanes],
            ref["k"][:, lanes],
            ref["v"][:, lanes],
            ref["o"][:, lanes],
            [ref["logs"][pair, h : h + 1, :] for h in range(2)],
            ref["g"][:, lanes],
        )
        mixed[:, lanes] = dq.astype(low)
        for i, value in enumerate((dk, dv)):
            to = pl.ds(i * width + pair * 128, 128)
            own_pair[:, to] = value[:rows]
            far_out[:, to] = value[rows:].astype(low)
        tick(*PLAN[1 + pair])
    pair_copy = send(far_out, far_in, core_sem.at[0], core_sem.at[1], *mate("core"))
    pair_copy.start()
    stream = ref["x"][...].astype(f32)
    normed, scaled, factor = norm_rows(stream, ref["gain"][...], ref["bias"][...])
    normed = normed.astype(low)
    pair_copy.wait()
    mixed[:, width:] = (own_pair[...] + far_in[...].astype(f32)).astype(low)

    half = mixed.shape[1] // 2
    for side, target in ((1 - core, outbox["qkv"]), (core, accs["qkv"])):
        for c in range(0, half, 384):
            part = mixed[:, pl.ds(pl.multiple_of(side * half + c, 128), 384)]
            value = outer_product(normed, part).astype(low)
            target[..., c : c + 384] = value.reshape(target.shape[:-1] + (384,))
        if target is outbox["qkv"]:
            tick(*PLAN[7])
    tick("qkv")
    tick(*PLAN[8])
    grad = back_product(mixed[...], ref["w_qkv"][...])
    gained, grad_gain, grad_bias = norm_back(grad, scaled, factor, ref["gain"][...])
    grad_tile[...] = (ref["stream"][...] + gained).astype(low).reshape(grad_tile.shape)

    small_wide[...] = ref["small"][...]
    for v, value in enumerate((grad_gain, grad_bias)):
        value = value.reshape(1, width)
        for j in range(width // 128):
            side, at = divmod(j, width // 256)
            row = side * (small_wide.shape[0] // 2) + LN_ROWS + 2 * v + at // 2
            small_wide[row : row + 1, at % 2 * 128 : at % 2 * 128 + 128] = value[
                :, j * 128 : (j + 1) * 128
            ]
    for side, target in ((core, accs["small"]), (1 - core, outbox["small"])):
        part = small_wide[:, pl.ds(pl.multiple_of(side * 128, 128), 128)].astype(low)
        target[...] = part.reshape(target.shape)
    tick("small")
    to_tiles_start(grad_tile, slot_grads, tile_send.at[1], tile_recv.at[1], sizes)
    while any(job.busy() for job in jobs.values()):
        for job in jobs.values():
            if job.busy():
                job.tick()
    to_tiles_wait(tiles, slot_tokens, tile_send.at[0], tile_recv.at[0], sizes)
    to_tiles_wait(grad_tile, slot_grads, tile_send.at[1], tile_recv.at[1], sizes)


def run_backward(inputs, tiles, early, grads, sizes):
    chips, slots, _ = sizes
    low, f32 = jnp.bfloat16, jnp.float32
    rows, width = inputs["q"].shape
    cut, accs = {}, {}
    for name in TURNS:
        if name in EARLY:
            accs[name] = early[name][0].shape
            continue
        if name in WHOLE:
            lead, height, across = grads[name].shape
            cut[name] = grads[name].reshape(lead, 2, 2, 2, 2, height // 16, across)
        else:
            lead = 1
            height, across = (width, 3 * width) if name == "qkv" else inputs["small"].shape
        accs[name] = (lead, 2, 2, 2, 2, height // 16, across // 2)
    shape = jax.ShapeDtypeStruct
    out_shape = [shape((slots,) + tiles.shape[1:], low)] * 2 + [
        shape(acc[:1] + (2, 2, 2, acc[-2], 2 * acc[-1]), low) for acc in accs.values()
    ]
    recvs = [value for acc in accs.values() for value in recv_shapes(acc)]
    hbm, vmem = pl.BlockSpec(memory_space=pltpu.HBM), pl.BlockSpec(memory_space=pltpu.VMEM)
    n = len(TURNS)
    slot_tokens, slot_grads, *sums = pl.pallas_call(
        functools.partial(backward_kernel, sizes),
        out_shape=out_shape,
        in_specs=[vmem] * len(BACK_INPUTS) + [hbm] * (1 + 2 * len(EARLY) + len(WHOLE)),
        out_specs=[hbm] * (2 + n),
        scratch_shapes=[pltpu.VMEM(value, low) for value in list(accs.values()) + recvs]
        + [
            pltpu.VMEM((rows, 3 * width), low),
            pltpu.VMEM((rows, 2 * width), low),
            pltpu.VMEM((rows, 2 * width), low),
            pltpu.VMEM((rows, 2 * width), f32),
            pltpu.VMEM(tiles.shape, low),
            pltpu.VMEM(inputs["small"].shape, f32),
            pltpu.VMEM(accs["qkv"], low),
            pltpu.VMEM(accs["small"], low),
            pltpu.SemaphoreType.DMA((2, 2 * chips)),
            pltpu.SemaphoreType.DMA((2, slots)),
            pltpu.SemaphoreType.DMA((2,)),
            pltpu.SemaphoreType.DMA((n, 2)),
            pltpu.SemaphoreType.DMA((n, 9)),
            pltpu.SemaphoreType.DMA((n, 9)),
        ],
        compiler_params=pltpu.CompilerParams(
            has_side_effects=True, vmem_limit_bytes=VMEM_LIMIT
        ),
    )(
        *(inputs[name] for name in BACK_INPUTS),
        tiles,
        *(early[name][0] for name in EARLY),
        *(early[name][1] for name in EARLY),
        *(cut[name] for name in WHOLE),
    )
    return (
        slot_tokens,
        slot_grads,
        {
            name: out.reshape(out.shape[0], 8 * out.shape[4], out.shape[5])
            for name, out in zip(TURNS, sums)
        },
    )


GELU_K, GELU_C = 0.7978845608028654, 0.044715


def gelu_slope(v):
    t = jnp.tanh(GELU_K * (v + GELU_C * v * v * v))
    return 0.5 * (1.0 + t) + 0.5 * v * (1.0 - t * t) * (GELU_K * (1.0 + 3.0 * GELU_C * v * v))


def block(row, size):
    return pl.ds(pl.multiple_of(row * size, size), size)


def turned(core, row, last):
    return core * (last - 2 * row) + row


def triple(dst, value, cols):
    rows, feat = value.shape
    col = lax.rem(lax.broadcasted_iota(jnp.int32, (rows, 1), 0), cols)
    left = jnp.where(col == 0, 0.0, pltpu.roll(value, 1, 0))
    right = jnp.where(col == cols - 1, 0.0, pltpu.roll(value, rows - 1, 0))
    body = pl.ds(cols, rows)
    dst[body, 0:feat] = left.astype(dst.dtype)
    dst[body, feat : 2 * feat] = value.astype(dst.dtype)
    dst[body, 2 * feat :] = right.astype(dst.dtype)


def clear_ends(dst, cols):
    zero = jnp.zeros((cols, dst.shape[1]), dst.dtype)
    dst[0:cols, :] = zero
    dst[dst.shape[0] - cols :, :] = zero


def taps(w_ref, line):
    value = w_ref[pl.ds(line * 3, 3)]
    return value.reshape(3 * value.shape[1], value.shape[2])


def conv_rows(src, w_ref, first, core, cols):
    rows = src.shape[0] - 2 * cols
    total = 0.0
    for a in range(3):
        total = total + jnp.dot(
            src[a * cols : a * cols + rows, :],
            taps(w_ref, first + turned(core, a, 2)),
            preferred_element_type=jnp.float32,
        )
    return total


def maps_forward(cols, own, f0_ref, first0_ref, f1_ref, first1_ref, w_ref, out_ref, wide):
    core = place()[2]
    clear_ends(wide, cols)
    for unit, (f, first, after) in enumerate(
        ((f0_ref, first0_ref, f1_ref), (f1_ref, first1_ref, None))
    ):
        triple(wide, jax.nn.gelu(f[...]), cols)
        first[...] = conv_rows(wide, w_ref, 6 * unit, core, cols)
        triple(wide, jax.nn.gelu(first[...]), cols)
        result = f[...] + conv_rows(wide, w_ref, 6 * unit + 3, core, cols)
        if after is not None:
            after[...] = result
    result = result.astype(out_ref.dtype)
    rows = own // cols + 2
    for j in range(rows):
        i = max(j - 1, 0)
        out_ref[block(turned(core, j, rows - 1), cols), :] = result[i * cols : (i + 1) * cols]


def kernel_grads(wide, grad, out_ref, first, core, cols):
    own = grad.shape[0]
    for a in range(3):
        value = outer_product(wide[a * cols : a * cols + own, :], grad)
        half = value.shape[1] // 2
        left, right = value[:, :half], value[:, half:]
        at = first + turned(core, a, 2)
        near, other = out_ref
        near[at] = jnp.where(core == 0, left, right).astype(near.dtype)
        other[at] = jnp.where(core == 0, right, left).astype(other.dtype)


def conv_back_rows(src, w_ref, first, core, cols):
    rows, feat = src.shape[0] - 2 * cols, w_ref.shape[2]
    total = 0.0
    for a in range(3):
        tap = taps(w_ref, first + turned(core, 2 - a, 2))
        for b in range(3):
            total = total + back_product(
                src[a * cols : a * cols + rows, b * feat : (b + 1) * feat],
                tap[(2 - b) * feat : (3 - b) * feat],
            )
    return total


def maps_back_kernel(
    tiles,
    cols,
    tall_ref,
    far_ref,
    f0_ref,
    first0_ref,
    f1_ref,
    first1_ref,
    w_ref,
    patch_ref,
    near_ref,
    other_ref,
    out_ref,
    slot_ref,
    wide,
    wide_g,
    total,
    parted,
    tile_send,
    tile_recv,
):
    chips = patch_ref.shape[0]
    sizes = (chips, slot_ref.shape[0], cols)
    to_tiles_start(patch_ref, slot_ref, tile_send, tile_recv, sizes)
    g_ref = (near_ref, other_ref)
    tile_rows, tile_cols = tiles
    core = place()[2]
    own_rows = 2 * tile_rows
    own = own_rows * cols * tile_cols
    line = cols * tile_cols
    edge = own_rows + 1

    def near(i):
        return tall_ref[block(turned(core, i, edge), line), :]

    def far(i):
        return far_ref[block(turned(1 - core, i, edge), line), :]

    for i in range(own_rows + 4):
        at = i * line
        if i < own_rows:
            value = near(i + 1)
            if i == 0:
                value = value + near(0)
            if i == own_rows - 1:
                value = value + far(edge)
        else:
            value = far(2 * own_rows - i)
            if i == own_rows:
                value = value + near(edge)
        total[at : at + line, :] = value
    rest = (own_rows + 4) * line
    total[rest:, :] = jnp.zeros((total.shape[0] - rest, total.shape[1]), jnp.float32)
    clear_ends(wide, line)
    clear_ends(wide_g, line)
    for unit, (f, first) in ((1, (f1_ref, first1_ref)), (0, (f0_ref, first0_ref))):
        triple(wide, jax.nn.gelu(first[...]), line)
        triple(wide_g, total[...], line)
        kernel_grads(
            wide, total[0:own, :].astype(wide.dtype), g_ref, 6 * unit + 3, core, line
        )
        middle = conv_back_rows(wide_g, w_ref, 6 * unit + 3, core, line)
        middle = gelu_slope(first[...]) * middle
        triple(wide, jax.nn.gelu(f[...]), line)
        triple(wide_g, middle, line)
        kernel_grads(wide, middle[0:own].astype(wide.dtype), g_ref, 6 * unit, core, line)
        inner = conv_back_rows(wide_g, w_ref, 6 * unit, core, line)
        total[...] += gelu_slope(f[...]) * inner
    for r in range(own_rows):
        row = turned(core, r, own_rows - 1)
        for z in range(cols):
            at = ((r // tile_rows) * cols + z) * tile_rows + r % tile_rows
            parted[at * tile_cols : (at + 1) * tile_cols, :] = total[
                block(row * cols + z, tile_cols), :
            ]
    out_ref[...] = parted[...].astype(out_ref.dtype)
    to_tiles_wait(patch_ref, slot_ref, tile_send, tile_recv, sizes)


def in_vmem(count):
    return [pl.BlockSpec(memory_space=pltpu.VMEM)] * count


def maps_backward(tall, far, saved, w_conv, patch, slots, tiles, cols):
    rows, feat = saved[0].shape
    line = cols * tiles[1]
    own = 2 * tiles[0] * line
    low, f32 = jnp.bfloat16, jnp.float32
    hbm = pl.BlockSpec(memory_space=pltpu.HBM)
    half = jax.ShapeDtypeStruct((12, 3 * feat, feat // 2), low)
    return pl.pallas_call(
        functools.partial(maps_back_kernel, tiles, cols),
        out_shape=[
            half,
            half,
            jax.ShapeDtypeStruct((own, feat), low),
            jax.ShapeDtypeStruct((slots,) + patch.shape[1:], low),
        ],
        in_specs=in_vmem(3 + len(saved)) + [hbm],
        out_specs=in_vmem(3) + [hbm],
        scratch_shapes=[pltpu.VMEM((rows + 2 * line, 3 * feat), low)] * 2
        + [
            pltpu.VMEM((rows, feat), f32),
            pltpu.VMEM((own, feat), f32),
            pltpu.SemaphoreType.DMA((2 * patch.shape[0],)),
            pltpu.SemaphoreType.DMA((slots,)),
        ],
        compiler_params=pltpu.CompilerParams(
            has_side_effects=True, vmem_limit_bytes=VMEM_LIMIT
        ),
    )(tall, far, *saved, w_conv, patch)


WEIGHTS = ("qkv", "out", "fc1", "fc2", "proj", "conv")
VECTORS = ("fc1_b", "fc2_b", "ln1_gain", "ln1_bias", "ln2_gain", "ln2_bias")
SAVED = ("x", "q", "k", "v", "o", "logs", "after_attn", "hidden", "tokens_low")
MAPS = ("f0", "first0", "f1", "first1", "coarse")
STAGES = 4


def chunks_of(name, master, whole, dp):
    if name == "conv":
        half = master.shape[1]
        rows = pl.ds(pl.multiple_of(dp * half, 16), half)
        return [(master.at[t], whole.at[t, rows]) for t in range(master.shape[0])]
    half, width = master.shape
    step = half if width > 1024 or half <= 512 else 384
    wide = min(width, 768)
    out = []
    for r in range(0, half, step):
        for c in range(0, width, wide):
            rows = pl.ds(pl.multiple_of(dp * half + r, 16), step)
            out.append((master.at[pl.ds(r, step), pl.ds(c, wide)], whole.at[rows, pl.ds(c, wide)]))
    return out


def forward_kernel(sizes, tiles, lengths, *refs):
    chips, slots, cols = sizes
    tile_rows, tile_cols = tiles
    refs = list(refs)

    def take(names):
        taken = {name: refs.pop(0) for name in names}
        return taken

    tile_in = take(("tokens", "cots", "patches"))
    masters = take(WEIGHTS)
    vectors = refs.pop(0)
    flag = refs.pop(0)
    image_out = take(("cots", "patches"))
    whole_out = take(WEIGHTS)
    vector_out = refs.pop(0)
    saved = take(SAVED)
    maps = take(MAPS)
    image = refs.pop(0)
    whole = take(WEIGHTS)
    far_vectors = refs.pop(0)
    keys, values, f0, hidden_low, flat, wide, stage = (refs.pop(0) for _ in range(7))
    kept = take(("o", "after_attn", "hidden", "first0", "f1", "first1"))
    tile_send, tile_recv, gather_send, gather_recv, vec_send, vec_recv, stage_sem, core_sem, out_sem = refs
    dp, y, core, z = place()
    low, f32 = jnp.bfloat16, jnp.float32

    to_images_start(tile_in["tokens"], image, tile_send.at[0], tile_recv.at[0], sizes)
    vector_copy = send(vectors, far_vectors, vec_send, vec_recv, *mate("dp"))
    vector_copy.start()

    work = [(name, c) for name in WEIGHTS for c in chunks_of(name, masters[name], whole[name], dp)]
    incoming = {}

    def fetch(i):
        if i < len(work):
            source = work[i][1][0]
            slot = stage.at[i % STAGES, pl.ds(0, source.shape[0]), pl.ds(0, source.shape[1])]
            incoming[i] = pltpu.make_async_copy(source, slot, stage_sem.at[i % STAGES])
            incoming[i].start()

    gathers = {
        name: Gather(whole[name], gather_send.at[i], gather_recv.at[i], name in ("qkv", "out"))
        for i, name in enumerate(WEIGHTS)
    }
    done = [0]
    for i in range(STAGES - 1):
        fetch(i)

    def round_next(name):
        while done[0] < len(work) and work[done[0]][0] == name:
            i = done[0]
            fetch(i + STAGES - 1)
            incoming.pop(i).wait()
            target = work[i][1][1]
            target[...] = stage[i % STAGES, : target.shape[0], : target.shape[1]].astype(low)
            done[0] += 1

    def tick(*names):
        for name in names:
            gathers[name].tick()

    out_copies = []

    def keep(src, dst):
        copy = pltpu.make_async_copy(src, dst, out_sem.at[len(out_copies)])
        copy.start()
        out_copies.append(copy)

    round_next("qkv")
    tick("qkv")
    round_next("out")
    tick("out")
    round_next("fc1")
    tick("qkv", "fc1")
    round_next("fc2")
    round_next("proj")
    tick("qkv")
    round_next("conv")
    tick("out", "qkv", "fc1", "fc2")
    gathers["qkv"].finish()
    vector_copy.wait()
    own, far = vectors[...], far_vectors[...]
    vec, at = {}, 0
    for name, length in zip(VECTORS, lengths):
        part = slice(at, at + length)
        row = jnp.concatenate(
            [jnp.where(dp == 0, own, far)[:, part], jnp.where(dp == 0, far, own)[:, part]], axis=1
        )
        vec[name] = row.astype(low).astype(f32)
        vector_out[:, 2 * at : 2 * (at + length)] = vec[name]
        at += length
    to_images_wait(tile_in["tokens"], image, tile_send.at[0], tile_recv.at[0], sizes)

    width = image.shape[3]
    x = jnp.where(flag[0:1, 0:1] > 0, image[1].astype(f32), image[0].astype(f32))
    x = x.reshape(-1, width)
    rows = x.shape[0]
    saved["x"][...] = x.astype(low)
    normed = norm_rows(x, vec["ln1_gain"], vec["ln1_bias"])[0].astype(low)
    mine = pl.ds(0, rows)
    theirs = pl.ds(rows, rows)
    core_copies = []
    for i, ref in ((1, keys), (2, values), (0, None)):
        part = jnp.dot(
            normed, whole["qkv"][:, i * width : (i + 1) * width], preferred_element_type=f32
        ).astype(low)
        if ref is None:
            saved["q"][...] = part
        else:
            ref[mine, :] = part
            copy = send(
                ref.at[mine], ref.at[theirs], core_sem.at[0, i], core_sem.at[1, i], *mate("core")
            )
            copy.start()
            core_copies.append(copy)
    tick("out")
    for copy in core_copies:
        copy.wait()
    tick("fc1", "fc2", "conv", "proj")
    to_images_start(tile_in["patches"], image_out["patches"], tile_send.at[1], tile_recv.at[1], sizes)
    keep(keys, saved["k"])
    keep(values, saved["v"])
    for name in ("qkv",):
        keep(whole[name], whole_out[name])

    for pair in range(width // 128):
        lanes = pl.ds(pair * 128, 128)
        out, logs = attend_pair(saved["q"][:, lanes], keys[:, lanes], values[:, lanes])
        kept["o"][:, lanes] = out
        for h in range(2):
            saved["logs"][pair, h : h + 1, :] = logs[h]
        if pair == 1:
            tick("out")
    gathers["out"].finish()
    tick("fc2", "conv", "proj")
    to_images_start(tile_in["cots"], image_out["cots"], tile_send.at[2], tile_recv.at[2], sizes)
    after_attn = saved["x"][...].astype(f32) + jnp.dot(
        kept["o"][...].astype(low), whole["out"][...], preferred_element_type=f32
    )
    kept["after_attn"][...] = after_attn
    keep(kept["o"], saved["o"])
    keep(kept["after_attn"], saved["after_attn"])
    normed_two = norm_rows(after_attn, vec["ln2_gain"], vec["ln2_bias"])[0].astype(low)
    gathers["fc1"].finish()
    for c in range(0, hidden_low.shape[1], width):
        part = pl.ds(c, width)
        hidden = jnp.dot(normed_two, whole["fc1"][:, part], preferred_element_type=f32)
        hidden = hidden + vec["fc1_b"][:, c : c + width]
        kept["hidden"][:, part] = hidden
        hidden_low[:, part] = jax.nn.gelu(hidden).astype(low)
    keep(kept["hidden"], saved["hidden"])
    gathers["fc2"].finish()
    after_mlp = kept["after_attn"][...] + (
        jnp.dot(hidden_low[...], whole["fc2"][...], preferred_element_type=f32) + vec["fc2_b"]
    )
    tokens_low = after_mlp.astype(low)
    saved["tokens_low"][...] = tokens_low
    tick("conv")
    gathers["proj"].finish()

    flat[...] = jnp.dot(tokens_low, whole["proj"][...], preferred_element_type=f32)
    half_rows, line = 2 * tile_rows, cols * tile_cols
    for r in range(half_rows):
        row = turned(core, r, half_rows - 1)
        for zz in range(cols):
            at = ((r // tile_rows) * cols + zz) * tile_rows + r % tile_rows
            f0[block(row * cols + zz, tile_cols), :] = flat[at * tile_cols : (at + 1) * tile_cols, :]
    core_copies = []
    for i in range(HALO):
        copy = send(
            f0.at[pl.ds((half_rows - 1 - i) * line, line)],
            f0.at[pl.ds((half_rows + i) * line, line)],
            core_sem.at[0, 3 + i],
            core_sem.at[1, 3 + i],
            *mate("core"),
        )
        copy.start()
        core_copies.append(copy)
    gathers["conv"].finish()
    for copy in core_copies:
        copy.wait()
    for name in WEIGHTS[1:]:
        keep(whole[name], whole_out[name])
    keep(f0, maps["f0"])
    maps_forward(
        line, rows, f0, kept["first0"], kept["f1"], kept["first1"], whole["conv"], maps["coarse"], wide
    )
    for name in ("first0", "f1", "first1"):
        keep(kept[name], maps[name])
    for copy in out_copies:
        copy.wait()
    to_images_wait(
        tile_in["patches"], image_out["patches"], tile_send.at[1], tile_recv.at[1], sizes
    )
    to_images_wait(tile_in["cots"], image_out["cots"], tile_send.at[2], tile_recv.at[2], sizes)


def run_forward(tile_in, masters, vectors, flag, sizes, tiles):
    chips, slots, cols = sizes
    low, f32 = jnp.bfloat16, jnp.float32
    shape = jax.ShapeDtypeStruct
    tile, width = tile_in[0].shape[1:]
    feat = masters["proj"].shape[1]
    hidden = masters["fc1"].shape[1]
    lengths = [v.shape[0] for v in vectors]
    rows, line = chips * tile, cols * tiles[1]
    ext = rows + HALO * line
    wholes = {
        name: shape(m.shape[:-2] + (2 * m.shape[-2], m.shape[-1]), low) for name, m in masters.items()
    }
    saved = {
        "x": shape((rows, width), low),
        "q": shape((rows, width), low),
        "k": shape((2 * rows, width), low),
        "v": shape((2 * rows, width), low),
        "o": shape((rows, width), f32),
        "logs": shape((width // 128, 2, rows), f32),
        "after_attn": shape((rows, width), f32),
        "hidden": shape((rows, hidden), f32),
        "tokens_low": shape((rows, width), low),
    }
    maps = {name: shape((ext, feat), f32) for name in MAPS[:-1]}
    maps["coarse"] = shape((rows + 2 * line, feat), low)
    far = [shape((2, chips) + t.shape[1:], t.dtype) for t in tile_in]
    hbm, vmem = pl.BlockSpec(memory_space=pltpu.HBM), pl.BlockSpec(memory_space=pltpu.VMEM)
    out_shape = (
        far[1:]
        + [wholes[name] for name in WEIGHTS]
        + [shape((1, 2 * sum(lengths)), f32)]
        + [saved[name] for name in SAVED]
        + [maps[name] for name in MAPS]
    )
    out_specs = (
        [hbm] * (2 + len(WEIGHTS))
        + [vmem]
        + [hbm if name in ("k", "v", "o", "after_attn", "hidden") else vmem for name in SAVED]
        + [vmem if name == "coarse" else hbm for name in MAPS]
    )
    n = len(WEIGHTS)
    outs = pl.pallas_call(
        functools.partial(forward_kernel, sizes, tiles, lengths),
        out_shape=out_shape,
        in_specs=[hbm] * (3 + n) + [vmem] * 2,
        out_specs=out_specs,
        scratch_shapes=[pltpu.VMEM(far[0].shape, low)]
        + [pltpu.VMEM(wholes[name].shape, low) for name in WEIGHTS]
        + [pltpu.VMEM((1, sum(lengths)), f32)]
        + [
            pltpu.VMEM((2 * rows, width), low),
            pltpu.VMEM((2 * rows, width), low),
            pltpu.VMEM((ext, feat), f32),
            pltpu.VMEM((rows, hidden), low),
            pltpu.VMEM((rows, feat), f32),
            pltpu.VMEM((ext + 2 * line, 3 * feat), low),
            pltpu.VMEM((STAGES, 384, 768), f32),
            pltpu.VMEM((rows, width), f32),
            pltpu.VMEM((rows, width), f32),
            pltpu.VMEM((rows, hidden), f32),
            pltpu.VMEM((ext, feat), f32),
            pltpu.VMEM((ext, feat), f32),
            pltpu.VMEM((ext, feat), f32),
            pltpu.SemaphoreType.DMA((3, slots)),
            pltpu.SemaphoreType.DMA((3, 2 * chips)),
            pltpu.SemaphoreType.DMA((n, 2, 4)),
            pltpu.SemaphoreType.DMA((n, 2, 4)),
            pltpu.SemaphoreType.DMA,
            pltpu.SemaphoreType.DMA,
            pltpu.SemaphoreType.DMA((STAGES,)),
            pltpu.SemaphoreType.DMA((2, 3 + HALO)),
            pltpu.SemaphoreType.DMA((n + 9,)),
        ],
        compiler_params=pltpu.CompilerParams(
            has_side_effects=True, vmem_limit_bytes=VMEM_LIMIT
        ),
    )(
        *tile_in,
        *(masters[name] for name in WEIGHTS),
        jnp.concatenate(vectors)[None],
        flag,
    )
    outs = list(outs)
    images = [outs.pop(0) for _ in range(2)]
    weights = {name: outs.pop(0) for name in WEIGHTS}
    joined, vec, at = outs.pop(0), {}, 0
    for name, length in zip(VECTORS, lengths):
        vec[name] = joined[:, 2 * at : 2 * (at + length)]
        at += length
    return (images, weights, vec) + tuple(
        {name: outs.pop(0) for name in names} for names in (SAVED, MAPS)
    )


def swap_cores(value):
    return lax.ppermute(value, "row", [(0, 1), (1, 0), (2, 3), (3, 2)])


def halve_patch(grad, axis):
    grad = jnp.moveaxis(grad, axis, 0)
    even, odd = grad[0::2], grad[1::2]
    zero = jnp.zeros_like(even[:1])
    middle = jnp.concatenate([zero, 0.75 * (even + odd), zero])
    before = jnp.concatenate([0.25 * even, zero, zero])
    after = jnp.concatenate([zero, zero, 0.25 * odd])
    return jnp.moveaxis(middle + before + after, 0, axis)


def on_chip(
    chips,
    tokens,
    cot_tokens,
    cot_merged,
    image_counts,
    scale_flags,
    shift_flags,
    qkv_w,
    attn_out_w,
    fc1_w,
    fc1_b,
    fc2_w,
    fc2_b,
    ln1_gain,
    ln1_bias,
    ln2_gain,
    ln2_bias,
    proj_w,
    conv_w,
    head_w,
    head_b,
    shift_row,
):
    slots, tile_rows, tile_cols, width = tokens.shape
    cols = lax.axis_size("col")
    sizes = (chips, slots, cols)
    tile = tile_rows * tile_cols
    feat = proj_w.shape[1]
    half_rows, all_cols = 2 * tile_rows, cols * tile_cols
    dp, y, core, z = place()
    low = jnp.bfloat16
    count = image_counts[0]
    present = (jnp.arange(slots) < count).astype(jnp.float32)
    factor = 0.5 + 0.5 * scale_flags.astype(jnp.float32)
    shift_sign = shift_flags.astype(jnp.float32)
    full_group = count == slots
    chip = slot_of(y, z, cols)
    borrowed = jnp.logical_and(jnp.logical_not(full_group), chip >= 2 * chips - slots)
    image_present = jnp.where(
        jnp.logical_or(jnp.logical_or(full_group, borrowed), chip < count), 1.0, 0.0
    )

    def both_halves(value):
        far = lax.ppermute(value, "dp", [(0, 1), (1, 0)])
        return jnp.where(dp == 0, jnp.stack([value, far]), jnp.stack([far, value]))

    w_head = both_halves(head_w.astype(low)).reshape(feat, feat)
    rows_small = both_halves(jnp.stack([head_b, shift_row]))
    b_head, w_shift = (
        rows_small[:, i].reshape(-1).astype(low).astype(jnp.float32) for i in range(2)
    )

    merged_grad = cot_merged.astype(jnp.float32).reshape(slots, -1, feat) * present[:, None, None]
    grad_shift = jnp.sum(merged_grad * shift_sign[:, None, None], (0, 1))
    head_grad = (merged_grad * factor[:, None, None]).astype(low).reshape(-1, feat)
    grad_head_b = jnp.sum(head_grad.astype(jnp.float32), 0)
    fine_grad = back_product(head_grad, w_head).astype(low).reshape(cot_merged.shape)
    patch_grad = halve_patch(halve_patch(fine_grad.astype(jnp.float32), 1), 2).astype(low)
    cells = (tile_rows + 2) * (tile_cols + 2)
    patch_grad = jnp.pad(
        patch_grad.reshape(slots, cells, feat), ((0, 0), (0, PATCH - cells), (0, 0))
    )

    vectors = (fc1_b, fc2_b, ln1_gain, ln1_bias, ln2_gain, ln2_bias)
    (image_cots, image_patches), weights, vec, saved, maps = run_forward(
        (tokens.reshape(slots, tile, width), cot_tokens.reshape(slots, tile, width), patch_grad),
        {
            "qkv": qkv_w,
            "out": attn_out_w,
            "fc1": fc1_w,
            "fc2": fc2_w,
            "proj": proj_w,
            "conv": conv_w.reshape((36,) + conv_w.shape[3:]),
        },
        vectors,
        jnp.full((8, 128), borrowed.astype(jnp.float32)),
        sizes,
        (tile_rows, tile_cols),
    )
    w_qkv, w_out, w_up, w_down, w_proj, w_conv = (weights[name] for name in WEIGHTS)
    gain_one, bias_one, gain_two, bias_two = (vec[name] for name in VECTORS[2:])

    def chosen(pair):
        return jnp.where(borrowed, pair[1], pair[0])

    rows = chips * tile
    tiles = (tile_rows, tile_cols)
    tokens_low = saved["tokens_low"]

    coarse = maps["coarse"].reshape(half_rows + 2, all_cols, feat)
    coarse = jnp.concatenate([coarse[:, :1], coarse, coarse[:, -1:]], 1)
    cuts = [
        coarse[
            r * tile_rows : (r + 1) * tile_rows + 2, c * tile_cols : (c + 1) * tile_cols + 2
        ].reshape(cells, feat)
        for r in range(2)
        for c in range(cols)
    ]
    patch = jnp.pad(jnp.stack(cuts), ((0, 0), (0, PATCH - cells), (0, 0)))
    parts = chosen(image_patches)[:, :cells].astype(jnp.float32)
    parts = parts.reshape(2, cols, tile_rows + 2, tile_cols + 2, feat)
    wide = sum(
        jnp.pad(parts[:, c], ((0, 0), (0, 0), (c * tile_cols, (cols - 1 - c) * tile_cols), (0, 0)))
        for c in range(cols)
    )
    wide = jnp.concatenate(
        [wide[:, :, 1:2] + wide[:, :, :1], wide[:, :, 2:-2], wide[:, :, -2:-1] + wide[:, :, -1:]], 2
    )
    tall = jnp.pad(wide[0], ((0, tile_rows), (0, 0), (0, 0))) + jnp.pad(
        wide[1], ((tile_rows, 0), (0, 0), (0, 0))
    )
    tall = tall.reshape(-1, feat)
    *grad_conv, proj_grad, slot_patch = maps_backward(
        tall, swap_cores(tall), [maps[name] for name in MAPS[:-1]], w_conv, patch, slots, tiles, cols
    )
    grad_conv = early_sum(*(g.reshape(36, feat, feat // 2) for g in grad_conv), TURNS["conv"][0])

    patch = slot_patch[:, :cells]
    patch = patch.reshape(slots, tile_rows + 2, tile_cols + 2, feat).astype(jnp.float32)
    patch = jnp.where(present[:, None, None, None] > 0, patch, 0.0)
    upsampled = double_axis(double_axis(patch, 1), 2).astype(low)
    fine_rows = upsampled.reshape(-1, feat)
    head_out = jnp.dot(fine_rows, w_head, preferred_element_type=jnp.float32) + b_head
    head_out = head_out.reshape(slots, -1, feat)
    merged = (head_out * factor[:, None, None] + shift_sign[:, None, None] * w_shift) * present[
        :, None, None
    ]
    merged_out = merged.astype(low).reshape(cot_merged.shape)
    grad_head_w = outer_product(fine_rows, head_grad)

    normed_two, scaled_two, factor_two = norm_rows(saved["after_attn"], gain_two, bias_two)
    normed_two_low = normed_two.astype(low)
    hidden = saved["hidden"]
    hidden_low = jax.nn.gelu(hidden).astype(low)
    attended = saved["o"].astype(low)
    grad_proj = outer_product(tokens_low, proj_grad)
    stream_grad = chosen(image_cots).reshape(rows, width).astype(jnp.float32)
    stream_grad = jnp.where(image_present > 0, stream_grad, 0.0) + back_product(proj_grad, w_proj)
    grad_conv, stream_grad = lax.optimization_barrier((grad_conv, stream_grad))
    grad_conv = (grad_conv[0], across(grad_conv[1], TURNS["conv"][0]))
    down_grad = stream_grad.astype(low)
    grad_down_b = jnp.sum(down_grad.astype(jnp.float32), 0)

    def halves_of(first_op, second_op):
        half = second_op.shape[1] // 2
        return [
            outer_product(
                first_op, lax.dynamic_slice_in_dim(second_op, side * half, half, 1)
            ).astype(low)[None]
            for side in (core, 1 - core)
        ]

    grad_down_w = early_sum(*halves_of(hidden_low, down_grad), TURNS["fc2"][0])
    up_grad = gelu_grad(hidden, back_product(down_grad, w_down)).astype(low)
    grad_up_b = jnp.sum(up_grad.astype(jnp.float32), 0)
    grad_up_w = early_sum(*halves_of(normed_two_low, up_grad), TURNS["fc1"][0])
    norm_grad, grad_gain_two, grad_bias_two = norm_back(
        back_product(up_grad, w_up), scaled_two, factor_two, gain_two
    )
    stream_grad = stream_grad + norm_grad
    branch_grad = stream_grad.astype(low)
    grad_out_w = outer_product(attended, branch_grad)
    attended_grad = back_product(branch_grad, w_out).astype(low)
    blank = jnp.zeros((2, (width // 2 + feat - 1) // feat * feat), jnp.float32)
    packed = []
    for v in (grad_up_b, grad_down_b, None, None, grad_gain_two, grad_bias_two, grad_head_b, grad_shift):
        if v is None:
            packed.append(blank)
            continue
        v = v.reshape(2, -1)
        packed.append(jnp.pad(v, ((0, 0), (0, -v.shape[1] % feat))))
    starts, at = [], 0
    for v in packed:
        starts.append(at)
        at += v.shape[1]
    packed = jnp.pad(jnp.concatenate(packed, 1), ((0, 0), (0, 128 * feat - at)))
    slot_tokens, slot_grads, sums = run_backward(
        {
            **{name: saved[name] for name in ("q", "k", "v", "o", "logs", "x")},
            "g": attended_grad,
            "stream": stream_grad,
            "w_qkv": w_qkv,
            "gain": gain_one,
            "bias": bias_one,
            "small": packed.reshape(256, feat),
        },
        tokens_low.reshape(chips, tile, width),
        {"conv": grad_conv, "fc2": grad_down_w, "fc1": grad_up_w},
        {
            "out": grad_out_w.astype(low)[None],
            "proj": grad_proj.astype(low)[None],
            "head": grad_head_w.astype(low)[None],
        },
        sizes,
    )
    here = present[:, None, None] > 0
    tokens_out = jnp.where(here, slot_tokens, 0).reshape(tokens.shape)
    grad_tokens = jnp.where(here, slot_grads.astype(jnp.float32), 0.0).reshape(tokens.shape)
    sums = {name: value.astype(jnp.float32) for name, value in sums.items()}
    packed = sums["small"].reshape(-1)
    pieces = [
        packed[at : at + v.shape[0]] for at, v in zip(starts, vectors + (head_b, shift_row))
    ]
    return (
        tokens_out,
        merged_out,
        grad_tokens,
        sums["qkv"][0],
        sums["out"][0],
        sums["fc1"][0],
        pieces[0],
        sums["fc2"][0],
        pieces[1],
        pieces[2],
        pieces[3],
        pieces[4],
        pieces[5],
        sums["proj"][0],
        sums["conv"].reshape(conv_w.shape),
        sums["head"][0],
        pieces[6],
        pieces[7],
    )


def solution(mesh):
    groups, tile_rows, tile_cols = (mesh.shape[axis] for axis in ("dp", "row", "col"))
    chips = tile_rows // 2 * tile_cols
    fits = groups == 2 and tile_rows == 4 and tile_cols == 4
    placed = (
        P("dp", "row", "col", None),
        P("dp", "row", "col", None),
        P("dp", "row", "col", None),
        P("dp"),
        P("dp"),
        P("dp"),
        P("dp", None),
        P("dp", None),
        P("dp", None),
        P("dp"),
        P("dp", None),
        P("dp"),
        P("dp"),
        P("dp"),
        P("dp"),
        P("dp"),
        P("dp", None),
        P(None, None, None, "dp", None),
        P("dp", None),
        P("dp"),
        P("dp"),
    )
    return jax.shard_map(
        functools.partial(on_chip, chips) if fits else on_device,
        mesh=mesh,
        in_specs=placed,
        out_specs=(
            P("dp", "row", "col", None),
            P("dp", "row", "col", None),
            P("dp", "row", "col", None),
            P("dp", None),
            P("dp", None),
            P("dp", None),
            P("dp"),
            P("dp", None),
            P("dp"),
            P("dp"),
            P("dp"),
            P("dp"),
            P("dp"),
            P("dp", None),
            P(None, None, None, "dp", None),
            P("dp", None),
            P("dp"),
            P("dp"),
        ),
        check_vma=False,
    )
```

```python
import functools

import jax
import jax.numpy as jnp
from jax import lax
from jax.experimental import pallas as pl
from jax.experimental.pallas import tpu as pltpu
from jax.sharding import PartitionSpec as P

HEADS = 12
HEAD_DIM = 64


epsilon = 1e-06


def extended(value, sides, width):
    for axis, dim in sides:
        peers, length = (lax.axis_size(axis), value.shape[dim])
        up = [(i, (i + 1) % peers) for i in range(peers - 1)]
        down = [(j, i) for i, j in up]
        last = lax.slice_in_dim(value, length - width, length, axis=dim)
        leading = lax.slice_in_dim(value, 0, width, axis=dim)
        before = lax.ppermute(last, axis, up)
        after = lax.ppermute(leading, axis, down)
        value = jnp.concatenate([before, value, after], axis=dim)
    return value


def norm_rows(stream, gain_row, bias_row):
    centre = stream - jnp.mean(stream, -1, keepdims=True)
    spread = jnp.mean(centre * centre, -1, keepdims=True)
    factor = lax.rsqrt(spread + epsilon)
    scaled = centre * factor
    return (scaled * gain_row + bias_row, scaled, factor)


def norm_back(cotangent, scaled, factor, gain_row):
    gained = cotangent * gain_row
    inner = (
        gained
        - jnp.mean(gained, -1, keepdims=True)
        - scaled * jnp.mean(gained * scaled, -1, keepdims=True)
    )
    return (factor * inner, jnp.sum(cotangent * scaled, 0), jnp.sum(cotangent, 0))


def gelu_grad(inputs, cotangent):
    return jax.vjp(jax.nn.gelu, inputs)[1](cotangent)[0]


def outer_product(first_op, second_op):
    return lax.dot_general(
        first_op, second_op, (((0,), (0,)), ((), ())), preferred_element_type=jnp.float32
    )


def back_product(first_op, weight):
    return lax.dot_general(
        first_op, weight, (((1,), (1,)), ((), ())), preferred_element_type=jnp.float32
    )


def add_rims(tile_map):
    return extended(tile_map, (("row", 1), ("col", 2)), 1)


def clamp_edges(padded):
    first_row = lax.axis_index("row") == 0
    last_row = lax.axis_index("row") == lax.axis_size("row") - 1
    upper = jnp.where(first_row, padded[:, 1:2], padded[:, 0:1])
    lower = jnp.where(last_row, padded[:, -2:-1], padded[:, -1:])
    padded = jnp.concatenate([upper, padded[:, 1:-1], lower], 1)
    first_col = lax.axis_index("col") == 0
    last_col = lax.axis_index("col") == lax.axis_size("col") - 1
    left_side = jnp.where(first_col, padded[:, :, 1:2], padded[:, :, 0:1])
    right_side = jnp.where(last_col, padded[:, :, -2:-1], padded[:, :, -1:])
    return jnp.concatenate([left_side, padded[:, :, 1:-1], right_side], 2)


def patches(padded):
    tall = padded.shape[1] - 2
    broad = padded.shape[2] - 2
    pieces = [
        padded[:, row_shift : row_shift + tall, col_shift : col_shift + broad]
        for row_shift in range(3)
        for col_shift in range(3)
    ]
    return jnp.concatenate(pieces, -1).reshape(-1, 9 * padded.shape[3])


def conv_apply(padded, kernel):
    result = jnp.dot(
        patches(padded), kernel.reshape(-1, kernel.shape[3]), preferred_element_type=jnp.float32
    )
    return result.reshape(padded.shape[0], padded.shape[1] - 2, padded.shape[2] - 2, -1)


def flip_kernel(kernel):
    return jnp.transpose(kernel[::-1, ::-1], (0, 1, 3, 2))


def double_axis(padded, axis_index):
    leading = jnp.moveaxis(padded, axis_index, 0)
    middle_part = leading[1:-1]
    even_part = 0.75 * middle_part + 0.25 * leading[:-2]
    odd_part = 0.75 * middle_part + 0.25 * leading[2:]
    joined = jnp.stack([even_part, odd_part], 1).reshape(
        (2 * middle_part.shape[0],) + middle_part.shape[1:]
    )
    return jnp.moveaxis(joined, 0, axis_index)


def halve_axis(padded, axis_index):
    leading = jnp.moveaxis(padded, axis_index, 0)
    even_part = leading[1:-1:2]
    odd_part = leading[2:-1:2]
    before_part = leading[0:-2:2]
    after_part = leading[3::2]
    joined = 0.75 * (even_part + odd_part) + 0.25 * (before_part + after_part)
    return jnp.moveaxis(joined, 0, axis_index)


def on_device(
    tokens,
    cot_tokens,
    cot_merged,
    image_counts,
    scale_flags,
    shift_flags,
    qkv_w,
    attn_out_w,
    fc1_w,
    fc1_b,
    fc2_w,
    fc2_b,
    ln1_gain,
    ln1_bias,
    ln2_gain,
    ln2_bias,
    proj_w,
    conv_w,
    head_w,
    head_b,
    shift_row,
):
    lowered = [
        master.astype(jnp.bfloat16)
        for master in (
            qkv_w,
            attn_out_w,
            fc1_w,
            fc1_b,
            fc2_w,
            fc2_b,
            ln1_gain,
            ln1_bias,
            ln2_gain,
            ln2_bias,
            proj_w,
            conv_w,
            head_w,
            head_b,
            shift_row,
        )
    ]
    gathered = (
        lax.all_gather(lowered[0], "dp", axis=0, tiled=True),
        lax.all_gather(lowered[1], "dp", axis=0, tiled=True),
        lax.all_gather(lowered[2], "dp", axis=0, tiled=True),
        lax.all_gather(lowered[3], "dp", axis=0, tiled=True),
        lax.all_gather(lowered[4], "dp", axis=0, tiled=True),
        lax.all_gather(lowered[5], "dp", axis=0, tiled=True),
        lax.all_gather(lowered[6], "dp", axis=0, tiled=True),
        lax.all_gather(lowered[7], "dp", axis=0, tiled=True),
        lax.all_gather(lowered[8], "dp", axis=0, tiled=True),
        lax.all_gather(lowered[9], "dp", axis=0, tiled=True),
        lax.all_gather(lowered[10], "dp", axis=0, tiled=True),
        lax.all_gather(lowered[11], "dp", axis=3, tiled=True),
        lax.all_gather(lowered[12], "dp", axis=0, tiled=True),
        lax.all_gather(lowered[13], "dp", axis=0, tiled=True),
        lax.all_gather(lowered[14], "dp", axis=0, tiled=True),
    )
    (
        w_qkv,
        w_out,
        w_up,
        b_up,
        w_down,
        b_down,
        gain_one,
        bias_one,
        gain_two,
        bias_two,
        w_proj,
        w_conv,
        w_head,
        b_head,
        w_shift,
    ) = gathered
    images = tokens.shape[0]
    tile_rows = tokens.shape[1]
    tile_cols = tokens.shape[2]
    tile_size = tile_rows * tile_cols
    model_width = tokens.shape[3]
    temper = HEAD_DIM ** (-0.5)
    present = (jnp.arange(images) < image_counts[0]).astype(jnp.float32)
    factor = 0.5 + 0.5 * scale_flags.astype(jnp.float32)
    shift_sign = shift_flags.astype(jnp.float32)
    present_rows = jnp.repeat(present, tile_size)[:, None]
    stream = tokens.astype(jnp.float32).reshape(-1, model_width)
    normed, scaled_one, factor_one = norm_rows(
        stream, gain_one.astype(jnp.float32), bias_one.astype(jnp.float32)
    )
    normed_low = normed.astype(jnp.bfloat16)
    projected = jnp.dot(normed_low, w_qkv, preferred_element_type=jnp.float32).astype(jnp.bfloat16)
    queries = projected[:, :model_width].reshape(images, tile_size, HEADS, HEAD_DIM)
    keys_own = projected[:, model_width : 2 * model_width].reshape(images, tile_size, model_width)
    values_own = projected[:, 2 * model_width :].reshape(images, tile_size, model_width)
    keys_all, values_all = (
        lax.all_gather(keys_own, ("row", "col"), axis=1, tiled=True),
        lax.all_gather(values_own, ("row", "col"), axis=1, tiled=True),
    )
    keys_heads = keys_all.reshape(images, -1, HEADS, HEAD_DIM)
    values_heads = values_all.reshape(images, -1, HEADS, HEAD_DIM)
    scores = (
        jnp.einsum("nqhd,nkhd->nhqk", queries, keys_heads, preferred_element_type=jnp.float32)
        * temper
    )
    highest_score = jnp.max(scores, -1, keepdims=True)
    exponent = jnp.exp(scores - highest_score)
    denominator = jnp.sum(exponent, -1, keepdims=True)
    log_total = highest_score + jnp.log(denominator)
    attention_low = (exponent / denominator).astype(jnp.bfloat16)
    attended = jnp.einsum(
        "nhqk,nkhd->nqhd", attention_low, values_heads, preferred_element_type=jnp.float32
    )
    attended = attended.reshape(-1, model_width).astype(jnp.bfloat16)
    after_attn = stream + jnp.dot(attended, w_out, preferred_element_type=jnp.float32)
    normed_two, scaled_two, factor_two = norm_rows(
        after_attn, gain_two.astype(jnp.float32), bias_two.astype(jnp.float32)
    )
    normed_two_low = normed_two.astype(jnp.bfloat16)
    hidden = jnp.dot(normed_two_low, w_up, preferred_element_type=jnp.float32) + b_up.astype(
        jnp.float32
    )
    hidden_low = jax.nn.gelu(hidden).astype(jnp.bfloat16)
    after_mlp = after_attn + (
        jnp.dot(hidden_low, w_down, preferred_element_type=jnp.float32) + b_down.astype(jnp.float32)
    )
    tokens_low = after_mlp.astype(jnp.bfloat16)
    tokens_out = (
        (tokens_low.astype(jnp.float32) * present_rows).astype(jnp.bfloat16).reshape(tokens.shape)
    )
    feature = jnp.dot(tokens_low, w_proj, preferred_element_type=jnp.float32).reshape(
        images, tile_rows, tile_cols, -1
    )
    channels = feature.shape[3]
    stored = []
    for unit_index in range(2):
        first_in = add_rims(jax.nn.gelu(feature).astype(jnp.bfloat16))
        first_out = conv_apply(first_in, w_conv[2 * unit_index])
        second_in = add_rims(jax.nn.gelu(first_out).astype(jnp.bfloat16))
        second_out = conv_apply(second_in, w_conv[2 * unit_index + 1])
        stored.append((feature, first_in, first_out, second_in))
        feature = feature + second_out
    coarse_map = clamp_edges(add_rims(feature.astype(jnp.bfloat16))).astype(jnp.float32)
    upsampled = double_axis(double_axis(coarse_map, 1), 2).astype(jnp.bfloat16)
    fine_rows = upsampled.reshape(-1, channels)
    head_out = jnp.dot(fine_rows, w_head, preferred_element_type=jnp.float32) + b_head.astype(
        jnp.float32
    )
    head_out = head_out.reshape(images, -1, channels)
    merged = (
        head_out * factor[:, None, None] + shift_sign[:, None, None] * w_shift.astype(jnp.float32)
    ) * present[:, None, None]
    merged_out = merged.astype(jnp.bfloat16).reshape(cot_merged.shape)
    gathered = (
        lax.all_gather(lowered[0], "dp", axis=0, tiled=True),
        lax.all_gather(lowered[1], "dp", axis=0, tiled=True),
        lax.all_gather(lowered[2], "dp", axis=0, tiled=True),
        lax.all_gather(lowered[3], "dp", axis=0, tiled=True),
        lax.all_gather(lowered[4], "dp", axis=0, tiled=True),
        lax.all_gather(lowered[5], "dp", axis=0, tiled=True),
        lax.all_gather(lowered[6], "dp", axis=0, tiled=True),
        lax.all_gather(lowered[7], "dp", axis=0, tiled=True),
        lax.all_gather(lowered[8], "dp", axis=0, tiled=True),
        lax.all_gather(lowered[9], "dp", axis=0, tiled=True),
        lax.all_gather(lowered[10], "dp", axis=0, tiled=True),
        lax.all_gather(lowered[11], "dp", axis=3, tiled=True),
        lax.all_gather(lowered[12], "dp", axis=0, tiled=True),
        lax.all_gather(lowered[13], "dp", axis=0, tiled=True),
        lax.all_gather(lowered[14], "dp", axis=0, tiled=True),
    )
    (
        w_qkv,
        w_out,
        w_up,
        b_up,
        w_down,
        b_down,
        gain_one,
        bias_one,
        gain_two,
        bias_two,
        w_proj,
        w_conv,
        w_head,
        b_head,
        w_shift,
    ) = gathered
    merged_grad = (
        cot_merged.astype(jnp.float32).reshape(images, -1, channels) * present[:, None, None]
    )
    grad_shift = jnp.sum(merged_grad * shift_sign[:, None, None], (0, 1))
    head_grad = (merged_grad * factor[:, None, None]).astype(jnp.bfloat16).reshape(-1, channels)
    grad_head_b = jnp.sum(head_grad.astype(jnp.float32), 0)
    grad_head_w = outer_product(fine_rows, head_grad)
    fine_grad = back_product(head_grad, w_head).astype(jnp.bfloat16).reshape(upsampled.shape)
    spread_grad = clamp_edges(extended(fine_grad, (("row", 1), ("col", 2)), 1)).astype(jnp.float32)
    feature_grad = halve_axis(halve_axis(spread_grad, 1), 2)
    conv_grads = [None, None, None, None]
    for unit_index in (1, 0):
        unit_input, first_in, first_out, second_in = stored[unit_index]
        second_grad = feature_grad.astype(jnp.bfloat16)
        conv_grads[2 * unit_index + 1] = outer_product(
            patches(second_in), second_grad.reshape(-1, channels)
        )
        middle_grad = conv_apply(add_rims(second_grad), flip_kernel(w_conv[2 * unit_index + 1]))
        first_grad = gelu_grad(first_out, middle_grad).astype(jnp.bfloat16)
        conv_grads[2 * unit_index] = outer_product(
            patches(first_in), first_grad.reshape(-1, channels)
        )
        inner_grad = conv_apply(add_rims(first_grad), flip_kernel(w_conv[2 * unit_index]))
        feature_grad = feature_grad + gelu_grad(unit_input, inner_grad)
    grad_conv = jnp.stack(conv_grads).reshape(4, 3, 3, channels, channels)
    proj_grad = feature_grad.astype(jnp.bfloat16).reshape(-1, channels)
    grad_proj = outer_product(tokens_low, proj_grad)
    stream_grad = cot_tokens.astype(jnp.float32).reshape(
        -1, model_width
    ) * present_rows + back_product(proj_grad, w_proj)
    down_grad = stream_grad.astype(jnp.bfloat16)
    grad_down_b = jnp.sum(down_grad.astype(jnp.float32), 0)
    grad_down_w = outer_product(hidden_low, down_grad)
    up_grad = gelu_grad(hidden, back_product(down_grad, w_down)).astype(jnp.bfloat16)
    grad_up_b = jnp.sum(up_grad.astype(jnp.float32), 0)
    grad_up_w = outer_product(normed_two_low, up_grad)
    norm_grad, grad_gain_two, grad_bias_two = norm_back(
        back_product(up_grad, w_up), scaled_two, factor_two, gain_two.astype(jnp.float32)
    )
    stream_grad = stream_grad + norm_grad
    branch_grad = stream_grad.astype(jnp.bfloat16)
    grad_out_w = outer_product(attended, branch_grad)
    attended_grad = (
        back_product(branch_grad, w_out)
        .astype(jnp.bfloat16)
        .reshape(images, tile_size, HEADS, HEAD_DIM)
    )
    keys_heads = keys_all.reshape(images, -1, HEADS, HEAD_DIM)
    values_heads = values_all.reshape(images, -1, HEADS, HEAD_DIM)
    scores = (
        jnp.einsum("nqhd,nkhd->nhqk", queries, keys_heads, preferred_element_type=jnp.float32)
        * temper
    )
    attention_full = jnp.exp(scores - log_total)
    attention_low = attention_full.astype(jnp.bfloat16)
    prob_grad = jnp.einsum(
        "nqhd,nkhd->nhqk", attended_grad, values_heads, preferred_element_type=jnp.float32
    )
    centre = jnp.sum(attention_full * prob_grad, -1, keepdims=True)
    score_grad = (attention_full * (prob_grad - centre)).astype(jnp.bfloat16)
    query_grad = (
        jnp.einsum("nhqk,nkhd->nqhd", score_grad, keys_heads, preferred_element_type=jnp.float32)
        * temper
    )
    key_part = (
        jnp.einsum("nhqk,nqhd->knhd", score_grad, queries, preferred_element_type=jnp.float32)
        * temper
    )
    value_part = jnp.einsum(
        "nhqk,nqhd->knhd", attention_low, attended_grad, preferred_element_type=jnp.float32
    )
    pair_grad = lax.psum_scatter(
        jnp.concatenate(
            [
                key_part.reshape(lax.axis_size(("row", "col")) * tile_size, images, model_width),
                value_part.reshape(lax.axis_size(("row", "col")) * tile_size, images, model_width),
            ],
            2,
        ).astype(jnp.bfloat16),
        ("row", "col"),
        scatter_dimension=0,
        tiled=True,
    ).astype(jnp.float32)
    pair_grad = jnp.transpose(pair_grad, (1, 0, 2))
    mixed_grad = jnp.concatenate([query_grad.reshape(images, tile_size, model_width), pair_grad], 2)
    mixed_grad = mixed_grad.astype(jnp.bfloat16).reshape(-1, 3 * model_width)
    grad_qkv = outer_product(normed_low, mixed_grad)
    norm_grad, grad_gain_one, grad_bias_one = norm_back(
        back_product(mixed_grad, w_qkv), scaled_one, factor_one, gain_one.astype(jnp.float32)
    )
    input_grad = (stream_grad + norm_grad).reshape(tokens.shape)
    shards = (
        lax.psum_scatter(
            grad_qkv.astype(jnp.bfloat16), "dp", scatter_dimension=0, tiled=True
        ).astype(jnp.float32),
        lax.psum_scatter(
            grad_out_w.astype(jnp.bfloat16), "dp", scatter_dimension=0, tiled=True
        ).astype(jnp.float32),
        lax.psum_scatter(
            grad_up_w.astype(jnp.bfloat16), "dp", scatter_dimension=0, tiled=True
        ).astype(jnp.float32),
        lax.psum_scatter(
            grad_up_b.astype(jnp.bfloat16), "dp", scatter_dimension=0, tiled=True
        ).astype(jnp.float32),
        lax.psum_scatter(
            grad_down_w.astype(jnp.bfloat16), "dp", scatter_dimension=0, tiled=True
        ).astype(jnp.float32),
        lax.psum_scatter(
            grad_down_b.astype(jnp.bfloat16), "dp", scatter_dimension=0, tiled=True
        ).astype(jnp.float32),
        lax.psum_scatter(
            grad_gain_one.astype(jnp.bfloat16), "dp", scatter_dimension=0, tiled=True
        ).astype(jnp.float32),
        lax.psum_scatter(
            grad_bias_one.astype(jnp.bfloat16), "dp", scatter_dimension=0, tiled=True
        ).astype(jnp.float32),
        lax.psum_scatter(
            grad_gain_two.astype(jnp.bfloat16), "dp", scatter_dimension=0, tiled=True
        ).astype(jnp.float32),
        lax.psum_scatter(
            grad_bias_two.astype(jnp.bfloat16), "dp", scatter_dimension=0, tiled=True
        ).astype(jnp.float32),
        lax.psum_scatter(
            grad_proj.astype(jnp.bfloat16), "dp", scatter_dimension=0, tiled=True
        ).astype(jnp.float32),
        lax.psum_scatter(
            grad_conv.astype(jnp.bfloat16), "dp", scatter_dimension=3, tiled=True
        ).astype(jnp.float32),
        lax.psum_scatter(
            grad_head_w.astype(jnp.bfloat16), "dp", scatter_dimension=0, tiled=True
        ).astype(jnp.float32),
        lax.psum_scatter(
            grad_head_b.astype(jnp.bfloat16), "dp", scatter_dimension=0, tiled=True
        ).astype(jnp.float32),
        lax.psum_scatter(
            grad_shift.astype(jnp.bfloat16), "dp", scatter_dimension=0, tiled=True
        ).astype(jnp.float32),
    )
    totals = (
        lax.psum(shards[0].astype(jnp.bfloat16), ("row", "col")).astype(jnp.float32),
        lax.psum(shards[1].astype(jnp.bfloat16), ("row", "col")).astype(jnp.float32),
        lax.psum(shards[2].astype(jnp.bfloat16), ("row", "col")).astype(jnp.float32),
        lax.psum(shards[3].astype(jnp.bfloat16), ("row", "col")).astype(jnp.float32),
        lax.psum(shards[4].astype(jnp.bfloat16), ("row", "col")).astype(jnp.float32),
        lax.psum(shards[5].astype(jnp.bfloat16), ("row", "col")).astype(jnp.float32),
        lax.psum(shards[6].astype(jnp.bfloat16), ("row", "col")).astype(jnp.float32),
        lax.psum(shards[7].astype(jnp.bfloat16), ("row", "col")).astype(jnp.float32),
        lax.psum(shards[8].astype(jnp.bfloat16), ("row", "col")).astype(jnp.float32),
        lax.psum(shards[9].astype(jnp.bfloat16), ("row", "col")).astype(jnp.float32),
        lax.psum(shards[10].astype(jnp.bfloat16), ("row", "col")).astype(jnp.float32),
        lax.psum(shards[11].astype(jnp.bfloat16), ("row", "col")).astype(jnp.float32),
        lax.psum(shards[12].astype(jnp.bfloat16), ("row", "col")).astype(jnp.float32),
        lax.psum(shards[13].astype(jnp.bfloat16), ("row", "col")).astype(jnp.float32),
        lax.psum(shards[14].astype(jnp.bfloat16), ("row", "col")).astype(jnp.float32),
    )
    return (
        tokens_out,
        merged_out,
        input_grad,
        totals[0],
        totals[1],
        totals[2],
        totals[3],
        totals[4],
        totals[5],
        totals[6],
        totals[7],
        totals[8],
        totals[9],
        totals[10],
        totals[11],
        totals[12],
        totals[13],
        totals[14],
    )


LOG2E = 1.4426950408889634
MESH = pl.DeviceIdType.MESH
HALO = 6
PATCH = 112
VMEM_LIMIT = 58 << 20


def place():
    dp, row, col = (lax.axis_index(axis) for axis in ("dp", "row", "col"))
    return dp, lax.div(row, 2), lax.rem(row, 2), col


def slot_of(y, z, cols):
    return 2 * lax.rem(z + cols + cols // 2 - y, cols) + y


def chip_of(slot, cols):
    y = slot % 2
    return y, (slot // 2 + cols // 2 + y) % cols


def send(src, dst, send_sem, recv_sem, dp, y, core, z):
    return pltpu.make_async_remote_copy(
        src_ref=src,
        dst_ref=dst,
        send_sem=send_sem,
        recv_sem=recv_sem,
        device_id={"dp": dp, "row": y * 2 + core, "col": z},
        device_id_type=MESH,
    )


def landed(ref, sem):
    return pltpu.make_async_copy(ref, ref, sem)


def to_images_start(src, dst, send_sem, recv_sem, sizes):
    chips, slots, cols = sizes
    dp, y, core, z = place()
    own = core * cols + z
    for step in range(chips):
        far_y = lax.rem(y + step // cols, 2)
        far_z = lax.rem(z + step % cols, cols)
        slot = slot_of(far_y, far_z, cols)
        copy = send(
            src.at[slot], dst.at[0, own], send_sem.at[step], recv_sem.at[own], dp, far_y, y, far_z
        )
        if step == 0:
            local = pltpu.make_async_copy(src.at[slot], dst.at[0, own], recv_sem.at[own])
            pl.when(core == y)(local.start)
            pl.when(core != y)(copy.start)
        else:
            copy.start()
    for extra in range(slots - chips):
        to_y, to_z = chip_of(2 * chips - slots + extra, cols)
        send(
            src.at[chips + extra],
            dst.at[1, own],
            send_sem.at[chips + extra],
            recv_sem.at[chips + own],
            1 - dp,
            to_y,
            y,
            to_z,
        ).start()


def to_images_wait(src, dst, send_sem, recv_sem, sizes):
    chips, slots, cols = sizes
    dp, y, core, z = place()
    for step in range(slots):
        left = landed(src.at[0], send_sem.at[step])
        if step == 0:
            pl.when(core != y)(left.wait)
        else:
            left.wait()
    for tile in range(chips):
        landed(dst.at[0, tile], recv_sem.at[tile]).wait()

    @pl.when(slot_of(y, z, cols) >= 2 * chips - slots)
    def _():
        for tile in range(chips):
            landed(dst.at[1, tile], recv_sem.at[chips + tile]).wait()


def to_tiles_start(src, dst, send_sem, recv_sem, sizes):
    chips, slots, cols = sizes
    dp, y, core, z = place()
    slot = slot_of(y, z, cols)
    for step in range(chips):
        far_core = lax.rem(core + step // cols, 2)
        far_z = lax.rem(z + step % cols, cols)
        tile = far_core * cols + far_z
        copy = send(
            src.at[tile], dst.at[slot], send_sem.at[step], recv_sem.at[slot], dp, core, far_core, far_z
        )
        if step == 0:
            local = pltpu.make_async_copy(src.at[tile], dst.at[slot], recv_sem.at[slot])
            pl.when(core == y)(local.start)
            pl.when(core != y)(copy.start)
        else:
            copy.start()

    @pl.when(slot >= 2 * chips - slots)
    def _():
        for step in range(chips):
            far_core = step // cols
            far_z = step % cols
            other = slot + slots - chips
            send(
                src.at[step],
                dst.at[other],
                send_sem.at[chips + step],
                recv_sem.at[other],
                1 - dp,
                core,
                far_core,
                far_z,
            ).start()


def to_tiles_wait(src, dst, send_sem, recv_sem, sizes):
    chips, slots, cols = sizes
    dp, y, core, z = place()
    for step in range(chips):
        left = landed(src.at[0], send_sem.at[step])
        if step == 0:
            pl.when(core != y)(left.wait)
        else:
            left.wait()

    @pl.when(slot_of(y, z, cols) >= 2 * chips - slots)
    def _():
        for step in range(chips):
            landed(src.at[0], send_sem.at[chips + step]).wait()

    for slot in range(slots):
        landed(dst.at[slot], recv_sem.at[slot]).wait()


BITS = ("dp", "y", "z1", "z2")


def mate(bit):
    dp, y, core, z = place()
    low, high = lax.rem(z, 2), lax.div(z, 2)
    if bit == "core":
        return dp, y, 1 - core, z
    if bit == "dp":
        return 1 - dp, y, core, z
    if bit == "y":
        return dp, 1 - y, core, z
    if bit == "z1":
        return dp, y, core, high * 2 + 1 - low
    return dp, y, core, (1 - high) * 2 + low


def bit_of(bit):
    dp, y, core, z = place()
    return {
        "dp": dp,
        "y": y,
        "core": core,
        "z1": lax.rem(z, 2),
        "z2": lax.div(z, 2),
    }[bit]


class Gather:
    def __init__(self, whole, send_sem, recv_sem, split):
        self.whole, self.send_sem, self.recv_sem = whole, send_sem, recv_sem
        if split:
            self.orders = (("core", "y", "z1"), ("core", "z1", "y"))
        else:
            self.orders = (("core", "y"), ("core", "z1"))
        self.next, self.copies = 0, []

    def at(self, step, side):
        order = self.orders[side]
        count = 2 ** len(order)
        rows = self.whole.shape[-2] // (2 * count)
        piece = 0
        for i, bit in enumerate(order):
            if i <= len(order) - max(step, 1):
                piece = piece + bit_of(bit) * 2 ** (len(order) - 1 - i)
        half = bit_of("dp") if step == 0 else 1 - bit_of("dp")
        size = 1 if step == 0 else 2 ** (step - 1)
        part = pl.ds(pl.multiple_of((half * count + piece) * rows, 16), size * rows)
        width = self.whole.shape[-1] // len(self.orders)
        return self.whole.at[
            (slice(None),) * (len(self.whole.shape) - 2) + (part, pl.ds(side * width, width))
        ]

    def tick(self):
        while self.copies:
            self.copies.pop().wait()
        if self.next <= len(self.orders[0]):
            for side, order in enumerate(self.orders):
                bit = (("dp",) + order[::-1])[self.next]
                part = self.at(self.next, side)
                sems = (self.send_sem.at[side, self.next], self.recv_sem.at[side, self.next])
                copy = send(part, part, *sems, *mate(bit))
                copy.start()
                self.copies.append(copy)
            self.next += 1

    def finish(self):
        while self.copies:
            self.tick()


TURNS = {
    "conv": ("z1", ("dp", "z2", "y"), ("z2", "z1", "y", "core")),
    "small": (None, ("dp", "y", "z1", "z2"), ("y", "z1", "z2", "core")),
    "fc1": ("z1", ("y", "dp", "z2"), ("z2", "y", "z1", "core")),
    "proj": (None, ("dp", "z2", "z1", "y"), ("z1", "y", "z2", "core")),
    "head": (None, ("dp", "y", "z2", "z1"), ("y", "z2", "z1", "core")),
    "fc2": ("y", ("dp", "z1", "z2"), ("z2", "z1", "y", "core")),
    "qkv": (None, ("dp", "y", "z1", "z2"), ("z2", "y", "z1", "core")),
    "out": (None, ("dp", "y", "z1", "z2"), ("y", "z2", "z1", "core")),
}
EARLY = ("conv", "fc2", "fc1")
ARRIVED = ("conv",)
WHOLE = ("out", "proj", "head")


class Reduce:
    def __init__(self, turn, near, away, acc, recvs, out, sems, arrived=False):
        self.arrived = arrived
        self.gone, self.sum_order, self.back_order = turn
        self.near, self.away, self.acc, self.recvs, self.out, self.sems = (
            near,
            away,
            acc,
            recvs,
            out,
            sems,
        )
        self.dims = [bit for bit in BITS if bit != self.gone]
        self.kept = {bit: None for bit in BITS}
        if self.gone is not None:
            self.kept[self.gone] = bit_of(self.gone)
        half = out.shape[-1] // 2
        self.mine = pl.ds(pl.multiple_of(bit_of("core") * half, 128), half)
        self.step, self.copies = 0, []
        self.forward = 1 + len(self.sum_order)
        self.last = self.forward + len(self.back_order)

    def index(self):
        free = slice(None)
        return (free,) + tuple(free if self.kept[b] is None else self.kept[b] for b in self.dims)

    def add(self, recv):
        acc, kept, whole = self.acc, self.kept, slice(None)
        free = [b for b in self.dims if kept[b] is None]

        def body(i, _):
            bits, left = {}, i
            for b in reversed(free):
                bits[b] = lax.rem(left, 2)
                left = lax.div(left, 2)
            here = (whole,) + tuple(bits[b] if b in bits else kept[b] for b in self.dims)
            there = (whole,) + tuple(bits[b] for b in free)
            total = acc[here].astype(jnp.float32) + recv[there].astype(jnp.float32)
            acc[here] = total.astype(acc.dtype)
            return 0

        lax.fori_loop(0, 2 ** len(free), body, 0)

    def begin(self, copy):
        copy.start()
        self.copies.append(copy)

    def travel(self, src, dst, step, bit):
        _, send_sem, recv_sem = self.sems
        self.begin(send(src, dst, send_sem.at[step], recv_sem.at[step], *mate(bit)))

    def tick(self):
        step, whole, kept = self.step, slice(None), self.kept
        local_sem = self.sems[0]
        while self.copies:
            self.copies.pop().wait()
        if 0 < step <= self.forward:
            self.add(self.recvs[step - 1])
        if step == self.forward:
            kept["core"] = bit_of("core")
            at = (whole,) + tuple(kept[b] for b in BITS[1:]) + (whole, self.mine)
            self.begin(
                pltpu.make_async_copy(self.acc.at[self.index()], self.out.at[at], local_sem.at[1])
            )
        elif step == 0:
            if self.near is not None:
                self.begin(pltpu.make_async_copy(self.near, self.acc, local_sem.at[0]))
            if self.arrived:
                self.begin(pltpu.make_async_copy(self.away, self.recvs[0], local_sem.at[1]))
            else:
                self.travel(self.away, self.recvs[0], 0, self.gone or "core")
        elif step < self.forward:
            bit = self.sum_order[step - 1]
            kept[bit] = 1 - bit_of(bit)
            src = self.acc.at[self.index()]
            kept[bit] = bit_of(bit)
            self.travel(src, self.recvs[step], step, bit)
        elif step <= self.last:
            if step > self.forward + 1:
                kept[self.back_order[step - self.forward - 2]] = None
            bit = self.back_order[step - self.forward - 1]
            at = (whole,) + tuple(whole if kept[b] is None else kept[b] for b in BITS[1:])
            at = self.out.at[at + (whole, whole if kept["core"] is None else self.mine)]
            self.travel(at, at, step - 1, bit)
        self.step += 1

    def busy(self):
        return self.step <= self.last + 1


def across(value, bit):
    if bit == "dp":
        return lax.ppermute(value, "dp", [(0, 1), (1, 0)])
    if bit == "y":
        return lax.ppermute(value, "row", [(0, 2), (1, 3), (2, 0), (3, 1)])
    return lax.ppermute(value, "col", [(i, i + 1 - 2 * (i % 2)) for i in range(4)])


def recv_shapes(shape):
    free = len(shape) - 3
    return [shape[:1] + (2,) * left + shape[-2:] for left in range(free, -1, -1)]


def early_sum(near, other, bit):
    lead, rows, width = near.shape
    total = near.astype(jnp.float32) + swap_cores(other).astype(jnp.float32)
    total = total.astype(jnp.bfloat16).reshape(lead, 2, 2, 2, 2, rows // 16, width)
    axis, own = 1 + BITS.index(bit), bit_of(bit)
    keep = lax.dynamic_index_in_dim(total, own, axis, keepdims=False)
    away = lax.dynamic_index_in_dim(total, 1 - own, axis, keepdims=False)
    return keep, away


SCALE = HEAD_DIM**-0.5


def attend_pair(q, k, v):
    lane = lax.broadcasted_iota(jnp.int32, (1, 128), 1)
    sub = lax.broadcasted_iota(jnp.int32, (128, 1), 0)
    out = jnp.zeros((128, q.shape[0]), jnp.float32)
    logs = []
    for h in range(2):
        mine = (lane >= 64) == (h == 1)
        scores = lax.dot_general(
            k, jnp.where(mine, q, 0), (((1,), (1,)), ((), ())), preferred_element_type=jnp.float32
        )
        top = jnp.max(scores, 0, keepdims=True) * (SCALE * LOG2E)
        e = jnp.exp2(scores * (SCALE * LOG2E) - top)
        total = jnp.sum(e, 0, keepdims=True)
        part = lax.dot_general(
            v, e.astype(jnp.bfloat16), (((0,), (0,)), ((), ())), preferred_element_type=jnp.float32
        )
        out = jnp.where((sub >= 64) == (h == 1), part / total, out)
        logs.append(top + jnp.log2(total))
    return out.T, logs


def attend_pair_back(q, k, v, o, logs, g):
    lane = lax.broadcasted_iota(jnp.int32, (1, 128), 1)
    sub = lax.broadcasted_iota(jnp.int32, (128, 1), 0)
    product = (g.astype(jnp.float32) * o).T
    dq = jnp.zeros((128, q.shape[0]), jnp.float32)
    dk = dv = 0.0
    for h in range(2):
        mine = (lane >= 64) == (h == 1)
        q_own, g_own = jnp.where(mine, q, 0), jnp.where(mine, g, 0)
        centre = jnp.sum(product[h * 64 : (h + 1) * 64], 0, keepdims=True)
        scores = lax.dot_general(
            k, q_own, (((1,), (1,)), ((), ())), preferred_element_type=jnp.float32
        )
        p = jnp.exp2(scores * (SCALE * LOG2E) - logs[h])
        dp = lax.dot_general(
            v, g_own, (((1,), (1,)), ((), ())), preferred_element_type=jnp.float32
        )
        ds = (p * (dp - centre)).astype(jnp.bfloat16)
        dq_own = lax.dot_general(
            k, ds, (((0,), (0,)), ((), ())), preferred_element_type=jnp.float32
        )
        dq = jnp.where((sub >= 64) == (h == 1), dq_own * SCALE, dq)
        dk = dk + jnp.dot(ds, q_own, preferred_element_type=jnp.float32) * SCALE
        dv = dv + jnp.dot(p.astype(jnp.bfloat16), g_own, preferred_element_type=jnp.float32)
    return dq.T, dk, dv


BACK_INPUTS = ("q", "k", "v", "o", "logs", "g", "x", "stream", "w_qkv", "gain", "bias", "small")
LN_ROWS = 8
PLAN = (
    ("fc1", "head", "proj"),
    ("fc2", "out", "conv"),
    ("proj", "out", "conv"),
    (),
    ("head", "conv", "out"),
    (),
    ("out", "proj"),
    (),
    ("fc2", "out", "conv"),
)


def backward_kernel(sizes, *refs):
    refs = list(refs)

    def take(names):
        return {name: refs.pop(0) for name in names}

    ref = take(BACK_INPUTS)
    tiles = refs.pop(0)
    near, away, grads = take(EARLY), take(EARLY), take(WHOLE)
    slot_tokens, slot_grads = refs.pop(0), refs.pop(0)
    outs = take(TURNS)
    accs = take(TURNS)
    recvs = {name: [refs.pop(0) for _ in range(4 if TURNS[name][0] else 5)] for name in TURNS}
    mixed, far_out, far_in, own_pair, grad_tile, small_wide = (refs.pop(0) for _ in range(6))
    outbox = take(("qkv", "small"))
    tile_send, tile_recv, core_sem, local_sem, send_sem, recv_sem = refs
    low, f32 = jnp.bfloat16, jnp.float32
    core = bit_of("core")

    jobs = {}
    for i, name in enumerate(TURNS):
        sems = (local_sem.at[i], send_sem.at[i], recv_sem.at[i])
        if name in EARLY:
            source = (near[name], away[name])
        elif name in WHOLE:
            half = grads[name].shape[-1] // 2
            source = tuple(
                grads[name].at[..., pl.ds(pl.multiple_of(side * half, 128), half)]
                for side in (core, 1 - core)
            )
        else:
            source = (None, outbox[name])
        jobs[name] = Reduce(
            TURNS[name], *source, accs[name], recvs[name], outs[name], sems, name in ARRIVED
        )

    def tick(*names):
        for name in names:
            jobs[name].tick()

    tick(*PLAN[0])
    to_tiles_start(tiles, slot_tokens, tile_send.at[0], tile_recv.at[0], sizes)
    rows, width = ref["q"].shape
    for pair in range(width // 128):
        lanes = pl.ds(pair * 128, 128)
        dq, dk, dv = attend_pair_back(
            ref["q"][:, lanes],
            ref["k"][:, lanes],
            ref["v"][:, lanes],
            ref["o"][:, lanes],
            [ref["logs"][pair, h : h + 1, :] for h in range(2)],
            ref["g"][:, lanes],
        )
        mixed[:, lanes] = dq.astype(low)
        for i, value in enumerate((dk, dv)):
            to = pl.ds(i * width + pair * 128, 128)
            own_pair[:, to] = value[:rows]
            far_out[:, to] = value[rows:].astype(low)
        tick(*PLAN[1 + pair])
    pair_copy = send(far_out, far_in, core_sem.at[0], core_sem.at[1], *mate("core"))
    pair_copy.start()
    stream = ref["x"][...].astype(f32)
    normed, scaled, factor = norm_rows(stream, ref["gain"][...], ref["bias"][...])
    normed = normed.astype(low)
    pair_copy.wait()
    mixed[:, width:] = (own_pair[...] + far_in[...].astype(f32)).astype(low)

    half = mixed.shape[1] // 2
    for side, target in ((1 - core, outbox["qkv"]), (core, accs["qkv"])):
        for c in range(0, half, 384):
            part = mixed[:, pl.ds(pl.multiple_of(side * half + c, 128), 384)]
            value = outer_product(normed, part).astype(low)
            target[..., c : c + 384] = value.reshape(target.shape[:-1] + (384,))
        if target is outbox["qkv"]:
            tick(*PLAN[7])
    tick("qkv")
    tick(*PLAN[8])
    grad = back_product(mixed[...], ref["w_qkv"][...])
    gained, grad_gain, grad_bias = norm_back(grad, scaled, factor, ref["gain"][...])
    grad_tile[...] = (ref["stream"][...] + gained).astype(low).reshape(grad_tile.shape)

    small_wide[...] = ref["small"][...]
    for v, value in enumerate((grad_gain, grad_bias)):
        value = value.reshape(1, width)
        for j in range(width // 128):
            side, at = divmod(j, width // 256)
            row = side * (small_wide.shape[0] // 2) + LN_ROWS + 2 * v + at // 2
            small_wide[row : row + 1, at % 2 * 128 : at % 2 * 128 + 128] = value[
                :, j * 128 : (j + 1) * 128
            ]
    for side, target in ((core, accs["small"]), (1 - core, outbox["small"])):
        part = small_wide[:, pl.ds(pl.multiple_of(side * 128, 128), 128)].astype(low)
        target[...] = part.reshape(target.shape)
    tick("small")
    to_tiles_start(grad_tile, slot_grads, tile_send.at[1], tile_recv.at[1], sizes)
    while any(job.busy() for job in jobs.values()):
        for job in jobs.values():
            if job.busy():
                job.tick()
    to_tiles_wait(tiles, slot_tokens, tile_send.at[0], tile_recv.at[0], sizes)
    to_tiles_wait(grad_tile, slot_grads, tile_send.at[1], tile_recv.at[1], sizes)


def run_backward(inputs, tiles, early, grads, sizes):
    chips, slots, _ = sizes
    low, f32 = jnp.bfloat16, jnp.float32
    rows, width = inputs["q"].shape
    cut, accs = {}, {}
    for name in TURNS:
        if name in EARLY:
            accs[name] = early[name][0].shape
            continue
        if name in WHOLE:
            lead, height, across = grads[name].shape
            cut[name] = grads[name].reshape(lead, 2, 2, 2, 2, height // 16, across)
        else:
            lead = 1
            height, across = (width, 3 * width) if name == "qkv" else inputs["small"].shape
        accs[name] = (lead, 2, 2, 2, 2, height // 16, across // 2)
    shape = jax.ShapeDtypeStruct
    out_shape = [shape((slots,) + tiles.shape[1:], low)] * 2 + [
        shape(acc[:1] + (2, 2, 2, acc[-2], 2 * acc[-1]), low) for acc in accs.values()
    ]
    recvs = [value for acc in accs.values() for value in recv_shapes(acc)]
    hbm, vmem = pl.BlockSpec(memory_space=pltpu.HBM), pl.BlockSpec(memory_space=pltpu.VMEM)
    n = len(TURNS)
    slot_tokens, slot_grads, *sums = pl.pallas_call(
        functools.partial(backward_kernel, sizes),
        out_shape=out_shape,
        in_specs=[vmem] * len(BACK_INPUTS) + [hbm] * (1 + 2 * len(EARLY) + len(WHOLE)),
        out_specs=[hbm] * (2 + n),
        scratch_shapes=[pltpu.VMEM(value, low) for value in list(accs.values()) + recvs]
        + [
            pltpu.VMEM((rows, 3 * width), low),
            pltpu.VMEM((rows, 2 * width), low),
            pltpu.VMEM((rows, 2 * width), low),
            pltpu.VMEM((rows, 2 * width), f32),
            pltpu.VMEM(tiles.shape, low),
            pltpu.VMEM(inputs["small"].shape, f32),
            pltpu.VMEM(accs["qkv"], low),
            pltpu.VMEM(accs["small"], low),
            pltpu.SemaphoreType.DMA((2, 2 * chips)),
            pltpu.SemaphoreType.DMA((2, slots)),
            pltpu.SemaphoreType.DMA((2,)),
            pltpu.SemaphoreType.DMA((n, 2)),
            pltpu.SemaphoreType.DMA((n, 9)),
            pltpu.SemaphoreType.DMA((n, 9)),
        ],
        compiler_params=pltpu.CompilerParams(
            has_side_effects=True, vmem_limit_bytes=VMEM_LIMIT
        ),
    )(
        *(inputs[name] for name in BACK_INPUTS),
        tiles,
        *(early[name][0] for name in EARLY),
        *(early[name][1] for name in EARLY),
        *(cut[name] for name in WHOLE),
    )
    return (
        slot_tokens,
        slot_grads,
        {
            name: out.reshape(out.shape[0], 8 * out.shape[4], out.shape[5])
            for name, out in zip(TURNS, sums)
        },
    )


GELU_K, GELU_C = 0.7978845608028654, 0.044715


def gelu_slope(v):
    t = jnp.tanh(GELU_K * (v + GELU_C * v * v * v))
    return 0.5 * (1.0 + t) + 0.5 * v * (1.0 - t * t) * (GELU_K * (1.0 + 3.0 * GELU_C * v * v))


def block(row, size):
    return pl.ds(pl.multiple_of(row * size, size), size)


def turned(core, row, last):
    return core * (last - 2 * row) + row


def triple(dst, value, cols):
    rows, feat = value.shape
    col = lax.rem(lax.broadcasted_iota(jnp.int32, (rows, 1), 0), cols)
    left = jnp.where(col == 0, 0.0, pltpu.roll(value, 1, 0))
    right = jnp.where(col == cols - 1, 0.0, pltpu.roll(value, rows - 1, 0))
    body = pl.ds(cols, rows)
    dst[body, 0:feat] = left.astype(dst.dtype)
    dst[body, feat : 2 * feat] = value.astype(dst.dtype)
    dst[body, 2 * feat :] = right.astype(dst.dtype)


def clear_ends(dst, cols):
    zero = jnp.zeros((cols, dst.shape[1]), dst.dtype)
    dst[0:cols, :] = zero
    dst[dst.shape[0] - cols :, :] = zero


def taps(w_ref, line):
    value = w_ref[pl.ds(line * 3, 3)]
    return value.reshape(3 * value.shape[1], value.shape[2])


def conv_rows(src, w_ref, first, core, cols):
    rows = src.shape[0] - 2 * cols
    total = 0.0
    for a in range(3):
        total = total + jnp.dot(
            src[a * cols : a * cols + rows, :],
            taps(w_ref, first + turned(core, a, 2)),
            preferred_element_type=jnp.float32,
        )
    return total


def maps_forward(cols, own, f0_ref, first0_ref, f1_ref, first1_ref, w_ref, out_ref, wide):
    core = place()[2]
    clear_ends(wide, cols)
    for unit, (f, first, after) in enumerate(
        ((f0_ref, first0_ref, f1_ref), (f1_ref, first1_ref, None))
    ):
        triple(wide, jax.nn.gelu(f[...]), cols)
        first[...] = conv_rows(wide, w_ref, 6 * unit, core, cols)
        triple(wide, jax.nn.gelu(first[...]), cols)
        result = f[...] + conv_rows(wide, w_ref, 6 * unit + 3, core, cols)
        if after is not None:
            after[...] = result
    result = result.astype(out_ref.dtype)
    rows = own // cols + 2
    for j in range(rows):
        i = max(j - 1, 0)
        out_ref[block(turned(core, j, rows - 1), cols), :] = result[i * cols : (i + 1) * cols]


def kernel_grads(wide, grad, out_ref, first, core, cols):
    own = grad.shape[0]
    for a in range(3):
        value = outer_product(wide[a * cols : a * cols + own, :], grad)
        half = value.shape[1] // 2
        left, right = value[:, :half], value[:, half:]
        at = first + turned(core, a, 2)
        near, other = out_ref
        near[at] = jnp.where(core == 0, left, right).astype(near.dtype)
        other[at] = jnp.where(core == 0, right, left).astype(other.dtype)


def conv_back_rows(src, w_ref, first, core, cols):
    rows, feat = src.shape[0] - 2 * cols, w_ref.shape[2]
    total = 0.0
    for a in range(3):
        tap = taps(w_ref, first + turned(core, 2 - a, 2))
        for b in range(3):
            total = total + back_product(
                src[a * cols : a * cols + rows, b * feat : (b + 1) * feat],
                tap[(2 - b) * feat : (3 - b) * feat],
            )
    return total


def maps_back_kernel(
    tiles,
    cols,
    tall_ref,
    far_ref,
    f0_ref,
    first0_ref,
    f1_ref,
    first1_ref,
    w_ref,
    patch_ref,
    near_ref,
    other_ref,
    out_ref,
    slot_ref,
    wide,
    wide_g,
    total,
    parted,
    tile_send,
    tile_recv,
):
    chips = patch_ref.shape[0]
    sizes = (chips, slot_ref.shape[0], cols)
    to_tiles_start(patch_ref, slot_ref, tile_send, tile_recv, sizes)
    g_ref = (near_ref, other_ref)
    tile_rows, tile_cols = tiles
    core = place()[2]
    own_rows = 2 * tile_rows
    own = own_rows * cols * tile_cols
    line = cols * tile_cols
    edge = own_rows + 1

    def near(i):
        return tall_ref[block(turned(core, i, edge), line), :]

    def far(i):
        return far_ref[block(turned(1 - core, i, edge), line), :]

    for i in range(own_rows + 4):
        at = i * line
        if i < own_rows:
            value = near(i + 1)
            if i == 0:
                value = value + near(0)
            if i == own_rows - 1:
                value = value + far(edge)
        else:
            value = far(2 * own_rows - i)
            if i == own_rows:
                value = value + near(edge)
        total[at : at + line, :] = value
    rest = (own_rows + 4) * line
    total[rest:, :] = jnp.zeros((total.shape[0] - rest, total.shape[1]), jnp.float32)
    clear_ends(wide, line)
    clear_ends(wide_g, line)
    for unit, (f, first) in ((1, (f1_ref, first1_ref)), (0, (f0_ref, first0_ref))):
        triple(wide, jax.nn.gelu(first[...]), line)
        triple(wide_g, total[...], line)
        kernel_grads(
            wide, total[0:own, :].astype(wide.dtype), g_ref, 6 * unit + 3, core, line
        )
        middle = conv_back_rows(wide_g, w_ref, 6 * unit + 3, core, line)
        middle = gelu_slope(first[...]) * middle
        triple(wide, jax.nn.gelu(f[...]), line)
        triple(wide_g, middle, line)
        kernel_grads(wide, middle[0:own].astype(wide.dtype), g_ref, 6 * unit, core, line)
        inner = conv_back_rows(wide_g, w_ref, 6 * unit, core, line)
        total[...] += gelu_slope(f[...]) * inner
    for r in range(own_rows):
        row = turned(core, r, own_rows - 1)
        for z in range(cols):
            at = ((r // tile_rows) * cols + z) * tile_rows + r % tile_rows
            parted[at * tile_cols : (at + 1) * tile_cols, :] = total[
                block(row * cols + z, tile_cols), :
            ]
    out_ref[...] = parted[...].astype(out_ref.dtype)
    to_tiles_wait(patch_ref, slot_ref, tile_send, tile_recv, sizes)


def in_vmem(count):
    return [pl.BlockSpec(memory_space=pltpu.VMEM)] * count


def maps_backward(tall, far, saved, w_conv, patch, slots, tiles, cols):
    rows, feat = saved[0].shape
    line = cols * tiles[1]
    own = 2 * tiles[0] * line
    low, f32 = jnp.bfloat16, jnp.float32
    hbm = pl.BlockSpec(memory_space=pltpu.HBM)
    half = jax.ShapeDtypeStruct((12, 3 * feat, feat // 2), low)
    return pl.pallas_call(
        functools.partial(maps_back_kernel, tiles, cols),
        out_shape=[
            half,
            half,
            jax.ShapeDtypeStruct((own, feat), low),
            jax.ShapeDtypeStruct((slots,) + patch.shape[1:], low),
        ],
        in_specs=in_vmem(3 + len(saved)) + [hbm],
        out_specs=in_vmem(3) + [hbm],
        scratch_shapes=[pltpu.VMEM((rows + 2 * line, 3 * feat), low)] * 2
        + [
            pltpu.VMEM((rows, feat), f32),
            pltpu.VMEM((own, feat), f32),
            pltpu.SemaphoreType.DMA((2 * patch.shape[0],)),
            pltpu.SemaphoreType.DMA((slots,)),
        ],
        compiler_params=pltpu.CompilerParams(
            has_side_effects=True, vmem_limit_bytes=VMEM_LIMIT
        ),
    )(tall, far, *saved, w_conv, patch)


WEIGHTS = ("qkv", "out", "fc1", "fc2", "proj", "conv")
VECTORS = ("fc1_b", "fc2_b", "ln1_gain", "ln1_bias", "ln2_gain", "ln2_bias")
SAVED = ("x", "q", "k", "v", "o", "logs", "after_attn", "hidden", "tokens_low")
MAPS = ("f0", "first0", "f1", "first1", "coarse")
STAGES = 4


def chunks_of(name, master, whole, dp):
    if name == "conv":
        half = master.shape[1]
        rows = pl.ds(pl.multiple_of(dp * half, 16), half)
        return [(master.at[t], whole.at[t, rows]) for t in range(master.shape[0])]
    half, width = master.shape
    step = half if width > 1024 or half <= 512 else 384
    wide = min(width, 768)
    out = []
    for r in range(0, half, step):
        for c in range(0, width, wide):
            rows = pl.ds(pl.multiple_of(dp * half + r, 16), step)
            out.append((master.at[pl.ds(r, step), pl.ds(c, wide)], whole.at[rows, pl.ds(c, wide)]))
    return out


def forward_kernel(sizes, tiles, lengths, *refs):
    chips, slots, cols = sizes
    tile_rows, tile_cols = tiles
    refs = list(refs)

    def take(names):
        taken = {name: refs.pop(0) for name in names}
        return taken

    tile_in = take(("tokens", "cots", "patches"))
    masters = take(WEIGHTS)
    vectors = refs.pop(0)
    flag = refs.pop(0)
    image_out = take(("cots", "patches"))
    whole_out = take(WEIGHTS)
    vector_out = refs.pop(0)
    saved = take(SAVED)
    maps = take(MAPS)
    image = refs.pop(0)
    whole = take(WEIGHTS)
    far_vectors = refs.pop(0)
    keys, values, f0, hidden_low, flat, wide, stage = (refs.pop(0) for _ in range(7))
    kept = take(("o", "after_attn", "hidden", "first0", "f1", "first1"))
    tile_send, tile_recv, gather_send, gather_recv, vec_send, vec_recv, stage_sem, core_sem, out_sem = refs
    dp, y, core, z = place()
    low, f32 = jnp.bfloat16, jnp.float32

    to_images_start(tile_in["tokens"], image, tile_send.at[0], tile_recv.at[0], sizes)
    vector_copy = send(vectors, far_vectors, vec_send, vec_recv, *mate("dp"))
    vector_copy.start()

    work = [(name, c) for name in WEIGHTS for c in chunks_of(name, masters[name], whole[name], dp)]
    incoming = {}

    def fetch(i):
        if i < len(work):
            source = work[i][1][0]
            slot = stage.at[i % STAGES, pl.ds(0, source.shape[0]), pl.ds(0, source.shape[1])]
            incoming[i] = pltpu.make_async_copy(source, slot, stage_sem.at[i % STAGES])
            incoming[i].start()

    gathers = {
        name: Gather(whole[name], gather_send.at[i], gather_recv.at[i], name in ("qkv", "out"))
        for i, name in enumerate(WEIGHTS)
    }
    done = [0]
    for i in range(STAGES - 1):
        fetch(i)

    def round_next(name):
        while done[0] < len(work) and work[done[0]][0] == name:
            i = done[0]
            fetch(i + STAGES - 1)
            incoming.pop(i).wait()
            target = work[i][1][1]
            target[...] = stage[i % STAGES, : target.shape[0], : target.shape[1]].astype(low)
            done[0] += 1

    def tick(*names):
        for name in names:
            gathers[name].tick()

    out_copies = []

    def keep(src, dst):
        copy = pltpu.make_async_copy(src, dst, out_sem.at[len(out_copies)])
        copy.start()
        out_copies.append(copy)

    round_next("qkv")
    tick("qkv")
    round_next("out")
    tick("out")
    round_next("fc1")
    tick("qkv", "fc1")
    round_next("fc2")
    round_next("proj")
    tick("qkv")
    round_next("conv")
    tick("out", "qkv", "fc1", "fc2")
    gathers["qkv"].finish()
    vector_copy.wait()
    own, far = vectors[...], far_vectors[...]
    vec, at = {}, 0
    for name, length in zip(VECTORS, lengths):
        part = slice(at, at + length)
        row = jnp.concatenate(
            [jnp.where(dp == 0, own, far)[:, part], jnp.where(dp == 0, far, own)[:, part]], axis=1
        )
        vec[name] = row.astype(low).astype(f32)
        vector_out[:, 2 * at : 2 * (at + length)] = vec[name]
        at += length
    to_images_wait(tile_in["tokens"], image, tile_send.at[0], tile_recv.at[0], sizes)

    width = image.shape[3]
    x = jnp.where(flag[0:1, 0:1] > 0, image[1].astype(f32), image[0].astype(f32))
    x = x.reshape(-1, width)
    rows = x.shape[0]
    saved["x"][...] = x.astype(low)
    normed = norm_rows(x, vec["ln1_gain"], vec["ln1_bias"])[0].astype(low)
    mine = pl.ds(0, rows)
    theirs = pl.ds(rows, rows)
    core_copies = []
    for i, ref in ((1, keys), (2, values), (0, None)):
        part = jnp.dot(
            normed, whole["qkv"][:, i * width : (i + 1) * width], preferred_element_type=f32
        ).astype(low)
        if ref is None:
            saved["q"][...] = part
        else:
            ref[mine, :] = part
            copy = send(
                ref.at[mine], ref.at[theirs], core_sem.at[0, i], core_sem.at[1, i], *mate("core")
            )
            copy.start()
            core_copies.append(copy)
    tick("out")
    for copy in core_copies:
        copy.wait()
    tick("fc1", "fc2", "conv", "proj")
    to_images_start(tile_in["patches"], image_out["patches"], tile_send.at[1], tile_recv.at[1], sizes)
    keep(keys, saved["k"])
    keep(values, saved["v"])
    for name in ("qkv",):
        keep(whole[name], whole_out[name])

    for pair in range(width // 128):
        lanes = pl.ds(pair * 128, 128)
        out, logs = attend_pair(saved["q"][:, lanes], keys[:, lanes], values[:, lanes])
        kept["o"][:, lanes] = out
        for h in range(2):
            saved["logs"][pair, h : h + 1, :] = logs[h]
        if pair == 1:
            tick("out")
        if pair == 3:
            tick("fc2")
    gathers["out"].finish()
    tick("fc2", "conv", "proj")
    to_images_start(tile_in["cots"], image_out["cots"], tile_send.at[2], tile_recv.at[2], sizes)
    after_attn = saved["x"][...].astype(f32) + jnp.dot(
        kept["o"][...].astype(low), whole["out"][...], preferred_element_type=f32
    )
    kept["after_attn"][...] = after_attn
    keep(kept["o"], saved["o"])
    keep(kept["after_attn"], saved["after_attn"])
    normed_two = norm_rows(after_attn, vec["ln2_gain"], vec["ln2_bias"])[0].astype(low)
    gathers["fc1"].finish()
    for c in range(0, hidden_low.shape[1], width):
        part = pl.ds(c, width)
        hidden = jnp.dot(normed_two, whole["fc1"][:, part], preferred_element_type=f32)
        hidden = hidden + vec["fc1_b"][:, c : c + width]
        kept["hidden"][:, part] = hidden
        hidden_low[:, part] = jax.nn.gelu(hidden).astype(low)
        if c == width:
            tick("conv", "proj")
    keep(kept["hidden"], saved["hidden"])
    gathers["fc2"].finish()
    after_mlp = kept["after_attn"][...] + (
        jnp.dot(hidden_low[...], whole["fc2"][...], preferred_element_type=f32) + vec["fc2_b"]
    )
    tokens_low = after_mlp.astype(low)
    saved["tokens_low"][...] = tokens_low
    gathers["proj"].finish()

    flat[...] = jnp.dot(tokens_low, whole["proj"][...], preferred_element_type=f32)
    half_rows, line = 2 * tile_rows, cols * tile_cols
    for r in range(half_rows):
        row = turned(core, r, half_rows - 1)
        for zz in range(cols):
            at = ((r // tile_rows) * cols + zz) * tile_rows + r % tile_rows
            f0[block(row * cols + zz, tile_cols), :] = flat[at * tile_cols : (at + 1) * tile_cols, :]
    core_copies = []
    for i in range(HALO):
        copy = send(
            f0.at[pl.ds((half_rows - 1 - i) * line, line)],
            f0.at[pl.ds((half_rows + i) * line, line)],
            core_sem.at[0, 3 + i],
            core_sem.at[1, 3 + i],
            *mate("core"),
        )
        copy.start()
        core_copies.append(copy)
    gathers["conv"].finish()
    for copy in core_copies:
        copy.wait()
    for name in WEIGHTS[1:]:
        keep(whole[name], whole_out[name])
    keep(f0, maps["f0"])
    maps_forward(
        line, rows, f0, kept["first0"], kept["f1"], kept["first1"], whole["conv"], maps["coarse"], wide
    )
    for name in ("first0", "f1", "first1"):
        keep(kept[name], maps[name])
    for copy in out_copies:
        copy.wait()
    to_images_wait(
        tile_in["patches"], image_out["patches"], tile_send.at[1], tile_recv.at[1], sizes
    )
    to_images_wait(tile_in["cots"], image_out["cots"], tile_send.at[2], tile_recv.at[2], sizes)


def run_forward(tile_in, masters, vectors, flag, sizes, tiles):
    chips, slots, cols = sizes
    low, f32 = jnp.bfloat16, jnp.float32
    shape = jax.ShapeDtypeStruct
    tile, width = tile_in[0].shape[1:]
    feat = masters["proj"].shape[1]
    hidden = masters["fc1"].shape[1]
    lengths = [v.shape[0] for v in vectors]
    rows, line = chips * tile, cols * tiles[1]
    ext = rows + HALO * line
    wholes = {
        name: shape(m.shape[:-2] + (2 * m.shape[-2], m.shape[-1]), low) for name, m in masters.items()
    }
    saved = {
        "x": shape((rows, width), low),
        "q": shape((rows, width), low),
        "k": shape((2 * rows, width), low),
        "v": shape((2 * rows, width), low),
        "o": shape((rows, width), f32),
        "logs": shape((width // 128, 2, rows), f32),
        "after_attn": shape((rows, width), f32),
        "hidden": shape((rows, hidden), f32),
        "tokens_low": shape((rows, width), low),
    }
    maps = {name: shape((ext, feat), f32) for name in MAPS[:-1]}
    maps["coarse"] = shape((rows + 2 * line, feat), low)
    far = [shape((2, chips) + t.shape[1:], t.dtype) for t in tile_in]
    hbm, vmem = pl.BlockSpec(memory_space=pltpu.HBM), pl.BlockSpec(memory_space=pltpu.VMEM)
    out_shape = (
        far[1:]
        + [wholes[name] for name in WEIGHTS]
        + [shape((1, 2 * sum(lengths)), f32)]
        + [saved[name] for name in SAVED]
        + [maps[name] for name in MAPS]
    )
    out_specs = (
        [hbm] * (2 + len(WEIGHTS))
        + [vmem]
        + [hbm if name in ("k", "v", "o", "after_attn", "hidden") else vmem for name in SAVED]
        + [vmem if name == "coarse" else hbm for name in MAPS]
    )
    n = len(WEIGHTS)
    outs = pl.pallas_call(
        functools.partial(forward_kernel, sizes, tiles, lengths),
        out_shape=out_shape,
        in_specs=[hbm] * (3 + n) + [vmem] * 2,
        out_specs=out_specs,
        scratch_shapes=[pltpu.VMEM(far[0].shape, low)]
        + [pltpu.VMEM(wholes[name].shape, low) for name in WEIGHTS]
        + [pltpu.VMEM((1, sum(lengths)), f32)]
        + [
            pltpu.VMEM((2 * rows, width), low),
            pltpu.VMEM((2 * rows, width), low),
            pltpu.VMEM((ext, feat), f32),
            pltpu.VMEM((rows, hidden), low),
            pltpu.VMEM((rows, feat), f32),
            pltpu.VMEM((ext + 2 * line, 3 * feat), low),
            pltpu.VMEM((STAGES, 384, 768), f32),
            pltpu.VMEM((rows, width), f32),
            pltpu.VMEM((rows, width), f32),
            pltpu.VMEM((rows, hidden), f32),
            pltpu.VMEM((ext, feat), f32),
            pltpu.VMEM((ext, feat), f32),
            pltpu.VMEM((ext, feat), f32),
            pltpu.SemaphoreType.DMA((3, slots)),
            pltpu.SemaphoreType.DMA((3, 2 * chips)),
            pltpu.SemaphoreType.DMA((n, 2, 4)),
            pltpu.SemaphoreType.DMA((n, 2, 4)),
            pltpu.SemaphoreType.DMA,
            pltpu.SemaphoreType.DMA,
            pltpu.SemaphoreType.DMA((STAGES,)),
            pltpu.SemaphoreType.DMA((2, 3 + HALO)),
            pltpu.SemaphoreType.DMA((n + 9,)),
        ],
        compiler_params=pltpu.CompilerParams(
            has_side_effects=True, vmem_limit_bytes=VMEM_LIMIT
        ),
    )(
        *tile_in,
        *(masters[name] for name in WEIGHTS),
        jnp.concatenate(vectors)[None],
        flag,
    )
    outs = list(outs)
    images = [outs.pop(0) for _ in range(2)]
    weights = {name: outs.pop(0) for name in WEIGHTS}
    joined, vec, at = outs.pop(0), {}, 0
    for name, length in zip(VECTORS, lengths):
        vec[name] = joined[:, 2 * at : 2 * (at + length)]
        at += length
    return (images, weights, vec) + tuple(
        {name: outs.pop(0) for name in names} for names in (SAVED, MAPS)
    )


def swap_cores(value):
    return lax.ppermute(value, "row", [(0, 1), (1, 0), (2, 3), (3, 2)])


def halve_patch(grad, axis):
    grad = jnp.moveaxis(grad, axis, 0)
    even, odd = grad[0::2], grad[1::2]
    zero = jnp.zeros_like(even[:1])
    middle = jnp.concatenate([zero, 0.75 * (even + odd), zero])
    before = jnp.concatenate([0.25 * even, zero, zero])
    after = jnp.concatenate([zero, zero, 0.25 * odd])
    return jnp.moveaxis(middle + before + after, 0, axis)


def on_chip(
    chips,
    tokens,
    cot_tokens,
    cot_merged,
    image_counts,
    scale_flags,
    shift_flags,
    qkv_w,
    attn_out_w,
    fc1_w,
    fc1_b,
    fc2_w,
    fc2_b,
    ln1_gain,
    ln1_bias,
    ln2_gain,
    ln2_bias,
    proj_w,
    conv_w,
    head_w,
    head_b,
    shift_row,
):
    slots, tile_rows, tile_cols, width = tokens.shape
    cols = lax.axis_size("col")
    sizes = (chips, slots, cols)
    tile = tile_rows * tile_cols
    feat = proj_w.shape[1]
    half_rows, all_cols = 2 * tile_rows, cols * tile_cols
    dp, y, core, z = place()
    low = jnp.bfloat16
    count = image_counts[0]
    present = (jnp.arange(slots) < count).astype(jnp.float32)
    factor = 0.5 + 0.5 * scale_flags.astype(jnp.float32)
    shift_sign = shift_flags.astype(jnp.float32)
    full_group = count == slots
    chip = slot_of(y, z, cols)
    borrowed = jnp.logical_and(jnp.logical_not(full_group), chip >= 2 * chips - slots)
    image_present = jnp.where(
        jnp.logical_or(jnp.logical_or(full_group, borrowed), chip < count), 1.0, 0.0
    )

    def both_halves(value):
        far = lax.ppermute(value, "dp", [(0, 1), (1, 0)])
        return jnp.where(dp == 0, jnp.stack([value, far]), jnp.stack([far, value]))

    w_head = both_halves(head_w.astype(low)).reshape(feat, feat)
    rows_small = both_halves(jnp.stack([head_b, shift_row]))
    b_head, w_shift = (
        rows_small[:, i].reshape(-1).astype(low).astype(jnp.float32) for i in range(2)
    )

    merged_grad = cot_merged.astype(jnp.float32).reshape(slots, -1, feat) * present[:, None, None]
    grad_shift = jnp.sum(merged_grad * shift_sign[:, None, None], (0, 1))
    head_grad = (merged_grad * factor[:, None, None]).astype(low).reshape(-1, feat)
    grad_head_b = jnp.sum(head_grad.astype(jnp.float32), 0)
    fine_grad = back_product(head_grad, w_head).astype(low).reshape(cot_merged.shape)
    patch_grad = halve_patch(halve_patch(fine_grad.astype(jnp.float32), 1), 2).astype(low)
    cells = (tile_rows + 2) * (tile_cols + 2)
    patch_grad = jnp.pad(
        patch_grad.reshape(slots, cells, feat), ((0, 0), (0, PATCH - cells), (0, 0))
    )

    vectors = (fc1_b, fc2_b, ln1_gain, ln1_bias, ln2_gain, ln2_bias)
    (image_cots, image_patches), weights, vec, saved, maps = run_forward(
        (tokens.reshape(slots, tile, width), cot_tokens.reshape(slots, tile, width), patch_grad),
        {
            "qkv": qkv_w,
            "out": attn_out_w,
            "fc1": fc1_w,
            "fc2": fc2_w,
            "proj": proj_w,
            "conv": conv_w.reshape((36,) + conv_w.shape[3:]),
        },
        vectors,
        jnp.full((8, 128), borrowed.astype(jnp.float32)),
        sizes,
        (tile_rows, tile_cols),
    )
    w_qkv, w_out, w_up, w_down, w_proj, w_conv = (weights[name] for name in WEIGHTS)
    gain_one, bias_one, gain_two, bias_two = (vec[name] for name in VECTORS[2:])

    def chosen(pair):
        return jnp.where(borrowed, pair[1], pair[0])

    rows = chips * tile
    tiles = (tile_rows, tile_cols)
    tokens_low = saved["tokens_low"]

    coarse = maps["coarse"].reshape(half_rows + 2, all_cols, feat)
    coarse = jnp.concatenate([coarse[:, :1], coarse, coarse[:, -1:]], 1)
    cuts = [
        coarse[
            r * tile_rows : (r + 1) * tile_rows + 2, c * tile_cols : (c + 1) * tile_cols + 2
        ].reshape(cells, feat)
        for r in range(2)
        for c in range(cols)
    ]
    patch = jnp.pad(jnp.stack(cuts), ((0, 0), (0, PATCH - cells), (0, 0)))
    parts = chosen(image_patches)[:, :cells].astype(jnp.float32)
    parts = parts.reshape(2, cols, tile_rows + 2, tile_cols + 2, feat)
    wide = sum(
        jnp.pad(parts[:, c], ((0, 0), (0, 0), (c * tile_cols, (cols - 1 - c) * tile_cols), (0, 0)))
        for c in range(cols)
    )
    wide = jnp.concatenate(
        [wide[:, :, 1:2] + wide[:, :, :1], wide[:, :, 2:-2], wide[:, :, -2:-1] + wide[:, :, -1:]], 2
    )
    tall = jnp.pad(wide[0], ((0, tile_rows), (0, 0), (0, 0))) + jnp.pad(
        wide[1], ((tile_rows, 0), (0, 0), (0, 0))
    )
    tall = tall.reshape(-1, feat)
    *grad_conv, proj_grad, slot_patch = maps_backward(
        tall, swap_cores(tall), [maps[name] for name in MAPS[:-1]], w_conv, patch, slots, tiles, cols
    )
    grad_conv = early_sum(*(g.reshape(36, feat, feat // 2) for g in grad_conv), TURNS["conv"][0])

    normed_two, scaled_two, factor_two = norm_rows(saved["after_attn"], gain_two, bias_two)
    normed_two_low = normed_two.astype(low)
    hidden = saved["hidden"]
    hidden_low = jax.nn.gelu(hidden).astype(low)
    attended = saved["o"].astype(low)
    grad_proj = outer_product(tokens_low, proj_grad)
    stream_grad = chosen(image_cots).reshape(rows, width).astype(jnp.float32)
    stream_grad = jnp.where(image_present > 0, stream_grad, 0.0) + back_product(proj_grad, w_proj)
    grad_conv, stream_grad = lax.optimization_barrier((grad_conv, stream_grad))
    grad_conv = (grad_conv[0], across(grad_conv[1], TURNS["conv"][0]))
    down_grad = stream_grad.astype(low)
    grad_down_b = jnp.sum(down_grad.astype(jnp.float32), 0)

    def halves_of(first_op, second_op):
        half = second_op.shape[1] // 2
        return [
            outer_product(
                first_op, lax.dynamic_slice_in_dim(second_op, side * half, half, 1)
            ).astype(low)[None]
            for side in (core, 1 - core)
        ]

    grad_down_w = early_sum(*halves_of(hidden_low, down_grad), TURNS["fc2"][0])
    up_grad = gelu_grad(hidden, back_product(down_grad, w_down)).astype(low)
    grad_up_b = jnp.sum(up_grad.astype(jnp.float32), 0)
    grad_up_w = early_sum(*halves_of(normed_two_low, up_grad), TURNS["fc1"][0])
    norm_grad, grad_gain_two, grad_bias_two = norm_back(
        back_product(up_grad, w_up), scaled_two, factor_two, gain_two
    )
    stream_grad = stream_grad + norm_grad
    branch_grad = stream_grad.astype(low)
    grad_out_w = outer_product(attended, branch_grad)
    attended_grad = back_product(branch_grad, w_out).astype(low)
    slot_patch, grad_up_b = lax.optimization_barrier((slot_patch, grad_up_b))
    patch = slot_patch[:, :cells]
    patch = patch.reshape(slots, tile_rows + 2, tile_cols + 2, feat).astype(jnp.float32)
    patch = jnp.where(present[:, None, None, None] > 0, patch, 0.0)
    upsampled = double_axis(double_axis(patch, 1), 2).astype(low)
    fine_rows = upsampled.reshape(-1, feat)
    head_out = jnp.dot(fine_rows, w_head, preferred_element_type=jnp.float32) + b_head
    head_out = head_out.reshape(slots, -1, feat)
    merged = (head_out * factor[:, None, None] + shift_sign[:, None, None] * w_shift) * present[
        :, None, None
    ]
    merged_out = merged.astype(low).reshape(cot_merged.shape)
    grad_head_w = outer_product(fine_rows, head_grad)

    blank = jnp.zeros((2, (width // 2 + feat - 1) // feat * feat), jnp.float32)
    packed = []
    for v in (grad_up_b, grad_down_b, None, None, grad_gain_two, grad_bias_two, grad_head_b, grad_shift):
        if v is None:
            packed.append(blank)
            continue
        v = v.reshape(2, -1)
        packed.append(jnp.pad(v, ((0, 0), (0, -v.shape[1] % feat))))
    starts, at = [], 0
    for v in packed:
        starts.append(at)
        at += v.shape[1]
    packed = jnp.pad(jnp.concatenate(packed, 1), ((0, 0), (0, 128 * feat - at)))
    slot_tokens, slot_grads, sums = run_backward(
        {
            **{name: saved[name] for name in ("q", "k", "v", "o", "logs", "x")},
            "g": attended_grad,
            "stream": stream_grad,
            "w_qkv": w_qkv,
            "gain": gain_one,
            "bias": bias_one,
            "small": packed.reshape(256, feat),
        },
        tokens_low.reshape(chips, tile, width),
        {"conv": grad_conv, "fc2": grad_down_w, "fc1": grad_up_w},
        {
            "out": grad_out_w.astype(low)[None],
            "proj": grad_proj.astype(low)[None],
            "head": grad_head_w.astype(low)[None],
        },
        sizes,
    )
    here = present[:, None, None] > 0
    tokens_out = jnp.where(here, slot_tokens, 0).reshape(tokens.shape)
    grad_tokens = jnp.where(here, slot_grads.astype(jnp.float32), 0.0).reshape(tokens.shape)
    sums = {name: value.astype(jnp.float32) for name, value in sums.items()}
    packed = sums["small"].reshape(-1)
    pieces = [
        packed[at : at + v.shape[0]] for at, v in zip(starts, vectors + (head_b, shift_row))
    ]
    return (
        tokens_out,
        merged_out,
        grad_tokens,
        sums["qkv"][0],
        sums["out"][0],
        sums["fc1"][0],
        pieces[0],
        sums["fc2"][0],
        pieces[1],
        pieces[2],
        pieces[3],
        pieces[4],
        pieces[5],
        sums["proj"][0],
        sums["conv"].reshape(conv_w.shape),
        sums["head"][0],
        pieces[6],
        pieces[7],
    )


def solution(mesh):
    groups, tile_rows, tile_cols = (mesh.shape[axis] for axis in ("dp", "row", "col"))
    chips = tile_rows // 2 * tile_cols
    fits = groups == 2 and tile_rows == 4 and tile_cols == 4
    placed = (
        P("dp", "row", "col", None),
        P("dp", "row", "col", None),
        P("dp", "row", "col", None),
        P("dp"),
        P("dp"),
        P("dp"),
        P("dp", None),
        P("dp", None),
        P("dp", None),
        P("dp"),
        P("dp", None),
        P("dp"),
        P("dp"),
        P("dp"),
        P("dp"),
        P("dp"),
        P("dp", None),
        P(None, None, None, "dp", None),
        P("dp", None),
        P("dp"),
        P("dp"),
    )
    return jax.shard_map(
        functools.partial(on_chip, chips) if fits else on_device,
        mesh=mesh,
        in_specs=placed,
        out_specs=(
            P("dp", "row", "col", None),
            P("dp", "row", "col", None),
            P("dp", "row", "col", None),
            P("dp", None),
            P("dp", None),
            P("dp", None),
            P("dp"),
            P("dp", None),
            P("dp"),
            P("dp"),
            P("dp"),
            P("dp"),
            P("dp"),
            P("dp", None),
            P(None, None, None, "dp", None),
            P("dp", None),
            P("dp"),
            P("dp"),
        ),
        check_vma=False,
    )
```

```python
import functools

import jax
import jax.numpy as jnp
from jax import lax
from jax.experimental import pallas as pl
from jax.experimental.pallas import tpu as pltpu
from jax.sharding import PartitionSpec as P

HEADS = 12
HEAD_DIM = 64


epsilon = 1e-06


def extended(value, sides, width):
    for axis, dim in sides:
        peers, length = (lax.axis_size(axis), value.shape[dim])
        up = [(i, (i + 1) % peers) for i in range(peers - 1)]
        down = [(j, i) for i, j in up]
        last = lax.slice_in_dim(value, length - width, length, axis=dim)
        leading = lax.slice_in_dim(value, 0, width, axis=dim)
        before = lax.ppermute(last, axis, up)
        after = lax.ppermute(leading, axis, down)
        value = jnp.concatenate([before, value, after], axis=dim)
    return value


def norm_rows(stream, gain_row, bias_row):
    centre = stream - jnp.mean(stream, -1, keepdims=True)
    spread = jnp.mean(centre * centre, -1, keepdims=True)
    factor = lax.rsqrt(spread + epsilon)
    scaled = centre * factor
    return (scaled * gain_row + bias_row, scaled, factor)


def norm_back(cotangent, scaled, factor, gain_row):
    gained = cotangent * gain_row
    inner = (
        gained
        - jnp.mean(gained, -1, keepdims=True)
        - scaled * jnp.mean(gained * scaled, -1, keepdims=True)
    )
    return (factor * inner, jnp.sum(cotangent * scaled, 0), jnp.sum(cotangent, 0))


def gelu_grad(inputs, cotangent):
    return jax.vjp(jax.nn.gelu, inputs)[1](cotangent)[0]


def outer_product(first_op, second_op):
    return lax.dot_general(
        first_op, second_op, (((0,), (0,)), ((), ())), preferred_element_type=jnp.float32
    )


def back_product(first_op, weight):
    return lax.dot_general(
        first_op, weight, (((1,), (1,)), ((), ())), preferred_element_type=jnp.float32
    )


def add_rims(tile_map):
    return extended(tile_map, (("row", 1), ("col", 2)), 1)


def clamp_edges(padded):
    first_row = lax.axis_index("row") == 0
    last_row = lax.axis_index("row") == lax.axis_size("row") - 1
    upper = jnp.where(first_row, padded[:, 1:2], padded[:, 0:1])
    lower = jnp.where(last_row, padded[:, -2:-1], padded[:, -1:])
    padded = jnp.concatenate([upper, padded[:, 1:-1], lower], 1)
    first_col = lax.axis_index("col") == 0
    last_col = lax.axis_index("col") == lax.axis_size("col") - 1
    left_side = jnp.where(first_col, padded[:, :, 1:2], padded[:, :, 0:1])
    right_side = jnp.where(last_col, padded[:, :, -2:-1], padded[:, :, -1:])
    return jnp.concatenate([left_side, padded[:, :, 1:-1], right_side], 2)


def patches(padded):
    tall = padded.shape[1] - 2
    broad = padded.shape[2] - 2
    pieces = [
        padded[:, row_shift : row_shift + tall, col_shift : col_shift + broad]
        for row_shift in range(3)
        for col_shift in range(3)
    ]
    return jnp.concatenate(pieces, -1).reshape(-1, 9 * padded.shape[3])


def conv_apply(padded, kernel):
    result = jnp.dot(
        patches(padded), kernel.reshape(-1, kernel.shape[3]), preferred_element_type=jnp.float32
    )
    return result.reshape(padded.shape[0], padded.shape[1] - 2, padded.shape[2] - 2, -1)


def flip_kernel(kernel):
    return jnp.transpose(kernel[::-1, ::-1], (0, 1, 3, 2))


def double_axis(padded, axis_index):
    leading = jnp.moveaxis(padded, axis_index, 0)
    middle_part = leading[1:-1]
    even_part = 0.75 * middle_part + 0.25 * leading[:-2]
    odd_part = 0.75 * middle_part + 0.25 * leading[2:]
    joined = jnp.stack([even_part, odd_part], 1).reshape(
        (2 * middle_part.shape[0],) + middle_part.shape[1:]
    )
    return jnp.moveaxis(joined, 0, axis_index)


def halve_axis(padded, axis_index):
    leading = jnp.moveaxis(padded, axis_index, 0)
    even_part = leading[1:-1:2]
    odd_part = leading[2:-1:2]
    before_part = leading[0:-2:2]
    after_part = leading[3::2]
    joined = 0.75 * (even_part + odd_part) + 0.25 * (before_part + after_part)
    return jnp.moveaxis(joined, 0, axis_index)


def on_device(
    tokens,
    cot_tokens,
    cot_merged,
    image_counts,
    scale_flags,
    shift_flags,
    qkv_w,
    attn_out_w,
    fc1_w,
    fc1_b,
    fc2_w,
    fc2_b,
    ln1_gain,
    ln1_bias,
    ln2_gain,
    ln2_bias,
    proj_w,
    conv_w,
    head_w,
    head_b,
    shift_row,
):
    lowered = [
        master.astype(jnp.bfloat16)
        for master in (
            qkv_w,
            attn_out_w,
            fc1_w,
            fc1_b,
            fc2_w,
            fc2_b,
            ln1_gain,
            ln1_bias,
            ln2_gain,
            ln2_bias,
            proj_w,
            conv_w,
            head_w,
            head_b,
            shift_row,
        )
    ]
    gathered = (
        lax.all_gather(lowered[0], "dp", axis=0, tiled=True),
        lax.all_gather(lowered[1], "dp", axis=0, tiled=True),
        lax.all_gather(lowered[2], "dp", axis=0, tiled=True),
        lax.all_gather(lowered[3], "dp", axis=0, tiled=True),
        lax.all_gather(lowered[4], "dp", axis=0, tiled=True),
        lax.all_gather(lowered[5], "dp", axis=0, tiled=True),
        lax.all_gather(lowered[6], "dp", axis=0, tiled=True),
        lax.all_gather(lowered[7], "dp", axis=0, tiled=True),
        lax.all_gather(lowered[8], "dp", axis=0, tiled=True),
        lax.all_gather(lowered[9], "dp", axis=0, tiled=True),
        lax.all_gather(lowered[10], "dp", axis=0, tiled=True),
        lax.all_gather(lowered[11], "dp", axis=3, tiled=True),
        lax.all_gather(lowered[12], "dp", axis=0, tiled=True),
        lax.all_gather(lowered[13], "dp", axis=0, tiled=True),
        lax.all_gather(lowered[14], "dp", axis=0, tiled=True),
    )
    (
        w_qkv,
        w_out,
        w_up,
        b_up,
        w_down,
        b_down,
        gain_one,
        bias_one,
        gain_two,
        bias_two,
        w_proj,
        w_conv,
        w_head,
        b_head,
        w_shift,
    ) = gathered
    images = tokens.shape[0]
    tile_rows = tokens.shape[1]
    tile_cols = tokens.shape[2]
    tile_size = tile_rows * tile_cols
    model_width = tokens.shape[3]
    temper = HEAD_DIM ** (-0.5)
    present = (jnp.arange(images) < image_counts[0]).astype(jnp.float32)
    factor = 0.5 + 0.5 * scale_flags.astype(jnp.float32)
    shift_sign = shift_flags.astype(jnp.float32)
    present_rows = jnp.repeat(present, tile_size)[:, None]
    stream = tokens.astype(jnp.float32).reshape(-1, model_width)
    normed, scaled_one, factor_one = norm_rows(
        stream, gain_one.astype(jnp.float32), bias_one.astype(jnp.float32)
    )
    normed_low = normed.astype(jnp.bfloat16)
    projected = jnp.dot(normed_low, w_qkv, preferred_element_type=jnp.float32).astype(jnp.bfloat16)
    queries = projected[:, :model_width].reshape(images, tile_size, HEADS, HEAD_DIM)
    keys_own = projected[:, model_width : 2 * model_width].reshape(images, tile_size, model_width)
    values_own = projected[:, 2 * model_width :].reshape(images, tile_size, model_width)
    keys_all, values_all = (
        lax.all_gather(keys_own, ("row", "col"), axis=1, tiled=True),
        lax.all_gather(values_own, ("row", "col"), axis=1, tiled=True),
    )
    keys_heads = keys_all.reshape(images, -1, HEADS, HEAD_DIM)
    values_heads = values_all.reshape(images, -1, HEADS, HEAD_DIM)
    scores = (
        jnp.einsum("nqhd,nkhd->nhqk", queries, keys_heads, preferred_element_type=jnp.float32)
        * temper
    )
    highest_score = jnp.max(scores, -1, keepdims=True)
    exponent = jnp.exp(scores - highest_score)
    denominator = jnp.sum(exponent, -1, keepdims=True)
    log_total = highest_score + jnp.log(denominator)
    attention_low = (exponent / denominator).astype(jnp.bfloat16)
    attended = jnp.einsum(
        "nhqk,nkhd->nqhd", attention_low, values_heads, preferred_element_type=jnp.float32
    )
    attended = attended.reshape(-1, model_width).astype(jnp.bfloat16)
    after_attn = stream + jnp.dot(attended, w_out, preferred_element_type=jnp.float32)
    normed_two, scaled_two, factor_two = norm_rows(
        after_attn, gain_two.astype(jnp.float32), bias_two.astype(jnp.float32)
    )
    normed_two_low = normed_two.astype(jnp.bfloat16)
    hidden = jnp.dot(normed_two_low, w_up, preferred_element_type=jnp.float32) + b_up.astype(
        jnp.float32
    )
    hidden_low = jax.nn.gelu(hidden).astype(jnp.bfloat16)
    after_mlp = after_attn + (
        jnp.dot(hidden_low, w_down, preferred_element_type=jnp.float32) + b_down.astype(jnp.float32)
    )
    tokens_low = after_mlp.astype(jnp.bfloat16)
    tokens_out = (
        (tokens_low.astype(jnp.float32) * present_rows).astype(jnp.bfloat16).reshape(tokens.shape)
    )
    feature = jnp.dot(tokens_low, w_proj, preferred_element_type=jnp.float32).reshape(
        images, tile_rows, tile_cols, -1
    )
    channels = feature.shape[3]
    stored = []
    for unit_index in range(2):
        first_in = add_rims(jax.nn.gelu(feature).astype(jnp.bfloat16))
        first_out = conv_apply(first_in, w_conv[2 * unit_index])
        second_in = add_rims(jax.nn.gelu(first_out).astype(jnp.bfloat16))
        second_out = conv_apply(second_in, w_conv[2 * unit_index + 1])
        stored.append((feature, first_in, first_out, second_in))
        feature = feature + second_out
    coarse_map = clamp_edges(add_rims(feature.astype(jnp.bfloat16))).astype(jnp.float32)
    upsampled = double_axis(double_axis(coarse_map, 1), 2).astype(jnp.bfloat16)
    fine_rows = upsampled.reshape(-1, channels)
    head_out = jnp.dot(fine_rows, w_head, preferred_element_type=jnp.float32) + b_head.astype(
        jnp.float32
    )
    head_out = head_out.reshape(images, -1, channels)
    merged = (
        head_out * factor[:, None, None] + shift_sign[:, None, None] * w_shift.astype(jnp.float32)
    ) * present[:, None, None]
    merged_out = merged.astype(jnp.bfloat16).reshape(cot_merged.shape)
    gathered = (
        lax.all_gather(lowered[0], "dp", axis=0, tiled=True),
        lax.all_gather(lowered[1], "dp", axis=0, tiled=True),
        lax.all_gather(lowered[2], "dp", axis=0, tiled=True),
        lax.all_gather(lowered[3], "dp", axis=0, tiled=True),
        lax.all_gather(lowered[4], "dp", axis=0, tiled=True),
        lax.all_gather(lowered[5], "dp", axis=0, tiled=True),
        lax.all_gather(lowered[6], "dp", axis=0, tiled=True),
        lax.all_gather(lowered[7], "dp", axis=0, tiled=True),
        lax.all_gather(lowered[8], "dp", axis=0, tiled=True),
        lax.all_gather(lowered[9], "dp", axis=0, tiled=True),
        lax.all_gather(lowered[10], "dp", axis=0, tiled=True),
        lax.all_gather(lowered[11], "dp", axis=3, tiled=True),
        lax.all_gather(lowered[12], "dp", axis=0, tiled=True),
        lax.all_gather(lowered[13], "dp", axis=0, tiled=True),
        lax.all_gather(lowered[14], "dp", axis=0, tiled=True),
    )
    (
        w_qkv,
        w_out,
        w_up,
        b_up,
        w_down,
        b_down,
        gain_one,
        bias_one,
        gain_two,
        bias_two,
        w_proj,
        w_conv,
        w_head,
        b_head,
        w_shift,
    ) = gathered
    merged_grad = (
        cot_merged.astype(jnp.float32).reshape(images, -1, channels) * present[:, None, None]
    )
    grad_shift = jnp.sum(merged_grad * shift_sign[:, None, None], (0, 1))
    head_grad = (merged_grad * factor[:, None, None]).astype(jnp.bfloat16).reshape(-1, channels)
    grad_head_b = jnp.sum(head_grad.astype(jnp.float32), 0)
    grad_head_w = outer_product(fine_rows, head_grad)
    fine_grad = back_product(head_grad, w_head).astype(jnp.bfloat16).reshape(upsampled.shape)
    spread_grad = clamp_edges(extended(fine_grad, (("row", 1), ("col", 2)), 1)).astype(jnp.float32)
    feature_grad = halve_axis(halve_axis(spread_grad, 1), 2)
    conv_grads = [None, None, None, None]
    for unit_index in (1, 0):
        unit_input, first_in, first_out, second_in = stored[unit_index]
        second_grad = feature_grad.astype(jnp.bfloat16)
        conv_grads[2 * unit_index + 1] = outer_product(
            patches(second_in), second_grad.reshape(-1, channels)
        )
        middle_grad = conv_apply(add_rims(second_grad), flip_kernel(w_conv[2 * unit_index + 1]))
        first_grad = gelu_grad(first_out, middle_grad).astype(jnp.bfloat16)
        conv_grads[2 * unit_index] = outer_product(
            patches(first_in), first_grad.reshape(-1, channels)
        )
        inner_grad = conv_apply(add_rims(first_grad), flip_kernel(w_conv[2 * unit_index]))
        feature_grad = feature_grad + gelu_grad(unit_input, inner_grad)
    grad_conv = jnp.stack(conv_grads).reshape(4, 3, 3, channels, channels)
    proj_grad = feature_grad.astype(jnp.bfloat16).reshape(-1, channels)
    grad_proj = outer_product(tokens_low, proj_grad)
    stream_grad = cot_tokens.astype(jnp.float32).reshape(
        -1, model_width
    ) * present_rows + back_product(proj_grad, w_proj)
    down_grad = stream_grad.astype(jnp.bfloat16)
    grad_down_b = jnp.sum(down_grad.astype(jnp.float32), 0)
    grad_down_w = outer_product(hidden_low, down_grad)
    up_grad = gelu_grad(hidden, back_product(down_grad, w_down)).astype(jnp.bfloat16)
    grad_up_b = jnp.sum(up_grad.astype(jnp.float32), 0)
    grad_up_w = outer_product(normed_two_low, up_grad)
    norm_grad, grad_gain_two, grad_bias_two = norm_back(
        back_product(up_grad, w_up), scaled_two, factor_two, gain_two.astype(jnp.float32)
    )
    stream_grad = stream_grad + norm_grad
    branch_grad = stream_grad.astype(jnp.bfloat16)
    grad_out_w = outer_product(attended, branch_grad)
    attended_grad = (
        back_product(branch_grad, w_out)
        .astype(jnp.bfloat16)
        .reshape(images, tile_size, HEADS, HEAD_DIM)
    )
    keys_heads = keys_all.reshape(images, -1, HEADS, HEAD_DIM)
    values_heads = values_all.reshape(images, -1, HEADS, HEAD_DIM)
    scores = (
        jnp.einsum("nqhd,nkhd->nhqk", queries, keys_heads, preferred_element_type=jnp.float32)
        * temper
    )
    attention_full = jnp.exp(scores - log_total)
    attention_low = attention_full.astype(jnp.bfloat16)
    prob_grad = jnp.einsum(
        "nqhd,nkhd->nhqk", attended_grad, values_heads, preferred_element_type=jnp.float32
    )
    centre = jnp.sum(attention_full * prob_grad, -1, keepdims=True)
    score_grad = (attention_full * (prob_grad - centre)).astype(jnp.bfloat16)
    query_grad = (
        jnp.einsum("nhqk,nkhd->nqhd", score_grad, keys_heads, preferred_element_type=jnp.float32)
        * temper
    )
    key_part = (
        jnp.einsum("nhqk,nqhd->knhd", score_grad, queries, preferred_element_type=jnp.float32)
        * temper
    )
    value_part = jnp.einsum(
        "nhqk,nqhd->knhd", attention_low, attended_grad, preferred_element_type=jnp.float32
    )
    pair_grad = lax.psum_scatter(
        jnp.concatenate(
            [
                key_part.reshape(lax.axis_size(("row", "col")) * tile_size, images, model_width),
                value_part.reshape(lax.axis_size(("row", "col")) * tile_size, images, model_width),
            ],
            2,
        ).astype(jnp.bfloat16),
        ("row", "col"),
        scatter_dimension=0,
        tiled=True,
    ).astype(jnp.float32)
    pair_grad = jnp.transpose(pair_grad, (1, 0, 2))
    mixed_grad = jnp.concatenate([query_grad.reshape(images, tile_size, model_width), pair_grad], 2)
    mixed_grad = mixed_grad.astype(jnp.bfloat16).reshape(-1, 3 * model_width)
    grad_qkv = outer_product(normed_low, mixed_grad)
    norm_grad, grad_gain_one, grad_bias_one = norm_back(
        back_product(mixed_grad, w_qkv), scaled_one, factor_one, gain_one.astype(jnp.float32)
    )
    input_grad = (stream_grad + norm_grad).reshape(tokens.shape)
    shards = (
        lax.psum_scatter(
            grad_qkv.astype(jnp.bfloat16), "dp", scatter_dimension=0, tiled=True
        ).astype(jnp.float32),
        lax.psum_scatter(
            grad_out_w.astype(jnp.bfloat16), "dp", scatter_dimension=0, tiled=True
        ).astype(jnp.float32),
        lax.psum_scatter(
            grad_up_w.astype(jnp.bfloat16), "dp", scatter_dimension=0, tiled=True
        ).astype(jnp.float32),
        lax.psum_scatter(
            grad_up_b.astype(jnp.bfloat16), "dp", scatter_dimension=0, tiled=True
        ).astype(jnp.float32),
        lax.psum_scatter(
            grad_down_w.astype(jnp.bfloat16), "dp", scatter_dimension=0, tiled=True
        ).astype(jnp.float32),
        lax.psum_scatter(
            grad_down_b.astype(jnp.bfloat16), "dp", scatter_dimension=0, tiled=True
        ).astype(jnp.float32),
        lax.psum_scatter(
            grad_gain_one.astype(jnp.bfloat16), "dp", scatter_dimension=0, tiled=True
        ).astype(jnp.float32),
        lax.psum_scatter(
            grad_bias_one.astype(jnp.bfloat16), "dp", scatter_dimension=0, tiled=True
        ).astype(jnp.float32),
        lax.psum_scatter(
            grad_gain_two.astype(jnp.bfloat16), "dp", scatter_dimension=0, tiled=True
        ).astype(jnp.float32),
        lax.psum_scatter(
            grad_bias_two.astype(jnp.bfloat16), "dp", scatter_dimension=0, tiled=True
        ).astype(jnp.float32),
        lax.psum_scatter(
            grad_proj.astype(jnp.bfloat16), "dp", scatter_dimension=0, tiled=True
        ).astype(jnp.float32),
        lax.psum_scatter(
            grad_conv.astype(jnp.bfloat16), "dp", scatter_dimension=3, tiled=True
        ).astype(jnp.float32),
        lax.psum_scatter(
            grad_head_w.astype(jnp.bfloat16), "dp", scatter_dimension=0, tiled=True
        ).astype(jnp.float32),
        lax.psum_scatter(
            grad_head_b.astype(jnp.bfloat16), "dp", scatter_dimension=0, tiled=True
        ).astype(jnp.float32),
        lax.psum_scatter(
            grad_shift.astype(jnp.bfloat16), "dp", scatter_dimension=0, tiled=True
        ).astype(jnp.float32),
    )
    totals = (
        lax.psum(shards[0].astype(jnp.bfloat16), ("row", "col")).astype(jnp.float32),
        lax.psum(shards[1].astype(jnp.bfloat16), ("row", "col")).astype(jnp.float32),
        lax.psum(shards[2].astype(jnp.bfloat16), ("row", "col")).astype(jnp.float32),
        lax.psum(shards[3].astype(jnp.bfloat16), ("row", "col")).astype(jnp.float32),
        lax.psum(shards[4].astype(jnp.bfloat16), ("row", "col")).astype(jnp.float32),
        lax.psum(shards[5].astype(jnp.bfloat16), ("row", "col")).astype(jnp.float32),
        lax.psum(shards[6].astype(jnp.bfloat16), ("row", "col")).astype(jnp.float32),
        lax.psum(shards[7].astype(jnp.bfloat16), ("row", "col")).astype(jnp.float32),
        lax.psum(shards[8].astype(jnp.bfloat16), ("row", "col")).astype(jnp.float32),
        lax.psum(shards[9].astype(jnp.bfloat16), ("row", "col")).astype(jnp.float32),
        lax.psum(shards[10].astype(jnp.bfloat16), ("row", "col")).astype(jnp.float32),
        lax.psum(shards[11].astype(jnp.bfloat16), ("row", "col")).astype(jnp.float32),
        lax.psum(shards[12].astype(jnp.bfloat16), ("row", "col")).astype(jnp.float32),
        lax.psum(shards[13].astype(jnp.bfloat16), ("row", "col")).astype(jnp.float32),
        lax.psum(shards[14].astype(jnp.bfloat16), ("row", "col")).astype(jnp.float32),
    )
    return (
        tokens_out,
        merged_out,
        input_grad,
        totals[0],
        totals[1],
        totals[2],
        totals[3],
        totals[4],
        totals[5],
        totals[6],
        totals[7],
        totals[8],
        totals[9],
        totals[10],
        totals[11],
        totals[12],
        totals[13],
        totals[14],
    )


LOG2E = 1.4426950408889634
MESH = pl.DeviceIdType.MESH
HALO = 6
PATCH = 112
VMEM_LIMIT = 58 << 20


def place():
    dp, row, col = (lax.axis_index(axis) for axis in ("dp", "row", "col"))
    return dp, lax.div(row, 2), lax.rem(row, 2), col


def slot_of(y, z, cols):
    return 2 * lax.rem(z + cols + cols // 2 - y, cols) + y


def chip_of(slot, cols):
    y = slot % 2
    return y, (slot // 2 + cols // 2 + y) % cols


def send(src, dst, send_sem, recv_sem, dp, y, core, z):
    return pltpu.make_async_remote_copy(
        src_ref=src,
        dst_ref=dst,
        send_sem=send_sem,
        recv_sem=recv_sem,
        device_id={"dp": dp, "row": y * 2 + core, "col": z},
        device_id_type=MESH,
    )


def landed(ref, sem):
    return pltpu.make_async_copy(ref, ref, sem)


def to_images_start(src, dst, send_sem, recv_sem, sizes):
    chips, slots, cols = sizes
    dp, y, core, z = place()
    own = core * cols + z
    for step in range(chips):
        far_y = lax.rem(y + step // cols, 2)
        far_z = lax.rem(z + step % cols, cols)
        slot = slot_of(far_y, far_z, cols)
        copy = send(
            src.at[slot], dst.at[0, own], send_sem.at[step], recv_sem.at[own], dp, far_y, y, far_z
        )
        if step == 0:
            local = pltpu.make_async_copy(src.at[slot], dst.at[0, own], recv_sem.at[own])
            pl.when(core == y)(local.start)
            pl.when(core != y)(copy.start)
        else:
            copy.start()
    for extra in range(slots - chips):
        to_y, to_z = chip_of(2 * chips - slots + extra, cols)
        send(
            src.at[chips + extra],
            dst.at[1, own],
            send_sem.at[chips + extra],
            recv_sem.at[chips + own],
            1 - dp,
            to_y,
            y,
            to_z,
        ).start()


def to_images_wait(src, dst, send_sem, recv_sem, sizes):
    chips, slots, cols = sizes
    dp, y, core, z = place()
    for step in range(slots):
        left = landed(src.at[0], send_sem.at[step])
        if step == 0:
            pl.when(core != y)(left.wait)
        else:
            left.wait()
    for tile in range(chips):
        landed(dst.at[0, tile], recv_sem.at[tile]).wait()

    @pl.when(slot_of(y, z, cols) >= 2 * chips - slots)
    def _():
        for tile in range(chips):
            landed(dst.at[1, tile], recv_sem.at[chips + tile]).wait()


def to_tiles_start(src, dst, send_sem, recv_sem, sizes):
    chips, slots, cols = sizes
    dp, y, core, z = place()
    slot = slot_of(y, z, cols)
    for step in range(chips):
        far_core = lax.rem(core + step // cols, 2)
        far_z = lax.rem(z + step % cols, cols)
        tile = far_core * cols + far_z
        copy = send(
            src.at[tile], dst.at[slot], send_sem.at[step], recv_sem.at[slot], dp, core, far_core, far_z
        )
        if step == 0:
            local = pltpu.make_async_copy(src.at[tile], dst.at[slot], recv_sem.at[slot])
            pl.when(core == y)(local.start)
            pl.when(core != y)(copy.start)
        else:
            copy.start()

    @pl.when(slot >= 2 * chips - slots)
    def _():
        for step in range(chips):
            far_core = step // cols
            far_z = step % cols
            other = slot + slots - chips
            send(
                src.at[step],
                dst.at[other],
                send_sem.at[chips + step],
                recv_sem.at[other],
                1 - dp,
                core,
                far_core,
                far_z,
            ).start()


def to_tiles_wait(src, dst, send_sem, recv_sem, sizes):
    chips, slots, cols = sizes
    dp, y, core, z = place()
    for step in range(chips):
        left = landed(src.at[0], send_sem.at[step])
        if step == 0:
            pl.when(core != y)(left.wait)
        else:
            left.wait()

    @pl.when(slot_of(y, z, cols) >= 2 * chips - slots)
    def _():
        for step in range(chips):
            landed(src.at[0], send_sem.at[chips + step]).wait()

    for slot in range(slots):
        landed(dst.at[slot], recv_sem.at[slot]).wait()


BITS = ("dp", "y", "z1", "z2")


def mate(bit):
    dp, y, core, z = place()
    low, high = lax.rem(z, 2), lax.div(z, 2)
    if bit == "core":
        return dp, y, 1 - core, z
    if bit == "dp":
        return 1 - dp, y, core, z
    if bit == "y":
        return dp, 1 - y, core, z
    if bit == "z1":
        return dp, y, core, high * 2 + 1 - low
    return dp, y, core, (1 - high) * 2 + low


def bit_of(bit):
    dp, y, core, z = place()
    return {
        "dp": dp,
        "y": y,
        "core": core,
        "z1": lax.rem(z, 2),
        "z2": lax.div(z, 2),
    }[bit]


class Gather:
    def __init__(self, whole, send_sem, recv_sem, split):
        self.whole, self.send_sem, self.recv_sem = whole, send_sem, recv_sem
        if split:
            self.orders = (("core", "y", "z1"), ("core", "z1", "y"))
        else:
            self.orders = (("core", "y"), ("core", "z1"))
        self.next, self.copies = 0, []

    def at(self, step, side):
        order = self.orders[side]
        count = 2 ** len(order)
        rows = self.whole.shape[-2] // (2 * count)
        piece = 0
        for i, bit in enumerate(order):
            if i <= len(order) - max(step, 1):
                piece = piece + bit_of(bit) * 2 ** (len(order) - 1 - i)
        half = bit_of("dp") if step == 0 else 1 - bit_of("dp")
        size = 1 if step == 0 else 2 ** (step - 1)
        part = pl.ds(pl.multiple_of((half * count + piece) * rows, 16), size * rows)
        width = self.whole.shape[-1] // len(self.orders)
        return self.whole.at[
            (slice(None),) * (len(self.whole.shape) - 2) + (part, pl.ds(side * width, width))
        ]

    def tick(self):
        while self.copies:
            self.copies.pop().wait()
        if self.next <= len(self.orders[0]):
            for side, order in enumerate(self.orders):
                bit = (("dp",) + order[::-1])[self.next]
                part = self.at(self.next, side)
                sems = (self.send_sem.at[side, self.next], self.recv_sem.at[side, self.next])
                copy = send(part, part, *sems, *mate(bit))
                copy.start()
                self.copies.append(copy)
            self.next += 1

    def finish(self):
        while self.copies:
            self.tick()


TURNS = {
    "conv": ("z1", ("dp", "z2", "y"), ("z2", "z1", "y", "core")),
    "small": (None, ("dp", "y", "z1", "z2"), ("y", "z1", "z2", "core")),
    "fc1": ("z1", ("y", "dp", "z2"), ("z2", "y", "z1", "core")),
    "proj": (None, ("dp", "z2", "z1", "y"), ("z1", "y", "z2", "core")),
    "head": (None, ("dp", "y", "z2", "z1"), ("y", "z2", "z1", "core")),
    "fc2": ("y", ("dp", "z1", "z2"), ("z2", "z1", "y", "core")),
    "qkv": (None, ("dp", "y", "z1", "z2"), ("z2", "y", "z1", "core")),
    "out": (None, ("dp", "y", "z1", "z2"), ("y", "z2", "z1", "core")),
}
EARLY = ("conv", "fc2", "fc1")
ARRIVED = ("conv",)
WHOLE = ("out", "proj", "head")


class Reduce:
    def __init__(self, turn, near, away, acc, recvs, out, sems, arrived=False):
        self.arrived = arrived
        self.gone, self.sum_order, self.back_order = turn
        self.near, self.away, self.acc, self.recvs, self.out, self.sems = (
            near,
            away,
            acc,
            recvs,
            out,
            sems,
        )
        self.dims = [bit for bit in BITS if bit != self.gone]
        self.kept = {bit: None for bit in BITS}
        if self.gone is not None:
            self.kept[self.gone] = bit_of(self.gone)
        half = out.shape[-1] // 2
        self.mine = pl.ds(pl.multiple_of(bit_of("core") * half, 128), half)
        self.step, self.copies = 0, []
        self.forward = 1 + len(self.sum_order)
        self.last = self.forward + len(self.back_order)

    def index(self):
        free = slice(None)
        return (free,) + tuple(free if self.kept[b] is None else self.kept[b] for b in self.dims)

    def add(self, recv):
        acc, kept, whole = self.acc, self.kept, slice(None)
        free = [b for b in self.dims if kept[b] is None]

        def body(i, _):
            bits, left = {}, i
            for b in reversed(free):
                bits[b] = lax.rem(left, 2)
                left = lax.div(left, 2)
            here = (whole,) + tuple(bits[b] if b in bits else kept[b] for b in self.dims)
            there = (whole,) + tuple(bits[b] for b in free)
            total = acc[here].astype(jnp.float32) + recv[there].astype(jnp.float32)
            acc[here] = total.astype(acc.dtype)
            return 0

        lax.fori_loop(0, 2 ** len(free), body, 0)

    def begin(self, copy):
        copy.start()
        self.copies.append(copy)

    def travel(self, src, dst, step, bit):
        _, send_sem, recv_sem = self.sems
        self.begin(send(src, dst, send_sem.at[step], recv_sem.at[step], *mate(bit)))

    def tick(self):
        step, whole, kept = self.step, slice(None), self.kept
        local_sem = self.sems[0]
        while self.copies:
            self.copies.pop().wait()
        if 0 < step <= self.forward:
            self.add(self.recvs[step - 1])
        if step == self.forward:
            kept["core"] = bit_of("core")
            at = (whole,) + tuple(kept[b] for b in BITS[1:]) + (whole, self.mine)
            self.begin(
                pltpu.make_async_copy(self.acc.at[self.index()], self.out.at[at], local_sem.at[1])
            )
        elif step == 0:
            if self.near is not None:
                self.begin(pltpu.make_async_copy(self.near, self.acc, local_sem.at[0]))
            if self.arrived:
                self.begin(pltpu.make_async_copy(self.away, self.recvs[0], local_sem.at[1]))
            else:
                self.travel(self.away, self.recvs[0], 0, self.gone or "core")
        elif step < self.forward:
            bit = self.sum_order[step - 1]
            kept[bit] = 1 - bit_of(bit)
            src = self.acc.at[self.index()]
            kept[bit] = bit_of(bit)
            self.travel(src, self.recvs[step], step, bit)
        elif step <= self.last:
            if step > self.forward + 1:
                kept[self.back_order[step - self.forward - 2]] = None
            bit = self.back_order[step - self.forward - 1]
            at = (whole,) + tuple(whole if kept[b] is None else kept[b] for b in BITS[1:])
            at = self.out.at[at + (whole, whole if kept["core"] is None else self.mine)]
            self.travel(at, at, step - 1, bit)
        self.step += 1

    def busy(self):
        return self.step <= self.last + 1


def across(value, bit):
    if bit == "dp":
        return lax.ppermute(value, "dp", [(0, 1), (1, 0)])
    if bit == "y":
        return lax.ppermute(value, "row", [(0, 2), (1, 3), (2, 0), (3, 1)])
    return lax.ppermute(value, "col", [(i, i + 1 - 2 * (i % 2)) for i in range(4)])


def recv_shapes(shape):
    free = len(shape) - 3
    return [shape[:1] + (2,) * left + shape[-2:] for left in range(free, -1, -1)]


def early_sum(near, other, bit):
    lead, rows, width = near.shape
    total = near.astype(jnp.float32) + swap_cores(other).astype(jnp.float32)
    total = total.astype(jnp.bfloat16).reshape(lead, 2, 2, 2, 2, rows // 16, width)
    axis, own = 1 + BITS.index(bit), bit_of(bit)
    keep = lax.dynamic_index_in_dim(total, own, axis, keepdims=False)
    away = lax.dynamic_index_in_dim(total, 1 - own, axis, keepdims=False)
    return keep, away


SCALE = HEAD_DIM**-0.5


def attend_pair(q, k, v):
    lane = lax.broadcasted_iota(jnp.int32, (1, 128), 1)
    sub = lax.broadcasted_iota(jnp.int32, (128, 1), 0)
    out = jnp.zeros((128, q.shape[0]), jnp.float32)
    logs = []
    for h in range(2):
        mine = (lane >= 64) == (h == 1)
        scores = lax.dot_general(
            k, jnp.where(mine, q, 0), (((1,), (1,)), ((), ())), preferred_element_type=jnp.float32
        )
        top = jnp.max(scores, 0, keepdims=True) * (SCALE * LOG2E)
        e = jnp.exp2(scores * (SCALE * LOG2E) - top)
        total = jnp.sum(e, 0, keepdims=True)
        part = lax.dot_general(
            v, e.astype(jnp.bfloat16), (((0,), (0,)), ((), ())), preferred_element_type=jnp.float32
        )
        out = jnp.where((sub >= 64) == (h == 1), part / total, out)
        logs.append(top + jnp.log2(total))
    return out.T, logs


def attend_pair_back(q, k, v, o, logs, g):
    lane = lax.broadcasted_iota(jnp.int32, (1, 128), 1)
    sub = lax.broadcasted_iota(jnp.int32, (128, 1), 0)
    product = (g.astype(jnp.float32) * o).T
    dq = jnp.zeros((128, q.shape[0]), jnp.float32)
    dk = dv = 0.0
    for h in range(2):
        mine = (lane >= 64) == (h == 1)
        q_own, g_own = jnp.where(mine, q, 0), jnp.where(mine, g, 0)
        centre = jnp.sum(product[h * 64 : (h + 1) * 64], 0, keepdims=True)
        scores = lax.dot_general(
            k, q_own, (((1,), (1,)), ((), ())), preferred_element_type=jnp.float32
        )
        p = jnp.exp2(scores * (SCALE * LOG2E) - logs[h])
        dp = lax.dot_general(
            v, g_own, (((1,), (1,)), ((), ())), preferred_element_type=jnp.float32
        )
        ds = (p * (dp - centre)).astype(jnp.bfloat16)
        dq_own = lax.dot_general(
            k, ds, (((0,), (0,)), ((), ())), preferred_element_type=jnp.float32
        )
        dq = jnp.where((sub >= 64) == (h == 1), dq_own * SCALE, dq)
        dk = dk + jnp.dot(ds, q_own, preferred_element_type=jnp.float32) * SCALE
        dv = dv + jnp.dot(p.astype(jnp.bfloat16), g_own, preferred_element_type=jnp.float32)
    return dq.T, dk, dv


BACK_INPUTS = ("q", "k", "v", "o", "logs", "g", "x", "stream", "w_qkv", "gain", "bias", "small")
LN_ROWS = 8
PLAN = (
    ("fc1", "head", "proj"),
    ("fc2", "out", "conv"),
    ("proj", "out", "conv"),
    (),
    ("head", "conv", "out"),
    (),
    ("out", "proj"),
    (),
    ("fc2", "out", "conv"),
)


def backward_kernel(sizes, *refs):
    refs = list(refs)

    def take(names):
        return {name: refs.pop(0) for name in names}

    ref = take(BACK_INPUTS)
    tiles = refs.pop(0)
    near, away, grads = take(EARLY), take(EARLY), take(WHOLE)
    slot_tokens, slot_grads = refs.pop(0), refs.pop(0)
    outs = take(TURNS)
    accs = take(TURNS)
    recvs = {name: [refs.pop(0) for _ in range(4 if TURNS[name][0] else 5)] for name in TURNS}
    mixed, far_out, far_in, own_pair, grad_tile, small_wide = (refs.pop(0) for _ in range(6))
    outbox = take(("qkv", "small"))
    tile_send, tile_recv, core_sem, local_sem, send_sem, recv_sem = refs
    low, f32 = jnp.bfloat16, jnp.float32
    core = bit_of("core")

    jobs = {}
    for i, name in enumerate(TURNS):
        sems = (local_sem.at[i], send_sem.at[i], recv_sem.at[i])
        if name in EARLY:
            source = (near[name], away[name])
        elif name in WHOLE:
            half = grads[name].shape[-1] // 2
            source = tuple(
                grads[name].at[..., pl.ds(pl.multiple_of(side * half, 128), half)]
                for side in (core, 1 - core)
            )
        else:
            source = (None, outbox[name])
        jobs[name] = Reduce(
            TURNS[name], *source, accs[name], recvs[name], outs[name], sems, name in ARRIVED
        )

    def tick(*names):
        for name in names:
            jobs[name].tick()

    tick(*PLAN[0])
    to_tiles_start(tiles, slot_tokens, tile_send.at[0], tile_recv.at[0], sizes)
    rows, width = ref["q"].shape
    for pair in range(width // 128):
        lanes = pl.ds(pair * 128, 128)
        dq, dk, dv = attend_pair_back(
            ref["q"][:, lanes],
            ref["k"][:, lanes],
            ref["v"][:, lanes],
            ref["o"][:, lanes],
            [ref["logs"][pair, h : h + 1, :] for h in range(2)],
            ref["g"][:, lanes],
        )
        mixed[:, lanes] = dq.astype(low)
        for i, value in enumerate((dk, dv)):
            to = pl.ds(i * width + pair * 128, 128)
            own_pair[:, to] = value[:rows]
            far_out[:, to] = value[rows:].astype(low)
        tick(*PLAN[1 + pair])
    pair_copy = send(far_out, far_in, core_sem.at[0], core_sem.at[1], *mate("core"))
    pair_copy.start()
    stream = ref["x"][...].astype(f32)
    normed, scaled, factor = norm_rows(stream, ref["gain"][...], ref["bias"][...])
    normed = normed.astype(low)
    pair_copy.wait()
    mixed[:, width:] = (own_pair[...] + far_in[...].astype(f32)).astype(low)

    half = mixed.shape[1] // 2
    for side, target in ((1 - core, outbox["qkv"]), (core, accs["qkv"])):
        for c in range(0, half, 384):
            part = mixed[:, pl.ds(pl.multiple_of(side * half + c, 128), 384)]
            value = outer_product(normed, part).astype(low)
            target[..., c : c + 384] = value.reshape(target.shape[:-1] + (384,))
        if target is outbox["qkv"]:
            tick(*PLAN[7])
    tick("qkv")
    tick(*PLAN[8])
    grad = back_product(mixed[...], ref["w_qkv"][...])
    gained, grad_gain, grad_bias = norm_back(grad, scaled, factor, ref["gain"][...])
    grad_tile[...] = (ref["stream"][...] + gained).astype(low).reshape(grad_tile.shape)

    small_wide[...] = ref["small"][...]
    for v, value in enumerate((grad_gain, grad_bias)):
        value = value.reshape(1, width)
        for j in range(width // 128):
            side, at = divmod(j, width // 256)
            row = side * (small_wide.shape[0] // 2) + LN_ROWS + 2 * v + at // 2
            small_wide[row : row + 1, at % 2 * 128 : at % 2 * 128 + 128] = value[
                :, j * 128 : (j + 1) * 128
            ]
    for side, target in ((core, accs["small"]), (1 - core, outbox["small"])):
        part = small_wide[:, pl.ds(pl.multiple_of(side * 128, 128), 128)].astype(low)
        target[...] = part.reshape(target.shape)
    tick("small")
    to_tiles_start(grad_tile, slot_grads, tile_send.at[1], tile_recv.at[1], sizes)
    while any(job.busy() for job in jobs.values()):
        for job in jobs.values():
            if job.busy():
                job.tick()
    to_tiles_wait(tiles, slot_tokens, tile_send.at[0], tile_recv.at[0], sizes)
    to_tiles_wait(grad_tile, slot_grads, tile_send.at[1], tile_recv.at[1], sizes)


def run_backward(inputs, tiles, early, grads, sizes):
    chips, slots, _ = sizes
    low, f32 = jnp.bfloat16, jnp.float32
    rows, width = inputs["q"].shape
    cut, accs = {}, {}
    for name in TURNS:
        if name in EARLY:
            accs[name] = early[name][0].shape
            continue
        if name in WHOLE:
            lead, height, across = grads[name].shape
            cut[name] = grads[name].reshape(lead, 2, 2, 2, 2, height // 16, across)
        else:
            lead = 1
            height, across = (width, 3 * width) if name == "qkv" else inputs["small"].shape
        accs[name] = (lead, 2, 2, 2, 2, height // 16, across // 2)
    shape = jax.ShapeDtypeStruct
    out_shape = [shape((slots,) + tiles.shape[1:], low)] * 2 + [
        shape(acc[:1] + (2, 2, 2, acc[-2], 2 * acc[-1]), low) for acc in accs.values()
    ]
    recvs = [value for acc in accs.values() for value in recv_shapes(acc)]
    hbm, vmem = pl.BlockSpec(memory_space=pltpu.HBM), pl.BlockSpec(memory_space=pltpu.VMEM)
    n = len(TURNS)
    slot_tokens, slot_grads, *sums = pl.pallas_call(
        functools.partial(backward_kernel, sizes),
        out_shape=out_shape,
        in_specs=[vmem] * len(BACK_INPUTS) + [hbm] * (1 + 2 * len(EARLY) + len(WHOLE)),
        out_specs=[hbm] * (2 + n),
        scratch_shapes=[pltpu.VMEM(value, low) for value in list(accs.values()) + recvs]
        + [
            pltpu.VMEM((rows, 3 * width), low),
            pltpu.VMEM((rows, 2 * width), low),
            pltpu.VMEM((rows, 2 * width), low),
            pltpu.VMEM((rows, 2 * width), f32),
            pltpu.VMEM(tiles.shape, low),
            pltpu.VMEM(inputs["small"].shape, f32),
            pltpu.VMEM(accs["qkv"], low),
            pltpu.VMEM(accs["small"], low),
            pltpu.SemaphoreType.DMA((2, 2 * chips)),
            pltpu.SemaphoreType.DMA((2, slots)),
            pltpu.SemaphoreType.DMA((2,)),
            pltpu.SemaphoreType.DMA((n, 2)),
            pltpu.SemaphoreType.DMA((n, 9)),
            pltpu.SemaphoreType.DMA((n, 9)),
        ],
        compiler_params=pltpu.CompilerParams(
            has_side_effects=True, vmem_limit_bytes=VMEM_LIMIT
        ),
    )(
        *(inputs[name] for name in BACK_INPUTS),
        tiles,
        *(early[name][0] for name in EARLY),
        *(early[name][1] for name in EARLY),
        *(cut[name] for name in WHOLE),
    )
    return (
        slot_tokens,
        slot_grads,
        {
            name: out.reshape(out.shape[0], 8 * out.shape[4], out.shape[5])
            for name, out in zip(TURNS, sums)
        },
    )


GELU_K, GELU_C = 0.7978845608028654, 0.044715


def gelu_slope(v):
    t = jnp.tanh(GELU_K * (v + GELU_C * v * v * v))
    return 0.5 * (1.0 + t) + 0.5 * v * (1.0 - t * t) * (GELU_K * (1.0 + 3.0 * GELU_C * v * v))


def block(row, size):
    return pl.ds(pl.multiple_of(row * size, size), size)


def turned(core, row, last):
    return core * (last - 2 * row) + row


def triple(dst, value, cols):
    rows, feat = value.shape
    col = lax.rem(lax.broadcasted_iota(jnp.int32, (rows, 1), 0), cols)
    left = jnp.where(col == 0, 0.0, pltpu.roll(value, 1, 0))
    right = jnp.where(col == cols - 1, 0.0, pltpu.roll(value, rows - 1, 0))
    body = pl.ds(cols, rows)
    dst[body, 0:feat] = left.astype(dst.dtype)
    dst[body, feat : 2 * feat] = value.astype(dst.dtype)
    dst[body, 2 * feat :] = right.astype(dst.dtype)


def clear_ends(dst, cols):
    zero = jnp.zeros((cols, dst.shape[1]), dst.dtype)
    dst[0:cols, :] = zero
    dst[dst.shape[0] - cols :, :] = zero


def taps(w_ref, line):
    value = w_ref[pl.ds(line * 3, 3)]
    return value.reshape(3 * value.shape[1], value.shape[2])


def conv_rows(src, w_ref, first, core, cols):
    rows = src.shape[0] - 2 * cols
    total = 0.0
    for a in range(3):
        total = total + jnp.dot(
            src[a * cols : a * cols + rows, :],
            taps(w_ref, first + turned(core, a, 2)),
            preferred_element_type=jnp.float32,
        )
    return total


def maps_forward(cols, own, f0_ref, first0_ref, f1_ref, first1_ref, w_ref, out_ref, wide):
    core = place()[2]
    clear_ends(wide, cols)
    for unit, (f, first, after) in enumerate(
        ((f0_ref, first0_ref, f1_ref), (f1_ref, first1_ref, None))
    ):
        triple(wide, jax.nn.gelu(f[...]), cols)
        first[...] = conv_rows(wide, w_ref, 6 * unit, core, cols)
        triple(wide, jax.nn.gelu(first[...]), cols)
        result = f[...] + conv_rows(wide, w_ref, 6 * unit + 3, core, cols)
        if after is not None:
            after[...] = result
    result = result.astype(out_ref.dtype)
    rows = own // cols + 2
    for j in range(rows):
        i = max(j - 1, 0)
        out_ref[block(turned(core, j, rows - 1), cols), :] = result[i * cols : (i + 1) * cols]


def kernel_grads(wide, grad, out_ref, first, core, cols):
    own = grad.shape[0]
    for a in range(3):
        value = outer_product(wide[a * cols : a * cols + own, :], grad)
        half = value.shape[1] // 2
        left, right = value[:, :half], value[:, half:]
        at = first + turned(core, a, 2)
        near, other = out_ref
        near[at] = jnp.where(core == 0, left, right).astype(near.dtype)
        other[at] = jnp.where(core == 0, right, left).astype(other.dtype)


def conv_back_rows(src, w_ref, first, core, cols):
    rows, feat = src.shape[0] - 2 * cols, w_ref.shape[2]
    total = 0.0
    for a in range(3):
        tap = taps(w_ref, first + turned(core, 2 - a, 2))
        for b in range(3):
            total = total + back_product(
                src[a * cols : a * cols + rows, b * feat : (b + 1) * feat],
                tap[(2 - b) * feat : (3 - b) * feat],
            )
    return total


def maps_back_kernel(
    tiles,
    cols,
    tall_ref,
    far_ref,
    f0_ref,
    first0_ref,
    f1_ref,
    first1_ref,
    w_ref,
    patch_ref,
    near_ref,
    other_ref,
    out_ref,
    slot_ref,
    wide,
    wide_g,
    total,
    parted,
    tile_send,
    tile_recv,
):
    chips = patch_ref.shape[0]
    sizes = (chips, slot_ref.shape[0], cols)
    to_tiles_start(patch_ref, slot_ref, tile_send, tile_recv, sizes)
    g_ref = (near_ref, other_ref)
    tile_rows, tile_cols = tiles
    core = place()[2]
    own_rows = 2 * tile_rows
    own = own_rows * cols * tile_cols
    line = cols * tile_cols
    edge = own_rows + 1

    def near(i):
        return tall_ref[block(turned(core, i, edge), line), :]

    def far(i):
        return far_ref[block(turned(1 - core, i, edge), line), :]

    for i in range(own_rows + 4):
        at = i * line
        if i < own_rows:
            value = near(i + 1)
            if i == 0:
                value = value + near(0)
            if i == own_rows - 1:
                value = value + far(edge)
        else:
            value = far(2 * own_rows - i)
            if i == own_rows:
                value = value + near(edge)
        total[at : at + line, :] = value
    rest = (own_rows + 4) * line
    total[rest:, :] = jnp.zeros((total.shape[0] - rest, total.shape[1]), jnp.float32)
    clear_ends(wide, line)
    clear_ends(wide_g, line)
    for unit, (f, first) in ((1, (f1_ref, first1_ref)), (0, (f0_ref, first0_ref))):
        triple(wide, jax.nn.gelu(first[...]), line)
        triple(wide_g, total[...], line)
        kernel_grads(
            wide, total[0:own, :].astype(wide.dtype), g_ref, 6 * unit + 3, core, line
        )
        middle = conv_back_rows(wide_g, w_ref, 6 * unit + 3, core, line)
        middle = gelu_slope(first[...]) * middle
        triple(wide, jax.nn.gelu(f[...]), line)
        triple(wide_g, middle, line)
        kernel_grads(wide, middle[0:own].astype(wide.dtype), g_ref, 6 * unit, core, line)
        inner = conv_back_rows(wide_g, w_ref, 6 * unit, core, line)
        total[...] += gelu_slope(f[...]) * inner
    for r in range(own_rows):
        row = turned(core, r, own_rows - 1)
        for z in range(cols):
            at = ((r // tile_rows) * cols + z) * tile_rows + r % tile_rows
            parted[at * tile_cols : (at + 1) * tile_cols, :] = total[
                block(row * cols + z, tile_cols), :
            ]
    out_ref[...] = parted[...].astype(out_ref.dtype)
    to_tiles_wait(patch_ref, slot_ref, tile_send, tile_recv, sizes)


def in_vmem(count):
    return [pl.BlockSpec(memory_space=pltpu.VMEM)] * count


def maps_backward(tall, far, saved, w_conv, patch, slots, tiles, cols):
    rows, feat = saved[0].shape
    line = cols * tiles[1]
    own = 2 * tiles[0] * line
    low, f32 = jnp.bfloat16, jnp.float32
    hbm = pl.BlockSpec(memory_space=pltpu.HBM)
    half = jax.ShapeDtypeStruct((12, 3 * feat, feat // 2), low)
    return pl.pallas_call(
        functools.partial(maps_back_kernel, tiles, cols),
        out_shape=[
            half,
            half,
            jax.ShapeDtypeStruct((own, feat), low),
            jax.ShapeDtypeStruct((slots,) + patch.shape[1:], low),
        ],
        in_specs=in_vmem(3 + len(saved)) + [hbm],
        out_specs=in_vmem(3) + [hbm],
        scratch_shapes=[pltpu.VMEM((rows + 2 * line, 3 * feat), low)] * 2
        + [
            pltpu.VMEM((rows, feat), f32),
            pltpu.VMEM((own, feat), f32),
            pltpu.SemaphoreType.DMA((2 * patch.shape[0],)),
            pltpu.SemaphoreType.DMA((slots,)),
        ],
        compiler_params=pltpu.CompilerParams(
            has_side_effects=True, vmem_limit_bytes=VMEM_LIMIT
        ),
    )(tall, far, *saved, w_conv, patch)


WEIGHTS = ("qkv", "out", "fc1", "fc2", "proj", "conv")
VECTORS = ("fc1_b", "fc2_b", "ln1_gain", "ln1_bias", "ln2_gain", "ln2_bias")
SAVED = ("x", "q", "k", "v", "o", "logs", "after_attn", "hidden", "tokens_low")
MAPS = ("f0", "first0", "f1", "first1", "coarse")
STAGES = 4


def chunks_of(name, master, whole, dp):
    if name == "conv":
        half = master.shape[1]
        rows = pl.ds(pl.multiple_of(dp * half, 16), half)
        return [(master.at[t], whole.at[t, rows]) for t in range(master.shape[0])]
    half, width = master.shape
    step = half if width > 1024 or half <= 512 else 384
    wide = min(width, 768)
    out = []
    for r in range(0, half, step):
        for c in range(0, width, wide):
            rows = pl.ds(pl.multiple_of(dp * half + r, 16), step)
            out.append((master.at[pl.ds(r, step), pl.ds(c, wide)], whole.at[rows, pl.ds(c, wide)]))
    return out


def forward_kernel(sizes, tiles, lengths, *refs):
    chips, slots, cols = sizes
    tile_rows, tile_cols = tiles
    refs = list(refs)

    def take(names):
        taken = {name: refs.pop(0) for name in names}
        return taken

    tile_in = take(("tokens", "cots", "patches"))
    masters = take(WEIGHTS)
    vectors = refs.pop(0)
    flag = refs.pop(0)
    image_out = take(("cots", "patches"))
    whole_out = take(WEIGHTS)
    vector_out = refs.pop(0)
    saved = take(SAVED)
    maps = take(MAPS)
    image = refs.pop(0)
    whole = take(WEIGHTS)
    far_vectors = refs.pop(0)
    keys, values, f0, hidden_low, flat, wide, stage = (refs.pop(0) for _ in range(7))
    kept = take(("o", "after_attn", "hidden", "first0", "f1", "first1"))
    tile_send, tile_recv, gather_send, gather_recv, vec_send, vec_recv, stage_sem, core_sem, out_sem = refs
    dp, y, core, z = place()
    low, f32 = jnp.bfloat16, jnp.float32

    to_images_start(tile_in["tokens"], image, tile_send.at[0], tile_recv.at[0], sizes)
    vector_copy = send(vectors, far_vectors, vec_send, vec_recv, *mate("dp"))
    vector_copy.start()

    work = [(name, c) for name in WEIGHTS for c in chunks_of(name, masters[name], whole[name], dp)]
    incoming = {}

    def fetch(i):
        if i < len(work):
            source = work[i][1][0]
            slot = stage.at[i % STAGES, pl.ds(0, source.shape[0]), pl.ds(0, source.shape[1])]
            incoming[i] = pltpu.make_async_copy(source, slot, stage_sem.at[i % STAGES])
            incoming[i].start()

    gathers = {
        name: Gather(whole[name], gather_send.at[i], gather_recv.at[i], name in ("qkv", "out"))
        for i, name in enumerate(WEIGHTS)
    }
    done = [0]
    for i in range(STAGES - 1):
        fetch(i)

    def round_next(name):
        while done[0] < len(work) and work[done[0]][0] == name:
            i = done[0]
            fetch(i + STAGES - 1)
            incoming.pop(i).wait()
            target = work[i][1][1]
            target[...] = stage[i % STAGES, : target.shape[0], : target.shape[1]].astype(low)
            done[0] += 1

    def tick(*names):
        for name in names:
            gathers[name].tick()

    out_copies = []

    def keep(src, dst):
        copy = pltpu.make_async_copy(src, dst, out_sem.at[len(out_copies)])
        copy.start()
        out_copies.append(copy)

    round_next("qkv")
    tick("qkv")
    round_next("out")
    tick("out")
    round_next("fc1")
    tick("qkv", "fc1")
    round_next("fc2")
    round_next("proj")
    tick("qkv")
    round_next("conv")
    tick("out", "qkv", "fc1", "fc2")
    gathers["qkv"].finish()
    vector_copy.wait()
    own, far = vectors[...], far_vectors[...]
    vec, at = {}, 0
    for name, length in zip(VECTORS, lengths):
        part = slice(at, at + length)
        row = jnp.concatenate(
            [jnp.where(dp == 0, own, far)[:, part], jnp.where(dp == 0, far, own)[:, part]], axis=1
        )
        vec[name] = row.astype(low).astype(f32)
        vector_out[:, 2 * at : 2 * (at + length)] = vec[name]
        at += length
    to_images_wait(tile_in["tokens"], image, tile_send.at[0], tile_recv.at[0], sizes)
    to_images_start(tile_in["patches"], image_out["patches"], tile_send.at[1], tile_recv.at[1], sizes)

    width = image.shape[3]
    x = jnp.where(flag[0:1, 0:1] > 0, image[1].astype(f32), image[0].astype(f32))
    x = x.reshape(-1, width)
    rows = x.shape[0]
    saved["x"][...] = x.astype(low)
    normed = norm_rows(x, vec["ln1_gain"], vec["ln1_bias"])[0].astype(low)
    mine = pl.ds(0, rows)
    theirs = pl.ds(rows, rows)
    core_copies = []
    for i, ref in ((1, keys), (2, values), (0, None)):
        part = jnp.dot(
            normed, whole["qkv"][:, i * width : (i + 1) * width], preferred_element_type=f32
        ).astype(low)
        if ref is None:
            saved["q"][...] = part
        else:
            ref[mine, :] = part
            copy = send(
                ref.at[mine], ref.at[theirs], core_sem.at[0, i], core_sem.at[1, i], *mate("core")
            )
            copy.start()
            core_copies.append(copy)
    tick("out")
    for copy in core_copies:
        copy.wait()
    tick("fc1", "fc2", "conv", "proj")
    keep(keys, saved["k"])
    keep(values, saved["v"])
    for name in ("qkv",):
        keep(whole[name], whole_out[name])

    for pair in range(width // 128):
        lanes = pl.ds(pair * 128, 128)
        out, logs = attend_pair(saved["q"][:, lanes], keys[:, lanes], values[:, lanes])
        kept["o"][:, lanes] = out
        for h in range(2):
            saved["logs"][pair, h : h + 1, :] = logs[h]
        if pair == 1:
            tick("out")
        if pair == 3:
            tick("fc2")
    gathers["out"].finish()
    tick("fc2", "conv", "proj")
    to_images_start(tile_in["cots"], image_out["cots"], tile_send.at[2], tile_recv.at[2], sizes)
    after_attn = saved["x"][...].astype(f32) + jnp.dot(
        kept["o"][...].astype(low), whole["out"][...], preferred_element_type=f32
    )
    kept["after_attn"][...] = after_attn
    keep(kept["o"], saved["o"])
    keep(kept["after_attn"], saved["after_attn"])
    normed_two = norm_rows(after_attn, vec["ln2_gain"], vec["ln2_bias"])[0].astype(low)
    gathers["fc1"].finish()
    for c in range(0, hidden_low.shape[1], width):
        part = pl.ds(c, width)
        hidden = jnp.dot(normed_two, whole["fc1"][:, part], preferred_element_type=f32)
        hidden = hidden + vec["fc1_b"][:, c : c + width]
        kept["hidden"][:, part] = hidden
        hidden_low[:, part] = jax.nn.gelu(hidden).astype(low)
        if c == width:
            tick("conv", "proj")
    keep(kept["hidden"], saved["hidden"])
    gathers["fc2"].finish()
    after_mlp = kept["after_attn"][...] + (
        jnp.dot(hidden_low[...], whole["fc2"][...], preferred_element_type=f32) + vec["fc2_b"]
    )
    tokens_low = after_mlp.astype(low)
    saved["tokens_low"][...] = tokens_low
    gathers["proj"].finish()

    flat[...] = jnp.dot(tokens_low, whole["proj"][...], preferred_element_type=f32)
    half_rows, line = 2 * tile_rows, cols * tile_cols
    for r in range(half_rows):
        row = turned(core, r, half_rows - 1)
        for zz in range(cols):
            at = ((r // tile_rows) * cols + zz) * tile_rows + r % tile_rows
            f0[block(row * cols + zz, tile_cols), :] = flat[at * tile_cols : (at + 1) * tile_cols, :]
    core_copies = []
    for i in range(HALO):
        copy = send(
            f0.at[pl.ds((half_rows - 1 - i) * line, line)],
            f0.at[pl.ds((half_rows + i) * line, line)],
            core_sem.at[0, 3 + i],
            core_sem.at[1, 3 + i],
            *mate("core"),
        )
        copy.start()
        core_copies.append(copy)
    gathers["conv"].finish()
    for copy in core_copies:
        copy.wait()
    for name in WEIGHTS[1:]:
        keep(whole[name], whole_out[name])
    keep(f0, maps["f0"])
    maps_forward(
        line, rows, f0, kept["first0"], kept["f1"], kept["first1"], whole["conv"], maps["coarse"], wide
    )
    for name in ("first0", "f1", "first1"):
        keep(kept[name], maps[name])
    for copy in out_copies:
        copy.wait()
    to_images_wait(
        tile_in["patches"], image_out["patches"], tile_send.at[1], tile_recv.at[1], sizes
    )
    to_images_wait(tile_in["cots"], image_out["cots"], tile_send.at[2], tile_recv.at[2], sizes)


def run_forward(tile_in, masters, vectors, flag, sizes, tiles):
    chips, slots, cols = sizes
    low, f32 = jnp.bfloat16, jnp.float32
    shape = jax.ShapeDtypeStruct
    tile, width = tile_in[0].shape[1:]
    feat = masters["proj"].shape[1]
    hidden = masters["fc1"].shape[1]
    lengths = [v.shape[0] for v in vectors]
    rows, line = chips * tile, cols * tiles[1]
    ext = rows + HALO * line
    wholes = {
        name: shape(m.shape[:-2] + (2 * m.shape[-2], m.shape[-1]), low) for name, m in masters.items()
    }
    saved = {
        "x": shape((rows, width), low),
        "q": shape((rows, width), low),
        "k": shape((2 * rows, width), low),
        "v": shape((2 * rows, width), low),
        "o": shape((rows, width), f32),
        "logs": shape((width // 128, 2, rows), f32),
        "after_attn": shape((rows, width), f32),
        "hidden": shape((rows, hidden), f32),
        "tokens_low": shape((rows, width), low),
    }
    maps = {name: shape((ext, feat), f32) for name in MAPS[:-1]}
    maps["coarse"] = shape((rows + 2 * line, feat), low)
    far = [shape((2, chips) + t.shape[1:], t.dtype) for t in tile_in]
    hbm, vmem = pl.BlockSpec(memory_space=pltpu.HBM), pl.BlockSpec(memory_space=pltpu.VMEM)
    out_shape = (
        far[1:]
        + [wholes[name] for name in WEIGHTS]
        + [shape((1, 2 * sum(lengths)), f32)]
        + [saved[name] for name in SAVED]
        + [maps[name] for name in MAPS]
    )
    out_specs = (
        [hbm] * (2 + len(WEIGHTS))
        + [vmem]
        + [hbm if name in ("k", "v", "o", "after_attn", "hidden") else vmem for name in SAVED]
        + [vmem if name == "coarse" else hbm for name in MAPS]
    )
    n = len(WEIGHTS)
    outs = pl.pallas_call(
        functools.partial(forward_kernel, sizes, tiles, lengths),
        out_shape=out_shape,
        in_specs=[hbm] * (3 + n) + [vmem] * 2,
        out_specs=out_specs,
        scratch_shapes=[pltpu.VMEM(far[0].shape, low)]
        + [pltpu.VMEM(wholes[name].shape, low) for name in WEIGHTS]
        + [pltpu.VMEM((1, sum(lengths)), f32)]
        + [
            pltpu.VMEM((2 * rows, width), low),
            pltpu.VMEM((2 * rows, width), low),
            pltpu.VMEM((ext, feat), f32),
            pltpu.VMEM((rows, hidden), low),
            pltpu.VMEM((rows, feat), f32),
            pltpu.VMEM((ext + 2 * line, 3 * feat), low),
            pltpu.VMEM((STAGES, 384, 768), f32),
            pltpu.VMEM((rows, width), f32),
            pltpu.VMEM((rows, width), f32),
            pltpu.VMEM((rows, hidden), f32),
            pltpu.VMEM((ext, feat), f32),
            pltpu.VMEM((ext, feat), f32),
            pltpu.VMEM((ext, feat), f32),
            pltpu.SemaphoreType.DMA((3, slots)),
            pltpu.SemaphoreType.DMA((3, 2 * chips)),
            pltpu.SemaphoreType.DMA((n, 2, 4)),
            pltpu.SemaphoreType.DMA((n, 2, 4)),
            pltpu.SemaphoreType.DMA,
            pltpu.SemaphoreType.DMA,
            pltpu.SemaphoreType.DMA((STAGES,)),
            pltpu.SemaphoreType.DMA((2, 3 + HALO)),
            pltpu.SemaphoreType.DMA((n + 9,)),
        ],
        compiler_params=pltpu.CompilerParams(
            has_side_effects=True, vmem_limit_bytes=VMEM_LIMIT
        ),
    )(
        *tile_in,
        *(masters[name] for name in WEIGHTS),
        jnp.concatenate(vectors)[None],
        flag,
    )
    outs = list(outs)
    images = [outs.pop(0) for _ in range(2)]
    weights = {name: outs.pop(0) for name in WEIGHTS}
    joined, vec, at = outs.pop(0), {}, 0
    for name, length in zip(VECTORS, lengths):
        vec[name] = joined[:, 2 * at : 2 * (at + length)]
        at += length
    return (images, weights, vec) + tuple(
        {name: outs.pop(0) for name in names} for names in (SAVED, MAPS)
    )


def swap_cores(value):
    return lax.ppermute(value, "row", [(0, 1), (1, 0), (2, 3), (3, 2)])


def halve_patch(grad, axis):
    grad = jnp.moveaxis(grad, axis, 0)
    even, odd = grad[0::2], grad[1::2]
    zero = jnp.zeros_like(even[:1])
    middle = jnp.concatenate([zero, 0.75 * (even + odd), zero])
    before = jnp.concatenate([0.25 * even, zero, zero])
    after = jnp.concatenate([zero, zero, 0.25 * odd])
    return jnp.moveaxis(middle + before + after, 0, axis)


def on_chip(
    chips,
    tokens,
    cot_tokens,
    cot_merged,
    image_counts,
    scale_flags,
    shift_flags,
    qkv_w,
    attn_out_w,
    fc1_w,
    fc1_b,
    fc2_w,
    fc2_b,
    ln1_gain,
    ln1_bias,
    ln2_gain,
    ln2_bias,
    proj_w,
    conv_w,
    head_w,
    head_b,
    shift_row,
):
    slots, tile_rows, tile_cols, width = tokens.shape
    cols = lax.axis_size("col")
    sizes = (chips, slots, cols)
    tile = tile_rows * tile_cols
    feat = proj_w.shape[1]
    half_rows, all_cols = 2 * tile_rows, cols * tile_cols
    dp, y, core, z = place()
    low = jnp.bfloat16
    count = image_counts[0]
    present = (jnp.arange(slots) < count).astype(jnp.float32)
    factor = 0.5 + 0.5 * scale_flags.astype(jnp.float32)
    shift_sign = shift_flags.astype(jnp.float32)
    full_group = count == slots
    chip = slot_of(y, z, cols)
    borrowed = jnp.logical_and(jnp.logical_not(full_group), chip >= 2 * chips - slots)
    image_present = jnp.where(
        jnp.logical_or(jnp.logical_or(full_group, borrowed), chip < count), 1.0, 0.0
    )

    def both_halves(value):
        far = lax.ppermute(value, "dp", [(0, 1), (1, 0)])
        return jnp.where(dp == 0, jnp.stack([value, far]), jnp.stack([far, value]))

    w_head = both_halves(head_w.astype(low)).reshape(feat, feat)
    rows_small = both_halves(jnp.stack([head_b, shift_row]))
    b_head, w_shift = (
        rows_small[:, i].reshape(-1).astype(low).astype(jnp.float32) for i in range(2)
    )

    merged_grad = cot_merged.astype(jnp.float32).reshape(slots, -1, feat) * present[:, None, None]
    grad_shift = jnp.sum(merged_grad * shift_sign[:, None, None], (0, 1))
    head_grad = (merged_grad * factor[:, None, None]).astype(low).reshape(-1, feat)
    grad_head_b = jnp.sum(head_grad.astype(jnp.float32), 0)
    fine_grad = back_product(head_grad, w_head).astype(low).reshape(cot_merged.shape)
    patch_grad = halve_patch(halve_patch(fine_grad.astype(jnp.float32), 1), 2).astype(low)
    cells = (tile_rows + 2) * (tile_cols + 2)
    patch_grad = jnp.pad(
        patch_grad.reshape(slots, cells, feat), ((0, 0), (0, PATCH - cells), (0, 0))
    )

    vectors = (fc1_b, fc2_b, ln1_gain, ln1_bias, ln2_gain, ln2_bias)
    (image_cots, image_patches), weights, vec, saved, maps = run_forward(
        (tokens.reshape(slots, tile, width), cot_tokens.reshape(slots, tile, width), patch_grad),
        {
            "qkv": qkv_w,
            "out": attn_out_w,
            "fc1": fc1_w,
            "fc2": fc2_w,
            "proj": proj_w,
            "conv": conv_w.reshape((36,) + conv_w.shape[3:]),
        },
        vectors,
        jnp.full((8, 128), borrowed.astype(jnp.float32)),
        sizes,
        (tile_rows, tile_cols),
    )
    w_qkv, w_out, w_up, w_down, w_proj, w_conv = (weights[name] for name in WEIGHTS)
    gain_one, bias_one, gain_two, bias_two = (vec[name] for name in VECTORS[2:])

    def chosen(pair):
        return jnp.where(borrowed, pair[1], pair[0])

    rows = chips * tile
    tiles = (tile_rows, tile_cols)
    tokens_low = saved["tokens_low"]

    coarse = maps["coarse"].reshape(half_rows + 2, all_cols, feat)
    coarse = jnp.concatenate([coarse[:, :1], coarse, coarse[:, -1:]], 1)
    cuts = [
        coarse[
            r * tile_rows : (r + 1) * tile_rows + 2, c * tile_cols : (c + 1) * tile_cols + 2
        ].reshape(cells, feat)
        for r in range(2)
        for c in range(cols)
    ]
    patch = jnp.pad(jnp.stack(cuts), ((0, 0), (0, PATCH - cells), (0, 0)))
    parts = chosen(image_patches)[:, :cells].astype(jnp.float32)
    parts = parts.reshape(2, cols, tile_rows + 2, tile_cols + 2, feat)
    wide = sum(
        jnp.pad(parts[:, c], ((0, 0), (0, 0), (c * tile_cols, (cols - 1 - c) * tile_cols), (0, 0)))
        for c in range(cols)
    )
    wide = jnp.concatenate(
        [wide[:, :, 1:2] + wide[:, :, :1], wide[:, :, 2:-2], wide[:, :, -2:-1] + wide[:, :, -1:]], 2
    )
    tall = jnp.pad(wide[0], ((0, tile_rows), (0, 0), (0, 0))) + jnp.pad(
        wide[1], ((tile_rows, 0), (0, 0), (0, 0))
    )
    tall = tall.reshape(-1, feat)
    *grad_conv, proj_grad, slot_patch = maps_backward(
        tall, swap_cores(tall), [maps[name] for name in MAPS[:-1]], w_conv, patch, slots, tiles, cols
    )
    grad_conv = early_sum(*(g.reshape(36, feat, feat // 2) for g in grad_conv), TURNS["conv"][0])

    normed_two, scaled_two, factor_two = norm_rows(saved["after_attn"], gain_two, bias_two)
    normed_two_low = normed_two.astype(low)
    hidden = saved["hidden"]
    hidden_low = jax.nn.gelu(hidden).astype(low)
    attended = saved["o"].astype(low)
    grad_proj = outer_product(tokens_low, proj_grad)
    stream_grad = chosen(image_cots).reshape(rows, width).astype(jnp.float32)
    stream_grad = jnp.where(image_present > 0, stream_grad, 0.0) + back_product(proj_grad, w_proj)
    grad_conv, stream_grad = lax.optimization_barrier((grad_conv, stream_grad))
    grad_conv = (grad_conv[0], across(grad_conv[1], TURNS["conv"][0]))
    down_grad = stream_grad.astype(low)
    grad_down_b = jnp.sum(down_grad.astype(jnp.float32), 0)

    def halves_of(first_op, second_op):
        half = second_op.shape[1] // 2
        return [
            outer_product(
                first_op, lax.dynamic_slice_in_dim(second_op, side * half, half, 1)
            ).astype(low)[None]
            for side in (core, 1 - core)
        ]

    grad_down_w = early_sum(*halves_of(hidden_low, down_grad), TURNS["fc2"][0])
    up_grad = gelu_grad(hidden, back_product(down_grad, w_down)).astype(low)
    grad_up_b = jnp.sum(up_grad.astype(jnp.float32), 0)
    grad_up_w = early_sum(*halves_of(normed_two_low, up_grad), TURNS["fc1"][0])
    norm_grad, grad_gain_two, grad_bias_two = norm_back(
        back_product(up_grad, w_up), scaled_two, factor_two, gain_two
    )
    stream_grad = stream_grad + norm_grad
    branch_grad = stream_grad.astype(low)
    grad_out_w = outer_product(attended, branch_grad)
    attended_grad = back_product(branch_grad, w_out).astype(low)
    slot_patch, grad_up_b = lax.optimization_barrier((slot_patch, grad_up_b))
    patch = slot_patch[:, :cells]
    patch = patch.reshape(slots, tile_rows + 2, tile_cols + 2, feat).astype(jnp.float32)
    patch = jnp.where(present[:, None, None, None] > 0, patch, 0.0)
    upsampled = double_axis(double_axis(patch, 1), 2).astype(low)
    fine_rows = upsampled.reshape(-1, feat)
    head_out = jnp.dot(fine_rows, w_head, preferred_element_type=jnp.float32) + b_head
    head_out = head_out.reshape(slots, -1, feat)
    merged = (head_out * factor[:, None, None] + shift_sign[:, None, None] * w_shift) * present[
        :, None, None
    ]
    merged_out = merged.astype(low).reshape(cot_merged.shape)
    grad_head_w = outer_product(fine_rows, head_grad)

    blank = jnp.zeros((2, (width // 2 + feat - 1) // feat * feat), jnp.float32)
    packed = []
    for v in (grad_up_b, grad_down_b, None, None, grad_gain_two, grad_bias_two, grad_head_b, grad_shift):
        if v is None:
            packed.append(blank)
            continue
        v = v.reshape(2, -1)
        packed.append(jnp.pad(v, ((0, 0), (0, -v.shape[1] % feat))))
    starts, at = [], 0
    for v in packed:
        starts.append(at)
        at += v.shape[1]
    packed = jnp.pad(jnp.concatenate(packed, 1), ((0, 0), (0, 128 * feat - at)))
    slot_tokens, slot_grads, sums = run_backward(
        {
            **{name: saved[name] for name in ("q", "k", "v", "o", "logs", "x")},
            "g": attended_grad,
            "stream": stream_grad,
            "w_qkv": w_qkv,
            "gain": gain_one,
            "bias": bias_one,
            "small": packed.reshape(256, feat),
        },
        tokens_low.reshape(chips, tile, width),
        {"conv": grad_conv, "fc2": grad_down_w, "fc1": grad_up_w},
        {
            "out": grad_out_w.astype(low)[None],
            "proj": grad_proj.astype(low)[None],
            "head": grad_head_w.astype(low)[None],
        },
        sizes,
    )
    here = present[:, None, None] > 0
    tokens_out = jnp.where(here, slot_tokens, 0).reshape(tokens.shape)
    grad_tokens = jnp.where(here, slot_grads.astype(jnp.float32), 0.0).reshape(tokens.shape)
    sums = {name: value.astype(jnp.float32) for name, value in sums.items()}
    packed = sums["small"].reshape(-1)
    pieces = [
        packed[at : at + v.shape[0]] for at, v in zip(starts, vectors + (head_b, shift_row))
    ]
    return (
        tokens_out,
        merged_out,
        grad_tokens,
        sums["qkv"][0],
        sums["out"][0],
        sums["fc1"][0],
        pieces[0],
        sums["fc2"][0],
        pieces[1],
        pieces[2],
        pieces[3],
        pieces[4],
        pieces[5],
        sums["proj"][0],
        sums["conv"].reshape(conv_w.shape),
        sums["head"][0],
        pieces[6],
        pieces[7],
    )


def solution(mesh):
    groups, tile_rows, tile_cols = (mesh.shape[axis] for axis in ("dp", "row", "col"))
    chips = tile_rows // 2 * tile_cols
    fits = groups == 2 and tile_rows == 4 and tile_cols == 4
    placed = (
        P("dp", "row", "col", None),
        P("dp", "row", "col", None),
        P("dp", "row", "col", None),
        P("dp"),
        P("dp"),
        P("dp"),
        P("dp", None),
        P("dp", None),
        P("dp", None),
        P("dp"),
        P("dp", None),
        P("dp"),
        P("dp"),
        P("dp"),
        P("dp"),
        P("dp"),
        P("dp", None),
        P(None, None, None, "dp", None),
        P("dp", None),
        P("dp"),
        P("dp"),
    )
    return jax.shard_map(
        functools.partial(on_chip, chips) if fits else on_device,
        mesh=mesh,
        in_specs=placed,
        out_specs=(
            P("dp", "row", "col", None),
            P("dp", "row", "col", None),
            P("dp", "row", "col", None),
            P("dp", None),
            P("dp", None),
            P("dp", None),
            P("dp"),
            P("dp", None),
            P("dp"),
            P("dp"),
            P("dp"),
            P("dp"),
            P("dp"),
            P("dp", None),
            P(None, None, None, "dp", None),
            P("dp", None),
            P("dp"),
            P("dp"),
        ),
        check_vma=False,
    )
```
